32 devices in a mesh: ctx: 8 (over z, y), uly: 4 (over x, core).
Axes of the slice: x: 2, y: 2, z: 4, core: 2. Of those that a mesh axis runs over, the one named last changes fastest.
Arguments:
- queries: bfloat16 [4096, 32, 128], P(('ctx', 'uly')), may hold values from -20 to 20
- keys: bfloat16 [4096, 8, 128], P(('ctx', 'uly')), may hold values from -20 to 20
- values: bfloat16 [4096, 8, 128], P(('ctx', 'uly')), may hold values from -6 to 6
- grad_out: bfloat16 [4096, 32, 128], P(('ctx', 'uly')), may hold values from -6 to 6
- doc_lengths: int32 [16], replicated, may hold values from 1 to 512, 4096 in all
Outputs:
- grad_queries: bfloat16 [4096, 32, 128], P(('ctx', 'uly'))
- grad_keys: bfloat16 [4096, 8, 128], P(('ctx', 'uly'))
- grad_values: bfloat16 [4096, 8, 128], P(('ctx', 'uly'))
The draws below stay inside these ranges and needn't reach their ends.
Inputs may be any that keep to these rules, and one draw needn't show every extreme that they name: `doc_lengths`: positive lengths that sum to 4096; the longest document has exactly 512 tokens.
All inputs are finite; a program needn't handle non-finite values.
Results may differ from the reference program's by a relative error of at most 0.0069.
Values may be sent and summed in bfloat16 or wider, within the bound.
No kernel may reach another device: no remote copies, remote signals or barrier semaphores. Data moves between devices by JAX's collectives and lax.ppermute only.
A program may use at most 64 MiB of HBM per device.

```python
import math
import jax
import jax.numpy as jnp
import numpy as np
from jax import lax

H = 32
KVH = 8
HD = 128
CTX_TOK = 512
SEQ = 4096
MAX_DOC = 512
DOCS = 16


def draw_queries(key, part):
    fresh = jax.random.fold_in(key, 21)
    return jnp.clip(jax.random.normal(fresh, (SEQ, H, HD), jnp.float32), -5.0, 5.0).astype(jnp.bfloat16)


def draw_keys(key, part):
    fresh = jax.random.fold_in(key, 22)
    return jnp.clip(jax.random.normal(fresh, (SEQ, KVH, HD), jnp.float32), -5.0, 5.0).astype(jnp.bfloat16)


def levels(own_key, dims, pieces, low, largest):
    level = 1.0
    for axis_at, parts in pieces:
        steps = jax.random.uniform(jax.random.fold_in(jax.random.fold_in(own_key, 6), axis_at), (parts,), jnp.float32, low / len(pieces), largest / len(pieces))
        level = level * jnp.repeat(jnp.exp(steps), dims[axis_at] // parts).reshape((-1,) + (1,) * (len(dims) - 1 - axis_at))
    return level


def length_profile(number_of, total, reach, slope):
    weights = [(1 << 20) // math.isqrt(standing ** slope) + 1 for standing in range(2, number_of + 1)]
    rest, holding = total - reach - (number_of - 1), [1] * (number_of - 1)
    while rest > 0:
        free = [i for i in range(number_of - 1) if holding[i] < reach]
        whole, budget = sum([weights[i] for i in free]), rest
        for i in free:
            more = min(reach - holding[i], max(1, budget * weights[i] // whole), rest)
            holding[i] = holding[i] + more
            rest = rest - more
    return np.array([reach] + holding)


def ragged_sizes(own_key, amount, total, bound, skew):
    if amount == 2:
        one = jax.random.randint(own_key, (), max(1, total - bound), min(bound, total - 1) + 1)
        return jnp.stack([one, total - one])
    lengths = jnp.asarray(length_profile(amount, total, bound, skew), jnp.int32)
    couples = (amount - 1) // 2
    source_of, sink = lengths[1:1 + 2 * couples:2], lengths[2:2 + 2 * couples:2]
    margin = jnp.minimum(source_of - 1, bound - sink)
    shifted = jax.random.randint(jax.random.fold_in(own_key, 1), (couples,), 0, 1 << 20) % (margin + 1)
    lengths = lengths.at[1:1 + 2 * couples:2].set(source_of - shifted).at[2:2 + 2 * couples:2].set(sink + shifted)
    return lengths[jax.random.permutation(jax.random.fold_in(own_key, 2), amount)]


def bell_draw(stream_key, extent, scale, limit, cuts=(), kind=jnp.bfloat16):
    array = jax.random.normal(stream_key, extent, jnp.float32) * scale
    if len(cuts) > 0:
        array = levels(stream_key, extent, cuts, -0.22, 0.18) * array
    return jnp.clip(array, min=-limit, max=limit).astype(kind)


def setup_inputs(seed: int = 0) -> dict:
    arg_keys = jax.random.split(jax.random.key(seed), 6)
    queries = draw_queries(jax.random.fold_in(arg_keys[5], 71), 0)
    keys = draw_keys(jax.random.fold_in(arg_keys[5], 71), 0)
    values = bell_draw(arg_keys[2], (SEQ, KVH, HD), 1.0, 6.0, ((0, 32),))
    grad_out = bell_draw(arg_keys[3], (SEQ, H, HD), 1.0, 6.0, ((0, 32),))
    doc_lengths = ragged_sizes(arg_keys[4], DOCS, SEQ, MAX_DOC, 2).astype(jnp.int32)
    return {"queries": queries, "keys": keys, "values": values, "grad_out": grad_out, "doc_lengths": doc_lengths}


def doc_number(positions, doc_ends):
    return jnp.sum((positions[:, None] >= doc_ends[None, :]).astype(jnp.int32), axis=1)


def reference(queries, keys, values, grad_out, doc_lengths):
    group_size = H // KVH
    softmax_scale = HD ** -0.5
    doc_ends = jnp.cumsum(doc_lengths).astype(jnp.int32)
    window = MAX_DOC + CTX_TOK
    padding = jnp.zeros((MAX_DOC, KVH, HD), keys.dtype)
    padded_keys = jnp.concatenate([padding, keys], axis=0)
    padded_values = jnp.concatenate([padding, values], axis=0)
    grouped_query_rows = queries.reshape(SEQ, KVH, group_size, HD)
    grouped_output_gradient = grad_out.reshape(SEQ, KVH, group_size, HD)

    def per_block(carry, block_number):
        grad_k, grad_v = carry
        offset = (block_number * CTX_TOK).astype(jnp.int32)
        query_tile_rows = lax.dynamic_slice_in_dim(grouped_query_rows, offset, CTX_TOK, 0).astype(jnp.float32)
        output_gradient_block = lax.dynamic_slice_in_dim(grouped_output_gradient, offset, CTX_TOK, 0).astype(jnp.float32)
        key_tile_rows = lax.dynamic_slice_in_dim(padded_keys, offset, window, 0).astype(jnp.float32)
        value_tile_rows = lax.dynamic_slice_in_dim(padded_values, offset, window, 0).astype(jnp.float32)
        query_pos = offset + jnp.arange(CTX_TOK, dtype=jnp.int32)
        key_pos = offset - MAX_DOC + jnp.arange(window, dtype=jnp.int32)
        query_doc = doc_number(query_pos, doc_ends)
        key_doc = doc_number(key_pos, doc_ends)
        allowed = (key_doc[None, :] == query_doc[:, None]) & (key_pos[None, :] <= query_pos[:, None]) & (key_pos[None, :] >= 0)
        logit_scores = jnp.einsum("nyej,xyj->yenx", query_tile_rows, key_tile_rows) * softmax_scale
        row_max = jnp.max(jnp.where(allowed, logit_scores, -1.0e30), axis=-1)
        expo = jnp.where(allowed, jnp.exp(logit_scores - row_max[..., None]), 0.0)
        log_total = row_max + jnp.log(jnp.sum(expo, axis=-1))
        prob = jnp.where(allowed, jnp.exp(logit_scores - log_total[..., None]), 0.0)
        probability_gradient = jnp.einsum("nyej,xyj->yenx", output_gradient_block, value_tile_rows)
        delta = jnp.sum(prob * probability_gradient, axis=-1)
        dscore = prob * (probability_gradient - delta[..., None])
        probability_block = lax.optimization_barrier(prob.astype(jnp.bfloat16)).astype(jnp.float32)
        score_gradient_block = lax.optimization_barrier(dscore.astype(jnp.bfloat16)).astype(jnp.float32)
        query_gradient = (jnp.einsum("evnz,zej->nevj", score_gradient_block, key_tile_rows) * softmax_scale).astype(jnp.bfloat16)
        partial_key_gradient = jnp.einsum("etpr,peti->rei", score_gradient_block, query_tile_rows) * softmax_scale
        partial_value_gradient = jnp.einsum("etpr,peti->rei", probability_block, output_gradient_block)
        grad_k = lax.dynamic_update_slice_in_dim(grad_k, lax.dynamic_slice_in_dim(grad_k, offset, window, 0) + partial_key_gradient, offset, 0)
        grad_v = lax.dynamic_update_slice_in_dim(grad_v, lax.dynamic_slice_in_dim(grad_v, offset, window, 0) + partial_value_gradient, offset, 0)
        return (grad_k, grad_v), query_gradient

    start_k = jnp.zeros((MAX_DOC + SEQ, KVH, HD), jnp.float32)
    start_v = jnp.zeros((MAX_DOC + SEQ, KVH, HD), jnp.float32)
    (grad_k, grad_v), query_gradient = lax.scan(per_block, (start_k, start_v), jnp.arange(SEQ // CTX_TOK, dtype=jnp.int32))
    grad_queries = query_gradient.reshape(SEQ, H, HD)
    grad_keys = grad_k[MAX_DOC:].astype(jnp.bfloat16)
    grad_values = grad_v[MAX_DOC:].astype(jnp.bfloat16)
    return (grad_queries, grad_keys, grad_values)
```

```python
import functools

import jax
import jax.numpy as jnp
from jax import lax
from jax.experimental import pallas as pl
from jax.experimental.pallas import tpu as pltpu
from jax.sharding import PartitionSpec as P

AXES = ("ctx", "uly")
LOG2E = 1.4426950408889634
MASKED = -1e30


def shifted(array, device_count, by, swap):
    pairs = []
    for d in range(device_count):
        to = (d ^ 1 if swap else d) + by
        if 0 <= to < device_count:
            pairs.append((d, to))
    return lax.ppermute(array, AXES, pairs)


def grads_kernel(halo, group, place_ref, lengths_ref, *refs):
    kv_refs = refs[: 2 * (halo + 1)]
    qd_refs = refs[2 * (halo + 1) : 2 * (halo + 1) + 2]
    outs = refs[2 * (halo + 1) + 2 : -3]
    dkv_refs, dq_refs = outs[: 2 * (halo + 1)], outs[2 * (halo + 1) :]
    kv_scr, qd_scr, acc = refs[-3:]
    tokens, dim = kv_refs[0].shape[2:]
    core, window_start = place_ref[0], place_ref[1]
    blocks = 2 * halo + 1
    keys = blocks * tokens
    scale = dim**-0.5

    for back in range(halo + 1):
        at = 2 * (halo - back)
        kv_scr[at + core] = kv_refs[2 * back][0]
        kv_scr[at + 1 - core] = kv_refs[2 * back + 1][0]
    qd_scr[core] = qd_refs[0][0]
    qd_scr[1 - core] = qd_refs[1][0]

    lane = lax.broadcasted_iota(jnp.int32, (1, tokens), 1)
    for e in range(2):
        query_pos = lane + (2 * halo + e) * tokens

        def start_of(d, carry):
            start, first = carry
            first = jnp.where(query_pos + window_start >= start, start, first)
            return start + lengths_ref[d], first

        _, first = lax.fori_loop(
            0, lengths_ref.shape[0], start_of, (jnp.int32(0), jnp.zeros((1, tokens), jnp.int32))
        )
        first = first - window_start
        key_pos = lax.broadcasted_iota(jnp.int32, (keys, tokens), 0) + e * tokens
        allowed = (key_pos >= first) & (key_pos <= query_pos)
        k = kv_scr[pl.ds(e, blocks), 0].reshape(keys, dim)
        v = kv_scr[pl.ds(e, blocks), 1].reshape(keys, dim)
        q = qd_scr[e, 0].reshape(group * tokens, dim)
        do = qd_scr[e, 1].reshape(group * tokens, dim)
        probs, dscores = [], []
        for g in range(group):
            rows = slice(g * tokens, (g + 1) * tokens)
            nt = (((1,), (1,)), ((), ()))
            s = lax.dot_general(k, q[rows], nt, preferred_element_type=jnp.float32)
            dp = lax.dot_general(v, do[rows], nt, preferred_element_type=jnp.float32)
            s = jnp.where(allowed, s, MASKED)
            top = jnp.max(s, axis=0, keepdims=True)
            w = jnp.exp2((s - top) * (scale * LOG2E))
            inv = 1.0 / jnp.sum(w, axis=0, keepdims=True)
            delta = jnp.sum(w * dp, axis=0, keepdims=True) * inv
            p = w * inv
            probs.append(p.astype(jnp.bfloat16))
            dscores.append((p * (dp - delta)).astype(jnp.bfloat16))
        p = jnp.concatenate(probs, axis=1)
        ds = jnp.concatenate(dscores, axis=1)
        dv = jnp.dot(p, do, preferred_element_type=jnp.float32)
        dk = jnp.dot(ds, q, preferred_element_type=jnp.float32) * scale
        dqt = jnp.dot(k.T, ds, preferred_element_type=jnp.float32) * scale
        for g in range(group):
            dq = dqt[:, g * tokens : (g + 1) * tokens].T
            qd_scr[e, 0, g] = dq.astype(jnp.bfloat16)
        dk = dk.reshape(blocks, tokens, dim)
        dv = dv.reshape(blocks, tokens, dim)
        if e == 0:
            acc[:blocks, 0] = dk
            acc[:blocks, 1] = dv
            acc[blocks] = jnp.zeros_like(acc[blocks])
        else:
            acc[1:, 0] += dk
            acc[1:, 1] += dv

    for back in range(halo + 1):
        at = 2 * (halo - back)
        for swap in range(2):
            out = dkv_refs[2 * back + swap]
            out[0] = acc[at + (1 - core if swap else core)].astype(out.dtype)
    dq_refs[0][0] = qd_scr[core, 0]
    dq_refs[1][0] = qd_scr[1 - core, 0]


def grads(place, lengths, kvs, qds):
    heads, _, group, tokens, dim = qds[0].shape
    halo = len(kvs) // 2 - 1
    kv_spec = pl.BlockSpec((1, 2, tokens, dim), lambda h, *_: (h, 0, 0, 0))
    qd_spec = pl.BlockSpec((1, 2, group, tokens, dim), lambda h, *_: (h, 0, 0, 0, 0))
    dq_spec = pl.BlockSpec((1, group, tokens, dim), lambda h, *_: (h, 0, 0, 0))
    dkv_shape = (heads, 2, tokens, dim)
    outs = [jax.ShapeDtypeStruct(dkv_shape, jnp.float32 if i == 0 else jnp.bfloat16) for i in range(len(kvs))]
    outs += [jax.ShapeDtypeStruct((heads, group, tokens, dim), jnp.bfloat16)] * 2
    window = 2 * halo + 2
    products = 5 * 2 * heads * group * 2 * tokens * (window - 1) * tokens * dim
    return pl.pallas_call(
        functools.partial(grads_kernel, halo, group),
        out_shape=outs,
        grid_spec=pltpu.PrefetchScalarGridSpec(
            num_scalar_prefetch=2,
            grid=(heads,),
            in_specs=[kv_spec] * len(kvs) + [qd_spec] * 2,
            out_specs=[kv_spec] * len(kvs) + [dq_spec] * 2,
            scratch_shapes=[
                pltpu.VMEM((window, 2, tokens, dim), jnp.bfloat16),
                pltpu.VMEM((2, 2, group, tokens, dim), jnp.bfloat16),
                pltpu.VMEM((window, 2, tokens, dim), jnp.float32),
            ],
        ),
        compiler_params=pltpu.CompilerParams(vmem_limit_bytes=48 * 2**20),
        cost_estimate=pl.CostEstimate(flops=products, bytes_accessed=8 * 2**20, transcendentals=0),
        name="grads",
    )(place, lengths, *kvs, *qds)


def local(queries, keys, values, grad_out, doc_lengths):
    uly_count = lax.axis_size("uly")
    device_count = lax.axis_size("ctx") * uly_count
    halo = uly_count // 2
    device = lax.axis_index("ctx") * uly_count + lax.axis_index("uly")
    core = device % 2
    tokens, heads, dim = queries.shape
    key_heads = keys.shape[1]
    group = heads // key_heads
    half = key_heads // 2

    kv = jnp.stack([keys, values]).reshape(2, tokens, 2, half, dim).transpose(2, 3, 0, 1, 4)
    kv_same = lax.dynamic_index_in_dim(kv, core, 0, keepdims=False)
    kv_cross = lax.dynamic_index_in_dim(kv, 1 - core, 0, keepdims=False)
    qd = jnp.stack([queries, grad_out]).reshape(2, tokens, 2, half, group, dim).transpose(2, 3, 0, 4, 1, 5)
    qd_same = lax.dynamic_index_in_dim(qd, core, 0, keepdims=False)
    qd_cross = lax.dynamic_index_in_dim(qd, 1 - core, 0, keepdims=False)

    kvs = [kv_same, shifted(kv_cross, device_count, 0, True)]
    for back in range(1, halo + 1):
        kvs.append(shifted(kv_same, device_count, 2 * back, False))
        kvs.append(shifted(kv_cross, device_count, 2 * back, True))
    qds = [qd_same, shifted(qd_cross, device_count, 0, True)]

    place = jnp.stack([core, (device // 2 - halo) * (2 * tokens)]).astype(jnp.int32)
    outs = grads(place, doc_lengths, kvs, qds)
    dkvs, (dq_same, dq_cross) = outs[:-2], outs[-2:]

    dkv_same = dkvs[0]
    dkv_cross = shifted(dkvs[1], device_count, 0, True).astype(jnp.float32)
    for back in range(1, halo + 1):
        dkv_same = dkv_same + shifted(dkvs[2 * back], device_count, -2 * back, False).astype(jnp.float32)
        dkv_cross = dkv_cross + shifted(dkvs[2 * back + 1], device_count, -2 * back, True).astype(jnp.float32)
    dq_cross = shifted(dq_cross, device_count, 0, True)

    def ordered(same, cross):
        low = jnp.where(core == 0, same, cross)
        high = jnp.where(core == 0, cross, same)
        return jnp.concatenate([low, high], axis=0)

    dkv = ordered(dkv_same, dkv_cross).astype(jnp.bfloat16).transpose(1, 2, 0, 3)
    dq = ordered(dq_same, dq_cross).transpose(2, 0, 1, 3).reshape(tokens, heads, dim)
    return dq, dkv[0], dkv[1]


def solution(mesh):
    spec = P(AXES, None, None)
    return jax.shard_map(
        local, mesh=mesh, in_specs=(spec,) * 4 + (P(),), out_specs=(spec,) * 3, check_vma=False
    )
```

```python
import functools

import jax
import jax.numpy as jnp
from jax import lax
from jax.experimental import pallas as pl
from jax.experimental.pallas import tpu as pltpu
from jax.sharding import PartitionSpec as P

AXES = ("ctx", "uly")
LOG2E = 1.4426950408889634
MASKED = -1e30
BF16, F32 = jnp.bfloat16, jnp.float32
NT = (((1,), (1,)), ((), ()))
VMEM_BYTES = 40 * 2**20


def moved(array, device_count, by):
    pairs = [(d, d + by) for d in range(device_count) if 0 <= d + by < device_count]
    return lax.ppermute(array, AXES, pairs)


def swapped(array, device_count):
    return lax.ppermute(array, AXES, [(d, d ^ 1) for d in range(device_count)])


def call(kernel, name, grid, place, inputs, in_specs, outs, out_specs, scratch, flops):
    scalars = place if isinstance(place, tuple) else (place,)
    return pl.pallas_call(
        kernel,
        out_shape=outs,
        grid_spec=pltpu.PrefetchScalarGridSpec(
            num_scalar_prefetch=len(scalars),
            grid=grid,
            in_specs=in_specs,
            out_specs=out_specs,
            scratch_shapes=scratch,
        ),
        compiler_params=pltpu.CompilerParams(vmem_limit_bytes=VMEM_BYTES),
        cost_estimate=pl.CostEstimate(flops=flops, bytes_accessed=2**20, transcendentals=0),
        name=name,
    )(*scalars, *inputs)


def arrange_kernel(group, place_ref, q_ref, do_ref, q_other_ref, do_other_ref, out_ref, scr):
    core = place_ref[0]
    rows, heads, dim = q_ref.shape
    for kind, (own, other) in enumerate([(q_ref, q_other_ref), (do_ref, do_other_ref)]):
        for which, ref in enumerate([own, other]):
            block = 1 - core if which else core
            scr[...] = ref[...].astype(F32).reshape(rows * heads, dim)
            for h in range(heads):
                out_ref[h // group, block, kind, h % group] = scr[pl.ds(h, rows, stride=heads), :].astype(BF16)


def arrange(place, queries, grad_out, q_other, do_other, key_heads):
    tokens, heads, dim = queries.shape
    half, group = heads // 2, heads // key_heads
    rows = 32
    in_spec = pl.BlockSpec((rows, half, dim), lambda i, place: (i, place[0], 0))
    out = (key_heads // 2, 2, 2, group, tokens, dim)
    return call(
        functools.partial(arrange_kernel, group),
        "arrange",
        (tokens // rows,),
        place,
        (queries, grad_out, q_other, do_other),
        [in_spec] * 4,
        jax.ShapeDtypeStruct(out, BF16),
        pl.BlockSpec(out[:4] + (rows, dim), lambda i, place: (0, 0, 0, 0, i, 0)),
        [pltpu.VMEM((rows * half, dim), F32)],
        10**9,
    )


def spread(block_refs, core, wide):
    tokens, heads, dim = block_refs[0].shape
    halo = len(block_refs) // 2 - 1
    for back in range(halo + 1):
        at = 2 * (halo - back)
        wide[at + core] = block_refs[2 * back][...].astype(F32).reshape(tokens * heads, dim)
        wide[at + 1 - core] = block_refs[2 * back + 1][...].astype(F32).reshape(tokens * heads, dim)


def one_head(wide, core, heads, narrow):
    head = core * (heads // 2) + pl.program_id(0)
    for r in range(narrow.shape[0]):
        narrow[r] = wide[r, pl.ds(head, narrow.shape[1], stride=heads), :].astype(BF16)


def first_allowed(lengths_ref, query_pos, window_start):
    def step(d, carry):
        start, first = carry
        first = jnp.where(query_pos + window_start >= start, start, first)
        return start + lengths_ref[d], first

    zero = jnp.zeros(query_pos.shape, jnp.int32)
    _, first = lax.fori_loop(0, lengths_ref.shape[0], step, (jnp.int32(0), zero))
    return first - window_start


def prob_kernel(halo, place_ref, lengths_ref, qd_ref, *refs):
    blocks = refs[: 2 * (halo + 1)]
    k_out, p_ref = refs[2 * (halo + 1) : 2 * (halo + 1) + 2]
    dv_refs = refs[2 * (halo + 1) + 2 : -2]
    wide, acc = refs[-2:]
    core, window_start = place_ref[0], place_ref[1]
    tokens, heads, dim = blocks[0].shape
    _, _, _, group, _, _ = qd_ref.shape
    count = 2 * halo + 1

    @pl.when(pl.program_id(0) == 0)
    def _():
        spread(blocks, core, wide)

    one_head(wide, core, heads, k_out.at[0])
    pair = 2 * tokens
    lane = lax.broadcasted_iota(jnp.int32, (1, pair), 1) % tokens
    row = lax.broadcasted_iota(jnp.int32, (tokens, pair), 0)
    for e in range(2):
        query_pos = lane + (2 * halo + e) * tokens
        first = first_allowed(lengths_ref, query_pos, window_start)
        k = k_out[0, pl.ds(e, count)].reshape(count * tokens, dim)
        q = qd_ref[0, e, 0].reshape(group * tokens, dim)
        do = qd_ref[0, e, 1].reshape(group * tokens, dim)
        for at in range(0, group * tokens, pair):
            s = lax.dot_general(k, q[at : at + pair], NT, preferred_element_type=F32)
            tiles = []
            for j in range(count):
                key_pos = row + (e + j) * tokens
                allowed = key_pos >= first
                if j == count - 1:
                    allowed &= key_pos <= query_pos
                tiles.append(jnp.where(allowed, s[j * tokens : (j + 1) * tokens], MASKED))
            s = jnp.concatenate(tiles, axis=0)
            top = jnp.max(s, axis=0, keepdims=True)
            w = jnp.exp2((s - top) * (dim**-0.5 * LOG2E))
            inv = 1.0 / jnp.sum(w, axis=0, keepdims=True)
            p_ref[0, e, :, at : at + pair] = (w * inv).astype(BF16)
        keep = (2 * halo - e) * tokens
        dv = jnp.dot(p_ref[0, e, :keep], do, preferred_element_type=F32).reshape(2 * halo - e, tokens, dim)
        if e == 0:
            acc[...] = dv
        else:
            acc[1:] += dv
    for back, ref in zip(range(1, halo + 1), dv_refs):
        ref[0] = acc[pl.ds(2 * (halo - back), 2)].astype(BF16)


def dscore_kernel(halo, place_ref, qd_ref, p_ref, *refs):
    blocks = refs[: 2 * (halo + 1)]
    ds_ref = refs[2 * (halo + 1)]
    dk_refs = refs[2 * (halo + 1) + 1 : -3]
    wide, narrow, acc = refs[-3:]
    core = place_ref[0]
    tokens, heads, dim = blocks[0].shape
    _, _, _, group, _, _ = qd_ref.shape
    count = 2 * halo + 1

    @pl.when(pl.program_id(0) == 0)
    def _():
        spread(blocks, core, wide)

    one_head(wide, core, heads, narrow)
    pair = 2 * tokens
    for e in range(2):
        v = narrow[pl.ds(e, count)].reshape(count * tokens, dim)
        q = qd_ref[0, e, 0].reshape(group * tokens, dim)
        do = qd_ref[0, e, 1].reshape(group * tokens, dim)
        for at in range(0, group * tokens, pair):
            dp = lax.dot_general(v, do[at : at + pair], NT, preferred_element_type=F32)
            p = p_ref[0, e, :, at : at + pair].astype(F32)
            delta = jnp.sum(p * dp, axis=0, keepdims=True)
            ds_ref[0, e, :, at : at + pair] = (p * (dp - delta)).astype(BF16)
        keep = (2 * halo - e) * tokens
        dk = jnp.dot(ds_ref[0, e, :keep], q, preferred_element_type=F32).reshape(2 * halo - e, tokens, dim)
        if e == 0:
            acc[...] = dk
        else:
            acc[1:] += dk
    for back, ref in zip(range(1, halo + 1), dk_refs):
        ref[0] = (acc[pl.ds(2 * (halo - back), 2)] * dim**-0.5).astype(BF16)


def own_kernel(halo, place_ref, qd_ref, k_ref, p_ref, ds_ref, dq_ref, dq_other_ref, dk_ref, dv_ref, scr):
    core = place_ref[0]
    _, _, _, group, tokens, dim = qd_ref.shape
    count = 2 * halo + 1
    scale = dim**-0.5
    for e in range(2):
        q = qd_ref[0, e, 0].reshape(group * tokens, dim)
        do = qd_ref[0, e, 1].reshape(group * tokens, dim)
        k = k_ref[0, pl.ds(e, count)].reshape(count * tokens, dim)
        dqt = jnp.dot(k.T, ds_ref[0, e], preferred_element_type=F32) * scale
        for g in range(group):
            scr[e, g] = dqt[:, g * tokens : (g + 1) * tokens].T.astype(BF16)
        keep = (2 * halo - e) * tokens
        dk = jnp.dot(ds_ref[0, e, keep:], q, preferred_element_type=F32) * scale
        dv = jnp.dot(p_ref[0, e, keep:], do, preferred_element_type=F32)
        if e == 0:
            dk_ref[0, 0], dv_ref[0, 0] = dk, dv
        else:
            dk_ref[0, 0] += dk[:tokens]
            dv_ref[0, 0] += dv[:tokens]
            dk_ref[0, 1], dv_ref[0, 1] = dk[tokens:], dv[tokens:]
    dq_ref[0] = scr[core]
    dq_other_ref[0] = scr[1 - core]


def merge_kernel(place_ref, own_ref, other_ref, out_ref, scr):
    core = place_ref[0]
    rows, heads, dim = out_ref.shape
    half = heads // 2
    for which, ref in enumerate([own_ref, other_ref]):
        side = 1 - core if which else core
        for h in range(half):
            scr[pl.ds(side * half + h, rows, stride=heads), :] = ref[h].astype(F32)
    out_ref[...] = scr[...].astype(BF16).reshape(rows, heads, dim)


def merge(place, own, other, rows, name):
    half, tokens, dim = own.shape
    in_spec = pl.BlockSpec((half, rows, dim), lambda i, place: (0, i, 0))
    return call(
        merge_kernel,
        name,
        (tokens // rows,),
        place,
        (own, other),
        [in_spec] * 2,
        jax.ShapeDtypeStruct((tokens, 2 * half, dim), BF16),
        pl.BlockSpec((rows, 2 * half, dim), lambda i, place: (i, 0, 0)),
        [pltpu.VMEM((rows * 2 * half, dim), F32)],
        10**9,
    )


def local(queries, keys, values, grad_out, doc_lengths):
    uly_count = lax.axis_size("uly")
    device_count = lax.axis_size("ctx") * uly_count
    halo = uly_count // 2
    device = lax.axis_index("ctx") * uly_count + lax.axis_index("uly")
    core = device % 2
    tokens, heads, dim = queries.shape
    key_heads = keys.shape[1]
    group = heads // key_heads
    half = key_heads // 2
    window, count = 2 * halo + 2, 2 * halo + 1
    place = jnp.stack([core, (device // 2 - halo) * (2 * tokens)]).astype(jnp.int32)

    far_first = range(halo, 0, -1)
    k_halo = {back: moved(keys, device_count, 2 * back) for back in far_first}
    v_halo = {back: moved(values, device_count, 2 * back) for back in far_first}

    def all_blocks(own, halos):
        blocks = [own, swapped(own, device_count)]
        for back in range(1, halo + 1):
            blocks += [halos[back], swapped(halos[back], device_count)]
        return blocks

    qd = arrange(
        place, queries, grad_out, swapped(queries, device_count), swapped(grad_out, device_count), key_heads
    )

    def per_head(*shape):
        return pl.BlockSpec((1,) + shape, lambda h, *_: (h,) + (0,) * len(shape))

    raw_spec = pl.BlockSpec(keys.shape, lambda h, *_: (0, 0, 0))
    qd_spec = per_head(2, 2, group, tokens, dim)
    k_spec = per_head(window, tokens, dim)
    p_spec = per_head(2, count * tokens, group * tokens)
    pair_spec = per_head(2, tokens, dim)
    p_shape = jax.ShapeDtypeStruct((half, 2, count * tokens, group * tokens), BF16)
    pair = (half, 2, tokens, dim)
    wide = pltpu.VMEM((window, tokens * key_heads, dim), F32)
    acc = pltpu.VMEM((2 * halo, tokens, dim), F32)
    product = 2 * half * 2 * count * tokens * group * tokens * dim

    k_arranged, prob, *dv_halo = call(
        functools.partial(prob_kernel, halo),
        "prob",
        (half,),
        (place, doc_lengths),
        (qd, *all_blocks(keys, k_halo)),
        [qd_spec] + [raw_spec] * window,
        [jax.ShapeDtypeStruct((half, window, tokens, dim), BF16), p_shape] + [jax.ShapeDtypeStruct(pair, BF16)] * halo,
        [k_spec, p_spec] + [pair_spec] * halo,
        [wide, acc],
        4 * product,
    )
    dv_back = [moved(dv_halo[back - 1], device_count, -2 * back) for back in far_first]
    dscore, *dk_halo = call(
        functools.partial(dscore_kernel, halo),
        "dscore",
        (half,),
        place,
        (qd, prob, *all_blocks(values, v_halo)),
        [qd_spec, p_spec] + [raw_spec] * window,
        [p_shape] + [jax.ShapeDtypeStruct(pair, BF16)] * halo,
        [p_spec] + [pair_spec] * halo,
        [wide, pltpu.VMEM((window, tokens, dim), BF16), acc],
        4 * product,
    )
    dk_back = [moved(dk_halo[back - 1], device_count, -2 * back) for back in far_first]
    dq_spec = per_head(group, tokens, dim)
    dq_shape = jax.ShapeDtypeStruct((half, group, tokens, dim), BF16)
    dq, dq_other, dk_own, dv_own = call(
        functools.partial(own_kernel, halo),
        "own",
        (half,),
        place,
        (qd, k_arranged, prob, dscore),
        [qd_spec, k_spec, p_spec, p_spec],
        [dq_shape] * 2 + [jax.ShapeDtypeStruct(pair, F32)] * 2,
        [dq_spec] * 2 + [pair_spec] * 2,
        [pltpu.VMEM((2, group, tokens, dim), BF16)],
        4 * product,
    )
    dq_other = swapped(dq_other, device_count)
    flat = (half * group, tokens, dim)
    grad_queries = merge(place, dq.reshape(flat), dq_other.reshape(flat), 32, "merge_dq")

    def summed(own, backs, name):
        total = own
        for back in backs:
            total = total + back.astype(F32)
        total = total.astype(BF16)
        mine = lax.dynamic_index_in_dim(total, core, 1, keepdims=False)
        other = lax.dynamic_index_in_dim(total, 1 - core, 1, keepdims=False)
        return merge(place, mine, swapped(other, device_count), tokens, name)

    grad_values = summed(dv_own, dv_back, "merge_dv")
    grad_keys = summed(dk_own, dk_back, "merge_dk")
    return grad_queries, grad_keys, grad_values


def solution(mesh):
    spec = P(AXES, None, None)
    return jax.shard_map(
        local, mesh=mesh, in_specs=(spec,) * 4 + (P(),), out_specs=(spec,) * 3, check_vma=False
    )
```

```python
import functools

import jax
import jax.numpy as jnp
from jax import lax
from jax.experimental import pallas as pl
from jax.experimental.pallas import tpu as pltpu
from jax.sharding import PartitionSpec as P

AXES = ("ctx", "uly")
LOG2E = 1.4426950408889634
MASKED = -1e30
BF16, F32 = jnp.bfloat16, jnp.float32
NT = (((1,), (1,)), ((), ()))
VMEM_BYTES = 24 * 2**20


def moved(array, device_count, by):
    pairs = [(d, d + by) for d in range(device_count) if 0 <= d + by < device_count]
    return lax.ppermute(array, AXES, pairs)


def swapped(array, device_count):
    return lax.ppermute(array, AXES, [(d, d ^ 1) for d in range(device_count)])


def call(kernel, name, grid, place, inputs, in_specs, outs, out_specs, scratch, flops):
    scalars = place if isinstance(place, tuple) else (place,)
    return pl.pallas_call(
        kernel,
        out_shape=outs,
        grid_spec=pltpu.PrefetchScalarGridSpec(
            num_scalar_prefetch=len(scalars),
            grid=grid,
            in_specs=in_specs,
            out_specs=out_specs,
            scratch_shapes=scratch,
        ),
        compiler_params=pltpu.CompilerParams(vmem_limit_bytes=VMEM_BYTES),
        cost_estimate=pl.CostEstimate(flops=flops, bytes_accessed=2**20, transcendentals=0),
        name=name,
    )(*scalars, *inputs)


def arrange_kernel(group, place_ref, q_ref, do_ref, q_other_ref, do_other_ref, out_ref, scr):
    core = place_ref[0]
    rows, heads, dim = q_ref.shape
    for kind, (own, other) in enumerate([(q_ref, q_other_ref), (do_ref, do_other_ref)]):
        for which, ref in enumerate([own, other]):
            block = 1 - core if which else core
            scr[...] = ref[...].astype(F32).reshape(rows * heads, dim)
            for h in range(heads):
                out_ref[h // group, block, kind, h % group] = scr[pl.ds(h, rows, stride=heads), :].astype(BF16)


def arrange(place, queries, grad_out, q_other, do_other, key_heads):
    tokens, heads, dim = queries.shape
    half, group = heads // 2, heads // key_heads
    rows = 32
    in_spec = pl.BlockSpec((rows, half, dim), lambda i, place: (i, place[0], 0))
    out = (key_heads // 2, 2, 2, group, tokens, dim)
    return call(
        functools.partial(arrange_kernel, group),
        "arrange",
        (tokens // rows,),
        place,
        (queries, grad_out, q_other, do_other),
        [in_spec] * 4,
        jax.ShapeDtypeStruct(out, BF16),
        pl.BlockSpec(out[:4] + (rows, dim), lambda i, place: (0, 0, 0, 0, i, 0)),
        [pltpu.VMEM((rows * half, dim), F32)],
        10**9,
    )


def pack_kernel(place_ref, own_ref, other_ref, out_ref, scr):
    core = place_ref[0]
    tokens, heads, dim = own_ref.shape
    half = heads // 2
    for which, ref in enumerate([own_ref, other_ref]):
        block = 1 - core if which else core
        scr[...] = ref[...].astype(F32).reshape(tokens * heads, dim)
        for h in range(half):
            out_ref[h, block] = scr[pl.ds(core * half + h, tokens, stride=heads), :].astype(BF16)


def pack(place, own, other, name):
    tokens, heads, dim = own.shape
    spec = pl.BlockSpec(own.shape, lambda i, place: (0, 0, 0))
    out = (heads // 2, 2, tokens, dim)
    return call(
        pack_kernel,
        name,
        (1,),
        place,
        (own, other),
        [spec] * 2,
        jax.ShapeDtypeStruct(out, BF16),
        pl.BlockSpec(out, lambda i, place: (0, 0, 0, 0)),
        [pltpu.VMEM((tokens * heads, dim), F32)],
        10**9,
    )


def first_allowed(lengths_ref, query_pos, window_start):
    def step(d, carry):
        start, first = carry
        first = jnp.where(query_pos + window_start >= start, start, first)
        return start + lengths_ref[d], first

    zero = jnp.zeros(query_pos.shape, jnp.int32)
    _, first = lax.fori_loop(0, lengths_ref.shape[0], step, (jnp.int32(0), zero))
    return first - window_start


def window_of(pair_refs, scr):
    halo = len(pair_refs) - 1
    for back, ref in enumerate(pair_refs):
        scr[pl.ds(2 * (halo - back), 2)] = ref[0]


def prob_kernel(halo, place_ref, lengths_ref, qd_ref, *refs):
    k_refs = refs[: halo + 1]
    p_ref = refs[halo + 1]
    dv_refs = refs[halo + 2 : -3]
    k_scr, acc, firsts = refs[-3:]
    _, _, _, group, tokens, dim = qd_ref.shape
    count = 2 * halo + 1
    pair = 2 * tokens
    lane = lax.broadcasted_iota(jnp.int32, (1, pair), 1) % tokens

    @pl.when(pl.program_id(0) == 0)
    def _():
        for e in range(2):
            query_pos = lane + (2 * halo + e) * tokens
            firsts[e] = first_allowed(lengths_ref, query_pos, place_ref[1])

    window_of(k_refs, k_scr)
    row = lax.broadcasted_iota(jnp.int32, (tokens, pair), 0)
    for e in range(2):
        first = firsts[e] - row
        k = k_scr[pl.ds(e, count)].reshape(count * tokens, dim)
        q = qd_ref[0, e, 0].reshape(group * tokens, dim)
        do = qd_ref[0, e, 1].reshape(group * tokens, dim)
        for at in range(0, group * tokens, pair):
            s = lax.dot_general(k, q[at : at + pair], NT, preferred_element_type=F32)
            tiles = []
            for j in range(count):
                allowed = first <= (e + j) * tokens
                if j == count - 1:
                    allowed &= row <= lane
                tiles.append(jnp.where(allowed, s[j * tokens : (j + 1) * tokens], MASKED))
            s = jnp.concatenate(tiles, axis=0)
            top = jnp.max(s, axis=0, keepdims=True)
            w = jnp.exp2((s - top) * (dim**-0.5 * LOG2E))
            inv = 1.0 / jnp.sum(w, axis=0, keepdims=True)
            p_ref[0, e, :, at : at + pair] = (w * inv).astype(BF16)
        keep = (2 * halo - e) * tokens
        dv = jnp.dot(p_ref[0, e, :keep], do, preferred_element_type=F32).reshape(2 * halo - e, tokens, dim)
        if e == 0:
            acc[...] = dv
        else:
            acc[1:] += dv
    for back, ref in zip(range(1, halo + 1), dv_refs):
        ref[0] = acc[pl.ds(2 * (halo - back), 2)].astype(BF16)


def dscore_kernel(halo, place_ref, qd_ref, p_ref, *refs):
    v_refs = refs[: halo + 1]
    ds_ref = refs[halo + 1]
    dk_refs = refs[halo + 2 : -2]
    v_scr, acc = refs[-2:]
    _, _, _, group, tokens, dim = qd_ref.shape
    count = 2 * halo + 1
    pair = 2 * tokens
    window_of(v_refs, v_scr)
    for e in range(2):
        v = v_scr[pl.ds(e, count)].reshape(count * tokens, dim)
        q = qd_ref[0, e, 0].reshape(group * tokens, dim)
        do = qd_ref[0, e, 1].reshape(group * tokens, dim)
        for at in range(0, group * tokens, pair):
            dp = lax.dot_general(v, do[at : at + pair], NT, preferred_element_type=F32)
            p = p_ref[0, e, :, at : at + pair].astype(F32)
            delta = jnp.sum(p * dp, axis=0, keepdims=True)
            ds_ref[0, e, :, at : at + pair] = (p * (dp - delta)).astype(BF16)
        keep = (2 * halo - e) * tokens
        dk = jnp.dot(ds_ref[0, e, :keep], q, preferred_element_type=F32).reshape(2 * halo - e, tokens, dim)
        if e == 0:
            acc[...] = dk
        else:
            acc[1:] += dk
    for back, ref in zip(range(1, halo + 1), dk_refs):
        ref[0] = (acc[pl.ds(2 * (halo - back), 2)] * dim**-0.5).astype(BF16)


def own_kernel(halo, place_ref, qd_ref, p_ref, ds_ref, *refs):
    k_refs, back_refs = refs[: halo + 1], refs[halo + 1 : 2 * halo + 1]
    dq_ref, dq_other_ref, dk_ref, dv_ref, dv_other_ref, k_scr, dq_scr, dv_scr = refs[2 * halo + 1 :]
    core = place_ref[0]
    _, _, _, group, tokens, dim = qd_ref.shape
    count = 2 * halo + 1
    scale = dim**-0.5
    window_of(k_refs, k_scr)
    for e in range(2):
        q = qd_ref[0, e, 0].reshape(group * tokens, dim)
        do = qd_ref[0, e, 1].reshape(group * tokens, dim)
        k = k_scr[pl.ds(e, count)].reshape(count * tokens, dim)
        dqt = jnp.dot(k.T, ds_ref[0, e], preferred_element_type=F32) * scale
        for g in range(group):
            dq_scr[e, g] = dqt[:, g * tokens : (g + 1) * tokens].T.astype(BF16)
        keep = (2 * halo - e) * tokens
        dk = jnp.dot(ds_ref[0, e, keep:], q, preferred_element_type=F32) * scale
        dv = jnp.dot(p_ref[0, e, keep:], do, preferred_element_type=F32)
        if e == 0:
            dk_ref[0, 0], dv_scr[0] = dk, dv
        else:
            dk_ref[0, 0] += dk[:tokens]
            dv_scr[0] += dv[:tokens]
            dk_ref[0, 1], dv_scr[1] = dk[tokens:], dv[tokens:]
    for ref in back_refs:
        dv_scr[...] += ref[0].astype(F32)
    dq_ref[0] = dq_scr[core]
    dq_other_ref[0] = dq_scr[1 - core]
    dv_ref[0] = dv_scr[core].astype(BF16)
    dv_other_ref[0] = dv_scr[1 - core].astype(BF16)


def merge_kernel(place_ref, own_ref, other_ref, out_ref, scr):
    core = place_ref[0]
    rows, heads, dim = out_ref.shape
    half = heads // 2
    for which, ref in enumerate([own_ref, other_ref]):
        side = 1 - core if which else core
        for h in range(half):
            scr[pl.ds(side * half + h, rows, stride=heads), :] = ref[h].astype(F32)
    out_ref[...] = scr[...].astype(BF16).reshape(rows, heads, dim)


def merge(place, own, other, rows, name):
    half, tokens, dim = own.shape
    in_spec = pl.BlockSpec((half, rows, dim), lambda i, place: (0, i, 0))
    return call(
        merge_kernel,
        name,
        (tokens // rows,),
        place,
        (own, other),
        [in_spec] * 2,
        jax.ShapeDtypeStruct((tokens, 2 * half, dim), BF16),
        pl.BlockSpec((rows, 2 * half, dim), lambda i, place: (i, 0, 0)),
        [pltpu.VMEM((rows * 2 * half, dim), F32)],
        10**9,
    )


def local(queries, keys, values, grad_out, doc_lengths):
    uly_count = lax.axis_size("uly")
    device_count = lax.axis_size("ctx") * uly_count
    halo = uly_count // 2
    device = lax.axis_index("ctx") * uly_count + lax.axis_index("uly")
    core = device % 2
    tokens, heads, dim = queries.shape
    key_heads = keys.shape[1]
    group = heads // key_heads
    half = key_heads // 2
    window, count = 2 * halo + 2, 2 * halo + 1
    place = jnp.stack([core, (device // 2 - halo) * (2 * tokens)]).astype(jnp.int32)

    far_first = range(halo, 0, -1)
    k_own = pack(place, keys, swapped(keys, device_count), "pack_k")
    v_own = pack(place, values, swapped(values, device_count), "pack_v")
    qd = arrange(
        place, queries, grad_out, swapped(queries, device_count), swapped(grad_out, device_count), key_heads
    )

    def halo_of(own):
        received = {back: moved(own, device_count, 2 * back) for back in far_first}
        return [own] + [received[back] for back in range(1, halo + 1)]

    def sent_back(partials):
        return [moved(partials[back - 1], device_count, -2 * back) for back in far_first]

    def per_head(*shape):
        return pl.BlockSpec((1,) + shape, lambda h, *_: (h,) + (0,) * len(shape))

    qd_spec = per_head(2, 2, group, tokens, dim)
    p_spec = per_head(2, count * tokens, group * tokens)
    p_shape = jax.ShapeDtypeStruct((half, 2, count * tokens, group * tokens), BF16)
    pair_spec = per_head(2, tokens, dim)
    pair = (half, 2, tokens, dim)
    one_spec = per_head(tokens, dim)
    one_shape = jax.ShapeDtypeStruct((half, tokens, dim), BF16)
    dq_spec = per_head(group, tokens, dim)
    dq_shape = jax.ShapeDtypeStruct((half, group, tokens, dim), BF16)
    run = pltpu.VMEM((window, tokens, dim), BF16)
    acc = pltpu.VMEM((2 * halo, tokens, dim), F32)
    product = 2 * half * 2 * count * tokens * group * tokens * dim

    k_pairs = halo_of(k_own)
    v_pairs = halo_of(v_own)
    prob, *dv_halo = call(
        functools.partial(prob_kernel, halo),
        "prob",
        (half,),
        (place, doc_lengths),
        (qd, *k_pairs),
        [qd_spec] + [pair_spec] * (halo + 1),
        [p_shape] + [jax.ShapeDtypeStruct(pair, BF16)] * halo,
        [p_spec] + [pair_spec] * halo,
        [run, acc, pltpu.VMEM((2, 1, 2 * tokens), jnp.int32)],
        4 * product,
    )
    dv_back = sent_back(dv_halo)
    dscore, *dk_halo = call(
        functools.partial(dscore_kernel, halo),
        "dscore",
        (half,),
        place,
        (qd, prob, *v_pairs),
        [qd_spec, p_spec] + [pair_spec] * (halo + 1),
        [p_shape] + [jax.ShapeDtypeStruct(pair, BF16)] * halo,
        [p_spec] + [pair_spec] * halo,
        [run, acc],
        4 * product,
    )
    dk_back = sent_back(dk_halo)
    dq, dq_other, dk_own, dv, dv_other = call(
        functools.partial(own_kernel, halo),
        "own",
        (half,),
        place,
        (qd, prob, dscore, *k_pairs, *dv_back),
        [qd_spec, p_spec, p_spec] + [pair_spec] * (2 * halo + 1),
        [dq_shape] * 2 + [jax.ShapeDtypeStruct(pair, F32)] + [one_shape] * 2,
        [dq_spec] * 2 + [pair_spec] + [one_spec] * 2,
        [
            run,
            pltpu.VMEM((2, group, tokens, dim), BF16),
            pltpu.VMEM((2, tokens, dim), F32),
        ],
        4 * product,
    )
    dq_other = swapped(dq_other, device_count)
    dv_other = swapped(dv_other, device_count)
    flat = (half * group, tokens, dim)
    grad_queries = merge(place, dq.reshape(flat), dq_other.reshape(flat), 32, "merge_dq")
    grad_values = merge(place, dv, dv_other, tokens, "merge_dv")

    total, grad_queries, grad_values = lax.optimization_barrier((dk_own, grad_queries, grad_values))
    for back in dk_back:
        total = total + back.astype(F32)
    total = total.astype(BF16)
    mine = lax.dynamic_index_in_dim(total, core, 1, keepdims=False)
    other = lax.dynamic_index_in_dim(total, 1 - core, 1, keepdims=False)
    grad_keys = merge(place, mine, swapped(other, device_count), tokens, "merge_dk")
    return grad_queries, grad_keys, grad_values


def solution(mesh):
    spec = P(AXES, None, None)
    return jax.shard_map(
        local, mesh=mesh, in_specs=(spec,) * 4 + (P(),), out_specs=(spec,) * 3, check_vma=False
    )
```

```python
import functools

import jax
import jax.numpy as jnp
from jax import lax
from jax.experimental import pallas as pl
from jax.experimental.pallas import tpu as pltpu
from jax.sharding import PartitionSpec as P

AXES = ("ctx", "uly")
LOG2E = 1.4426950408889634
MASKED = -1e30
BF16, F32 = jnp.bfloat16, jnp.float32
NT = (((1,), (1,)), ((), ()))
VMEM_BYTES = 24 * 2**20


def moved(array, device_count, by):
    pairs = [(d, d + by) for d in range(device_count) if 0 <= d + by < device_count]
    return lax.ppermute(array, AXES, pairs)


def swapped(array, device_count):
    return lax.ppermute(array, AXES, [(d, d ^ 1) for d in range(device_count)])


def call(kernel, name, grid, place, inputs, in_specs, outs, out_specs, scratch, flops):
    scalars = place if isinstance(place, tuple) else (place,)
    return pl.pallas_call(
        kernel,
        out_shape=outs,
        grid_spec=pltpu.PrefetchScalarGridSpec(
            num_scalar_prefetch=len(scalars),
            grid=grid,
            in_specs=in_specs,
            out_specs=out_specs,
            scratch_shapes=scratch,
        ),
        compiler_params=pltpu.CompilerParams(vmem_limit_bytes=VMEM_BYTES),
        cost_estimate=pl.CostEstimate(flops=flops, bytes_accessed=0, transcendentals=0),
        name=name,
    )(*scalars, *inputs)


def arrange_kernel(group, place_ref, q_ref, do_ref, q_other_ref, do_other_ref, out_ref, scr):
    core = place_ref[0]
    rows, heads, dim = q_ref.shape
    for kind, (own, other) in enumerate([(q_ref, q_other_ref), (do_ref, do_other_ref)]):
        for which, ref in enumerate([own, other]):
            block = 1 - core if which else core
            scr[...] = ref[...].astype(F32).reshape(rows * heads, dim)
            for h in range(heads):
                out_ref[h // group, block, kind, h % group] = scr[pl.ds(h, rows, stride=heads), :].astype(BF16)


def arrange(place, queries, grad_out, q_other, do_other, key_heads):
    tokens, heads, dim = queries.shape
    half, group = heads // 2, heads // key_heads
    rows = 32
    in_spec = pl.BlockSpec((rows, half, dim), lambda i, place: (i, place[0], 0))
    out = (key_heads // 2, 2, 2, group, tokens, dim)
    return call(
        functools.partial(arrange_kernel, group),
        "arrange",
        (tokens // rows,),
        place,
        (queries, grad_out, q_other, do_other),
        [in_spec] * 4,
        jax.ShapeDtypeStruct(out, BF16),
        pl.BlockSpec(out[:4] + (rows, dim), lambda i, place: (0, 0, 0, 0, i, 0)),
        [pltpu.VMEM((rows * half, dim), F32)],
        10**9,
    )


def pack_kernel(place_ref, own_ref, other_ref, out_ref, scr):
    core = place_ref[0]
    tokens, heads, dim = own_ref.shape
    half = heads // 2
    for which, ref in enumerate([own_ref, other_ref]):
        block = 1 - core if which else core
        scr[...] = ref[...].astype(F32).reshape(tokens * heads, dim)
        for h in range(half):
            out_ref[h, block] = scr[pl.ds(core * half + h, tokens, stride=heads), :].astype(BF16)


def pack(place, own, other, name):
    tokens, heads, dim = own.shape
    spec = pl.BlockSpec(own.shape, lambda i, place: (0, 0, 0))
    out = (heads // 2, 2, tokens, dim)
    return call(
        pack_kernel,
        name,
        (1,),
        place,
        (own, other),
        [spec] * 2,
        jax.ShapeDtypeStruct(out, BF16),
        pl.BlockSpec(out, lambda i, place: (0, 0, 0, 0)),
        [pltpu.VMEM((tokens * heads, dim), F32)],
        10**9,
    )


def first_allowed(lengths_ref, query_pos, window_start):
    def step(d, carry):
        start, first = carry
        first = jnp.where(query_pos + window_start >= start, start, first)
        return start + lengths_ref[d], first

    zero = jnp.zeros(query_pos.shape, jnp.int32)
    _, first = lax.fori_loop(0, lengths_ref.shape[0], step, (jnp.int32(0), zero))
    return first - window_start


def window_of(pair_refs, scr):
    halo = len(pair_refs) - 1
    for back, ref in enumerate(pair_refs):
        scr[pl.ds(2 * (halo - back), 2)] = ref[0]


def prob_kernel(halo, place_ref, lengths_ref, qd_ref, *refs):
    k_refs = refs[: halo + 1]
    p_ref = refs[halo + 1]
    dv_refs = refs[halo + 2 : -3]
    k_scr, acc, firsts = refs[-3:]
    _, _, _, group, tokens, dim = qd_ref.shape
    count = 2 * halo + 1
    pair = 2 * tokens
    lane = lax.broadcasted_iota(jnp.int32, (1, pair), 1) % tokens

    @pl.when(pl.program_id(0) == 0)
    def _():
        for e in range(2):
            query_pos = lane + (2 * halo + e) * tokens
            firsts[e] = first_allowed(lengths_ref, query_pos, place_ref[1])

    window_of(k_refs, k_scr)
    row = lax.broadcasted_iota(jnp.int32, (tokens, pair), 0)
    for e in range(2):
        first = firsts[e] - row
        k = k_scr[pl.ds(e, count)].reshape(count * tokens, dim)
        q = qd_ref[0, e, 0].reshape(group * tokens, dim)
        do = qd_ref[0, e, 1].reshape(group * tokens, dim)
        for at in range(0, group * tokens, pair):
            s = lax.dot_general(k, q[at : at + pair], NT, preferred_element_type=F32)
            tiles = []
            for j in range(count):
                allowed = first <= (e + j) * tokens
                if j == count - 1:
                    allowed &= row <= lane
                tiles.append(jnp.where(allowed, s[j * tokens : (j + 1) * tokens], MASKED))
            s = jnp.concatenate(tiles, axis=0)
            top = jnp.max(s, axis=0, keepdims=True)
            w = jnp.exp2((s - top) * (dim**-0.5 * LOG2E))
            inv = 1.0 / jnp.sum(w, axis=0, keepdims=True)
            p_ref[0, e, :, at : at + pair] = (w * inv).astype(BF16)
        keep = (2 * halo - e) * tokens
        dv = jnp.dot(p_ref[0, e, :keep], do, preferred_element_type=F32).reshape(2 * halo - e, tokens, dim)
        if e == 0:
            acc[...] = dv
        else:
            acc[1:] += dv
    for back, ref in zip(range(1, halo + 1), dv_refs):
        ref[0] = acc[pl.ds(2 * (halo - back), 2)].astype(BF16)


def dscore_kernel(halo, place_ref, qd_ref, p_ref, *refs):
    v_refs = refs[: halo + 1]
    ds_ref = refs[halo + 1]
    dk_refs = refs[halo + 2 : -2]
    v_scr, acc = refs[-2:]
    _, _, _, group, tokens, dim = qd_ref.shape
    count = 2 * halo + 1
    pair = 2 * tokens
    window_of(v_refs, v_scr)
    for e in range(2):
        v = v_scr[pl.ds(e, count)].reshape(count * tokens, dim)
        q = qd_ref[0, e, 0].reshape(group * tokens, dim)
        do = qd_ref[0, e, 1].reshape(group * tokens, dim)
        for at in range(0, group * tokens, pair):
            dp = lax.dot_general(v, do[at : at + pair], NT, preferred_element_type=F32)
            p = p_ref[0, e, :, at : at + pair].astype(F32)
            delta = jnp.sum(p * dp, axis=0, keepdims=True)
            ds_ref[0, e, :, at : at + pair] = (p * (dp - delta)).astype(BF16)
        keep = (2 * halo - e) * tokens
        dk = jnp.dot(ds_ref[0, e, :keep], q, preferred_element_type=F32).reshape(2 * halo - e, tokens, dim)
        if e == 0:
            acc[...] = dk
        else:
            acc[1:] += dk
    for back, ref in zip(range(1, halo + 1), dk_refs):
        ref[0] = (acc[pl.ds(2 * (halo - back), 2)] * dim**-0.5).astype(BF16)


def own_kernel(halo, place_ref, qd_ref, p_ref, ds_ref, *refs):
    k_refs, back_refs = refs[: halo + 1], refs[halo + 1 : 2 * halo + 1]
    dq_ref, dq_other_ref, dk_ref, dv_ref, dv_other_ref, k_scr, dq_scr, dv_scr = refs[2 * halo + 1 :]
    core = place_ref[0]
    _, _, _, group, tokens, dim = qd_ref.shape
    count = 2 * halo + 1
    scale = dim**-0.5
    window_of(k_refs, k_scr)
    for e in range(2):
        q = qd_ref[0, e, 0].reshape(group * tokens, dim)
        do = qd_ref[0, e, 1].reshape(group * tokens, dim)
        k = k_scr[pl.ds(e, count)].reshape(count * tokens, dim)
        dqt = jnp.dot(k.T, ds_ref[0, e], preferred_element_type=F32) * scale
        for g in range(group):
            dq_scr[e, g] = dqt[:, g * tokens : (g + 1) * tokens].T.astype(BF16)
        keep = (2 * halo - e) * tokens
        dk = jnp.dot(ds_ref[0, e, keep:], q, preferred_element_type=F32) * scale
        dv = jnp.dot(p_ref[0, e, keep:], do, preferred_element_type=F32)
        if e == 0:
            dk_ref[0, 0], dv_scr[0] = dk, dv
        else:
            dk_ref[0, 0] += dk[:tokens]
            dv_scr[0] += dv[:tokens]
            dk_ref[0, 1], dv_scr[1] = dk[tokens:], dv[tokens:]
    for ref in back_refs:
        dv_scr[...] += ref[0].astype(F32)
    dq_ref[0] = dq_scr[core]
    dq_other_ref[0] = dq_scr[1 - core]
    dv_ref[0] = dv_scr[core].astype(BF16)
    dv_other_ref[0] = dv_scr[1 - core].astype(BF16)


def merge_kernel(place_ref, own_ref, other_ref, out_ref, scr):
    core = place_ref[0]
    rows, heads, dim = out_ref.shape
    half = heads // 2
    for which, ref in enumerate([own_ref, other_ref]):
        side = 1 - core if which else core
        for h in range(half):
            scr[pl.ds(side * half + h, rows, stride=heads), :] = ref[h].astype(F32)
    out_ref[...] = scr[...].astype(BF16).reshape(rows, heads, dim)


def merge(place, own, other, rows, name):
    half, tokens, dim = own.shape
    in_spec = pl.BlockSpec((half, rows, dim), lambda i, place: (0, i, 0))
    return call(
        merge_kernel,
        name,
        (tokens // rows,),
        place,
        (own, other),
        [in_spec] * 2,
        jax.ShapeDtypeStruct((tokens, 2 * half, dim), BF16),
        pl.BlockSpec((rows, 2 * half, dim), lambda i, place: (i, 0, 0)),
        [pltpu.VMEM((rows * 2 * half, dim), F32)],
        4 * 10**9,
    )


def local(queries, keys, values, grad_out, doc_lengths):
    uly_count = lax.axis_size("uly")
    device_count = lax.axis_size("ctx") * uly_count
    halo = uly_count // 2
    device = lax.axis_index("ctx") * uly_count + lax.axis_index("uly")
    core = device % 2
    tokens, heads, dim = queries.shape
    key_heads = keys.shape[1]
    group = heads // key_heads
    half = key_heads // 2
    window, count = 2 * halo + 2, 2 * halo + 1
    place = jnp.stack([core, (device // 2 - halo) * (2 * tokens)]).astype(jnp.int32)

    far_first = range(halo, 0, -1)
    k_own = pack(place, keys, swapped(keys, device_count), "pack_k")
    k_own, queries, grad_out = lax.optimization_barrier((k_own, queries, grad_out))
    v_own = pack(place, values, swapped(values, device_count), "pack_v")
    qd = arrange(
        place, queries, grad_out, swapped(queries, device_count), swapped(grad_out, device_count), key_heads
    )

    def halo_of(own):
        received = {back: moved(own, device_count, 2 * back) for back in far_first}
        return [own] + [received[back] for back in range(1, halo + 1)]

    def sent_back(partials):
        return [moved(partials[back - 1], device_count, -2 * back) for back in far_first]

    def per_head(*shape):
        return pl.BlockSpec((1,) + shape, lambda h, *_: (h,) + (0,) * len(shape))

    qd_spec = per_head(2, 2, group, tokens, dim)
    p_spec = per_head(2, count * tokens, group * tokens)
    p_shape = jax.ShapeDtypeStruct((half, 2, count * tokens, group * tokens), BF16)
    pair_spec = per_head(2, tokens, dim)
    pair = (half, 2, tokens, dim)
    one_spec = per_head(tokens, dim)
    one_shape = jax.ShapeDtypeStruct((half, tokens, dim), BF16)
    dq_spec = per_head(group, tokens, dim)
    dq_shape = jax.ShapeDtypeStruct((half, group, tokens, dim), BF16)
    run = pltpu.VMEM((window, tokens, dim), BF16)
    acc = pltpu.VMEM((2 * halo, tokens, dim), F32)
    product = 2 * half * 2 * count * tokens * group * tokens * dim

    k_pairs = halo_of(k_own)
    v_pairs = halo_of(v_own)
    prob, *dv_halo = call(
        functools.partial(prob_kernel, halo),
        "prob",
        (half,),
        (place, doc_lengths),
        (qd, *k_pairs),
        [qd_spec] + [pair_spec] * (halo + 1),
        [p_shape] + [jax.ShapeDtypeStruct(pair, BF16)] * halo,
        [p_spec] + [pair_spec] * halo,
        [run, acc, pltpu.VMEM((2, 1, 2 * tokens), jnp.int32)],
        4 * product,
    )
    dv_back = sent_back(dv_halo)
    dscore, *dk_halo = call(
        functools.partial(dscore_kernel, halo),
        "dscore",
        (half,),
        place,
        (qd, prob, *v_pairs),
        [qd_spec, p_spec] + [pair_spec] * (halo + 1),
        [p_shape] + [jax.ShapeDtypeStruct(pair, BF16)] * halo,
        [p_spec] + [pair_spec] * halo,
        [run, acc],
        4 * product,
    )
    dk_back = sent_back(dk_halo)
    dq, dq_other, dk_own, dv, dv_other = call(
        functools.partial(own_kernel, halo),
        "own",
        (half,),
        place,
        (qd, prob, dscore, *k_pairs, *dv_back),
        [qd_spec, p_spec, p_spec] + [pair_spec] * (2 * halo + 1),
        [dq_shape] * 2 + [jax.ShapeDtypeStruct(pair, F32)] + [one_shape] * 2,
        [dq_spec] * 2 + [pair_spec] + [one_spec] * 2,
        [
            run,
            pltpu.VMEM((2, group, tokens, dim), BF16),
            pltpu.VMEM((2, tokens, dim), F32),
        ],
        0,
    )
    dq_other = swapped(dq_other, device_count)
    dv_other = swapped(dv_other, device_count)
    flat = (half * group, tokens, dim)
    grad_queries = merge(place, dq.reshape(flat), dq_other.reshape(flat), 32, "merge_dq")
    grad_values = merge(place, dv, dv_other, tokens, "merge_dv")

    total = dk_own
    for back in dk_back:
        total = total + back.astype(F32)
    total = total.astype(BF16)
    mine = lax.dynamic_index_in_dim(total, core, 1, keepdims=False)
    other = lax.dynamic_index_in_dim(total, 1 - core, 1, keepdims=False)
    grad_keys = merge(place, mine, swapped(other, device_count), tokens, "merge_dk")
    return grad_queries, grad_keys, grad_values


def solution(mesh):
    spec = P(AXES, None, None)
    return jax.shard_map(
        local, mesh=mesh, in_specs=(spec,) * 4 + (P(),), out_specs=(spec,) * 3, check_vma=False
    )
```

```python
import functools

import jax
import jax.numpy as jnp
from jax import lax
from jax.experimental import pallas as pl
from jax.experimental.pallas import tpu as pltpu
from jax.sharding import PartitionSpec as P

AXES = ("ctx", "uly")
LOG2E = 1.4426950408889634
MASKED = -1e30
BF16, F32 = jnp.bfloat16, jnp.float32
NT = (((1,), (1,)), ((), ()))
VMEM_BYTES = 24 * 2**20


def moved(array, device_count, by):
    pairs = [(d, d + by) for d in range(device_count) if 0 <= d + by < device_count]
    return lax.ppermute(array, AXES, pairs)


def swapped(array, device_count):
    return lax.ppermute(array, AXES, [(d, d ^ 1) for d in range(device_count)])


def call(kernel, name, grid, place, inputs, in_specs, outs, out_specs, scratch, flops):
    scalars = place if isinstance(place, tuple) else (place,)
    return pl.pallas_call(
        kernel,
        out_shape=outs,
        grid_spec=pltpu.PrefetchScalarGridSpec(
            num_scalar_prefetch=len(scalars),
            grid=grid,
            in_specs=in_specs,
            out_specs=out_specs,
            scratch_shapes=scratch,
        ),
        compiler_params=pltpu.CompilerParams(vmem_limit_bytes=VMEM_BYTES),
        cost_estimate=pl.CostEstimate(flops=flops, bytes_accessed=0, transcendentals=0),
        name=name,
    )(*scalars, *inputs)


def arrange_kernel(group, place_ref, q_ref, do_ref, q_other_ref, do_other_ref, out_ref, scr):
    core = place_ref[0]
    rows, heads, dim = q_ref.shape
    for kind, (own, other) in enumerate([(q_ref, q_other_ref), (do_ref, do_other_ref)]):
        for which, ref in enumerate([own, other]):
            block = 1 - core if which else core
            scr[...] = ref[...].astype(F32).reshape(rows * heads, dim)
            for h in range(heads):
                out_ref[h // group, block, kind, h % group] = scr[pl.ds(h, rows, stride=heads), :].astype(BF16)


def arrange(place, queries, grad_out, q_other, do_other, key_heads):
    tokens, heads, dim = queries.shape
    half, group = heads // 2, heads // key_heads
    rows = 32
    in_spec = pl.BlockSpec((rows, half, dim), lambda i, place: (i, place[0], 0))
    out = (key_heads // 2, 2, 2, group, tokens, dim)
    return call(
        functools.partial(arrange_kernel, group),
        "arrange",
        (tokens // rows,),
        place,
        (queries, grad_out, q_other, do_other),
        [in_spec] * 4,
        pltpu.VMEM(out, BF16),
        pl.BlockSpec(out[:4] + (rows, dim), lambda i, place: (0, 0, 0, 0, i, 0)),
        [pltpu.VMEM((rows * half, dim), F32)],
        10**9,
    )


def pack_kernel(place_ref, own_ref, other_ref, out_ref, scr):
    core = place_ref[0]
    tokens, heads, dim = own_ref.shape
    half = heads // 2
    for which, ref in enumerate([own_ref, other_ref]):
        block = 1 - core if which else core
        scr[...] = ref[...].astype(F32).reshape(tokens * heads, dim)
        for h in range(half):
            out_ref[h, block] = scr[pl.ds(core * half + h, tokens, stride=heads), :].astype(BF16)


def pack(place, own, other, name):
    tokens, heads, dim = own.shape
    spec = pl.BlockSpec(own.shape, lambda i, place: (0, 0, 0))
    out = (heads // 2, 2, tokens, dim)
    return call(
        pack_kernel,
        name,
        (1,),
        place,
        (own, other),
        [spec] * 2,
        jax.ShapeDtypeStruct(out, BF16),
        pl.BlockSpec(out, lambda i, place: (0, 0, 0, 0)),
        [pltpu.VMEM((tokens * heads, dim), F32)],
        10**9,
    )


def first_allowed(lengths_ref, query_pos, window_start):
    def step(d, carry):
        start, first = carry
        first = jnp.where(query_pos + window_start >= start, start, first)
        return start + lengths_ref[d], first

    zero = jnp.zeros(query_pos.shape, jnp.int32)
    _, first = lax.fori_loop(0, lengths_ref.shape[0], step, (jnp.int32(0), zero))
    return first - window_start


def window_of(pair_refs, scr):
    halo = len(pair_refs) - 1
    for back, ref in enumerate(pair_refs):
        scr[pl.ds(2 * (halo - back), 2)] = ref[0]


def split_tile(tile):
    tokens, lanes = tile.shape
    row = lax.broadcasted_iota(jnp.int32, tile.shape, 0)
    lane = lax.broadcasted_iota(jnp.int32, tile.shape, 1) % tokens
    diagonal = row <= lane
    zero = jnp.zeros_like(tile)
    return jnp.where(diagonal, zero, tile), jnp.where(diagonal, tile, zero)


def prob_kernel(halo, place_ref, lengths_ref, qd_ref, *refs):
    k_refs = refs[: halo + 1]
    p_ref = refs[halo + 1]
    dv_refs = refs[halo + 2 : -3]
    k_scr, acc, firsts = refs[-3:]
    _, _, _, group, tokens, dim = qd_ref.shape
    count = 2 * halo + 1
    pair = 2 * tokens
    lane = lax.broadcasted_iota(jnp.int32, (1, pair), 1) % tokens

    @pl.when(pl.program_id(0) == 0)
    def _():
        for e in range(2):
            query_pos = lane + (2 * halo + e) * tokens
            firsts[e] = first_allowed(lengths_ref, query_pos, place_ref[1])

    window_of(k_refs, k_scr)
    row = lax.broadcasted_iota(jnp.int32, (tokens, pair), 0)
    diagonal = row <= lane
    for e in range(2):
        first = firsts[e] - row
        k = k_scr[pl.ds(e, count)].reshape(count * tokens, dim)
        q = qd_ref[0, e, 0].reshape(group * tokens, dim)
        do = qd_ref[0, e, 1].reshape(group * tokens, dim)
        for at in range(0, group * tokens, pair):
            s = lax.dot_general(k, q[at : at + pair], NT, preferred_element_type=F32)
            tiles = [s[j * tokens : (j + 1) * tokens] for j in range(count)]
            last = (e + count - 1) * tokens
            bound = jnp.where(diagonal, last, e * tokens)
            tiles[0] = jnp.where(first <= bound, jnp.where(diagonal, tiles.pop(), tiles[0]), MASKED)
            for j in range(1, count - 1):
                tiles[j] = jnp.where(first <= (e + j) * tokens, tiles[j], MASKED)
            s = jnp.concatenate(tiles, axis=0)
            top = jnp.max(s, axis=0, keepdims=True)
            w = jnp.exp2((s - top) * (dim**-0.5 * LOG2E))
            inv = 1.0 / jnp.sum(w, axis=0, keepdims=True)
            p_ref[0, e, :, at : at + pair] = (w * inv).astype(BF16)
        far, _ = split_tile(p_ref[0, e, :tokens])
        keep = (2 * halo - e) * tokens
        dv = jnp.dot(far, do, preferred_element_type=F32)
        near = jnp.dot(p_ref[0, e, tokens:keep], do, preferred_element_type=F32)
        near = near.reshape(2 * halo - e - 1, tokens, dim)
        if e == 0:
            acc[0], acc[1:] = dv, near
        else:
            acc[1] += dv
            acc[2:] += near
    for back, ref in zip(range(1, halo + 1), dv_refs):
        ref[0] = acc[pl.ds(2 * (halo - back), 2)].astype(BF16)


def dscore_kernel(halo, place_ref, qd_ref, p_ref, *refs):
    v_refs = refs[: halo + 1]
    ds_ref = refs[halo + 1]
    dk_refs = refs[halo + 2 : -2]
    v_scr, acc = refs[-2:]
    _, _, _, group, tokens, dim = qd_ref.shape
    count = 2 * halo + 1
    pair = 2 * tokens
    window_of(v_refs, v_scr)
    row = lax.broadcasted_iota(jnp.int32, (tokens, pair), 0)
    diagonal = row <= lax.broadcasted_iota(jnp.int32, (tokens, pair), 1) % tokens
    for e in range(2):
        v = v_scr[pl.ds(e, count)].reshape(count * tokens, dim)
        q = qd_ref[0, e, 0].reshape(group * tokens, dim)
        do = qd_ref[0, e, 1].reshape(group * tokens, dim)
        for at in range(0, group * tokens, pair):
            dp = lax.dot_general(v, do[at : at + pair], NT, preferred_element_type=F32)
            last = (count - 1) * tokens
            shared = jnp.where(diagonal, dp[last:], dp[:tokens])
            dp = jnp.concatenate([shared, dp[tokens:last]], axis=0)
            p = p_ref[0, e, :, at : at + pair].astype(F32)
            delta = jnp.sum(p * dp, axis=0, keepdims=True)
            ds_ref[0, e, :, at : at + pair] = (p * (dp - delta)).astype(BF16)
        far, _ = split_tile(ds_ref[0, e, :tokens])
        keep = (2 * halo - e) * tokens
        dk = jnp.dot(far, q, preferred_element_type=F32)
        near = jnp.dot(ds_ref[0, e, tokens:keep], q, preferred_element_type=F32)
        near = near.reshape(2 * halo - e - 1, tokens, dim)
        if e == 0:
            acc[0], acc[1:] = dk, near
        else:
            acc[1] += dk
            acc[2:] += near
    for back, ref in zip(range(1, halo + 1), dk_refs):
        ref[0] = (acc[pl.ds(2 * (halo - back), 2)] * dim**-0.5).astype(BF16)


def own_kernel(halo, place_ref, qd_ref, p_ref, ds_ref, *refs):
    k_refs, back_refs = refs[: halo + 1], refs[halo + 1 : 2 * halo + 1]
    dq_ref, dq_other_ref, dk_ref, dv_ref, dv_other_ref, k_scr, dq_scr, dv_scr = refs[2 * halo + 1 :]
    core, head = place_ref[0], pl.program_id(0)
    _, _, _, group, tokens, dim = qd_ref.shape
    rows = dq_ref.shape[1]
    count = 2 * halo + 1
    scale = dim**-0.5
    window_of(k_refs, k_scr)
    for e in range(2):
        q = qd_ref[0, e, 0].reshape(group * tokens, dim)
        do = qd_ref[0, e, 1].reshape(group * tokens, dim)
        k = k_scr[pl.ds(e, count)].reshape(count * tokens, dim)
        far, diagonal = split_tile(ds_ref[0, e, :tokens])
        ds = jnp.concatenate([far, ds_ref[0, e, tokens:], diagonal], axis=0)
        dqt = jnp.dot(k.T, ds, preferred_element_type=F32) * scale
        for g in range(group):
            dq_scr[e, pl.ds(head * group + g, tokens, stride=rows), :] = dqt[:, g * tokens : (g + 1) * tokens].T
        _, p_diagonal = split_tile(p_ref[0, e, :tokens])
        dk = jnp.dot(diagonal, q, preferred_element_type=F32) * scale
        dv = jnp.dot(p_diagonal, do, preferred_element_type=F32)
        dk_ref[0, e], dv_scr[e] = dk, dv
        if e == 1:
            last = (count - 2) * tokens
            dk_ref[0, 0] += jnp.dot(ds_ref[0, e, last:], q, preferred_element_type=F32) * scale
            dv_scr[0] += jnp.dot(p_ref[0, e, last:], do, preferred_element_type=F32)
    for ref in back_refs:
        dv_scr[...] += ref[0].astype(F32)
    dv_ref[0] = dv_scr[core].astype(BF16)
    dv_other_ref[0] = dv_scr[1 - core].astype(BF16)

    @pl.when(head == pl.num_programs(0) - 1)
    def _():
        dq_ref[...] = dq_scr[core].astype(BF16).reshape(dq_ref.shape)
        dq_other_ref[...] = dq_scr[1 - core].astype(BF16).reshape(dq_ref.shape)


def join_kernel(place_ref, own_ref, other_ref, out_ref, own_sem, other_sem):
    core = place_ref[0]
    half = own_ref.shape[1]
    own = pltpu.make_async_copy(own_ref, out_ref.at[:, pl.ds(pl.multiple_of(core * half, half), half)], own_sem)
    other = pltpu.make_async_copy(
        other_ref, out_ref.at[:, pl.ds(pl.multiple_of((1 - core) * half, half), half)], other_sem
    )
    own.start()
    other.start()
    own.wait()
    other.wait()


def join(place, own, other):
    tokens, half, dim = own.shape
    anywhere = pl.BlockSpec(memory_space=pl.ANY)
    return call(
        join_kernel,
        "join",
        (1,),
        place,
        (own, other),
        [anywhere] * 2,
        jax.ShapeDtypeStruct((tokens, 2 * half, dim), BF16),
        anywhere,
        [pltpu.SemaphoreType.DMA, pltpu.SemaphoreType.DMA],
        10**9,
    )


def merge_kernel(place_ref, own_ref, other_ref, out_ref, scr):
    core = place_ref[0]
    rows, heads, dim = out_ref.shape
    half = heads // 2
    for which, ref in enumerate([own_ref, other_ref]):
        side = 1 - core if which else core
        for h in range(half):
            scr[pl.ds(side * half + h, rows, stride=heads), :] = ref[h].astype(F32)
    out_ref[...] = scr[...].astype(BF16).reshape(rows, heads, dim)


def merge(place, own, other, rows, name):
    half, tokens, dim = own.shape
    in_spec = pl.BlockSpec((half, rows, dim), lambda i, place: (0, i, 0))
    return call(
        merge_kernel,
        name,
        (tokens // rows,),
        place,
        (own, other),
        [in_spec] * 2,
        jax.ShapeDtypeStruct((tokens, 2 * half, dim), BF16),
        pl.BlockSpec((rows, 2 * half, dim), lambda i, place: (i, 0, 0)),
        [pltpu.VMEM((rows * 2 * half, dim), F32)],
        4 * 10**9,
    )


def local(queries, keys, values, grad_out, doc_lengths):
    uly_count = lax.axis_size("uly")
    device_count = lax.axis_size("ctx") * uly_count
    halo = uly_count // 2
    device = lax.axis_index("ctx") * uly_count + lax.axis_index("uly")
    core = device % 2
    tokens, heads, dim = queries.shape
    key_heads = keys.shape[1]
    group = heads // key_heads
    half = key_heads // 2
    window, count = 2 * halo + 2, 2 * halo + 1
    place = jnp.stack([core, (device // 2 - halo) * (2 * tokens)]).astype(jnp.int32)

    far_first = range(halo, 0, -1)
    k_own = pack(place, keys, swapped(keys, device_count), "pack_k")
    k_own, queries, grad_out = lax.optimization_barrier((k_own, queries, grad_out))
    qd = arrange(
        place, queries, grad_out, swapped(queries, device_count), swapped(grad_out, device_count), key_heads
    )
    v_other = swapped(values, device_count)
    qd, values, v_other = lax.optimization_barrier((qd, values, v_other))
    v_own = pack(place, values, v_other, "pack_v")

    def halo_of(own):
        received = {back: moved(own, device_count, 2 * back) for back in far_first}
        return [own] + [received[back] for back in range(1, halo + 1)]

    def sent_back(partials):
        return [moved(partials[back - 1], device_count, -2 * back) for back in far_first]

    def per_head(*shape):
        return pl.BlockSpec((1,) + shape, lambda h, *_: (h,) + (0,) * len(shape))

    qd_spec = per_head(2, 2, group, tokens, dim)
    p_spec = per_head(2, (count - 1) * tokens, group * tokens)
    p_shape = pltpu.VMEM((half, 2, (count - 1) * tokens, group * tokens), BF16)
    pair_spec = per_head(2, tokens, dim)
    pair = (half, 2, tokens, dim)
    one_spec = per_head(tokens, dim)
    one_shape = jax.ShapeDtypeStruct((half, tokens, dim), BF16)
    dq_shape = jax.ShapeDtypeStruct((tokens, heads // 2, dim), BF16)
    dq_spec = pl.BlockSpec(dq_shape.shape, lambda h, *_: (0, 0, 0))
    run = pltpu.VMEM((window, tokens, dim), BF16)
    acc = pltpu.VMEM((2 * halo, tokens, dim), F32)
    product = 2 * half * 2 * count * tokens * group * tokens * dim

    k_pairs = halo_of(k_own)
    v_pairs = halo_of(v_own)
    prob, *dv_halo = call(
        functools.partial(prob_kernel, halo),
        "prob",
        (half,),
        (place, doc_lengths),
        (qd, *k_pairs),
        [qd_spec] + [pair_spec] * (halo + 1),
        [p_shape] + [jax.ShapeDtypeStruct(pair, BF16)] * halo,
        [p_spec] + [pair_spec] * halo,
        [run, acc, pltpu.VMEM((2, 1, 2 * tokens), jnp.int32)],
        4 * product,
    )
    dv_back = sent_back(dv_halo)
    dscore, *dk_halo = call(
        functools.partial(dscore_kernel, halo),
        "dscore",
        (half,),
        place,
        (qd, prob, *v_pairs),
        [qd_spec, p_spec] + [pair_spec] * (halo + 1),
        [p_shape] + [jax.ShapeDtypeStruct(pair, BF16)] * halo,
        [p_spec] + [pair_spec] * halo,
        [run, acc],
        4 * product,
    )
    dk_back = sent_back(dk_halo)
    dq, dq_other, dk_own, dv, dv_other = call(
        functools.partial(own_kernel, halo),
        "own",
        (half,),
        place,
        (qd, prob, dscore, *k_pairs, *dv_back),
        [qd_spec, p_spec, p_spec] + [pair_spec] * (2 * halo + 1),
        [dq_shape] * 2 + [jax.ShapeDtypeStruct(pair, F32)] + [one_shape] * 2,
        [dq_spec] * 2 + [pair_spec] + [one_spec] * 2,
        [
            run,
            pltpu.VMEM((2, tokens * heads // 2, dim), F32),
            pltpu.VMEM((2, tokens, dim), F32),
        ],
        0,
    )
    dq_other = swapped(dq_other, device_count)
    dv_other = swapped(dv_other, device_count)
    grad_queries = join(place, dq, dq_other)
    grad_values = merge(place, dv, dv_other, tokens, "merge_dv")

    total = dk_own
    for back in dk_back:
        total = total + back.astype(F32)
    total = total.astype(BF16)
    mine = lax.dynamic_index_in_dim(total, core, 1, keepdims=False)
    other = lax.dynamic_index_in_dim(total, 1 - core, 1, keepdims=False)
    grad_keys = merge(place, mine, swapped(other, device_count), tokens, "merge_dk")
    return grad_queries, grad_keys, grad_values


def solution(mesh):
    spec = P(AXES, None, None)
    return jax.shard_map(
        local, mesh=mesh, in_specs=(spec,) * 4 + (P(),), out_specs=(spec,) * 3, check_vma=False
    )
```

```python
import functools

import jax
import jax.numpy as jnp
from jax import lax
from jax.experimental import pallas as pl
from jax.experimental.pallas import tpu as pltpu
from jax.sharding import PartitionSpec as P

AXES = ("ctx", "uly")
LOG2E = 1.4426950408889634
MASKED = -1e30
BF16, F32 = jnp.bfloat16, jnp.float32
NT = (((1,), (1,)), ((), ()))
VMEM_BYTES = 16 * 2**20


def moved(array, device_count, by):
    pairs = [(d, d + by) for d in range(device_count) if 0 <= d + by < device_count]
    return lax.ppermute(array, AXES, pairs)


def swapped(array, device_count):
    return lax.ppermute(array, AXES, [(d, d ^ 1) for d in range(device_count)])


def in_vmem(array):
    return pltpu.with_memory_space_constraint(array, pltpu.VMEM)


def call(kernel, name, grid, place, inputs, in_specs, outs, out_specs, scratch, flops):
    scalars = place if isinstance(place, tuple) else (place,)
    return pl.pallas_call(
        kernel,
        out_shape=outs,
        grid_spec=pltpu.PrefetchScalarGridSpec(
            num_scalar_prefetch=len(scalars),
            grid=grid,
            in_specs=in_specs,
            out_specs=out_specs,
            scratch_shapes=scratch,
        ),
        compiler_params=pltpu.CompilerParams(vmem_limit_bytes=VMEM_BYTES),
        cost_estimate=pl.CostEstimate(flops=flops, bytes_accessed=0, transcendentals=0),
        name=name,
    )(*scalars, *inputs)


def arrange_kernel(group, place_ref, q_ref, do_ref, q_other_ref, do_other_ref, out_ref, scr):
    core = place_ref[0]
    rows, heads, dim = q_ref.shape
    for kind, (own, other) in enumerate([(q_ref, q_other_ref), (do_ref, do_other_ref)]):
        for which, ref in enumerate([own, other]):
            block = 1 - core if which else core
            scr[...] = ref[...].astype(F32).reshape(rows * heads, dim)
            for h in range(heads):
                out_ref[h // group, block, kind, h % group] = scr[pl.ds(h, rows, stride=heads), :].astype(BF16)


def arrange(place, queries, grad_out, q_other, do_other, key_heads):
    tokens, heads, dim = queries.shape
    half, group = heads // 2, heads // key_heads
    rows = 32
    in_spec = pl.BlockSpec((rows, half, dim), lambda i, place: (i, place[0], 0))
    out = (key_heads // 2, 2, 2, group, tokens, dim)
    return call(
        functools.partial(arrange_kernel, group),
        "arrange",
        (tokens // rows,),
        place,
        (queries, grad_out, q_other, do_other),
        [in_spec] * 4,
        pltpu.VMEM(out, BF16),
        pl.BlockSpec(out[:4] + (rows, dim), lambda i, place: (0, 0, 0, 0, i, 0)),
        [pltpu.VMEM((rows * half, dim), F32)],
        10**9,
    )


def pack_kernel(place_ref, own_ref, other_ref, out_ref, own_scr, scr, sem):
    core = place_ref[0]
    tokens, heads, dim = other_ref.shape
    half = heads // 2
    fetch = pltpu.make_async_copy(own_ref, own_scr, sem)
    fetch.start()
    for which, ref in enumerate([other_ref, own_scr]):
        if which:
            fetch.wait()
        block = core if which else 1 - core
        scr[...] = ref[...].astype(F32).reshape(tokens * heads, dim)
        for h in range(half):
            out_ref[h, block] = scr[pl.ds(core * half + h, tokens, stride=heads), :].astype(BF16)


def pack(place, own, other, name):
    tokens, heads, dim = own.shape
    out = (heads // 2, 2, tokens, dim)
    return call(
        pack_kernel,
        name,
        (1,),
        place,
        (pltpu.with_memory_space_constraint(own, pltpu.HBM), other),
        [pl.BlockSpec(memory_space=pltpu.HBM), pl.BlockSpec(own.shape, lambda i, place: (0, 0, 0))],
        jax.ShapeDtypeStruct(out, BF16),
        pl.BlockSpec(out, lambda i, place: (0, 0, 0, 0)),
        [
            pltpu.VMEM(own.shape, BF16),
            pltpu.VMEM((tokens * heads, dim), F32),
            pltpu.SemaphoreType.DMA,
        ],
        10**9,
    )


def first_allowed(lengths_ref, query_pos, window_start):
    def step(d, carry):
        start, first = carry
        first = jnp.where(query_pos + window_start >= start, start, first)
        return start + lengths_ref[d], first

    zero = jnp.zeros(query_pos.shape, jnp.int32)
    _, first = lax.fori_loop(0, lengths_ref.shape[0], step, (jnp.int32(0), zero))
    return first - window_start


def window_of(pair_refs, scr):
    halo = len(pair_refs) - 1
    for back, ref in enumerate(pair_refs):
        scr[pl.ds(2 * (halo - back), 2)] = ref[0]


def on_diagonal(tokens, copies):
    row = lax.broadcasted_iota(jnp.int32, (tokens, tokens), 0)
    lane = lax.broadcasted_iota(jnp.int32, (tokens, tokens), 1)
    return jnp.concatenate([row] * copies, axis=1), jnp.concatenate([lane] * copies, axis=1)


def store_tiles(ref, e, at, tile, diagonal):
    tokens, pair = diagonal.shape
    lanes = slice(at, at + pair)
    shared, rest = tile[:tokens], tile[tokens:]
    ref[0, e, :tokens, lanes] = jnp.where(diagonal, 0.0, shared).astype(BF16)
    ref[0, e, tokens:-tokens, lanes] = rest.astype(BF16)
    ref[0, e, -tokens:, lanes] = jnp.where(diagonal, shared, 0.0).astype(BF16)


def prob_kernel(halo, place_ref, lengths_ref, qd_ref, *refs):
    k_refs = refs[: halo + 1]
    p_ref = refs[halo + 1]
    dv_refs = refs[halo + 2 : -3]
    k_scr, acc, firsts = refs[-3:]
    _, _, _, group, tokens, dim = qd_ref.shape
    count = 2 * halo + 1
    pair = 2 * tokens
    row, lane = on_diagonal(tokens, 2)
    diagonal = row <= lane

    @pl.when(pl.program_id(0) == 0)
    def _():
        for e in range(2):
            query_pos = lane[:1] + (2 * halo + e) * tokens
            firsts[e] = first_allowed(lengths_ref, query_pos, place_ref[1])

    window_of(k_refs, k_scr)
    for e in range(2):
        first = firsts[e] - row
        k = k_scr[pl.ds(e, count)].reshape(count * tokens, dim)
        q = qd_ref[0, e, 0].reshape(group * tokens, dim)
        do = qd_ref[0, e, 1].reshape(group * tokens, dim)
        for at in range(0, group * tokens, pair):
            s = lax.dot_general(k, q[at : at + pair], NT, preferred_element_type=F32)
            tiles = [s[j * tokens : (j + 1) * tokens] for j in range(count)]
            last = (e + count - 1) * tokens
            bound = jnp.where(diagonal, last, e * tokens)
            tiles[0] = jnp.where(first <= bound, jnp.where(diagonal, tiles.pop(), tiles[0]), MASKED)
            for j in range(1, count - 1):
                tiles[j] = jnp.where(first <= (e + j) * tokens, tiles[j], MASKED)
            s = jnp.concatenate(tiles, axis=0)
            top = jnp.max(s, axis=0, keepdims=True)
            w = jnp.exp2((s - top) * (dim**-0.5 * LOG2E))
            inv = 1.0 / jnp.sum(w, axis=0, keepdims=True)
            store_tiles(p_ref, e, at, w * inv, diagonal)
        keep = (2 * halo - e) * tokens
        dv = jnp.dot(p_ref[0, e, :keep], do, preferred_element_type=F32).reshape(2 * halo - e, tokens, dim)
        if e == 0:
            acc[...] = dv
        else:
            acc[1:] += dv
    for back, ref in zip(range(1, halo + 1), dv_refs):
        ref[0] = acc[pl.ds(2 * (halo - back), 2)].astype(BF16)


def dscore_kernel(halo, place_ref, qd_ref, p_ref, *refs):
    v_refs = refs[: halo + 1]
    ds_ref = refs[halo + 1]
    dk_refs = refs[halo + 2 : -2]
    v_scr, acc = refs[-2:]
    _, _, _, group, tokens, dim = qd_ref.shape
    count = 2 * halo + 1
    pair = 2 * tokens
    window_of(v_refs, v_scr)
    row, lane = on_diagonal(tokens, 2)
    diagonal = row <= lane
    for e in range(2):
        v = v_scr[pl.ds(e, count)].reshape(count * tokens, dim)
        q = qd_ref[0, e, 0].reshape(group * tokens, dim)
        do = qd_ref[0, e, 1].reshape(group * tokens, dim)
        for at in range(0, group * tokens, pair):
            dp = lax.dot_general(v, do[at : at + pair], NT, preferred_element_type=F32)
            last = (count - 1) * tokens
            shared = jnp.where(diagonal, dp[last:], dp[:tokens])
            dp = jnp.concatenate([shared, dp[tokens:last]], axis=0)
            p = p_ref[0, e, :, at : at + pair]
            p = jnp.concatenate([p[:tokens] + p[last:], p[tokens:last]], axis=0).astype(F32)
            delta = jnp.sum(p * dp, axis=0, keepdims=True)
            store_tiles(ds_ref, e, at, p * (dp - delta), diagonal)
        keep = (2 * halo - e) * tokens
        dk = jnp.dot(ds_ref[0, e, :keep], q, preferred_element_type=F32).reshape(2 * halo - e, tokens, dim)
        if e == 0:
            acc[...] = dk
        else:
            acc[1:] += dk
    for back, ref in zip(range(1, halo + 1), dk_refs):
        ref[0] = (acc[pl.ds(2 * (halo - back), 2)] * dim**-0.5).astype(BF16)


def own_kernel(halo, place_ref, qd_ref, p_ref, ds_ref, *refs):
    k_refs, back_refs = refs[: halo + 1], refs[halo + 1 : 2 * halo + 1]
    dq_ref, dq_other_ref, dk_ref, dv_ref, dv_other_ref, k_scr, dq_scr, dv_scr = refs[2 * halo + 1 :]
    core, head = place_ref[0], pl.program_id(0)
    _, _, _, group, tokens, dim = qd_ref.shape
    rows = dq_ref.shape[1]
    count = 2 * halo + 1
    scale = dim**-0.5
    window_of(k_refs, k_scr)
    for e in range(2):
        q = qd_ref[0, e, 0].reshape(group * tokens, dim)
        do = qd_ref[0, e, 1].reshape(group * tokens, dim)
        k = k_scr[pl.ds(e, count)].reshape(count * tokens, dim)
        dqt = jnp.dot(k.T, ds_ref[0, e], preferred_element_type=F32) * scale
        for g in range(group):
            dq_scr[e, pl.ds(head * group + g, tokens, stride=rows), :] = dqt[:, g * tokens : (g + 1) * tokens].T
        keep = (2 * halo - e) * tokens
        dk = jnp.dot(ds_ref[0, e, keep:], q, preferred_element_type=F32) * scale
        dv = jnp.dot(p_ref[0, e, keep:], do, preferred_element_type=F32)
        if e == 0:
            dk_ref[0, 0], dv_scr[0] = dk, dv
        else:
            dk_ref[0, 0] += dk[:tokens]
            dv_scr[0] += dv[:tokens]
            dk_ref[0, 1], dv_scr[1] = dk[tokens:], dv[tokens:]
    for ref in back_refs:
        dv_scr[...] += ref[0].astype(F32)
    dv_ref[0] = dv_scr[core].astype(BF16)
    dv_other_ref[0] = dv_scr[1 - core].astype(BF16)

    @pl.when(head == pl.num_programs(0) - 1)
    def _():
        dq_ref[...] = dq_scr[core].astype(BF16).reshape(dq_ref.shape)
        dq_other_ref[...] = dq_scr[1 - core].astype(BF16).reshape(dq_ref.shape)


def sum_kernel(place_ref, own_ref, *refs):
    back_refs, (mine_ref, other_ref) = refs[:-2], refs[-2:]
    core = place_ref[0]
    for block, ref in [(1 - core, other_ref), (core, mine_ref)]:
        total = own_ref[:, block]
        for back in back_refs:
            total += back[:, block].astype(F32)
        ref[...] = total.astype(BF16)


def summed(place, own, backs):
    half, _, tokens, dim = own.shape
    pair_spec = pl.BlockSpec(own.shape, lambda i, place: (0, 0, 0, 0))
    one = (half, tokens, dim)
    return call(
        sum_kernel,
        "sum_dk",
        (1,),
        place,
        (own, *backs),
        [pair_spec] * (1 + len(backs)),
        [jax.ShapeDtypeStruct(one, BF16)] * 2,
        [pl.BlockSpec(one, lambda i, place: (0, 0, 0))] * 2,
        [],
        10**8,
    )


def join_kernel(place_ref, own_ref, other_ref, out_ref, sems):
    core = place_ref[0]
    half = own_ref.shape[1]
    copies = []
    for which, ref in enumerate([own_ref, other_ref]):
        side = 1 - core if which else core
        at = pl.multiple_of(side * half, half)
        copies.append(pltpu.make_async_copy(ref, out_ref.at[:, pl.ds(at, half)], sems.at[which]))
        copies[-1].start()
    for copy in copies:
        copy.wait()


def join(place, own, other):
    tokens, half, dim = own.shape
    anywhere = pl.BlockSpec(memory_space=pl.ANY)
    return call(
        join_kernel,
        "join",
        (1,),
        place,
        (own, other),
        [anywhere] * 2,
        jax.ShapeDtypeStruct((tokens, 2 * half, dim), BF16),
        anywhere,
        [pltpu.SemaphoreType.DMA((2,))],
        10**9,
    )


def merge_kernel(place_ref, own_ref, other_ref, out_ref, scr):
    core = place_ref[0]
    rows, heads, dim = out_ref.shape
    half = heads // 2
    for which, ref in enumerate([own_ref, other_ref]):
        side = 1 - core if which else core
        for h in range(half):
            scr[pl.ds(side * half + h, rows, stride=heads), :] = ref[h].astype(F32)
    out_ref[...] = scr[...].astype(BF16).reshape(rows, heads, dim)


def merge(place, own, other, name):
    half, tokens, dim = own.shape
    spec = pl.BlockSpec(own.shape, lambda i, place: (0, 0, 0))
    out = (tokens, 2 * half, dim)
    return call(
        merge_kernel,
        name,
        (1,),
        place,
        (own, other),
        [spec] * 2,
        jax.ShapeDtypeStruct(out, BF16),
        pl.BlockSpec(out, lambda i, place: (0, 0, 0)),
        [pltpu.VMEM((tokens * 2 * half, dim), F32)],
        4 * 10**9,
    )


def local(queries, keys, values, grad_out, doc_lengths):
    uly_count = lax.axis_size("uly")
    device_count = lax.axis_size("ctx") * uly_count
    halo = uly_count // 2
    device = lax.axis_index("ctx") * uly_count + lax.axis_index("uly")
    core = device % 2
    tokens, heads, dim = queries.shape
    key_heads = keys.shape[1]
    group = heads // key_heads
    half = key_heads // 2
    window, count = 2 * halo + 2, 2 * halo + 1
    place = jnp.stack([core, (device // 2 - halo) * (2 * tokens)]).astype(jnp.int32)

    far_first = range(halo, 0, -1)
    k_own = pack(place, keys, swapped(keys, device_count), "pack_k")
    k_own, queries, grad_out = lax.optimization_barrier((k_own, queries, grad_out))
    qd = arrange(
        place, queries, grad_out, swapped(queries, device_count), swapped(grad_out, device_count), key_heads
    )
    v_other = swapped(values, device_count)
    qd, values, v_other = lax.optimization_barrier((qd, values, v_other))
    v_own = pack(place, values, v_other, "pack_v")

    def halo_of(own):
        received = {back: moved(own, device_count, 2 * back) for back in far_first}
        return [own] + [received[back] for back in range(1, halo + 1)]

    def sent_back(partials):
        return [moved(partials[back - 1], device_count, -2 * back) for back in far_first]

    def per_head(*shape):
        return pl.BlockSpec((1,) + shape, lambda h, *_: (h,) + (0,) * len(shape))

    qd_spec = per_head(2, 2, group, tokens, dim)
    p_spec = per_head(2, count * tokens, group * tokens)
    p_shape = pltpu.VMEM((half, 2, count * tokens, group * tokens), BF16)
    pair_spec = per_head(2, tokens, dim)
    pair = (half, 2, tokens, dim)
    one_spec = per_head(tokens, dim)
    one_shape = jax.ShapeDtypeStruct((half, tokens, dim), BF16)
    dq_shape = jax.ShapeDtypeStruct((tokens, heads // 2, dim), BF16)
    dq_spec = pl.BlockSpec(dq_shape.shape, lambda h, *_: (0, 0, 0))
    run = pltpu.VMEM((window, tokens, dim), BF16)
    acc = pltpu.VMEM((2 * halo, tokens, dim), F32)
    product = 2 * half * 2 * count * tokens * group * tokens * dim

    k_pairs = halo_of(k_own)
    v_pairs = halo_of(v_own)
    prob, *dv_halo = call(
        functools.partial(prob_kernel, halo),
        "prob",
        (half,),
        (place, doc_lengths),
        (in_vmem(qd), *k_pairs),
        [qd_spec] + [pair_spec] * (halo + 1),
        [p_shape] + [jax.ShapeDtypeStruct(pair, BF16)] * halo,
        [p_spec] + [pair_spec] * halo,
        [run, acc, pltpu.VMEM((2, 1, 2 * tokens), jnp.int32)],
        4 * product,
    )
    dv_back = sent_back(dv_halo)
    dscore, *dk_halo = call(
        functools.partial(dscore_kernel, halo),
        "dscore",
        (half,),
        place,
        (in_vmem(qd), in_vmem(prob), *v_pairs),
        [qd_spec, p_spec] + [pair_spec] * (halo + 1),
        [p_shape] + [jax.ShapeDtypeStruct(pair, BF16)] * halo,
        [p_spec] + [pair_spec] * halo,
        [run, acc],
        4 * product,
    )
    dk_back = sent_back(dk_halo)
    dq, dq_other, dk_own, dv, dv_other = call(
        functools.partial(own_kernel, halo),
        "own",
        (half,),
        place,
        (in_vmem(qd), in_vmem(prob), in_vmem(dscore), *k_pairs, *dv_back),
        [qd_spec, p_spec, p_spec] + [pair_spec] * (2 * halo + 1),
        [dq_shape] * 2 + [jax.ShapeDtypeStruct(pair, F32)] + [one_shape] * 2,
        [dq_spec] * 2 + [pair_spec] + [one_spec] * 2,
        [
            run,
            pltpu.VMEM((2, tokens * heads // 2, dim), F32),
            pltpu.VMEM((2, tokens, dim), F32),
        ],
        0,
    )
    dq_other = swapped(dq_other, device_count)
    dv_other = swapped(dv_other, device_count)
    dk, dk_other = summed(place, dk_own, dk_back)
    grad_queries = join(place, dq, dq_other)
    grad_values = merge(place, dv, dv_other, "merge_dv")
    grad_keys = merge(place, dk, swapped(dk_other, device_count), "merge_dk")
    return grad_queries, grad_keys, grad_values


def solution(mesh):
    spec = P(AXES, None, None)
    return jax.shard_map(
        local, mesh=mesh, in_specs=(spec,) * 4 + (P(),), out_specs=(spec,) * 3, check_vma=False
    )
```

```python
import functools

import jax
import jax.numpy as jnp
from jax import lax
from jax.experimental import pallas as pl
from jax.experimental.pallas import tpu as pltpu
from jax.sharding import PartitionSpec as P

AXES = ("ctx", "uly")
LOG2E = 1.4426950408889634
MASKED = -1e30
BF16, F32 = jnp.bfloat16, jnp.float32
NT = (((1,), (1,)), ((), ()))
VMEM_BYTES = 16 * 2**20


def moved(array, device_count, by):
    pairs = [(d, d + by) for d in range(device_count) if 0 <= d + by < device_count]
    return lax.ppermute(array, AXES, pairs)


def swapped(array, device_count):
    return lax.ppermute(array, AXES, [(d, d ^ 1) for d in range(device_count)])


def in_vmem(array):
    return pltpu.with_memory_space_constraint(array, pltpu.VMEM)


def call(kernel, name, grid, place, inputs, in_specs, outs, out_specs, scratch, flops, aliases={}):
    scalars = place if isinstance(place, tuple) else (place,)
    return pl.pallas_call(
        kernel,
        out_shape=outs,
        grid_spec=pltpu.PrefetchScalarGridSpec(
            num_scalar_prefetch=len(scalars),
            grid=grid,
            in_specs=in_specs,
            out_specs=out_specs,
            scratch_shapes=scratch,
        ),
        compiler_params=pltpu.CompilerParams(vmem_limit_bytes=VMEM_BYTES),
        cost_estimate=pl.CostEstimate(flops=flops, bytes_accessed=0, transcendentals=0),
        input_output_aliases=aliases,
        name=name,
    )(*scalars, *inputs)


def arrange_kernel(group, place_ref, q_ref, do_ref, q_other_ref, do_other_ref, out_ref, scr):
    core = place_ref[0]
    rows, heads, dim = q_ref.shape
    for kind, (own, other) in enumerate([(q_ref, q_other_ref), (do_ref, do_other_ref)]):
        for which, ref in enumerate([own, other]):
            block = 1 - core if which else core
            scr[...] = ref[...].astype(F32).reshape(rows * heads, dim)
            for h in range(heads):
                out_ref[h // group, block, kind, h % group] = scr[pl.ds(h, rows, stride=heads), :].astype(BF16)


def arrange(place, queries, grad_out, q_other, do_other, key_heads):
    tokens, heads, dim = queries.shape
    half, group = heads // 2, heads // key_heads
    rows = 32
    in_spec = pl.BlockSpec((rows, half, dim), lambda i, place: (i, place[0], 0))
    out = (key_heads // 2, 2, 2, group, tokens, dim)
    return call(
        functools.partial(arrange_kernel, group),
        "arrange",
        (tokens // rows,),
        place,
        (queries, grad_out, q_other, do_other),
        [in_spec] * 4,
        pltpu.VMEM(out, BF16),
        pl.BlockSpec(out[:4] + (rows, dim), lambda i, place: (0, 0, 0, 0, i, 0)),
        [pltpu.VMEM((rows * half, dim), F32)],
        10**9,
    )


def pack_block(raw, core, block, out_ref, scr):
    tokens, heads, dim = raw.shape
    half = heads // 2
    scr[...] = raw[...].astype(F32).reshape(tokens * heads, dim)
    for h in range(half):
        out_ref[h, block] = scr[pl.ds(core * half + h, tokens, stride=heads), :].astype(BF16)


def fetch_kernel(place_ref, key_ref, *refs):
    count = (len(refs) - 4) // 2
    sources, out_ref, targets = refs[:count], refs[count], refs[count + 1 : 2 * count + 1]
    raw, scr, sems = refs[-3:]
    first = pltpu.make_async_copy(key_ref, raw, sems.at[0])
    first.start()
    copies = [pltpu.make_async_copy(s, t, sems.at[i + 1]) for i, (s, t) in enumerate(zip(sources, targets))]
    for copy in copies:
        copy.start()
    first.wait()
    pack_block(raw, place_ref[0], place_ref[0], out_ref, scr)
    for copy in copies:
        copy.wait()


def fetch(place, keys, arrays):
    tokens, heads, dim = keys.shape
    out = (heads // 2, 2, tokens, dim)
    return call(
        fetch_kernel,
        "fetch",
        (1,),
        place,
        [pltpu.with_memory_space_constraint(x, pltpu.HBM) for x in (keys, *arrays)],
        [pl.BlockSpec(memory_space=pltpu.HBM)] * (1 + len(arrays)),
        [pltpu.VMEM(out, BF16)] + [pltpu.VMEM(x.shape, x.dtype) for x in arrays],
        [pl.BlockSpec(memory_space=pltpu.VMEM)] * (1 + len(arrays)),
        [
            pltpu.VMEM(keys.shape, BF16),
            pltpu.VMEM((tokens * heads, dim), F32),
            pltpu.SemaphoreType.DMA((1 + len(arrays),)),
        ],
        10**9,
    )


def pack_other_kernel(place_ref, other_ref, _, out_ref, scr):
    pack_block(other_ref, place_ref[0], 1 - place_ref[0], out_ref, scr)


def pack_other(place, other, packed):
    tokens, heads, dim = other.shape
    whole = pl.BlockSpec(memory_space=pltpu.VMEM)
    return call(
        pack_other_kernel,
        "pack_other",
        (1,),
        place,
        (in_vmem(other), in_vmem(packed)),
        [whole] * 2,
        pltpu.VMEM(packed.shape, BF16),
        whole,
        [pltpu.VMEM((tokens * heads, dim), F32)],
        10**9,
        {2: 0},
    )


def pack_both_kernel(place_ref, own_ref, other_ref, out_ref, scr):
    core = place_ref[0]
    pack_block(own_ref, core, core, out_ref, scr)
    pack_block(other_ref, core, 1 - core, out_ref, scr)


def pack_both(place, own, other):
    tokens, heads, dim = own.shape
    out = (heads // 2, 2, tokens, dim)
    whole = pl.BlockSpec(memory_space=pltpu.VMEM)
    return call(
        pack_both_kernel,
        "pack_both",
        (1,),
        place,
        (in_vmem(own), in_vmem(other)),
        [whole] * 2,
        pltpu.VMEM(out, BF16),
        whole,
        [pltpu.VMEM((tokens * heads, dim), F32)],
        10**9,
    )


def folded(op, x):
    while x.shape[0] > 8:
        half = x.shape[0] // 2
        x = op(x[:half], x[half:])
    reduce = jnp.max if op is jnp.maximum else jnp.sum
    return reduce(x, axis=0, keepdims=True)


def first_allowed(lengths_ref, query_pos, window_start):
    def step(d, carry):
        start, first = carry
        first = jnp.where(query_pos + window_start >= start, start, first)
        return start + lengths_ref[d], first

    zero = jnp.zeros(query_pos.shape, jnp.int32)
    _, first = lax.fori_loop(0, lengths_ref.shape[0], step, (jnp.int32(0), zero))
    return first - window_start


def window_of(pair_refs, scr):
    halo = len(pair_refs) - 1
    for back, ref in enumerate(pair_refs):
        scr[pl.ds(2 * (halo - back), 2)] = ref[0]


def on_diagonal(tokens, copies):
    row = lax.broadcasted_iota(jnp.int32, (tokens, tokens), 0)
    lane = lax.broadcasted_iota(jnp.int32, (tokens, tokens), 1)
    return jnp.concatenate([row] * copies, axis=1), jnp.concatenate([lane] * copies, axis=1)


def store_tiles(ref, e, at, tiles, diagonal):
    tokens, pair = diagonal.shape
    lanes = slice(at, at + pair)
    ref[0, e, :tokens, lanes] = jnp.where(diagonal, 0.0, tiles[0]).astype(BF16)
    for j, tile in enumerate(tiles[1:], 1):
        ref[0, e, j * tokens : (j + 1) * tokens, lanes] = tile.astype(BF16)
    ref[0, e, -tokens:, lanes] = jnp.where(diagonal, tiles[0], 0.0).astype(BF16)


def prob_kernel(halo, place_ref, lengths_ref, qd_ref, *refs):
    k_refs = refs[: halo + 1]
    p_ref = refs[halo + 1]
    dv_refs = refs[halo + 2 : -3]
    k_scr, acc, firsts = refs[-3:]
    _, _, _, group, tokens, dim = qd_ref.shape
    count = 2 * halo + 1
    pair = 2 * tokens
    row, lane = on_diagonal(tokens, 2)
    diagonal = row <= lane

    @pl.when(pl.program_id(0) == 0)
    def _():
        for e in range(2):
            query_pos = lane[:1] + (2 * halo + e) * tokens
            firsts[e] = first_allowed(lengths_ref, query_pos, place_ref[1])

    window_of(k_refs, k_scr)
    for e in range(2):
        first = firsts[e] - row
        k = k_scr[pl.ds(e, count)].reshape(count * tokens, dim)
        q = qd_ref[0, e, 0].reshape(group * tokens, dim)
        do = qd_ref[0, e, 1].reshape(group * tokens, dim)
        for at in range(0, group * tokens, pair):
            s = lax.dot_general(k, q[at : at + pair], NT, preferred_element_type=F32)
            tiles = [s[j * tokens : (j + 1) * tokens] for j in range(count)]
            last = (e + count - 1) * tokens
            bound = jnp.where(diagonal, last, e * tokens)
            tiles[0] = jnp.where(first <= bound, jnp.where(diagonal, tiles.pop(), tiles[0]), MASKED)
            for j in range(1, count - 1):
                tiles[j] = jnp.where(first <= (e + j) * tokens, tiles[j], MASKED)
            top = folded(jnp.maximum, functools.reduce(jnp.maximum, tiles))
            tiles = [jnp.exp2((tile - top) * (dim**-0.5 * LOG2E)) for tile in tiles]
            inv = 1.0 / folded(jnp.add, functools.reduce(jnp.add, tiles))
            store_tiles(p_ref, e, at, [tile * inv for tile in tiles], diagonal)
        keep = (2 * halo - e) * tokens
        dv = jnp.dot(p_ref[0, e, :keep], do, preferred_element_type=F32).reshape(2 * halo - e, tokens, dim)
        if e == 0:
            acc[...] = dv
        else:
            acc[1:] += dv
    for back, ref in zip(range(1, halo + 1), dv_refs):
        ref[0] = acc[pl.ds(2 * (halo - back), 2)].astype(BF16)


def dscore_kernel(halo, place_ref, qd_ref, p_ref, *refs):
    v_refs = refs[: halo + 1]
    ds_ref = refs[halo + 1]
    dk_refs = refs[halo + 2 : -2]
    v_scr, acc = refs[-2:]
    _, _, _, group, tokens, dim = qd_ref.shape
    count = 2 * halo + 1
    pair = 2 * tokens
    window_of(v_refs, v_scr)
    row, lane = on_diagonal(tokens, 2)
    diagonal = row <= lane
    for e in range(2):
        v = v_scr[pl.ds(e, count)].reshape(count * tokens, dim)
        q = qd_ref[0, e, 0].reshape(group * tokens, dim)
        do = qd_ref[0, e, 1].reshape(group * tokens, dim)
        for at in range(0, group * tokens, pair):
            dp = lax.dot_general(v, do[at : at + pair], NT, preferred_element_type=F32)
            dps = [dp[j * tokens : (j + 1) * tokens] for j in range(count)]
            dps[0] = jnp.where(diagonal, dps.pop(), dps[0])
            ps = [p_ref[0, e, j * tokens : (j + 1) * tokens, at : at + pair] for j in range(count)]
            ps[0] += ps.pop()
            ps = [p.astype(F32) for p in ps]
            delta = folded(jnp.add, functools.reduce(jnp.add, [p * dp for p, dp in zip(ps, dps)]))
            store_tiles(ds_ref, e, at, [p * (dp - delta) for p, dp in zip(ps, dps)], diagonal)
        keep = (2 * halo - e) * tokens
        dk = jnp.dot(ds_ref[0, e, :keep], q, preferred_element_type=F32).reshape(2 * halo - e, tokens, dim)
        if e == 0:
            acc[...] = dk
        else:
            acc[1:] += dk
    for back, ref in zip(range(1, halo + 1), dk_refs):
        ref[0] = (acc[pl.ds(2 * (halo - back), 2)] * dim**-0.5).astype(BF16)


def own_kernel(halo, place_ref, qd_ref, p_ref, ds_ref, *refs):
    k_refs, back_refs = refs[: halo + 1], refs[halo + 1 : 2 * halo + 1]
    dq_ref, dq_other_ref, dk_ref, dv_ref, dv_other_ref, k_scr, dq_scr, dv_scr = refs[2 * halo + 1 :]
    core, head = place_ref[0], pl.program_id(0)
    _, _, _, group, tokens, dim = qd_ref.shape
    rows = dq_ref.shape[1]
    count = 2 * halo + 1
    scale = dim**-0.5
    window_of(k_refs, k_scr)
    for e in range(2):
        q = qd_ref[0, e, 0].reshape(group * tokens, dim)
        do = qd_ref[0, e, 1].reshape(group * tokens, dim)
        k = k_scr[pl.ds(e, count)].reshape(count * tokens, dim)
        dqt = jnp.dot(k.T, ds_ref[0, e], preferred_element_type=F32) * scale
        for g in range(group):
            dq_scr[e, pl.ds(head * group + g, tokens, stride=rows), :] = dqt[:, g * tokens : (g + 1) * tokens].T
        keep = (2 * halo - e) * tokens
        dk = jnp.dot(ds_ref[0, e, keep:], q, preferred_element_type=F32) * scale
        dv = jnp.dot(p_ref[0, e, keep:], do, preferred_element_type=F32)
        if e == 0:
            dk_ref[0, 0], dv_scr[0] = dk, dv
        else:
            dk_ref[0, 0] += dk[:tokens]
            dv_scr[0] += dv[:tokens]
            dk_ref[0, 1], dv_scr[1] = dk[tokens:], dv[tokens:]
    for ref in back_refs:
        dv_scr[...] += ref[0].astype(F32)
    dv_ref[0] = dv_scr[core].astype(BF16)
    dv_other_ref[0] = dv_scr[1 - core].astype(BF16)

    @pl.when(head == pl.num_programs(0) - 1)
    def _():
        dq_ref[...] = dq_scr[core].astype(BF16).reshape(dq_ref.shape)
        dq_other_ref[...] = dq_scr[1 - core].astype(BF16).reshape(dq_ref.shape)


def sum_kernel(place_ref, own_ref, *refs):
    back_refs, (mine_ref, other_ref) = refs[:-2], refs[-2:]
    core = place_ref[0]
    for block, ref in [(1 - core, other_ref), (core, mine_ref)]:
        total = own_ref[:, block]
        for back in back_refs:
            total += back[:, block].astype(F32)
        ref[...] = total.astype(BF16)


def summed(place, own, backs):
    half, _, tokens, dim = own.shape
    pair_spec = pl.BlockSpec(own.shape, lambda i, place: (0, 0, 0, 0))
    one = (half, tokens, dim)
    return call(
        sum_kernel,
        "sum_dk",
        (1,),
        place,
        (own, *backs),
        [pair_spec] * (1 + len(backs)),
        [jax.ShapeDtypeStruct(one, BF16)] * 2,
        [pl.BlockSpec(one, lambda i, place: (0, 0, 0))] * 2,
        [],
        10**8,
    )


def join_kernel(place_ref, own_ref, other_ref, out_ref, sems):
    core = place_ref[0]
    half = own_ref.shape[1]
    copies = []
    for which, ref in enumerate([own_ref, other_ref]):
        side = 1 - core if which else core
        at = pl.multiple_of(side * half, half)
        copies.append(pltpu.make_async_copy(ref, out_ref.at[:, pl.ds(at, half)], sems.at[which]))
        copies[-1].start()
    for copy in copies:
        copy.wait()


def join(place, own, other):
    tokens, half, dim = own.shape
    anywhere = pl.BlockSpec(memory_space=pl.ANY)
    return call(
        join_kernel,
        "join",
        (1,),
        place,
        (own, other),
        [anywhere] * 2,
        jax.ShapeDtypeStruct((tokens, 2 * half, dim), BF16),
        anywhere,
        [pltpu.SemaphoreType.DMA((2,))],
        10**9,
    )


def merge_kernel(place_ref, own_ref, other_ref, out_ref, scr):
    core = place_ref[0]
    rows, heads, dim = out_ref.shape
    half = heads // 2
    for which, ref in enumerate([own_ref, other_ref]):
        side = 1 - core if which else core
        for h in range(half):
            scr[pl.ds(side * half + h, rows, stride=heads), :] = ref[h].astype(F32)
    out_ref[...] = scr[...].astype(BF16).reshape(rows, heads, dim)


def merge(place, own, other, name):
    half, tokens, dim = own.shape
    spec = pl.BlockSpec(own.shape, lambda i, place: (0, 0, 0))
    out = (tokens, 2 * half, dim)
    return call(
        merge_kernel,
        name,
        (1,),
        place,
        (own, other),
        [spec] * 2,
        jax.ShapeDtypeStruct(out, BF16),
        pl.BlockSpec(out, lambda i, place: (0, 0, 0)),
        [pltpu.VMEM((tokens * 2 * half, dim), F32)],
        4 * 10**9,
    )


def local(queries, keys, values, grad_out, doc_lengths):
    uly_count = lax.axis_size("uly")
    device_count = lax.axis_size("ctx") * uly_count
    halo = uly_count // 2
    device = lax.axis_index("ctx") * uly_count + lax.axis_index("uly")
    core = device % 2
    tokens, heads, dim = queries.shape
    key_heads = keys.shape[1]
    group = heads // key_heads
    half = key_heads // 2
    window, count = 2 * halo + 2, 2 * halo + 1
    place = jnp.stack([core, (device // 2 - halo) * (2 * tokens)]).astype(jnp.int32)

    far_first = range(halo, 0, -1)
    k_other = swapped(keys, device_count)
    k_mine, v_mine, q_mine, do_mine = fetch(place, keys, (values, queries, grad_out))
    k_own = pack_other(place, k_other, k_mine)
    k_own, q_mine, do_mine, v_mine = lax.optimization_barrier((k_own, q_mine, do_mine, v_mine))
    q_other, do_other, v_other = (swapped(x, device_count) for x in (q_mine, do_mine, v_mine))
    qd = arrange(place, in_vmem(q_mine), in_vmem(do_mine), q_other, do_other, key_heads)
    qd, v_mine, v_other = lax.optimization_barrier((qd, v_mine, v_other))
    v_own = pack_both(place, v_mine, v_other)

    def halo_of(own):
        received = {back: moved(own, device_count, 2 * back) for back in far_first}
        return [own] + [received[back] for back in range(1, halo + 1)]

    def sent_back(partials):
        return [moved(partials[back - 1], device_count, -2 * back) for back in far_first]

    def per_head(*shape):
        return pl.BlockSpec((1,) + shape, lambda h, *_: (h,) + (0,) * len(shape))

    qd_spec = per_head(2, 2, group, tokens, dim)
    p_spec = per_head(2, count * tokens, group * tokens)
    p_shape = pltpu.VMEM((half, 2, count * tokens, group * tokens), BF16)
    pair_spec = per_head(2, tokens, dim)
    pair = (half, 2, tokens, dim)
    one_spec = per_head(tokens, dim)
    one_shape = jax.ShapeDtypeStruct((half, tokens, dim), BF16)
    dq_shape = jax.ShapeDtypeStruct((tokens, heads // 2, dim), BF16)
    dq_spec = pl.BlockSpec(dq_shape.shape, lambda h, *_: (0, 0, 0))
    run = pltpu.VMEM((window, tokens, dim), BF16)
    acc = pltpu.VMEM((2 * halo, tokens, dim), F32)
    product = 2 * half * 2 * count * tokens * group * tokens * dim

    k_pairs = halo_of(k_own)
    v_pairs = halo_of(v_own)
    prob, *dv_halo = call(
        functools.partial(prob_kernel, halo),
        "prob",
        (half,),
        (place, doc_lengths),
        (in_vmem(qd), *k_pairs),
        [qd_spec] + [pair_spec] * (halo + 1),
        [p_shape] + [jax.ShapeDtypeStruct(pair, BF16)] * halo,
        [p_spec] + [pair_spec] * halo,
        [run, acc, pltpu.VMEM((2, 1, 2 * tokens), jnp.int32)],
        4 * product,
    )
    dv_back = sent_back(dv_halo)
    dscore, *dk_halo = call(
        functools.partial(dscore_kernel, halo),
        "dscore",
        (half,),
        place,
        (in_vmem(qd), in_vmem(prob), *v_pairs),
        [qd_spec, p_spec] + [pair_spec] * (halo + 1),
        [p_shape] + [jax.ShapeDtypeStruct(pair, BF16)] * halo,
        [p_spec] + [pair_spec] * halo,
        [run, acc],
        4 * product,
    )
    dk_back = sent_back(dk_halo)
    dq, dq_other, dk_own, dv, dv_other = call(
        functools.partial(own_kernel, halo),
        "own",
        (half,),
        place,
        (in_vmem(qd), in_vmem(prob), in_vmem(dscore), *k_pairs, *dv_back),
        [qd_spec, p_spec, p_spec] + [pair_spec] * (2 * halo + 1),
        [dq_shape] * 2 + [jax.ShapeDtypeStruct(pair, F32)] + [one_shape] * 2,
        [dq_spec] * 2 + [pair_spec] + [one_spec] * 2,
        [
            run,
            pltpu.VMEM((2, tokens * heads // 2, dim), F32),
            pltpu.VMEM((2, tokens, dim), F32),
        ],
        0,
    )
    dq_other = swapped(dq_other, device_count)
    dv_other = swapped(dv_other, device_count)
    dk, dk_other = summed(place, dk_own, dk_back)
    grad_queries = join(place, dq, dq_other)
    grad_values = merge(place, dv, dv_other, "merge_dv")
    grad_keys = merge(place, dk, swapped(dk_other, device_count), "merge_dk")
    return grad_queries, grad_keys, grad_values


def solution(mesh):
    spec = P(AXES, None, None)
    return jax.shard_map(
        local, mesh=mesh, in_specs=(spec,) * 4 + (P(),), out_specs=(spec,) * 3, check_vma=False
    )
```

```python
import functools

import jax
import jax.numpy as jnp
from jax import lax
from jax.experimental import pallas as pl
from jax.experimental.pallas import tpu as pltpu
from jax.sharding import PartitionSpec as P

AXES = ("ctx", "uly")
MASKED = -1e30
HEADS_AT_ONCE = 4
BF16, F32 = jnp.bfloat16, jnp.float32
NT = (((1,), (1,)), ((), ()))
VMEM_BYTES = 16 * 2**20


def moved(array, device_count, by):
    pairs = [(d, d + by) for d in range(device_count) if 0 <= d + by < device_count]
    return lax.ppermute(array, AXES, pairs)


def swapped(array, device_count):
    return lax.ppermute(array, AXES, [(d, d ^ 1) for d in range(device_count)])


def in_vmem(array):
    return pltpu.with_memory_space_constraint(array, pltpu.VMEM)


def in_hbm(array):
    return pltpu.with_memory_space_constraint(array, pltpu.HBM)


def call(kernel, name, grid, place, inputs, in_specs, outs, out_specs, scratch, flops, aliases={}):
    scalars = place if isinstance(place, tuple) else (place,)
    return pl.pallas_call(
        kernel,
        out_shape=outs,
        grid_spec=pltpu.PrefetchScalarGridSpec(
            num_scalar_prefetch=len(scalars),
            grid=grid,
            in_specs=in_specs,
            out_specs=out_specs,
            scratch_shapes=scratch,
        ),
        compiler_params=pltpu.CompilerParams(vmem_limit_bytes=VMEM_BYTES),
        cost_estimate=pl.CostEstimate(flops=flops, bytes_accessed=0, transcendentals=0),
        input_output_aliases=aliases,
        name=name,
    )(*scalars, *inputs)


def arrange_kernel(group, place_ref, q_ref, do_ref, q_other_ref, do_other_ref, out_ref, scr):
    core = place_ref[0]
    rows, heads, dim = q_ref.shape
    for kind, (own, other) in enumerate([(q_ref, q_other_ref), (do_ref, do_other_ref)]):
        for which, ref in enumerate([own, other]):
            block = 1 - core if which else core
            scr[...] = ref[...].astype(F32).reshape(rows * heads, dim)
            for h in range(heads):
                out_ref[h // group, block, kind, h % group] = scr[pl.ds(h, rows, stride=heads), :].astype(BF16)


def arrange(place, queries, grad_out, q_other, do_other, key_heads):
    tokens, heads, dim = queries.shape
    half, group = heads // 2, heads // key_heads
    rows = 32
    in_spec = pl.BlockSpec((rows, half, dim), lambda i, place: (i, place[0], 0))
    out = (key_heads // 2, 2, 2, group, tokens, dim)
    return call(
        functools.partial(arrange_kernel, group),
        "arrange",
        (tokens // rows,),
        place,
        (queries, grad_out, q_other, do_other),
        [in_spec] * 4,
        pltpu.VMEM(out, BF16),
        pl.BlockSpec(out[:4] + (rows, dim), lambda i, place: (0, 0, 0, 0, i, 0)),
        [pltpu.VMEM((rows * half, dim), F32)],
        10**9,
    )


def pack_block(raw, core, block, out_ref, scr):
    tokens, heads, dim = raw.shape
    half = heads // 2
    scr[...] = raw[...].astype(F32).reshape(tokens * heads, dim)
    for h in range(half):
        out_ref[h, block] = scr[pl.ds(core * half + h, tokens, stride=heads), :].astype(BF16)


def fetch_kernel(place_ref, key_ref, *refs):
    count = (len(refs) - 4) // 2
    sources, out_ref, targets = refs[:count], refs[count], refs[count + 1 : 2 * count + 1]
    raw, scr, sems = refs[-3:]
    first = pltpu.make_async_copy(key_ref, raw, sems.at[0])
    first.start()
    copies = [pltpu.make_async_copy(s, t, sems.at[i + 1]) for i, (s, t) in enumerate(zip(sources, targets))]
    for copy in copies:
        copy.start()
    first.wait()
    pack_block(raw, place_ref[0], place_ref[0], out_ref, scr)
    for copy in copies:
        copy.wait()


def fetch(place, keys, arrays):
    tokens, heads, dim = keys.shape
    out = (heads // 2, 2, tokens, dim)
    return call(
        fetch_kernel,
        "fetch",
        (1,),
        place,
        [in_hbm(x) for x in (keys, *arrays)],
        [pl.BlockSpec(memory_space=pltpu.HBM)] * (1 + len(arrays)),
        [pltpu.VMEM(out, BF16)] + [pltpu.VMEM(x.shape, x.dtype) for x in arrays],
        [pl.BlockSpec(memory_space=pltpu.VMEM)] * (1 + len(arrays)),
        [
            pltpu.VMEM(keys.shape, BF16),
            pltpu.VMEM((tokens * heads, dim), F32),
            pltpu.SemaphoreType.DMA((1 + len(arrays),)),
        ],
        10**9,
    )


def pack_other_kernel(place_ref, other_ref, _, out_ref, scr):
    pack_block(other_ref, place_ref[0], 1 - place_ref[0], out_ref, scr)


def pack_other(place, other, packed):
    tokens, heads, dim = other.shape
    whole = pl.BlockSpec(memory_space=pltpu.VMEM)
    return call(
        pack_other_kernel,
        "pack_other",
        (1,),
        place,
        (in_vmem(other), in_vmem(packed)),
        [whole] * 2,
        pltpu.VMEM(packed.shape, BF16),
        whole,
        [pltpu.VMEM((tokens * heads, dim), F32)],
        10**9,
        {2: 0},
    )


def pack_both_kernel(place_ref, own_ref, other_ref, out_ref, scr):
    core = place_ref[0]
    pack_block(own_ref, core, core, out_ref, scr)
    pack_block(other_ref, core, 1 - core, out_ref, scr)


def pack_both(place, own, other):
    tokens, heads, dim = own.shape
    out = (heads // 2, 2, tokens, dim)
    whole = pl.BlockSpec(memory_space=pltpu.VMEM)
    return call(
        pack_both_kernel,
        "pack_both",
        (1,),
        place,
        (in_vmem(own), in_vmem(other)),
        [whole] * 2,
        pltpu.VMEM(out, BF16),
        whole,
        [pltpu.VMEM((tokens * heads, dim), F32)],
        10**9,
    )


def folded(op, x):
    while x.shape[0] > 8:
        half = x.shape[0] // 2
        x = op(x[:half], x[half:])
    reduce = jnp.max if op is jnp.maximum else jnp.sum
    return reduce(x, axis=0, keepdims=True)


def first_allowed(lengths_ref, query_pos, window_start):
    def step(d, carry):
        start, first = carry
        first = jnp.where(query_pos + window_start >= start, start, first)
        return start + lengths_ref[d], first

    zero = jnp.zeros(query_pos.shape, jnp.int32)
    _, first = lax.fori_loop(0, lengths_ref.shape[0], step, (jnp.int32(0), zero))
    return first - window_start


def window_of(pair_refs, scr):
    halo = len(pair_refs) - 1
    for back, ref in enumerate(pair_refs):
        scr[pl.ds(2 * (halo - back), 2)] = ref[0]


def on_diagonal(tokens, copies):
    row = lax.broadcasted_iota(jnp.int32, (tokens, tokens), 0)
    lane = lax.broadcasted_iota(jnp.int32, (tokens, tokens), 1)
    return jnp.concatenate([row] * copies, axis=1), jnp.concatenate([lane] * copies, axis=1)


def store_tiles(ref, e, at, tiles, diagonal):
    tokens, pair = diagonal.shape
    lanes = slice(at, at + pair)
    ref[0, e, :tokens, lanes] = jnp.where(diagonal, 0.0, tiles[0]).astype(BF16)
    for j, tile in enumerate(tiles[1:], 1):
        ref[0, e, j * tokens : (j + 1) * tokens, lanes] = tile.astype(BF16)
    ref[0, e, -tokens:, lanes] = jnp.where(diagonal, tiles[0], 0.0).astype(BF16)


def prob_kernel(halo, place_ref, lengths_ref, qd_ref, *refs):
    k_refs = refs[: halo + 1]
    p_ref = refs[halo + 1]
    dv_refs = refs[halo + 2 : -3]
    k_scr, acc, firsts = refs[-3:]
    _, _, _, group, tokens, dim = qd_ref.shape
    count = 2 * halo + 1
    pair = HEADS_AT_ONCE * tokens
    row, lane = on_diagonal(tokens, HEADS_AT_ONCE)
    diagonal = row <= lane

    @pl.when(pl.program_id(0) == 0)
    def _():
        for e in range(2):
            query_pos = lane[:1] + (2 * halo + e) * tokens
            firsts[e] = first_allowed(lengths_ref, query_pos, place_ref[1])

    window_of(k_refs, k_scr)
    for e in range(2):
        first = firsts[e] - row
        k = k_scr[pl.ds(e, count)].reshape(count * tokens, dim)
        q = qd_ref[0, e, 0].reshape(group * tokens, dim)
        do = qd_ref[0, e, 1].reshape(group * tokens, dim)
        for at in range(0, group * tokens, pair):
            s = lax.dot_general(k, q[at : at + pair], NT, preferred_element_type=F32)
            tiles = [s[j * tokens : (j + 1) * tokens] for j in range(count)]
            last = (e + count - 1) * tokens
            bound = jnp.where(diagonal, last, e * tokens)
            tiles[0] = jnp.where(first <= bound, jnp.where(diagonal, tiles.pop(), tiles[0]), MASKED)
            for j in range(1, count - 1):
                tiles[j] = jnp.where(first <= (e + j) * tokens, tiles[j], MASKED)
            top = folded(jnp.maximum, functools.reduce(jnp.maximum, tiles))
            tiles = [jnp.exp((tile - top) * dim**-0.5) for tile in tiles]
            inv = 1.0 / folded(jnp.add, functools.reduce(jnp.add, tiles))
            store_tiles(p_ref, e, at, [tile * inv for tile in tiles], diagonal)
        keep = (2 * halo - e) * tokens
        dv = jnp.dot(p_ref[0, e, :keep], do, preferred_element_type=F32).reshape(2 * halo - e, tokens, dim)
        if e == 0:
            acc[...] = dv
        else:
            acc[1:] += dv
    for back, ref in zip(range(1, halo + 1), dv_refs):
        ref[0] = acc[pl.ds(2 * (halo - back), 2)].astype(BF16)


def dscore_kernel(halo, place_ref, qd_ref, p_ref, *refs):
    v_refs = refs[: halo + 1]
    ds_ref = refs[halo + 1]
    dk_refs = refs[halo + 2 : -2]
    v_scr, acc = refs[-2:]
    _, _, _, group, tokens, dim = qd_ref.shape
    count = 2 * halo + 1
    pair = HEADS_AT_ONCE * tokens
    window_of(v_refs, v_scr)
    row, lane = on_diagonal(tokens, HEADS_AT_ONCE)
    diagonal = row <= lane
    for e in range(2):
        v = v_scr[pl.ds(e, count)].reshape(count * tokens, dim)
        q = qd_ref[0, e, 0].reshape(group * tokens, dim)
        do = qd_ref[0, e, 1].reshape(group * tokens, dim)
        for at in range(0, group * tokens, pair):
            dp = lax.dot_general(v, do[at : at + pair], NT, preferred_element_type=F32)
            dps = [dp[j * tokens : (j + 1) * tokens] for j in range(count)]
            dps[0] = jnp.where(diagonal, dps.pop(), dps[0])
            ps = [p_ref[0, e, j * tokens : (j + 1) * tokens, at : at + pair] for j in range(count)]
            ps[0] += ps.pop()
            ps = [p.astype(F32) for p in ps]
            delta = folded(jnp.add, functools.reduce(jnp.add, [p * dp for p, dp in zip(ps, dps)]))
            store_tiles(ds_ref, e, at, [p * (dp - delta) for p, dp in zip(ps, dps)], diagonal)
        keep = (2 * halo - e) * tokens
        dk = jnp.dot(ds_ref[0, e, :keep], q, preferred_element_type=F32).reshape(2 * halo - e, tokens, dim)
        if e == 0:
            acc[...] = dk
        else:
            acc[1:] += dk
    for back, ref in zip(range(1, halo + 1), dk_refs):
        ref[0] = (acc[pl.ds(2 * (halo - back), 2)] * dim**-0.5).astype(BF16)


def own_kernel(halo, place_ref, qd_ref, p_ref, ds_ref, *refs):
    k_refs, back_refs = refs[: halo + 1], refs[halo + 1 : 2 * halo + 1]
    dq_ref, *dq_other_refs, dk_ref, dv_ref, dv_other_ref, k_scr, dq_scr, dv_scr = refs[2 * halo + 1 :]
    core, head = place_ref[0], pl.program_id(0)
    _, _, _, group, tokens, dim = qd_ref.shape
    rows = dq_ref.shape[1]
    count = 2 * halo + 1
    scale = dim**-0.5
    window_of(k_refs, k_scr)
    for e in range(2):
        q = qd_ref[0, e, 0].reshape(group * tokens, dim)
        do = qd_ref[0, e, 1].reshape(group * tokens, dim)
        k = k_scr[pl.ds(e, count)].reshape(count * tokens, dim)
        dqt = jnp.dot(k.T, ds_ref[0, e], preferred_element_type=F32) * scale
        for g in range(group):
            dq_scr[e, pl.ds(head * group + g, tokens, stride=rows), :] = dqt[:, g * tokens : (g + 1) * tokens].T
        keep = (2 * halo - e) * tokens
        dk = jnp.dot(ds_ref[0, e, keep:], q, preferred_element_type=F32) * scale
        dv = jnp.dot(p_ref[0, e, keep:], do, preferred_element_type=F32)
        if e == 0:
            dk_ref[0, 0], dv_scr[0] = dk, dv
        else:
            dk_ref[0, 0] += dk[:tokens]
            dv_scr[0] += dv[:tokens]
            dk_ref[0, 1], dv_scr[1] = dk[tokens:], dv[tokens:]
    for ref in back_refs:
        dv_scr[...] += ref[0].astype(F32)
    dv_ref[0] = dv_scr[core].astype(BF16)
    dv_other_ref[0] = dv_scr[1 - core].astype(BF16)

    @pl.when(head == pl.num_programs(0) - 1)
    def _():
        dq_ref[...] = dq_scr[core].astype(BF16).reshape(dq_ref.shape)
        at = 0
        for ref in dq_other_refs:
            part = ref.shape[0] * rows
            ref[...] = dq_scr[1 - core, at : at + part].astype(BF16).reshape(ref.shape)
            at += part


def sum_kernel(place_ref, own_ref, *refs):
    back_refs, (mine_ref, other_ref) = refs[:-2], refs[-2:]
    core = place_ref[0]
    for block, ref in [(1 - core, other_ref), (core, mine_ref)]:
        total = own_ref[:, block]
        for back in back_refs:
            total += back[:, block].astype(F32)
        ref[...] = total.astype(BF16)


def summed(place, own, backs):
    half, _, tokens, dim = own.shape
    pair_spec = pl.BlockSpec(own.shape, lambda i, place: (0, 0, 0, 0))
    one = (half, tokens, dim)
    return call(
        sum_kernel,
        "sum_dk",
        (1,),
        place,
        (own, *backs),
        [pair_spec] * (1 + len(backs)),
        [jax.ShapeDtypeStruct(one, BF16)] * 2,
        [pl.BlockSpec(one, lambda i, place: (0, 0, 0))] * 2,
        [],
        0,
    )


def finish_kernel(parts, place_ref, *refs):
    dq, others, (dk, dk_other, dv, dv_other) = refs[0], refs[1 : 1 + parts], refs[1 + parts : 5 + parts]
    dq_out, dk_out, dv_out, scr, sems = refs[5 + parts :]
    core = place_ref[0]
    rows, heads, dim = dk_out.shape
    half, q_half = heads // 2, dq.shape[1]
    at = pl.multiple_of(core * q_half, q_half)
    copies = [pltpu.make_async_copy(dq, dq_out.at[:, pl.ds(at, q_half)], sems.at[0])]
    at = pl.multiple_of((1 - core) * q_half, q_half)
    first = 0
    for i, part in enumerate(others):
        to = dq_out.at[pl.ds(first, part.shape[0]), pl.ds(at, q_half)]
        copies.append(pltpu.make_async_copy(part, to, sems.at[1 + i]))
        first += part.shape[0]
    for copy in copies:
        copy.start()
    for n, (own, other, out) in enumerate([(dk, dk_other, dk_out), (dv, dv_other, dv_out)]):
        for which, ref in enumerate([own, other]):
            side = 1 - core if which else core
            for h in range(half):
                scr[n, pl.ds(side * half + h, rows, stride=heads), :] = ref[h].astype(F32)
        out[...] = scr[n].astype(BF16).reshape(rows, heads, dim)
    for copy in copies:
        copy.wait()


def finish(place, dq, dq_others, dk, dk_other, dv, dv_other):
    half, tokens, dim = dk.shape
    anywhere = pl.BlockSpec(memory_space=pl.ANY)
    in_spec = pl.BlockSpec(dk.shape, lambda i, place: (0, 0, 0))
    out = (tokens, 2 * half, dim)
    parts = len(dq_others)
    return call(
        functools.partial(finish_kernel, parts),
        "finish",
        (1,),
        place,
        (dq, *dq_others, dk, dk_other, dv, dv_other),
        [anywhere] * (1 + parts) + [in_spec] * 4,
        [jax.ShapeDtypeStruct((tokens, 2 * dq.shape[1], dim), BF16)] + [jax.ShapeDtypeStruct(out, BF16)] * 2,
        [anywhere] + [pl.BlockSpec(out, lambda i, place: (0, 0, 0))] * 2,
        [pltpu.VMEM((2, tokens * 2 * half, dim), F32), pltpu.SemaphoreType.DMA((1 + parts,))],
        0,
    )


def local(queries, keys, values, grad_out, doc_lengths):
    uly_count = lax.axis_size("uly")
    device_count = lax.axis_size("ctx") * uly_count
    halo = uly_count // 2
    device = lax.axis_index("ctx") * uly_count + lax.axis_index("uly")
    core = device % 2
    tokens, heads, dim = queries.shape
    key_heads = keys.shape[1]
    group = heads // key_heads
    half = key_heads // 2
    window, count = 2 * halo + 2, 2 * halo + 1
    place = jnp.stack([core, (device // 2 - halo) * (2 * tokens)]).astype(jnp.int32)

    far_first = range(halo, 0, -1)
    k_other = swapped(keys, device_count)
    k_mine, v_mine = fetch(place, keys, (values,))
    k_own = pack_other(place, k_other, k_mine)
    k_own, queries, grad_out, v_mine = lax.optimization_barrier((k_own, queries, grad_out, v_mine))
    q_other, do_other, v_other = (swapped(x, device_count) for x in (queries, grad_out, v_mine))
    qd = arrange(place, in_hbm(queries), in_hbm(grad_out), q_other, do_other, key_heads)
    qd, v_mine, v_other = lax.optimization_barrier((qd, v_mine, v_other))
    v_own = pack_both(place, v_mine, v_other)

    def halo_of(own):
        received = {back: moved(own, device_count, 2 * back) for back in far_first}
        return [own] + [received[back] for back in range(1, halo + 1)]

    def sent_back(partials):
        return [moved(partials[back - 1], device_count, -2 * back) for back in far_first]

    def per_head(*shape):
        return pl.BlockSpec((1,) + shape, lambda h, *_: (h,) + (0,) * len(shape))

    qd_spec = per_head(2, 2, group, tokens, dim)
    p_spec = per_head(2, count * tokens, group * tokens)
    p_shape = pltpu.VMEM((half, 2, count * tokens, group * tokens), BF16)
    pair_spec = per_head(2, tokens, dim)
    pair = (half, 2, tokens, dim)
    one_spec = per_head(tokens, dim)
    one_shape = jax.ShapeDtypeStruct((half, tokens, dim), BF16)
    dq_shape = jax.ShapeDtypeStruct((tokens, heads // 2, dim), BF16)
    dq_spec = pl.BlockSpec(dq_shape.shape, lambda h, *_: (0, 0, 0))
    dq_part_shape = jax.ShapeDtypeStruct((tokens // 2, heads // 2, dim), BF16)
    dq_part_spec = pl.BlockSpec(dq_part_shape.shape, lambda h, *_: (0, 0, 0))
    run = pltpu.VMEM((window, tokens, dim), BF16)
    acc = pltpu.VMEM((2 * halo, tokens, dim), F32)
    product = 2 * half * 2 * count * tokens * group * tokens * dim

    k_pairs = halo_of(k_own)
    v_pairs = halo_of(v_own)
    prob, *dv_halo = call(
        functools.partial(prob_kernel, halo),
        "prob",
        (half,),
        (place, doc_lengths),
        (in_vmem(qd), *k_pairs),
        [qd_spec] + [pair_spec] * (halo + 1),
        [p_shape] + [jax.ShapeDtypeStruct(pair, BF16)] * halo,
        [p_spec] + [pair_spec] * halo,
        [run, acc, pltpu.VMEM((2, 1, HEADS_AT_ONCE * tokens), jnp.int32)],
        4 * product,
    )
    dv_back = sent_back(dv_halo)
    dscore, *dk_halo = call(
        functools.partial(dscore_kernel, halo),
        "dscore",
        (half,),
        place,
        (in_vmem(qd), in_vmem(prob), *v_pairs),
        [qd_spec, p_spec] + [pair_spec] * (halo + 1),
        [p_shape] + [jax.ShapeDtypeStruct(pair, BF16)] * halo,
        [p_spec] + [pair_spec] * halo,
        [run, acc],
        4 * product,
    )
    dk_back = sent_back(dk_halo)
    dq, *dq_others, dk_own, dv, dv_other = call(
        functools.partial(own_kernel, halo),
        "own",
        (half,),
        place,
        (in_vmem(qd), in_vmem(prob), in_vmem(dscore), *k_pairs, *dv_back),
        [qd_spec, p_spec, p_spec] + [pair_spec] * (2 * halo + 1),
        [dq_shape] + [dq_part_shape] * 2 + [jax.ShapeDtypeStruct(pair, F32)] + [one_shape] * 2,
        [dq_spec] + [dq_part_spec] * 2 + [pair_spec] + [one_spec] * 2,
        [
            run,
            pltpu.VMEM((2, tokens * heads // 2, dim), F32),
            pltpu.VMEM((2, tokens, dim), F32),
        ],
        0,
    )
    dq_others = [swapped(part, device_count) for part in dq_others]
    dv_other = swapped(dv_other, device_count)
    dk, dk_other = summed(place, dk_own, dk_back)
    return tuple(finish(place, dq, dq_others, dk, swapped(dk_other, device_count), dv, dv_other))


def solution(mesh):
    spec = P(AXES, None, None)
    return jax.shard_map(
        local, mesh=mesh, in_specs=(spec,) * 4 + (P(),), out_specs=(spec,) * 3, check_vma=False
    )
```

```python
import functools

import jax
import jax.numpy as jnp
from jax import lax
from jax.experimental import pallas as pl
from jax.experimental.pallas import tpu as pltpu
from jax.sharding import PartitionSpec as P

AXES = ("ctx", "uly")
MASKED = -1e30
HEADS_AT_ONCE = 2
BF16, F32 = jnp.bfloat16, jnp.float32
NT = (((1,), (1,)), ((), ()))
VMEM_BYTES = 16 * 2**20


def moved(array, device_count, by):
    pairs = [(d, d + by) for d in range(device_count) if 0 <= d + by < device_count]
    return lax.ppermute(array, AXES, pairs)


def swapped(array, device_count):
    return lax.ppermute(array, AXES, [(d, d ^ 1) for d in range(device_count)])


def in_vmem(array):
    return pltpu.with_memory_space_constraint(array, pltpu.VMEM)


def in_hbm(array):
    return pltpu.with_memory_space_constraint(array, pltpu.HBM)


def call(kernel, name, grid, place, inputs, in_specs, outs, out_specs, scratch, flops, aliases={}):
    scalars = place if isinstance(place, tuple) else (place,)
    return pl.pallas_call(
        kernel,
        out_shape=outs,
        grid_spec=pltpu.PrefetchScalarGridSpec(
            num_scalar_prefetch=len(scalars),
            grid=grid,
            in_specs=in_specs,
            out_specs=out_specs,
            scratch_shapes=scratch,
        ),
        compiler_params=pltpu.CompilerParams(vmem_limit_bytes=VMEM_BYTES),
        cost_estimate=pl.CostEstimate(flops=flops, bytes_accessed=0, transcendentals=0),
        input_output_aliases=aliases,
        name=name,
    )(*scalars, *inputs)


def arrange_kernel(group, place_ref, q_ref, do_ref, q_other_ref, do_other_ref, out_ref, scr):
    core = place_ref[0]
    tokens, heads, dim = q_ref.shape
    half = heads // 2
    mine = pl.ds(pl.multiple_of(core * half, half), half)
    turn = 0
    for kind, (own, other) in enumerate([(q_ref, q_other_ref), (do_ref, do_other_ref)]):
        for which, ref in enumerate([own, other]):
            block = 1 - core if which else core
            wide = scr.at[turn % 2]
            wide[...] = ref[:, mine].astype(F32).reshape(tokens * half, dim)
            for h in range(half):
                out_ref[h // group, block, kind, h % group] = wide[pl.ds(h, tokens, stride=half), :].astype(BF16)
            turn += 1


def arrange(place, queries, grad_out, q_other, do_other, key_heads):
    tokens, heads, dim = queries.shape
    half, group = heads // 2, heads // key_heads
    whole = pl.BlockSpec(memory_space=pltpu.VMEM)
    return call(
        functools.partial(arrange_kernel, group),
        "arrange",
        (1,),
        place,
        [in_vmem(x) for x in (queries, grad_out, q_other, do_other)],
        [whole] * 4,
        pltpu.VMEM((key_heads // 2, 2, 2, group, tokens, dim), BF16),
        whole,
        [pltpu.VMEM((2, tokens * half, dim), F32)],
        10**9,
    )


def pack_block(raw, core, block, out_ref, scr):
    tokens, heads, dim = raw.shape
    half = heads // 2
    scr[...] = raw[...].astype(F32).reshape(tokens * heads, dim)
    for h in range(half):
        out_ref[h, block] = scr[pl.ds(core * half + h, tokens, stride=heads), :].astype(BF16)


def fetch_kernel(place_ref, key_ref, *refs):
    count = (len(refs) - 4) // 2
    sources, out_ref, targets = refs[:count], refs[count], refs[count + 1 : 2 * count + 1]
    raw, scr, sems = refs[-3:]
    first = pltpu.make_async_copy(key_ref, raw, sems.at[0])
    first.start()
    copies = [pltpu.make_async_copy(s, t, sems.at[i + 1]) for i, (s, t) in enumerate(zip(sources, targets))]
    for copy in copies:
        copy.start()
    first.wait()
    pack_block(raw, place_ref[0], place_ref[0], out_ref, scr)
    for copy in copies:
        copy.wait()


def fetch(place, keys, arrays):
    tokens, heads, dim = keys.shape
    out = (heads // 2, 2, tokens, dim)
    return call(
        fetch_kernel,
        "fetch",
        (1,),
        place,
        [in_hbm(x) for x in (keys, *arrays)],
        [pl.BlockSpec(memory_space=pltpu.HBM)] * (1 + len(arrays)),
        [pltpu.VMEM(out, BF16)] + [pltpu.VMEM(x.shape, x.dtype) for x in arrays],
        [pl.BlockSpec(memory_space=pltpu.VMEM)] * (1 + len(arrays)),
        [
            pltpu.VMEM(keys.shape, BF16),
            pltpu.VMEM((tokens * heads, dim), F32),
            pltpu.SemaphoreType.DMA((1 + len(arrays),)),
        ],
        10**9,
    )


def pack_other_kernel(place_ref, other_ref, _, out_ref, scr):
    pack_block(other_ref, place_ref[0], 1 - place_ref[0], out_ref, scr)


def pack_other(place, other, packed):
    tokens, heads, dim = other.shape
    whole = pl.BlockSpec(memory_space=pltpu.VMEM)
    return call(
        pack_other_kernel,
        "pack_other",
        (1,),
        place,
        (in_vmem(other), in_vmem(packed)),
        [whole] * 2,
        pltpu.VMEM(packed.shape, BF16),
        whole,
        [pltpu.VMEM((tokens * heads, dim), F32)],
        10**9,
        {2: 0},
    )


def pack_both_kernel(place_ref, own_ref, other_ref, out_ref, scr):
    core = place_ref[0]
    pack_block(own_ref, core, core, out_ref, scr)
    pack_block(other_ref, core, 1 - core, out_ref, scr)


def pack_both(place, own, other):
    tokens, heads, dim = own.shape
    out = (heads // 2, 2, tokens, dim)
    whole = pl.BlockSpec(memory_space=pltpu.VMEM)
    return call(
        pack_both_kernel,
        "pack_both",
        (1,),
        place,
        (in_vmem(own), in_vmem(other)),
        [whole] * 2,
        pltpu.VMEM(out, BF16),
        whole,
        [pltpu.VMEM((tokens * heads, dim), F32)],
        10**9,
    )


def folded(op, x):
    while x.shape[0] > 8:
        half = x.shape[0] // 2
        x = op(x[:half], x[half:])
    reduce = jnp.max if op is jnp.maximum else jnp.sum
    return reduce(x, axis=0, keepdims=True)


def first_allowed(lengths_ref, query_pos, window_start):
    def step(d, carry):
        start, first = carry
        first = jnp.where(query_pos + window_start >= start, start, first)
        return start + lengths_ref[d], first

    zero = jnp.zeros(query_pos.shape, jnp.int32)
    _, first = lax.fori_loop(0, lengths_ref.shape[0], step, (jnp.int32(0), zero))
    return first - window_start


def window_of(pair_refs, scr):
    halo = len(pair_refs) - 1
    for back, ref in enumerate(pair_refs):
        scr[pl.ds(2 * (halo - back), 2)] = ref[0]


def on_diagonal(tokens, copies):
    row = lax.broadcasted_iota(jnp.int32, (tokens, tokens), 0)
    lane = lax.broadcasted_iota(jnp.int32, (tokens, tokens), 1)
    return jnp.concatenate([row] * copies, axis=1), jnp.concatenate([lane] * copies, axis=1)


def store_tiles(ref, e, at, tiles, diagonal):
    tokens, pair = diagonal.shape
    lanes = slice(at, at + pair)
    ref[0, e, :tokens, lanes] = jnp.where(diagonal, 0.0, tiles[0]).astype(BF16)
    for j, tile in enumerate(tiles[1:], 1):
        ref[0, e, j * tokens : (j + 1) * tokens, lanes] = tile.astype(BF16)
    ref[0, e, -tokens:, lanes] = jnp.where(diagonal, tiles[0], 0.0).astype(BF16)


def prob_kernel(halo, place_ref, lengths_ref, qd_ref, *refs):
    k_refs = refs[: halo + 1]
    p_ref = refs[halo + 1]
    dv_refs = refs[halo + 2 : -3]
    k_scr, acc, firsts = refs[-3:]
    _, _, _, group, tokens, dim = qd_ref.shape
    count = 2 * halo + 1
    pair = HEADS_AT_ONCE * tokens
    row, lane = on_diagonal(tokens, HEADS_AT_ONCE)
    diagonal = row <= lane

    @pl.when(pl.program_id(0) == 0)
    def _():
        for e in range(2):
            query_pos = lane[:1] + (2 * halo + e) * tokens
            firsts[e] = first_allowed(lengths_ref, query_pos, place_ref[1])

    window_of(k_refs, k_scr)
    chunks = [(e, at) for e in range(2) for at in range(0, group * tokens, pair)]

    def scores(e, at):
        k = k_scr[pl.ds(e, count)].reshape(count * tokens, dim)
        q = qd_ref[0, e, 0].reshape(group * tokens, dim)[at : at + pair]
        return lax.dot_general(k, q, NT, preferred_element_type=F32)

    ahead = scores(*chunks[0])
    for i, (e, at) in enumerate(chunks):
        s = ahead
        if i + 1 < len(chunks):
            ahead = scores(*chunks[i + 1])
        first = firsts[e] - row
        tiles = [s[j * tokens : (j + 1) * tokens] for j in range(count)]
        last = (e + count - 1) * tokens
        bound = jnp.where(diagonal, last, e * tokens)
        tiles[0] = jnp.where(first <= bound, jnp.where(diagonal, tiles.pop(), tiles[0]), MASKED)
        for j in range(1, count - 1):
            tiles[j] = jnp.where(first <= (e + j) * tokens, tiles[j], MASKED)
        top = folded(jnp.maximum, functools.reduce(jnp.maximum, tiles))
        tiles = [jnp.exp((tile - top) * dim**-0.5) for tile in tiles]
        inv = 1.0 / folded(jnp.add, functools.reduce(jnp.add, tiles))
        store_tiles(p_ref, e, at, [tile * inv for tile in tiles], diagonal)
        if at + pair == group * tokens:
            do = qd_ref[0, e, 1].reshape(group * tokens, dim)
            keep = (2 * halo - e) * tokens
            dv = jnp.dot(p_ref[0, e, :keep], do, preferred_element_type=F32).reshape(2 * halo - e, tokens, dim)
            if e == 0:
                acc[...] = dv
            else:
                acc[1:] += dv
    for back, ref in zip(range(1, halo + 1), dv_refs):
        ref[0] = acc[pl.ds(2 * (halo - back), 2)].astype(BF16)


def dscore_kernel(halo, place_ref, qd_ref, p_ref, *refs):
    v_refs = refs[: halo + 1]
    ds_ref = refs[halo + 1]
    dk_refs = refs[halo + 2 : -2]
    v_scr, acc = refs[-2:]
    _, _, _, group, tokens, dim = qd_ref.shape
    count = 2 * halo + 1
    pair = HEADS_AT_ONCE * tokens
    window_of(v_refs, v_scr)
    row, lane = on_diagonal(tokens, HEADS_AT_ONCE)
    diagonal = row <= lane
    chunks = [(e, at) for e in range(2) for at in range(0, group * tokens, pair)]

    def dprobs(e, at):
        v = v_scr[pl.ds(e, count)].reshape(count * tokens, dim)
        do = qd_ref[0, e, 1].reshape(group * tokens, dim)[at : at + pair]
        return lax.dot_general(v, do, NT, preferred_element_type=F32)

    ahead = dprobs(*chunks[0])
    for i, (e, at) in enumerate(chunks):
        dp = ahead
        if i + 1 < len(chunks):
            ahead = dprobs(*chunks[i + 1])
        dps = [dp[j * tokens : (j + 1) * tokens] for j in range(count)]
        dps[0] = jnp.where(diagonal, dps.pop(), dps[0])
        ps = [p_ref[0, e, j * tokens : (j + 1) * tokens, at : at + pair] for j in range(count)]
        ps[0] += ps.pop()
        ps = [p.astype(F32) for p in ps]
        delta = folded(jnp.add, functools.reduce(jnp.add, [p * dp for p, dp in zip(ps, dps)]))
        store_tiles(ds_ref, e, at, [p * (dp - delta) for p, dp in zip(ps, dps)], diagonal)
        if at + pair == group * tokens:
            q = qd_ref[0, e, 0].reshape(group * tokens, dim)
            keep = (2 * halo - e) * tokens
            dk = jnp.dot(ds_ref[0, e, :keep], q, preferred_element_type=F32).reshape(2 * halo - e, tokens, dim)
            if e == 0:
                acc[...] = dk
            else:
                acc[1:] += dk
    for back, ref in zip(range(1, halo + 1), dk_refs):
        ref[0] = (acc[pl.ds(2 * (halo - back), 2)] * dim**-0.5).astype(BF16)


def own_kernel(halo, place_ref, qd_ref, p_ref, ds_ref, *refs):
    k_refs, back_refs = refs[: halo + 1], refs[halo + 1 : 2 * halo + 1]
    dq_ref, *dq_other_refs, dk_ref, dv_ref, dv_other_ref, k_scr, dq_scr, dv_scr = refs[2 * halo + 1 :]
    core, head = place_ref[0], pl.program_id(0)
    _, _, _, group, tokens, dim = qd_ref.shape
    rows = dq_ref.shape[1]
    count = 2 * halo + 1
    scale = dim**-0.5
    window_of(k_refs, k_scr)
    for e in range(2):
        q = qd_ref[0, e, 0].reshape(group * tokens, dim)
        do = qd_ref[0, e, 1].reshape(group * tokens, dim)
        k = k_scr[pl.ds(e, count)].reshape(count * tokens, dim)
        dqt = jnp.dot(k.T, ds_ref[0, e], preferred_element_type=F32) * scale
        for g in range(group):
            dq_scr[e, pl.ds(head * group + g, tokens, stride=rows), :] = dqt[:, g * tokens : (g + 1) * tokens].T
        keep = (2 * halo - e) * tokens
        dk = jnp.dot(ds_ref[0, e, keep:], q, preferred_element_type=F32) * scale
        dv = jnp.dot(p_ref[0, e, keep:], do, preferred_element_type=F32)
        if e == 0:
            dk_ref[0, 0], dv_scr[0] = dk, dv
        else:
            dk_ref[0, 0] += dk[:tokens]
            dv_scr[0] += dv[:tokens]
            dk_ref[0, 1], dv_scr[1] = dk[tokens:], dv[tokens:]
    for ref in back_refs:
        dv_scr[...] += ref[0].astype(F32)
    dv_ref[0] = dv_scr[core].astype(BF16)
    dv_other_ref[0] = dv_scr[1 - core].astype(BF16)

    @pl.when(head == pl.num_programs(0) - 1)
    def _():
        dq_ref[...] = dq_scr[core].astype(BF16).reshape(dq_ref.shape)
        at = 0
        for ref in dq_other_refs:
            part = ref.shape[0] * rows
            ref[...] = dq_scr[1 - core, at : at + part].astype(BF16).reshape(ref.shape)
            at += part


def sum_kernel(place_ref, own_ref, *refs):
    back_refs, (mine_ref, other_ref) = refs[:-2], refs[-2:]
    core = place_ref[0]
    for block, ref in [(1 - core, other_ref), (core, mine_ref)]:
        total = own_ref[:, block]
        for back in back_refs:
            total += back[:, block].astype(F32)
        ref[...] = total.astype(BF16)


def summed(place, own, backs):
    half, _, tokens, dim = own.shape
    pair_spec = pl.BlockSpec(own.shape, lambda i, place: (0, 0, 0, 0))
    one = (half, tokens, dim)
    return call(
        sum_kernel,
        "sum_dk",
        (1,),
        place,
        (own, *backs),
        [pair_spec] * (1 + len(backs)),
        [jax.ShapeDtypeStruct(one, BF16)] * 2,
        [pl.BlockSpec(one, lambda i, place: (0, 0, 0))] * 2,
        [],
        0,
    )


def finish_kernel(parts, place_ref, *refs):
    dq, others, (dk, dk_other, dv, dv_other) = refs[0], refs[1 : 1 + parts], refs[1 + parts : 5 + parts]
    dq_out, dk_out, dv_out, scr, sems = refs[5 + parts :]
    core = place_ref[0]
    rows, heads, dim = dk_out.shape
    half, q_half = heads // 2, dq.shape[1]
    at = pl.multiple_of(core * q_half, q_half)
    copies = [pltpu.make_async_copy(dq, dq_out.at[:, pl.ds(at, q_half)], sems.at[0])]
    at = pl.multiple_of((1 - core) * q_half, q_half)
    first = 0
    for i, part in enumerate(others):
        to = dq_out.at[pl.ds(first, part.shape[0]), pl.ds(at, q_half)]
        copies.append(pltpu.make_async_copy(part, to, sems.at[1 + i]))
        first += part.shape[0]
    for copy in copies:
        copy.start()
    for n, (own, other, out) in enumerate([(dk, dk_other, dk_out), (dv, dv_other, dv_out)]):
        for which, ref in enumerate([own, other]):
            side = 1 - core if which else core
            for h in range(half):
                scr[n, pl.ds(side * half + h, rows, stride=heads), :] = ref[h].astype(F32)
        out[...] = scr[n].astype(BF16).reshape(rows, heads, dim)
    for copy in copies:
        copy.wait()


def finish(place, dq, dq_others, dk, dk_other, dv, dv_other):
    half, tokens, dim = dk.shape
    anywhere = pl.BlockSpec(memory_space=pl.ANY)
    in_spec = pl.BlockSpec(dk.shape, lambda i, place: (0, 0, 0))
    out = (tokens, 2 * half, dim)
    parts = len(dq_others)
    return call(
        functools.partial(finish_kernel, parts),
        "finish",
        (1,),
        place,
        (dq, *dq_others, dk, dk_other, dv, dv_other),
        [anywhere] * (1 + parts) + [in_spec] * 4,
        [jax.ShapeDtypeStruct((tokens, 2 * dq.shape[1], dim), BF16)] + [jax.ShapeDtypeStruct(out, BF16)] * 2,
        [anywhere] + [pl.BlockSpec(out, lambda i, place: (0, 0, 0))] * 2,
        [pltpu.VMEM((2, tokens * 2 * half, dim), F32), pltpu.SemaphoreType.DMA((1 + parts,))],
        0,
    )


def local(queries, keys, values, grad_out, doc_lengths):
    uly_count = lax.axis_size("uly")
    device_count = lax.axis_size("ctx") * uly_count
    halo = uly_count // 2
    device = lax.axis_index("ctx") * uly_count + lax.axis_index("uly")
    core = device % 2
    tokens, heads, dim = queries.shape
    key_heads = keys.shape[1]
    group = heads // key_heads
    half = key_heads // 2
    window, count = 2 * halo + 2, 2 * halo + 1
    place = jnp.stack([core, (device // 2 - halo) * (2 * tokens)]).astype(jnp.int32)

    far_first = range(halo, 0, -1)
    k_other = swapped(keys, device_count)
    k_mine, v_mine = fetch(place, keys, (values,))
    k_own = pack_other(place, k_other, k_mine)
    k_own, queries, grad_out, v_mine = lax.optimization_barrier((k_own, queries, grad_out, v_mine))
    q_other, do_other, v_other = (swapped(x, device_count) for x in (queries, grad_out, v_mine))
    qd = arrange(place, queries, grad_out, q_other, do_other, key_heads)
    qd, v_mine, v_other = lax.optimization_barrier((qd, v_mine, v_other))
    v_own = pack_both(place, v_mine, v_other)

    def halo_of(own):
        received = {back: moved(own, device_count, 2 * back) for back in far_first}
        return [own] + [received[back] for back in range(1, halo + 1)]

    def sent_back(partials):
        return [moved(partials[back - 1], device_count, -2 * back) for back in far_first]

    def per_head(*shape):
        return pl.BlockSpec((1,) + shape, lambda h, *_: (h,) + (0,) * len(shape))

    qd_spec = per_head(2, 2, group, tokens, dim)
    p_spec = per_head(2, count * tokens, group * tokens)
    p_shape = pltpu.VMEM((half, 2, count * tokens, group * tokens), BF16)
    pair_spec = per_head(2, tokens, dim)
    pair = (half, 2, tokens, dim)
    one_spec = per_head(tokens, dim)
    one_shape = jax.ShapeDtypeStruct((half, tokens, dim), BF16)
    dq_shape = jax.ShapeDtypeStruct((tokens, heads // 2, dim), BF16)
    dq_spec = pl.BlockSpec(dq_shape.shape, lambda h, *_: (0, 0, 0))
    dq_part_shape = jax.ShapeDtypeStruct((tokens // 2, heads // 2, dim), BF16)
    dq_part_spec = pl.BlockSpec(dq_part_shape.shape, lambda h, *_: (0, 0, 0))
    run = pltpu.VMEM((window, tokens, dim), BF16)
    acc = pltpu.VMEM((2 * halo, tokens, dim), F32)
    product = 2 * half * 2 * count * tokens * group * tokens * dim

    k_pairs = halo_of(k_own)
    v_pairs = halo_of(v_own)
    prob, *dv_halo = call(
        functools.partial(prob_kernel, halo),
        "prob",
        (half,),
        (place, doc_lengths),
        (in_vmem(qd), *k_pairs),
        [qd_spec] + [pair_spec] * (halo + 1),
        [p_shape] + [jax.ShapeDtypeStruct(pair, BF16)] * halo,
        [p_spec] + [pair_spec] * halo,
        [run, acc, pltpu.VMEM((2, 1, HEADS_AT_ONCE * tokens), jnp.int32)],
        4 * product,
    )
    dv_back = sent_back(dv_halo)
    dscore, *dk_halo = call(
        functools.partial(dscore_kernel, halo),
        "dscore",
        (half,),
        place,
        (in_vmem(qd), in_vmem(prob), *v_pairs),
        [qd_spec, p_spec] + [pair_spec] * (halo + 1),
        [p_shape] + [jax.ShapeDtypeStruct(pair, BF16)] * halo,
        [p_spec] + [pair_spec] * halo,
        [run, acc],
        4 * product,
    )
    dk_back = sent_back(dk_halo)
    dq, *dq_others, dk_own, dv, dv_other = call(
        functools.partial(own_kernel, halo),
        "own",
        (half,),
        place,
        (in_vmem(qd), in_vmem(prob), in_vmem(dscore), *k_pairs, *dv_back),
        [qd_spec, p_spec, p_spec] + [pair_spec] * (2 * halo + 1),
        [dq_shape] + [dq_part_shape] * 2 + [jax.ShapeDtypeStruct(pair, F32)] + [one_shape] * 2,
        [dq_spec] + [dq_part_spec] * 2 + [pair_spec] + [one_spec] * 2,
        [
            run,
            pltpu.VMEM((2, tokens * heads // 2, dim), F32),
            pltpu.VMEM((2, tokens, dim), F32),
        ],
        0,
    )
    dq_others = [swapped(part, device_count) for part in dq_others]
    dv_other = swapped(dv_other, device_count)
    dk, dk_other = summed(place, dk_own, dk_back)
    return tuple(finish(place, dq, dq_others, dk, swapped(dk_other, device_count), dv, dv_other))


def solution(mesh):
    spec = P(AXES, None, None)
    return jax.shard_map(
        local, mesh=mesh, in_specs=(spec,) * 4 + (P(),), out_specs=(spec,) * 3, check_vma=False
    )
```

```python
import functools

import jax
import jax.numpy as jnp
from jax import lax
from jax.experimental import pallas as pl
from jax.experimental.pallas import tpu as pltpu
from jax.sharding import PartitionSpec as P

AXES = ("ctx", "uly")
MASKED = -1e30
HEADS_AT_ONCE = 2
BF16, F32 = jnp.bfloat16, jnp.float32
NT = (((1,), (1,)), ((), ()))
VMEM_BYTES = 16 * 2**20


def moved(array, device_count, by):
    pairs = [(d, d + by) for d in range(device_count) if 0 <= d + by < device_count]
    return lax.ppermute(array, AXES, pairs)


def swapped(array, device_count):
    return lax.ppermute(array, AXES, [(d, d ^ 1) for d in range(device_count)])


def in_vmem(array):
    return pltpu.with_memory_space_constraint(array, pltpu.VMEM)


def in_hbm(array):
    return pltpu.with_memory_space_constraint(array, pltpu.HBM)


def call(kernel, name, grid, place, inputs, in_specs, outs, out_specs, scratch, flops, aliases={}):
    scalars = place if isinstance(place, tuple) else (place,)
    return pl.pallas_call(
        kernel,
        out_shape=outs,
        grid_spec=pltpu.PrefetchScalarGridSpec(
            num_scalar_prefetch=len(scalars),
            grid=grid,
            in_specs=in_specs,
            out_specs=out_specs,
            scratch_shapes=scratch,
        ),
        compiler_params=pltpu.CompilerParams(vmem_limit_bytes=VMEM_BYTES),
        cost_estimate=pl.CostEstimate(flops=flops, bytes_accessed=0, transcendentals=0),
        input_output_aliases=aliases,
        name=name,
    )(*scalars, *inputs)


def arrange_kernel(group, place_ref, q_ref, do_ref, q_other_ref, do_other_ref, out_ref, scr):
    core = place_ref[0]
    tokens, heads, dim = q_ref.shape
    half = heads // 2
    mine = pl.ds(pl.multiple_of(core * half, half), half)
    turn = 0
    for kind, (own, other) in enumerate([(q_ref, q_other_ref), (do_ref, do_other_ref)]):
        for which, ref in enumerate([own, other]):
            block = 1 - core if which else core
            wide = scr.at[turn % 2]
            wide[...] = ref[:, mine].astype(F32).reshape(tokens * half, dim)
            for h in range(half):
                out_ref[h // group, block, kind, h % group] = wide[pl.ds(h, tokens, stride=half), :].astype(BF16)
            turn += 1


def arrange(place, queries, grad_out, q_other, do_other, key_heads):
    tokens, heads, dim = queries.shape
    half, group = heads // 2, heads // key_heads
    whole = pl.BlockSpec(memory_space=pltpu.VMEM)
    return call(
        functools.partial(arrange_kernel, group),
        "arrange",
        (1,),
        place,
        [in_vmem(x) for x in (queries, grad_out, q_other, do_other)],
        [whole] * 4,
        pltpu.VMEM((key_heads // 2, 2, 2, group, tokens, dim), BF16),
        whole,
        [pltpu.VMEM((2, tokens * half, dim), F32)],
        10**9,
    )


def pack_block(raw, core, block, out_ref, scr):
    tokens, heads, dim = raw.shape
    half = heads // 2
    scr[...] = raw[...].astype(F32).reshape(tokens * heads, dim)
    for h in range(half):
        out_ref[h, block] = scr[pl.ds(core * half + h, tokens, stride=heads), :].astype(BF16)


def fetch_kernel(place_ref, key_ref, *refs):
    count = (len(refs) - 4) // 2
    sources, out_ref, targets = refs[:count], refs[count], refs[count + 1 : 2 * count + 1]
    raw, scr, sems = refs[-3:]
    first = pltpu.make_async_copy(key_ref, raw, sems.at[0])
    first.start()
    copies = [pltpu.make_async_copy(s, t, sems.at[i + 1]) for i, (s, t) in enumerate(zip(sources, targets))]
    for copy in copies:
        copy.start()
    first.wait()
    pack_block(raw, place_ref[0], place_ref[0], out_ref, scr)
    for copy in copies:
        copy.wait()


def fetch(place, keys, arrays):
    tokens, heads, dim = keys.shape
    out = (heads // 2, 2, tokens, dim)
    return call(
        fetch_kernel,
        "fetch",
        (1,),
        place,
        [in_hbm(x) for x in (keys, *arrays)],
        [pl.BlockSpec(memory_space=pltpu.HBM)] * (1 + len(arrays)),
        [pltpu.VMEM(out, BF16)] + [pltpu.VMEM(x.shape, x.dtype) for x in arrays],
        [pl.BlockSpec(memory_space=pltpu.VMEM)] * (1 + len(arrays)),
        [
            pltpu.VMEM(keys.shape, BF16),
            pltpu.VMEM((tokens * heads, dim), F32),
            pltpu.SemaphoreType.DMA((1 + len(arrays),)),
        ],
        10**9,
    )


def pack_other_kernel(place_ref, other_ref, _, out_ref, scr):
    pack_block(other_ref, place_ref[0], 1 - place_ref[0], out_ref, scr)


def pack_other(place, other, packed):
    tokens, heads, dim = other.shape
    whole = pl.BlockSpec(memory_space=pltpu.VMEM)
    return call(
        pack_other_kernel,
        "pack_other",
        (1,),
        place,
        (in_vmem(other), in_vmem(packed)),
        [whole] * 2,
        pltpu.VMEM(packed.shape, BF16),
        whole,
        [pltpu.VMEM((tokens * heads, dim), F32)],
        10**9,
        {2: 0},
    )


def pack_both_kernel(place_ref, own_ref, other_ref, out_ref, scr):
    core = place_ref[0]
    pack_block(own_ref, core, core, out_ref, scr)
    pack_block(other_ref, core, 1 - core, out_ref, scr)


def pack_both(place, own, other):
    tokens, heads, dim = own.shape
    out = (heads // 2, 2, tokens, dim)
    whole = pl.BlockSpec(memory_space=pltpu.VMEM)
    return call(
        pack_both_kernel,
        "pack_both",
        (1,),
        place,
        (in_vmem(own), in_vmem(other)),
        [whole] * 2,
        pltpu.VMEM(out, BF16),
        whole,
        [pltpu.VMEM((tokens * heads, dim), F32)],
        10**9,
    )


def folded(op, x):
    while x.shape[0] > 8:
        half = x.shape[0] // 2
        x = op(x[:half], x[half:])
    reduce = jnp.max if op is jnp.maximum else jnp.sum
    return reduce(x, axis=0, keepdims=True)


def first_allowed(lengths_ref, query_pos, window_start):
    def step(d, carry):
        start, first = carry
        first = jnp.where(query_pos + window_start >= start, start, first)
        return start + lengths_ref[d], first

    zero = jnp.zeros(query_pos.shape, jnp.int32)
    _, first = lax.fori_loop(0, lengths_ref.shape[0], step, (jnp.int32(0), zero))
    return first - window_start


def window_of(pair_refs, scr):
    count = len(pair_refs)
    for back, ref in enumerate(pair_refs):
        scr[pl.ds(2 * (count - 1 - back), 2)] = ref[0]


def on_diagonal(tokens, copies):
    row = lax.broadcasted_iota(jnp.int32, (tokens, tokens), 0)
    lane = lax.broadcasted_iota(jnp.int32, (tokens, tokens), 1)
    return jnp.concatenate([row] * copies, axis=1), jnp.concatenate([lane] * copies, axis=1)


def store_tiles(ref, e, at, tiles, diagonal):
    tokens, pair = diagonal.shape
    lanes = slice(at, at + pair)
    ref[0, e, :tokens, lanes] = jnp.where(diagonal, 0.0, tiles[0]).astype(BF16)
    for j, tile in enumerate(tiles[1:], 1):
        ref[0, e, j * tokens : (j + 1) * tokens, lanes] = tile.astype(BF16)
    ref[0, e, -tokens:, lanes] = jnp.where(diagonal, tiles[0], 0.0).astype(BF16)


def near_kernel(halo, place_ref, lengths_ref, qd_ref, k_ref, v_ref, s_ref, dp_ref, firsts):
    _, _, _, group, tokens, dim = qd_ref.shape
    lanes = group * tokens
    row, lane = on_diagonal(tokens, group)

    @pl.when(pl.program_id(0) == 0)
    def _():
        for e in range(2):
            query_pos = lane[:1] + (2 * halo + e) * tokens
            firsts[e] = first_allowed(lengths_ref, query_pos, place_ref[1])

    for e in range(2):
        rows = (e + 1) * tokens
        q = qd_ref[0, e, 0].reshape(lanes, dim)
        do = qd_ref[0, e, 1].reshape(lanes, dim)
        k = k_ref[0, : e + 1].reshape(rows, dim)
        v = v_ref[0, : e + 1].reshape(rows, dim)
        s = lax.dot_general(k, q, NT, preferred_element_type=F32)
        dp_ref[0, e * tokens : e * tokens + rows] = lax.dot_general(v, do, NT, preferred_element_type=F32)
        first = firsts[e] - row
        for j in range(e + 1):
            allowed = first <= (2 * halo + j) * tokens
            if j == e:
                allowed &= row <= lane
            tile = jnp.where(allowed, s[j * tokens : (j + 1) * tokens], MASKED)
            s_ref[0, (e + j) * tokens : (e + j + 1) * tokens] = tile


def prob_kernel(halo, place_ref, lengths_ref, qd_ref, near_ref, *refs):
    k_refs = refs[:halo]
    p_ref = refs[halo]
    dv_refs = refs[halo + 1 : -3]
    k_scr, acc, firsts = refs[-3:]
    _, _, _, group, tokens, dim = qd_ref.shape
    pair = HEADS_AT_ONCE * tokens
    row, lane = on_diagonal(tokens, HEADS_AT_ONCE)
    diagonal = row <= lane

    @pl.when(pl.program_id(0) == 0)
    def _():
        for e in range(2):
            query_pos = lane[:1] + (2 * halo + e) * tokens
            firsts[e] = first_allowed(lengths_ref, query_pos, place_ref[1])

    window_of(k_refs, k_scr)
    for e in range(2):
        first = firsts[e] - row
        far = 2 * halo - e
        k = k_scr[pl.ds(e, far)].reshape(far * tokens, dim)
        q = qd_ref[0, e, 0].reshape(group * tokens, dim)
        do = qd_ref[0, e, 1].reshape(group * tokens, dim)
        for at in range(0, group * tokens, pair):
            s = lax.dot_general(k, q[at : at + pair], NT, preferred_element_type=F32)
            tiles = [
                jnp.where(first <= (e + j) * tokens, s[j * tokens : (j + 1) * tokens], MASKED) for j in range(far)
            ]
            tiles += near_tiles(near_ref, e, at, pair)
            tiles[0] = jnp.where(diagonal, tiles.pop(), tiles[0])
            top = folded(jnp.maximum, functools.reduce(jnp.maximum, tiles))
            tiles = [jnp.exp((tile - top) * dim**-0.5) for tile in tiles]
            inv = 1.0 / folded(jnp.add, functools.reduce(jnp.add, tiles))
            store_tiles(p_ref, e, at, [tile * inv for tile in tiles], diagonal)
        dv = jnp.dot(p_ref[0, e, : far * tokens], do, preferred_element_type=F32).reshape(far, tokens, dim)
        if e == 0:
            acc[...] = dv
        else:
            acc[1:] += dv
    for back, ref in zip(range(1, halo + 1), dv_refs):
        ref[0] = acc[pl.ds(2 * (halo - back), 2)].astype(BF16)


def near_tiles(ref, e, at, pair):
    tokens = ref.shape[1] // 3
    return [ref[0, (e + j) * tokens : (e + j + 1) * tokens, at : at + pair] for j in range(e + 1)]


def dscore_kernel(halo, place_ref, qd_ref, p_ref, near_ref, *refs):
    v_refs = refs[:halo]
    ds_ref = refs[halo]
    dk_refs = refs[halo + 1 : -2]
    v_scr, acc = refs[-2:]
    _, _, _, group, tokens, dim = qd_ref.shape
    count = 2 * halo + 1
    pair = HEADS_AT_ONCE * tokens
    row, lane = on_diagonal(tokens, HEADS_AT_ONCE)
    diagonal = row <= lane
    window_of(v_refs, v_scr)
    for e in range(2):
        far = 2 * halo - e
        v = v_scr[pl.ds(e, far)].reshape(far * tokens, dim)
        q = qd_ref[0, e, 0].reshape(group * tokens, dim)
        do = qd_ref[0, e, 1].reshape(group * tokens, dim)
        for at in range(0, group * tokens, pair):
            dp = lax.dot_general(v, do[at : at + pair], NT, preferred_element_type=F32)
            dps = [dp[j * tokens : (j + 1) * tokens] for j in range(far)]
            dps += near_tiles(near_ref, e, at, pair)
            dps[0] = jnp.where(diagonal, dps.pop(), dps[0])
            ps = [p_ref[0, e, j * tokens : (j + 1) * tokens, at : at + pair] for j in range(count)]
            ps[0] += ps.pop()
            ps = [p.astype(F32) for p in ps]
            delta = folded(jnp.add, functools.reduce(jnp.add, [p * dp for p, dp in zip(ps, dps)]))
            store_tiles(ds_ref, e, at, [p * (dp - delta) for p, dp in zip(ps, dps)], diagonal)
        dk = jnp.dot(ds_ref[0, e, : far * tokens], q, preferred_element_type=F32).reshape(far, tokens, dim)
        if e == 0:
            acc[...] = dk
        else:
            acc[1:] += dk
    for back, ref in zip(range(1, halo + 1), dk_refs):
        ref[0] = (acc[pl.ds(2 * (halo - back), 2)] * dim**-0.5).astype(BF16)


def own_kernel(halo, place_ref, qd_ref, p_ref, ds_ref, *refs):
    k_refs, back_refs = refs[: halo + 1], refs[halo + 1 : 2 * halo + 1]
    dq_ref, *dq_other_refs, dk_ref, dv_ref, dv_other_ref, k_scr, dq_scr, dv_scr = refs[2 * halo + 1 :]
    core, head = place_ref[0], pl.program_id(0)
    _, _, _, group, tokens, dim = qd_ref.shape
    rows = dq_ref.shape[1]
    count = 2 * halo + 1
    scale = dim**-0.5
    window_of(k_refs, k_scr)
    for e in range(2):
        q = qd_ref[0, e, 0].reshape(group * tokens, dim)
        do = qd_ref[0, e, 1].reshape(group * tokens, dim)
        k = k_scr[pl.ds(e, count)].reshape(count * tokens, dim)
        dqt = jnp.dot(k.T, ds_ref[0, e], preferred_element_type=F32) * scale
        for g in range(group):
            dq_scr[e, pl.ds(head * group + g, tokens, stride=rows), :] = dqt[:, g * tokens : (g + 1) * tokens].T
        keep = (2 * halo - e) * tokens
        dk = jnp.dot(ds_ref[0, e, keep:], q, preferred_element_type=F32) * scale
        dv = jnp.dot(p_ref[0, e, keep:], do, preferred_element_type=F32)
        if e == 0:
            dk_ref[0, 0], dv_scr[0] = dk, dv
        else:
            dk_ref[0, 0] += dk[:tokens]
            dv_scr[0] += dv[:tokens]
            dk_ref[0, 1], dv_scr[1] = dk[tokens:], dv[tokens:]
    for ref in back_refs:
        dv_scr[...] += ref[0].astype(F32)
    dv_ref[0] = dv_scr[core].astype(BF16)
    dv_other_ref[0] = dv_scr[1 - core].astype(BF16)

    @pl.when(head == pl.num_programs(0) - 1)
    def _():
        dq_ref[...] = dq_scr[core].astype(BF16).reshape(dq_ref.shape)
        at = 0
        for ref in dq_other_refs:
            part = ref.shape[0] * rows
            ref[...] = dq_scr[1 - core, at : at + part].astype(BF16).reshape(ref.shape)
            at += part


def sum_kernel(place_ref, own_ref, *refs):
    back_refs, (mine_ref, other_ref) = refs[:-2], refs[-2:]
    core = place_ref[0]
    for block, ref in [(1 - core, other_ref), (core, mine_ref)]:
        total = own_ref[:, block]
        for back in back_refs:
            total += back[:, block].astype(F32)
        ref[...] = total.astype(BF16)


def summed(place, own, backs):
    half, _, tokens, dim = own.shape
    pair_spec = pl.BlockSpec(own.shape, lambda i, place: (0, 0, 0, 0))
    one = (half, tokens, dim)
    return call(
        sum_kernel,
        "sum_dk",
        (1,),
        place,
        (own, *backs),
        [pair_spec] * (1 + len(backs)),
        [jax.ShapeDtypeStruct(one, BF16)] * 2,
        [pl.BlockSpec(one, lambda i, place: (0, 0, 0))] * 2,
        [],
        0,
    )


def finish_kernel(parts, place_ref, *refs):
    dq, others, (dk, dk_other, dv, dv_other) = refs[0], refs[1 : 1 + parts], refs[1 + parts : 5 + parts]
    dq_out, dk_out, dv_out, scr, sems = refs[5 + parts :]
    core = place_ref[0]
    rows, heads, dim = dk_out.shape
    half, q_half = heads // 2, dq.shape[1]
    at = pl.multiple_of(core * q_half, q_half)
    copies = [pltpu.make_async_copy(dq, dq_out.at[:, pl.ds(at, q_half)], sems.at[0])]
    at = pl.multiple_of((1 - core) * q_half, q_half)
    first = 0
    for i, part in enumerate(others):
        to = dq_out.at[pl.ds(first, part.shape[0]), pl.ds(at, q_half)]
        copies.append(pltpu.make_async_copy(part, to, sems.at[1 + i]))
        first += part.shape[0]
    for copy in copies:
        copy.start()
    for n, (own, other, out) in enumerate([(dk, dk_other, dk_out), (dv, dv_other, dv_out)]):
        for which, ref in enumerate([own, other]):
            side = 1 - core if which else core
            for h in range(half):
                scr[n, pl.ds(side * half + h, rows, stride=heads), :] = ref[h].astype(F32)
        out[...] = scr[n].astype(BF16).reshape(rows, heads, dim)
    for copy in copies:
        copy.wait()


def finish(place, dq, dq_others, dk, dk_other, dv, dv_other):
    half, tokens, dim = dk.shape
    anywhere = pl.BlockSpec(memory_space=pl.ANY)
    in_spec = pl.BlockSpec(dk.shape, lambda i, place: (0, 0, 0))
    out = (tokens, 2 * half, dim)
    parts = len(dq_others)
    return call(
        functools.partial(finish_kernel, parts),
        "finish",
        (1,),
        place,
        (dq, *dq_others, dk, dk_other, dv, dv_other),
        [anywhere] * (1 + parts) + [in_spec] * 4,
        [jax.ShapeDtypeStruct((tokens, 2 * dq.shape[1], dim), BF16)] + [jax.ShapeDtypeStruct(out, BF16)] * 2,
        [anywhere] + [pl.BlockSpec(out, lambda i, place: (0, 0, 0))] * 2,
        [pltpu.VMEM((2, tokens * 2 * half, dim), F32), pltpu.SemaphoreType.DMA((1 + parts,))],
        0,
    )


def local(queries, keys, values, grad_out, doc_lengths):
    uly_count = lax.axis_size("uly")
    device_count = lax.axis_size("ctx") * uly_count
    halo = uly_count // 2
    device = lax.axis_index("ctx") * uly_count + lax.axis_index("uly")
    core = device % 2
    tokens, heads, dim = queries.shape
    key_heads = keys.shape[1]
    group = heads // key_heads
    half = key_heads // 2
    window, count = 2 * halo + 2, 2 * halo + 1
    place = jnp.stack([core, (device // 2 - halo) * (2 * tokens)]).astype(jnp.int32)

    far_first = range(halo, 0, -1)
    k_other = swapped(keys, device_count)
    k_mine, v_mine = fetch(place, keys, (values,))
    k_own = pack_other(place, k_other, k_mine)
    k_own, queries, grad_out, v_mine = lax.optimization_barrier((k_own, queries, grad_out, v_mine))
    q_other, do_other, v_other = (swapped(x, device_count) for x in (queries, grad_out, v_mine))
    qd = arrange(place, queries, grad_out, q_other, do_other, key_heads)
    v_own = pack_both(place, v_mine, v_other)

    def per_head(*shape):
        return pl.BlockSpec((1,) + shape, lambda h, *_: (h,) + (0,) * len(shape))

    qd_spec = per_head(2, 2, group, tokens, dim)
    pair_spec = per_head(2, tokens, dim)
    near_spec = per_head(3 * tokens, group * tokens)
    near_shape = pltpu.VMEM((half, 3 * tokens, group * tokens), F32)
    firsts = pltpu.VMEM((2, 1, group * tokens), jnp.int32)
    product = 2 * half * 2 * count * tokens * group * tokens * dim

    s_near, dp_near = call(
        functools.partial(near_kernel, halo),
        "near",
        (half,),
        (place, doc_lengths),
        (in_vmem(qd), in_vmem(k_own), in_vmem(v_own)),
        [qd_spec] + [pair_spec] * 2,
        [near_shape] * 2,
        [near_spec] * 2,
        [firsts],
        2 * product,
    )
    s_near, dp_near, v_own = lax.optimization_barrier((s_near, dp_near, v_own))

    def halo_of(own):
        received = {back: moved(own, device_count, 2 * back) for back in far_first}
        return [own] + [received[back] for back in range(1, halo + 1)]

    def sent_back(partials):
        return [moved(partials[back - 1], device_count, -2 * back) for back in far_first]

    p_spec = per_head(2, count * tokens, group * tokens)
    p_shape = pltpu.VMEM((half, 2, count * tokens, group * tokens), BF16)
    pair = (half, 2, tokens, dim)
    one_spec = per_head(tokens, dim)
    one_shape = jax.ShapeDtypeStruct((half, tokens, dim), BF16)
    dq_shape = jax.ShapeDtypeStruct((tokens, heads // 2, dim), BF16)
    dq_spec = pl.BlockSpec(dq_shape.shape, lambda h, *_: (0, 0, 0))
    dq_part_shape = jax.ShapeDtypeStruct((tokens // 2, heads // 2, dim), BF16)
    dq_part_spec = pl.BlockSpec(dq_part_shape.shape, lambda h, *_: (0, 0, 0))
    run = pltpu.VMEM((window, tokens, dim), BF16)
    halo_run = pltpu.VMEM((2 * halo, tokens, dim), BF16)
    acc = pltpu.VMEM((2 * halo, tokens, dim), F32)

    k_pairs = halo_of(k_own)
    v_pairs = halo_of(v_own)
    prob, *dv_halo = call(
        functools.partial(prob_kernel, halo),
        "prob",
        (half,),
        (place, doc_lengths),
        (in_vmem(qd), in_vmem(s_near), *k_pairs[1:]),
        [qd_spec, near_spec] + [pair_spec] * halo,
        [p_shape] + [jax.ShapeDtypeStruct(pair, BF16)] * halo,
        [p_spec] + [pair_spec] * halo,
        [halo_run, acc, pltpu.VMEM((2, 1, HEADS_AT_ONCE * tokens), jnp.int32)],
        4 * product,
    )
    dv_back = sent_back(dv_halo)
    dscore, *dk_halo = call(
        functools.partial(dscore_kernel, halo),
        "dscore",
        (half,),
        place,
        (in_vmem(qd), in_vmem(prob), in_vmem(dp_near), *v_pairs[1:]),
        [qd_spec, p_spec, near_spec] + [pair_spec] * halo,
        [p_shape] + [jax.ShapeDtypeStruct(pair, BF16)] * halo,
        [p_spec] + [pair_spec] * halo,
        [halo_run, acc],
        4 * product,
    )
    dk_back = sent_back(dk_halo)
    dq, *dq_others, dk_own, dv, dv_other = call(
        functools.partial(own_kernel, halo),
        "own",
        (half,),
        place,
        (in_vmem(qd), in_vmem(prob), in_vmem(dscore), *k_pairs, *dv_back),
        [qd_spec, p_spec, p_spec] + [pair_spec] * (2 * halo + 1),
        [dq_shape] + [dq_part_shape] * 2 + [jax.ShapeDtypeStruct(pair, F32)] + [one_shape] * 2,
        [dq_spec] + [dq_part_spec] * 2 + [pair_spec] + [one_spec] * 2,
        [
            run,
            pltpu.VMEM((2, tokens * heads // 2, dim), F32),
            pltpu.VMEM((2, tokens, dim), F32),
        ],
        0,
    )
    dq_others = [swapped(part, device_count) for part in dq_others]
    dv_other = swapped(dv_other, device_count)
    dk, dk_other = summed(place, dk_own, dk_back)
    return tuple(finish(place, dq, dq_others, dk, swapped(dk_other, device_count), dv, dv_other))


def solution(mesh):
    spec = P(AXES, None, None)
    return jax.shard_map(
        local, mesh=mesh, in_specs=(spec,) * 4 + (P(),), out_specs=(spec,) * 3, check_vma=False
    )
```

```python
import functools

import jax
import jax.numpy as jnp
from jax import lax
from jax.experimental import pallas as pl
from jax.experimental.pallas import tpu as pltpu
from jax.sharding import PartitionSpec as P

AXES = ("ctx", "uly")
MASKED = -1e30
LOG2E = 1.4426950408889634
HEADS_AT_ONCE = 2
BF16, F32 = jnp.bfloat16, jnp.float32
NT = (((1,), (1,)), ((), ()))
VMEM_BYTES = 16 * 2**20


def moved(array, device_count, by):
    pairs = [(d, d + by) for d in range(device_count) if 0 <= d + by < device_count]
    return lax.ppermute(array, AXES, pairs)


def swapped(array, device_count):
    return lax.ppermute(array, AXES, [(d, d ^ 1) for d in range(device_count)])


def in_vmem(array):
    return pltpu.with_memory_space_constraint(array, pltpu.VMEM)


def in_hbm(array):
    return pltpu.with_memory_space_constraint(array, pltpu.HBM)


def call(kernel, name, grid, place, inputs, in_specs, outs, out_specs, scratch, flops, aliases={}):
    scalars = place if isinstance(place, tuple) else (place,)
    return pl.pallas_call(
        kernel,
        out_shape=outs,
        grid_spec=pltpu.PrefetchScalarGridSpec(
            num_scalar_prefetch=len(scalars),
            grid=grid,
            in_specs=in_specs,
            out_specs=out_specs,
            scratch_shapes=scratch,
        ),
        compiler_params=pltpu.CompilerParams(vmem_limit_bytes=VMEM_BYTES),
        cost_estimate=pl.CostEstimate(flops=flops, bytes_accessed=0, transcendentals=0),
        input_output_aliases=aliases,
        name=name,
    )(*scalars, *inputs)


def arrange_kernel(group, place_ref, q_ref, do_ref, q_other_ref, do_other_ref, out_ref, scr):
    core = place_ref[0]
    tokens, heads, dim = q_ref.shape
    half = heads // 2
    mine = pl.ds(pl.multiple_of(core * half, half), half)
    turn = 0
    for kind, (own, other) in enumerate([(q_ref, q_other_ref), (do_ref, do_other_ref)]):
        for which, ref in enumerate([own, other]):
            block = 1 - core if which else core
            wide = scr.at[turn % 2]
            wide[...] = ref[:, mine].astype(F32).reshape(tokens * half, dim)
            for h in range(half):
                out_ref[h // group, block, kind, h % group] = wide[pl.ds(h, tokens, stride=half), :].astype(BF16)
            turn += 1


def arrange(place, queries, grad_out, q_other, do_other, key_heads):
    tokens, heads, dim = queries.shape
    half, group = heads // 2, heads // key_heads
    whole = pl.BlockSpec(memory_space=pltpu.VMEM)
    return call(
        functools.partial(arrange_kernel, group),
        "arrange",
        (1,),
        place,
        [in_vmem(x) for x in (queries, grad_out, q_other, do_other)],
        [whole] * 4,
        pltpu.VMEM((key_heads // 2, 2, 2, group, tokens, dim), BF16),
        whole,
        [pltpu.VMEM((2, tokens * half, dim), F32)],
        10**9,
    )


def pack_block(raw, core, block, out_ref, scr):
    tokens, heads, dim = raw.shape
    half = heads // 2
    scr[...] = raw[...].astype(F32).reshape(tokens * heads, dim)
    for h in range(half):
        out_ref[h, block] = scr[pl.ds(core * half + h, tokens, stride=heads), :].astype(BF16)


def fetch_kernel(place_ref, key_ref, *refs):
    count = (len(refs) - 4) // 2
    sources, out_ref, targets = refs[:count], refs[count], refs[count + 1 : 2 * count + 1]
    raw, scr, sems = refs[-3:]
    first = pltpu.make_async_copy(key_ref, raw, sems.at[0])
    first.start()
    copies = [pltpu.make_async_copy(s, t, sems.at[i + 1]) for i, (s, t) in enumerate(zip(sources, targets))]
    for copy in copies:
        copy.start()
    first.wait()
    pack_block(raw, place_ref[0], place_ref[0], out_ref, scr)
    for copy in copies:
        copy.wait()


def fetch(place, keys, arrays):
    tokens, heads, dim = keys.shape
    out = (heads // 2, 2, tokens, dim)
    return call(
        fetch_kernel,
        "fetch",
        (1,),
        place,
        [in_hbm(x) for x in (keys, *arrays)],
        [pl.BlockSpec(memory_space=pltpu.HBM)] * (1 + len(arrays)),
        [pltpu.VMEM(out, BF16)] + [pltpu.VMEM(x.shape, x.dtype) for x in arrays],
        [pl.BlockSpec(memory_space=pltpu.VMEM)] * (1 + len(arrays)),
        [
            pltpu.VMEM(keys.shape, BF16),
            pltpu.VMEM((tokens * heads, dim), F32),
            pltpu.SemaphoreType.DMA((1 + len(arrays),)),
        ],
        10**9,
    )


def pack_other_kernel(place_ref, other_ref, _, out_ref, scr):
    pack_block(other_ref, place_ref[0], 1 - place_ref[0], out_ref, scr)


def pack_other(place, other, packed):
    tokens, heads, dim = other.shape
    whole = pl.BlockSpec(memory_space=pltpu.VMEM)
    return call(
        pack_other_kernel,
        "pack_other",
        (1,),
        place,
        (in_vmem(other), in_vmem(packed)),
        [whole] * 2,
        pltpu.VMEM(packed.shape, BF16),
        whole,
        [pltpu.VMEM((tokens * heads, dim), F32)],
        10**9,
        {2: 0},
    )


def pack_both_kernel(place_ref, own_ref, other_ref, out_ref, scr):
    core = place_ref[0]
    pack_block(own_ref, core, core, out_ref, scr)
    pack_block(other_ref, core, 1 - core, out_ref, scr)


def pack_both(place, own, other):
    tokens, heads, dim = own.shape
    out = (heads // 2, 2, tokens, dim)
    whole = pl.BlockSpec(memory_space=pltpu.VMEM)
    return call(
        pack_both_kernel,
        "pack_both",
        (1,),
        place,
        (in_vmem(own), in_vmem(other)),
        [whole] * 2,
        pltpu.VMEM(out, BF16),
        whole,
        [pltpu.VMEM((tokens * heads, dim), F32)],
        10**9,
    )


def folded(op, x):
    while x.shape[0] > 8:
        half = x.shape[0] // 2
        x = op(x[:half], x[half:])
    reduce = jnp.max if op is jnp.maximum else jnp.sum
    return reduce(x, axis=0, keepdims=True)


def first_allowed(lengths_ref, query_pos, window_start):
    def step(d, carry):
        start, first = carry
        first = jnp.where(query_pos + window_start >= start, start, first)
        return start + lengths_ref[d], first

    zero = jnp.zeros(query_pos.shape, jnp.int32)
    _, first = lax.fori_loop(0, lengths_ref.shape[0], step, (jnp.int32(0), zero))
    return first - window_start


def window_of(pair_refs, scr):
    halo = len(pair_refs) - 1
    for back, ref in enumerate(pair_refs):
        scr[pl.ds(2 * (halo - back), 2)] = ref[0]


def on_diagonal(tokens, copies):
    row = lax.broadcasted_iota(jnp.int32, (tokens, tokens), 0)
    lane = lax.broadcasted_iota(jnp.int32, (tokens, tokens), 1)
    return jnp.concatenate([row] * copies, axis=1), jnp.concatenate([lane] * copies, axis=1)


def store_tiles(ref, e, at, tiles, diagonal):
    tokens, pair = diagonal.shape
    lanes = slice(at, at + pair)
    ref[0, e, :tokens, lanes] = jnp.where(diagonal, 0.0, tiles[0]).astype(BF16)
    for j, tile in enumerate(tiles[1:], 1):
        ref[0, e, j * tokens : (j + 1) * tokens, lanes] = tile.astype(BF16)
    ref[0, e, -tokens:, lanes] = jnp.where(diagonal, tiles[0], 0.0).astype(BF16)


def prob_kernel(halo, place_ref, lengths_ref, qd_ref, *refs):
    k_refs = refs[: halo + 1]
    w_ref, inv_ref, do_ref = refs[halo + 1 : halo + 4]
    dv_refs = refs[halo + 4 : -3]
    k_scr, acc, firsts = refs[-3:]
    _, _, _, group, tokens, dim = qd_ref.shape
    count = 2 * halo + 1
    pair = HEADS_AT_ONCE * tokens
    row, lane = on_diagonal(tokens, HEADS_AT_ONCE)
    diagonal = row <= lane

    @pl.when(pl.program_id(0) == 0)
    def _():
        for e in range(2):
            query_pos = lane[:1] + (2 * halo + e) * tokens
            firsts[e] = first_allowed(lengths_ref, query_pos, place_ref[1])

    window_of(k_refs, k_scr)
    for e in range(2):
        first = firsts[e] - row
        k = k_scr[pl.ds(e, count)].reshape(count * tokens, dim)
        q = qd_ref[0, e, 0].reshape(group * tokens, dim)
        for at in range(0, group * tokens, pair):
            s = lax.dot_general(k, q[at : at + pair], NT, preferred_element_type=F32)
            tiles = [s[j * tokens : (j + 1) * tokens] for j in range(count)]
            last = (e + count - 1) * tokens
            bound = jnp.where(diagonal, last, e * tokens)
            tiles[0] = jnp.where(first <= bound, jnp.where(diagonal, tiles.pop(), tiles[0]), MASKED)
            for j in range(1, count - 1):
                tiles[j] = jnp.where(first <= (e + j) * tokens, tiles[j], MASKED)
            top = folded(jnp.maximum, functools.reduce(jnp.maximum, tiles))
            tiles = [jnp.exp2((tile - top) * (dim**-0.5 * LOG2E)) for tile in tiles]
            store_tiles(w_ref, e, at, tiles, diagonal)
            inv = 1.0 / folded(jnp.add, functools.reduce(jnp.add, tiles))
            inv_ref[0, e, :, at : at + pair] = inv
            for g in range(at // tokens, (at + pair) // tokens):
                of_row = jnp.broadcast_to(inv[:, g * tokens - at : (g + 1) * tokens - at], (dim, tokens)).T
                do_ref[0, e, g] = (qd_ref[0, e, 1, g].astype(F32) * of_row).astype(BF16)
        do = do_ref[0, e].reshape(group * tokens, dim)
        keep = (2 * halo - e) * tokens
        dv = jnp.dot(w_ref[0, e, :keep], do, preferred_element_type=F32).reshape(2 * halo - e, tokens, dim)
        if e == 0:
            acc[...] = dv
        else:
            acc[1:] += dv
    for back, ref in zip(range(1, halo + 1), dv_refs):
        ref[0] = acc[pl.ds(2 * (halo - back), 2)].astype(BF16)


def dscore_kernel(halo, place_ref, qd_ref, w_ref, inv_ref, do_ref, *refs):
    v_refs = refs[: halo + 1]
    ds_ref = refs[halo + 1]
    dk_refs = refs[halo + 2 : -2]
    v_scr, acc = refs[-2:]
    _, _, _, group, tokens, dim = qd_ref.shape
    count = 2 * halo + 1
    pair = HEADS_AT_ONCE * tokens
    row, lane = on_diagonal(tokens, HEADS_AT_ONCE)
    diagonal = row <= lane
    window_of(v_refs, v_scr)
    for e in range(2):
        v = v_scr[pl.ds(e, count)].reshape(count * tokens, dim)
        q = qd_ref[0, e, 0].reshape(group * tokens, dim)
        do = do_ref[0, e].reshape(group * tokens, dim)
        for at in range(0, group * tokens, pair):
            dp = lax.dot_general(v, do[at : at + pair], NT, preferred_element_type=F32)
            dps = [dp[j * tokens : (j + 1) * tokens] for j in range(count)]
            dps[0] = jnp.where(diagonal, dps.pop(), dps[0])
            ws = [w_ref[0, e, j * tokens : (j + 1) * tokens, at : at + pair] for j in range(count)]
            ws[0] += ws.pop()
            ws = [w.astype(F32) for w in ws]
            delta = folded(jnp.add, functools.reduce(jnp.add, [w * dp for w, dp in zip(ws, dps)]))
            delta = delta * inv_ref[0, e, :, at : at + pair]
            store_tiles(ds_ref, e, at, [w * (dp - delta) for w, dp in zip(ws, dps)], diagonal)
        keep = (2 * halo - e) * tokens
        dk = jnp.dot(ds_ref[0, e, :keep], q, preferred_element_type=F32).reshape(2 * halo - e, tokens, dim)
        if e == 0:
            acc[...] = dk
        else:
            acc[1:] += dk
    for back, ref in zip(range(1, halo + 1), dk_refs):
        ref[0] = (acc[pl.ds(2 * (halo - back), 2)] * dim**-0.5).astype(BF16)


def own_kernel(halo, place_ref, qd_ref, w_ref, do_ref, ds_ref, *refs):
    k_refs, back_refs = refs[: halo + 1], refs[halo + 1 : 2 * halo + 1]
    dq_ref, *dq_other_refs, dk_ref, dv_ref, dv_other_ref, k_scr, dq_scr, dv_scr = refs[2 * halo + 1 :]
    core, head = place_ref[0], pl.program_id(0)
    _, _, _, group, tokens, dim = qd_ref.shape
    rows = dq_ref.shape[1]
    count = 2 * halo + 1
    scale = dim**-0.5
    window_of(k_refs, k_scr)
    for e in range(2):
        q = qd_ref[0, e, 0].reshape(group * tokens, dim)
        do = do_ref[0, e].reshape(group * tokens, dim)
        k = k_scr[pl.ds(e, count)].reshape(count * tokens, dim)
        dqt = jnp.dot(k.T, ds_ref[0, e], preferred_element_type=F32) * scale
        for g in range(group):
            dq_scr[e, pl.ds(head * group + g, tokens, stride=rows), :] = dqt[:, g * tokens : (g + 1) * tokens].T
        keep = (2 * halo - e) * tokens
        dk = jnp.dot(ds_ref[0, e, keep:], q, preferred_element_type=F32) * scale
        dv = jnp.dot(w_ref[0, e, keep:], do, preferred_element_type=F32)
        if e == 0:
            dk_ref[0, 0], dv_scr[0] = dk, dv
        else:
            dk_ref[0, 0] += dk[:tokens]
            dv_scr[0] += dv[:tokens]
            dk_ref[0, 1], dv_scr[1] = dk[tokens:], dv[tokens:]
    for ref in back_refs:
        dv_scr[...] += ref[0].astype(F32)
    dv_ref[0] = dv_scr[core].astype(BF16)
    dv_other_ref[0] = dv_scr[1 - core].astype(BF16)

    @pl.when(head == pl.num_programs(0) - 1)
    def _():
        dq_ref[...] = dq_scr[core].astype(BF16).reshape(dq_ref.shape)
        at = 0
        for ref in dq_other_refs:
            part = ref.shape[0] * rows
            ref[...] = dq_scr[1 - core, at : at + part].astype(BF16).reshape(ref.shape)
            at += part


def sum_kernel(place_ref, own_ref, *refs):
    back_refs, (mine_ref, other_ref) = refs[:-2], refs[-2:]
    core = place_ref[0]
    for block, ref in [(1 - core, other_ref), (core, mine_ref)]:
        total = own_ref[:, block]
        for back in back_refs:
            total += back[:, block].astype(F32)
        ref[...] = total.astype(BF16)


def summed(place, own, backs):
    half, _, tokens, dim = own.shape
    pair_spec = pl.BlockSpec(own.shape, lambda i, place: (0, 0, 0, 0))
    one = (half, tokens, dim)
    return call(
        sum_kernel,
        "sum_dk",
        (1,),
        place,
        (own, *backs),
        [pair_spec] * (1 + len(backs)),
        [jax.ShapeDtypeStruct(one, BF16)] * 2,
        [pl.BlockSpec(one, lambda i, place: (0, 0, 0))] * 2,
        [],
        0,
    )


def finish_kernel(parts, place_ref, *refs):
    dq, others, (dk, dk_other, dv, dv_other) = refs[0], refs[1 : 1 + parts], refs[1 + parts : 5 + parts]
    dq_out, dk_out, dv_out, scr, sems = refs[5 + parts :]
    core = place_ref[0]
    rows, heads, dim = dk_out.shape
    half, q_half = heads // 2, dq.shape[1]
    at = pl.multiple_of(core * q_half, q_half)
    copies = [pltpu.make_async_copy(dq, dq_out.at[:, pl.ds(at, q_half)], sems.at[0])]
    at = pl.multiple_of((1 - core) * q_half, q_half)
    first = 0
    for i, part in enumerate(others):
        to = dq_out.at[pl.ds(first, part.shape[0]), pl.ds(at, q_half)]
        copies.append(pltpu.make_async_copy(part, to, sems.at[1 + i]))
        first += part.shape[0]
    for copy in copies:
        copy.start()
    for n, (own, other, out) in enumerate([(dk, dk_other, dk_out), (dv, dv_other, dv_out)]):
        for which, ref in enumerate([own, other]):
            side = 1 - core if which else core
            for h in range(half):
                scr[n, pl.ds(side * half + h, rows, stride=heads), :] = ref[h].astype(F32)
        out[...] = scr[n].astype(BF16).reshape(rows, heads, dim)
    for copy in copies:
        copy.wait()


def finish(place, dq, dq_others, dk, dk_other, dv, dv_other):
    half, tokens, dim = dk.shape
    anywhere = pl.BlockSpec(memory_space=pl.ANY)
    in_spec = pl.BlockSpec(dk.shape, lambda i, place: (0, 0, 0))
    out = (tokens, 2 * half, dim)
    parts = len(dq_others)
    return call(
        functools.partial(finish_kernel, parts),
        "finish",
        (1,),
        place,
        (dq, *dq_others, dk, dk_other, dv, dv_other),
        [anywhere] * (1 + parts) + [in_spec] * 4,
        [jax.ShapeDtypeStruct((tokens, 2 * dq.shape[1], dim), BF16)] + [jax.ShapeDtypeStruct(out, BF16)] * 2,
        [anywhere] + [pl.BlockSpec(out, lambda i, place: (0, 0, 0))] * 2,
        [pltpu.VMEM((2, tokens * 2 * half, dim), F32), pltpu.SemaphoreType.DMA((1 + parts,))],
        0,
    )


def local(queries, keys, values, grad_out, doc_lengths):
    uly_count = lax.axis_size("uly")
    device_count = lax.axis_size("ctx") * uly_count
    halo = uly_count // 2
    device = lax.axis_index("ctx") * uly_count + lax.axis_index("uly")
    core = device % 2
    tokens, heads, dim = queries.shape
    key_heads = keys.shape[1]
    group = heads // key_heads
    half = key_heads // 2
    window, count = 2 * halo + 2, 2 * halo + 1
    place = jnp.stack([core, (device // 2 - halo) * (2 * tokens)]).astype(jnp.int32)

    far_first = range(halo, 0, -1)
    k_other = swapped(keys, device_count)
    k_mine, v_mine = fetch(place, keys, (values,))
    k_own = pack_other(place, k_other, k_mine)
    k_own, queries, grad_out, v_mine = lax.optimization_barrier((k_own, queries, grad_out, v_mine))
    q_other, do_other, v_other = (swapped(x, device_count) for x in (queries, grad_out, v_mine))
    qd = arrange(place, queries, grad_out, q_other, do_other, key_heads)
    qd, v_mine, v_other = lax.optimization_barrier((qd, v_mine, v_other))
    v_own = pack_both(place, v_mine, v_other)

    def halo_of(own):
        received = {back: moved(own, device_count, 2 * back) for back in far_first}
        return [own] + [received[back] for back in range(1, halo + 1)]

    def sent_back(partials):
        return [moved(partials[back - 1], device_count, -2 * back) for back in far_first]

    def per_head(*shape):
        return pl.BlockSpec((1,) + shape, lambda h, *_: (h,) + (0,) * len(shape))

    qd_spec = per_head(2, 2, group, tokens, dim)
    p_spec = per_head(2, count * tokens, group * tokens)
    p_shape = pltpu.VMEM((half, 2, count * tokens, group * tokens), BF16)
    inv_shape = pltpu.VMEM((half, 2, 1, group * tokens), F32)
    inv_spec = per_head(2, 1, group * tokens)
    do_shape = pltpu.VMEM((half, 2, group, tokens, dim), BF16)
    do_spec = per_head(2, group, tokens, dim)
    pair_spec = per_head(2, tokens, dim)
    pair = (half, 2, tokens, dim)
    one_spec = per_head(tokens, dim)
    one_shape = jax.ShapeDtypeStruct((half, tokens, dim), BF16)
    dq_shape = jax.ShapeDtypeStruct((tokens, heads // 2, dim), BF16)
    dq_spec = pl.BlockSpec(dq_shape.shape, lambda h, *_: (0, 0, 0))
    dq_part_shape = jax.ShapeDtypeStruct((tokens // 2, heads // 2, dim), BF16)
    dq_part_spec = pl.BlockSpec(dq_part_shape.shape, lambda h, *_: (0, 0, 0))
    run = pltpu.VMEM((window, tokens, dim), BF16)
    acc = pltpu.VMEM((2 * halo, tokens, dim), F32)
    product = 2 * half * 2 * count * tokens * group * tokens * dim

    k_pairs = halo_of(k_own)
    v_pairs = halo_of(v_own)
    prob, inverse, scaled, *dv_halo = call(
        functools.partial(prob_kernel, halo),
        "prob",
        (half,),
        (place, doc_lengths),
        (in_vmem(qd), *k_pairs),
        [qd_spec] + [pair_spec] * (halo + 1),
        [p_shape, inv_shape, do_shape] + [jax.ShapeDtypeStruct(pair, BF16)] * halo,
        [p_spec, inv_spec, do_spec] + [pair_spec] * halo,
        [run, acc, pltpu.VMEM((2, 1, HEADS_AT_ONCE * tokens), jnp.int32)],
        4 * product,
    )
    dv_back = sent_back(dv_halo)
    dscore, *dk_halo = call(
        functools.partial(dscore_kernel, halo),
        "dscore",
        (half,),
        place,
        (in_vmem(qd), in_vmem(prob), in_vmem(inverse), in_vmem(scaled), *v_pairs),
        [qd_spec, p_spec, inv_spec, do_spec] + [pair_spec] * (halo + 1),
        [p_shape] + [jax.ShapeDtypeStruct(pair, BF16)] * halo,
        [p_spec] + [pair_spec] * halo,
        [run, acc],
        4 * product,
    )
    dk_back = sent_back(dk_halo)
    dq, *dq_others, dk_own, dv, dv_other = call(
        functools.partial(own_kernel, halo),
        "own",
        (half,),
        place,
        (in_vmem(qd), in_vmem(prob), in_vmem(scaled), in_vmem(dscore), *k_pairs, *dv_back),
        [qd_spec, p_spec, do_spec, p_spec] + [pair_spec] * (2 * halo + 1),
        [dq_shape] + [dq_part_shape] * 2 + [jax.ShapeDtypeStruct(pair, F32)] + [one_shape] * 2,
        [dq_spec] + [dq_part_spec] * 2 + [pair_spec] + [one_spec] * 2,
        [
            run,
            pltpu.VMEM((2, tokens * heads // 2, dim), F32),
            pltpu.VMEM((2, tokens, dim), F32),
        ],
        0,
    )
    dq_others = [swapped(part, device_count) for part in dq_others]
    dv_other = swapped(dv_other, device_count)
    dk, dk_other = summed(place, dk_own, dk_back)
    return tuple(finish(place, dq, dq_others, dk, swapped(dk_other, device_count), dv, dv_other))


def solution(mesh):
    spec = P(AXES, None, None)
    return jax.shard_map(
        local, mesh=mesh, in_specs=(spec,) * 4 + (P(),), out_specs=(spec,) * 3, check_vma=False
    )
```

```python
import functools

import jax
import jax.numpy as jnp
from jax import lax
from jax.experimental import pallas as pl
from jax.experimental.pallas import tpu as pltpu
from jax.sharding import PartitionSpec as P

AXES = ("ctx", "uly")
MASKED = -1e30
LOG2E = 1.4426950408889634
HEADS_AT_ONCE = 2
BF16, F32 = jnp.bfloat16, jnp.float32
NT = (((1,), (1,)), ((), ()))
VMEM_BYTES = 16 * 2**20


def moved(array, device_count, by):
    pairs = [(d, d + by) for d in range(device_count) if 0 <= d + by < device_count]
    return lax.ppermute(array, AXES, pairs)


def swapped(array, device_count):
    return lax.ppermute(array, AXES, [(d, d ^ 1) for d in range(device_count)])


def in_vmem(array):
    return pltpu.with_memory_space_constraint(array, pltpu.VMEM)


def in_hbm(array):
    return pltpu.with_memory_space_constraint(array, pltpu.HBM)


def call(kernel, name, grid, place, inputs, in_specs, outs, out_specs, scratch, flops, aliases={}):
    scalars = place if isinstance(place, tuple) else (place,)
    return pl.pallas_call(
        kernel,
        out_shape=outs,
        grid_spec=pltpu.PrefetchScalarGridSpec(
            num_scalar_prefetch=len(scalars),
            grid=grid,
            in_specs=in_specs,
            out_specs=out_specs,
            scratch_shapes=scratch,
        ),
        compiler_params=pltpu.CompilerParams(vmem_limit_bytes=VMEM_BYTES),
        cost_estimate=pl.CostEstimate(flops=flops, bytes_accessed=0, transcendentals=0),
        input_output_aliases=aliases,
        name=name,
    )(*scalars, *inputs)


def arrange_kernel(group, place_ref, q_ref, do_ref, q_other_ref, do_other_ref, out_ref, scr):
    core = place_ref[0]
    tokens, heads, dim = q_ref.shape
    half = heads // 2
    mine = pl.ds(pl.multiple_of(core * half, half), half)
    turn = 0
    for kind, (own, other) in enumerate([(q_ref, q_other_ref), (do_ref, do_other_ref)]):
        for which, ref in enumerate([own, other]):
            block = 1 - core if which else core
            wide = scr.at[turn % 2]
            wide[...] = ref[:, mine].astype(F32).reshape(tokens * half, dim)
            for h in range(half):
                out_ref[h // group, block, kind, h % group] = wide[pl.ds(h, tokens, stride=half), :].astype(BF16)
            turn += 1


def arrange(place, queries, grad_out, q_other, do_other, key_heads):
    tokens, heads, dim = queries.shape
    half, group = heads // 2, heads // key_heads
    whole = pl.BlockSpec(memory_space=pltpu.VMEM)
    return call(
        functools.partial(arrange_kernel, group),
        "arrange",
        (1,),
        place,
        [in_vmem(x) for x in (queries, grad_out, q_other, do_other)],
        [whole] * 4,
        pltpu.VMEM((key_heads // 2, 2, 2, group, tokens, dim), BF16),
        whole,
        [pltpu.VMEM((2, tokens * half, dim), F32)],
        10**9,
    )


def pack_block(raw, core, block, out_ref, scr):
    tokens, heads, dim = raw.shape
    half = heads // 2
    scr[...] = raw[...].astype(F32).reshape(tokens * heads, dim)
    for h in range(half):
        out_ref[h, block] = scr[pl.ds(core * half + h, tokens, stride=heads), :].astype(BF16)


def fetch_kernel(place_ref, key_ref, *refs):
    count = (len(refs) - 4) // 2
    sources, out_ref, targets = refs[:count], refs[count], refs[count + 1 : 2 * count + 1]
    raw, scr, sems = refs[-3:]
    first = pltpu.make_async_copy(key_ref, raw, sems.at[0])
    first.start()
    copies = [pltpu.make_async_copy(s, t, sems.at[i + 1]) for i, (s, t) in enumerate(zip(sources, targets))]
    for copy in copies:
        copy.start()
    first.wait()
    pack_block(raw, place_ref[0], place_ref[0], out_ref, scr)
    for copy in copies:
        copy.wait()


def fetch(place, keys, arrays):
    tokens, heads, dim = keys.shape
    out = (heads // 2, 2, tokens, dim)
    return call(
        fetch_kernel,
        "fetch",
        (1,),
        place,
        [in_hbm(x) for x in (keys, *arrays)],
        [pl.BlockSpec(memory_space=pltpu.HBM)] * (1 + len(arrays)),
        [pltpu.VMEM(out, BF16)] + [pltpu.VMEM(x.shape, x.dtype) for x in arrays],
        [pl.BlockSpec(memory_space=pltpu.VMEM)] * (1 + len(arrays)),
        [
            pltpu.VMEM(keys.shape, BF16),
            pltpu.VMEM((tokens * heads, dim), F32),
            pltpu.SemaphoreType.DMA((1 + len(arrays),)),
        ],
        10**9,
    )


def pack_other_kernel(place_ref, other_ref, _, out_ref, scr):
    pack_block(other_ref, place_ref[0], 1 - place_ref[0], out_ref, scr)


def pack_other(place, other, packed):
    tokens, heads, dim = other.shape
    whole = pl.BlockSpec(memory_space=pltpu.VMEM)
    return call(
        pack_other_kernel,
        "pack_other",
        (1,),
        place,
        (in_vmem(other), in_vmem(packed)),
        [whole] * 2,
        pltpu.VMEM(packed.shape, BF16),
        whole,
        [pltpu.VMEM((tokens * heads, dim), F32)],
        10**9,
        {2: 0},
    )


def pack_both_kernel(place_ref, own_ref, other_ref, out_ref, scr):
    core = place_ref[0]
    pack_block(own_ref, core, core, out_ref, scr)
    pack_block(other_ref, core, 1 - core, out_ref, scr)


def pack_both(place, own, other):
    tokens, heads, dim = own.shape
    out = (heads // 2, 2, tokens, dim)
    whole = pl.BlockSpec(memory_space=pltpu.VMEM)
    return call(
        pack_both_kernel,
        "pack_both",
        (1,),
        place,
        (in_vmem(own), in_vmem(other)),
        [whole] * 2,
        pltpu.VMEM(out, BF16),
        whole,
        [pltpu.VMEM((tokens * heads, dim), F32)],
        10**9,
    )


def folded(op, x):
    while x.shape[0] > 8:
        half = x.shape[0] // 2
        x = op(x[:half], x[half:])
    reduce = jnp.max if op is jnp.maximum else jnp.sum
    return reduce(x, axis=0, keepdims=True)


def first_allowed(lengths_ref, query_pos, window_start):
    def step(d, carry):
        start, first = carry
        first = jnp.where(query_pos + window_start >= start, start, first)
        return start + lengths_ref[d], first

    zero = jnp.zeros(query_pos.shape, jnp.int32)
    _, first = lax.fori_loop(0, lengths_ref.shape[0], step, (jnp.int32(0), zero))
    return first - window_start


def window_of(pair_refs, scr):
    halo = len(pair_refs) - 1
    for back, ref in enumerate(pair_refs):
        scr[pl.ds(2 * (halo - back), 2)] = ref[0]


def on_diagonal(tokens, copies):
    row = lax.broadcasted_iota(jnp.int32, (tokens, tokens), 0)
    lane = lax.broadcasted_iota(jnp.int32, (tokens, tokens), 1)
    return jnp.concatenate([row] * copies, axis=1), jnp.concatenate([lane] * copies, axis=1)


def store_tiles(ref, e, at, tiles, diagonal):
    tokens, pair = diagonal.shape
    lanes = slice(at, at + pair)
    ref[0, e, :tokens, lanes] = jnp.where(diagonal, 0.0, tiles[0]).astype(BF16)
    for j, tile in enumerate(tiles[1:], 1):
        ref[0, e, j * tokens : (j + 1) * tokens, lanes] = tile.astype(BF16)
    ref[0, e, -tokens:, lanes] = jnp.where(diagonal, tiles[0], 0.0).astype(BF16)


def prob_kernel(halo, place_ref, lengths_ref, qd_ref, *refs):
    k_refs = refs[: halo + 1]
    p_ref = refs[halo + 1]
    dv_refs = refs[halo + 2 : -3]
    k_scr, acc, firsts = refs[-3:]
    _, _, _, group, tokens, dim = qd_ref.shape
    count = 2 * halo + 1
    pair = HEADS_AT_ONCE * tokens
    row, lane = on_diagonal(tokens, HEADS_AT_ONCE)
    diagonal = row <= lane

    @pl.when(pl.program_id(0) == 0)
    def _():
        for e in range(2):
            query_pos = lane[:1] + (2 * halo + e) * tokens
            firsts[e] = first_allowed(lengths_ref, query_pos, place_ref[1])

    window_of(k_refs, k_scr)
    for e in range(2):
        first = firsts[e] - row
        k = k_scr[pl.ds(e, count)].reshape(count * tokens, dim)
        q = qd_ref[0, e, 0].reshape(group * tokens, dim)
        do = qd_ref[0, e, 1].reshape(group * tokens, dim)
        for at in range(0, group * tokens, pair):
            s = lax.dot_general(k, q[at : at + pair], NT, preferred_element_type=F32)
            tiles = [s[j * tokens : (j + 1) * tokens] for j in range(count)]
            last = (e + count - 1) * tokens
            bound = jnp.where(diagonal, last, e * tokens)
            tiles[0] = jnp.where(first <= bound, jnp.where(diagonal, tiles.pop(), tiles[0]), MASKED)
            for j in range(1, count - 1):
                tiles[j] = jnp.where(first <= (e + j) * tokens, tiles[j], MASKED)
            top = folded(jnp.maximum, functools.reduce(jnp.maximum, tiles))
            tiles = [jnp.exp2((tile - top) * (dim**-0.5 * LOG2E)) for tile in tiles]
            inv = 1.0 / folded(jnp.add, functools.reduce(jnp.add, tiles))
            store_tiles(p_ref, e, at, [tile * inv for tile in tiles], diagonal)
        keep = (2 * halo - e) * tokens
        dv = jnp.dot(p_ref[0, e, :keep], do, preferred_element_type=F32).reshape(2 * halo - e, tokens, dim)
        if e == 0:
            acc[...] = dv
        else:
            acc[1:] += dv
    for back, ref in zip(range(1, halo + 1), dv_refs):
        ref[0] = acc[pl.ds(2 * (halo - back), 2)].astype(BF16)


def dscore_kernel(halo, place_ref, qd_ref, p_ref, *refs):
    v_refs = refs[: halo + 1]
    ds_ref = refs[halo + 1]
    dk_refs = refs[halo + 2 : -2]
    v_scr, acc = refs[-2:]
    _, _, _, group, tokens, dim = qd_ref.shape
    count = 2 * halo + 1
    pair = HEADS_AT_ONCE * tokens
    window_of(v_refs, v_scr)
    row, lane = on_diagonal(tokens, HEADS_AT_ONCE)
    diagonal = row <= lane
    for e in range(2):
        v = v_scr[pl.ds(e, count)].reshape(count * tokens, dim)
        q = qd_ref[0, e, 0].reshape(group * tokens, dim)
        do = qd_ref[0, e, 1].reshape(group * tokens, dim)
        for at in range(0, group * tokens, pair):
            dp = lax.dot_general(v, do[at : at + pair], NT, preferred_element_type=F32)
            dps = [dp[j * tokens : (j + 1) * tokens] for j in range(count)]
            dps[0] = jnp.where(diagonal, dps.pop(), dps[0])
            ps = [p_ref[0, e, j * tokens : (j + 1) * tokens, at : at + pair] for j in range(count)]
            ps[0] += ps.pop()
            ps = [p.astype(F32) for p in ps]
            delta = folded(jnp.add, functools.reduce(jnp.add, [p * dp for p, dp in zip(ps, dps)]))
            store_tiles(ds_ref, e, at, [p * (dp - delta) for p, dp in zip(ps, dps)], diagonal)
        keep = (2 * halo - e) * tokens
        dk = jnp.dot(ds_ref[0, e, :keep], q, preferred_element_type=F32).reshape(2 * halo - e, tokens, dim)
        if e == 0:
            acc[...] = dk
        else:
            acc[1:] += dk
    for back, ref in zip(range(1, halo + 1), dk_refs):
        ref[0] = (acc[pl.ds(2 * (halo - back), 2)] * dim**-0.5).astype(BF16)


def own_kernel(halo, place_ref, qd_ref, p_ref, ds_ref, *refs):
    k_refs, back_refs = refs[: halo + 1], refs[halo + 1 : 2 * halo + 1]
    dq_ref, *other_refs, dk_ref, dv_ref, k_scr, dq_scr, dv_scr, far_scr = refs[2 * halo + 1 :]
    core, head = place_ref[0], pl.program_id(0)
    _, _, _, group, tokens, dim = qd_ref.shape
    rows = dq_ref.shape[1]
    count = 2 * halo + 1
    scale = dim**-0.5
    window_of(k_refs, k_scr)
    for e in range(2):
        q = qd_ref[0, e, 0].reshape(group * tokens, dim)
        do = qd_ref[0, e, 1].reshape(group * tokens, dim)
        k = k_scr[pl.ds(e, count)].reshape(count * tokens, dim)
        dqt = jnp.dot(k.T, ds_ref[0, e], preferred_element_type=F32) * scale
        for g in range(group):
            dq_scr[e, pl.ds(head * group + g, tokens, stride=rows), :] = dqt[:, g * tokens : (g + 1) * tokens].T
        keep = (2 * halo - e) * tokens
        dk = jnp.dot(ds_ref[0, e, keep:], q, preferred_element_type=F32) * scale
        dv = jnp.dot(p_ref[0, e, keep:], do, preferred_element_type=F32)
        if e == 0:
            dk_ref[0, 0], dv_scr[0] = dk, dv
        else:
            dk_ref[0, 0] += dk[:tokens]
            dv_scr[0] += dv[:tokens]
            dk_ref[0, 1], dv_scr[1] = dk[tokens:], dv[tokens:]
    for ref in back_refs:
        dv_scr[...] += ref[0].astype(F32)
    dv_ref[0] = dv_scr[core].astype(BF16)
    dq_rows = tokens * rows
    at = dq_rows + head * tokens
    far_scr[pl.ds(pl.multiple_of(at, tokens), tokens)] = dv_scr[1 - core].astype(BF16)

    @pl.when(head == pl.num_programs(0) - 1)
    def _():
        dq_ref[...] = dq_scr[core].astype(BF16).reshape(dq_ref.shape)
        far_scr[:dq_rows] = dq_scr[1 - core].astype(BF16)
        start = 0
        for ref in other_refs:
            part = ref.shape[0] * rows
            ref[...] = far_scr[start : start + part].reshape(ref.shape)
            start += part


def sum_kernel(count, place_ref, own_ref, *refs):
    back_refs, (mine_ref, other_ref) = refs[:count], refs[-2:]
    core = place_ref[0]
    for block, ref in [(1 - core, other_ref), (core, mine_ref)]:
        total = own_ref[:, block]
        for back in back_refs:
            total += back[:, block].astype(F32)
        ref[...] = total.astype(BF16)


def summed(place, own, backs, before):
    half, _, tokens, dim = own.shape
    pair_spec = pl.BlockSpec(own.shape, lambda i, place: (0, 0, 0, 0))
    one = (half, tokens, dim)
    return call(
        functools.partial(sum_kernel, len(backs)),
        "sum_dk",
        (1,),
        place,
        (own, *backs, *(in_hbm(x) for x in before)),
        [pair_spec] * (1 + len(backs)) + [pl.BlockSpec(memory_space=pltpu.HBM)] * len(before),
        [jax.ShapeDtypeStruct(one, BF16)] * 2,
        [pl.BlockSpec(one, lambda i, place: (0, 0, 0))] * 2,
        [],
        0,
    )


def join_kernel(parts, place_ref, own_ref, *refs):
    others, out_ref, sems = refs[:parts], refs[-2], refs[-1]
    core = place_ref[0]
    tokens, half, _ = own_ref.shape
    at = pl.multiple_of(core * half, half)
    copies = [pltpu.make_async_copy(own_ref, out_ref.at[:, pl.ds(at, half)], sems.at[0])]
    at = pl.multiple_of((1 - core) * half, half)
    first = 0
    for i, part in enumerate(others):
        count = min(part.shape[0], tokens - first)
        to = out_ref.at[pl.ds(first, count), pl.ds(at, half)]
        copies.append(pltpu.make_async_copy(part.at[pl.ds(0, count)], to, sems.at[1 + i]))
        first += count
    for copy in copies:
        copy.start()
    for copy in copies:
        copy.wait()


def join(place, own, others):
    tokens, half, dim = own.shape
    anywhere = pl.BlockSpec(memory_space=pl.ANY)
    return call(
        functools.partial(join_kernel, len(others)),
        "join",
        (1,),
        place,
        (own, *others),
        [anywhere] * (1 + len(others)),
        jax.ShapeDtypeStruct((tokens, 2 * half, dim), BF16),
        anywhere,
        [pltpu.SemaphoreType.DMA((1 + len(others),))],
        0,
    )


def merge_kernel(place_ref, own_ref, other_ref, out_ref, scr):
    core = place_ref[0]
    rows, heads, dim = out_ref.shape
    half = heads // 2
    other = other_ref[...].reshape(-1, dim)
    skip = other.shape[0] - half * rows
    for h in range(half):
        scr[pl.ds(core * half + h, rows, stride=heads), :] = own_ref[h].astype(F32)
        rest = other[skip + h * rows : skip + (h + 1) * rows]
        scr[pl.ds((1 - core) * half + h, rows, stride=heads), :] = rest.astype(F32)
    out_ref[...] = scr[...].astype(BF16).reshape(rows, heads, dim)


def merge(place, own, other, name):
    half, tokens, dim = own.shape
    out = (tokens, 2 * half, dim)
    return call(
        merge_kernel,
        name,
        (1,),
        place,
        (own, other),
        [pl.BlockSpec(x.shape, lambda i, place: (0, 0, 0)) for x in (own, other)],
        jax.ShapeDtypeStruct(out, BF16),
        pl.BlockSpec(out, lambda i, place: (0, 0, 0)),
        [pltpu.VMEM((tokens * 2 * half, dim), F32)],
        0,
    )


def local(queries, keys, values, grad_out, doc_lengths):
    uly_count = lax.axis_size("uly")
    device_count = lax.axis_size("ctx") * uly_count
    halo = uly_count // 2
    device = lax.axis_index("ctx") * uly_count + lax.axis_index("uly")
    core = device % 2
    tokens, heads, dim = queries.shape
    key_heads = keys.shape[1]
    group = heads // key_heads
    half = key_heads // 2
    window, count = 2 * halo + 2, 2 * halo + 1
    place = jnp.stack([core, (device // 2 - halo) * (2 * tokens)]).astype(jnp.int32)

    far_first = range(halo, 0, -1)
    k_other = swapped(keys, device_count)
    k_mine, v_mine = fetch(place, keys, (values,))
    k_own = pack_other(place, k_other, k_mine)
    k_own, queries, grad_out, v_mine = lax.optimization_barrier((k_own, queries, grad_out, v_mine))
    q_other, do_other, v_other = (swapped(x, device_count) for x in (queries, grad_out, v_mine))
    qd = arrange(place, queries, grad_out, q_other, do_other, key_heads)
    qd, v_mine, v_other = lax.optimization_barrier((qd, v_mine, v_other))
    v_own = pack_both(place, v_mine, v_other)

    def halo_of(own):
        received = {back: moved(own, device_count, 2 * back) for back in far_first}
        return [own] + [received[back] for back in range(1, halo + 1)]

    def sent_back(partials):
        return [moved(partials[back - 1], device_count, -2 * back) for back in far_first]

    def per_head(*shape):
        return pl.BlockSpec((1,) + shape, lambda h, *_: (h,) + (0,) * len(shape))

    qd_spec = per_head(2, 2, group, tokens, dim)
    p_spec = per_head(2, count * tokens, group * tokens)
    p_shape = pltpu.VMEM((half, 2, count * tokens, group * tokens), BF16)
    pair_spec = per_head(2, tokens, dim)
    pair = (half, 2, tokens, dim)
    one_spec = per_head(tokens, dim)
    one_shape = jax.ShapeDtypeStruct((half, tokens, dim), BF16)
    dq_shape = jax.ShapeDtypeStruct((tokens, heads // 2, dim), BF16)
    dq_spec = pl.BlockSpec(dq_shape.shape, lambda h, *_: (0, 0, 0))
    far_rows = tokens + half * tokens // (heads // 2)
    step = (far_rows // 3 + 7) // 8 * 8
    parts = [
        jax.ShapeDtypeStruct((rows, heads // 2, dim), BF16) for rows in (step, step, far_rows - 2 * step)
    ]
    part_specs = [pl.BlockSpec(part.shape, lambda h, *_: (0, 0, 0)) for part in parts]
    run = pltpu.VMEM((window, tokens, dim), BF16)
    acc = pltpu.VMEM((2 * halo, tokens, dim), F32)
    product = 2 * half * 2 * count * tokens * group * tokens * dim

    k_pairs = halo_of(k_own)
    v_pairs = halo_of(v_own)
    prob, *dv_halo = call(
        functools.partial(prob_kernel, halo),
        "prob",
        (half,),
        (place, doc_lengths),
        (in_vmem(qd), *k_pairs),
        [qd_spec] + [pair_spec] * (halo + 1),
        [p_shape] + [jax.ShapeDtypeStruct(pair, BF16)] * halo,
        [p_spec] + [pair_spec] * halo,
        [run, acc, pltpu.VMEM((2, 1, HEADS_AT_ONCE * tokens), jnp.int32)],
        4 * product,
    )
    dv_back = sent_back(dv_halo)
    dscore, *dk_halo = call(
        functools.partial(dscore_kernel, halo),
        "dscore",
        (half,),
        place,
        (in_vmem(qd), in_vmem(prob), *v_pairs),
        [qd_spec, p_spec] + [pair_spec] * (halo + 1),
        [p_shape] + [jax.ShapeDtypeStruct(pair, BF16)] * halo,
        [p_spec] + [pair_spec] * halo,
        [run, acc],
        4 * product,
    )
    dk_back = sent_back(dk_halo)
    dq, *others, dk_own, dv = call(
        functools.partial(own_kernel, halo),
        "own",
        (half,),
        place,
        (in_vmem(qd), in_vmem(prob), in_vmem(dscore), *k_pairs, *dv_back),
        [qd_spec, p_spec, p_spec] + [pair_spec] * (2 * halo + 1),
        [dq_shape, *parts, jax.ShapeDtypeStruct(pair, F32), one_shape],
        [dq_spec, *part_specs, pair_spec, one_spec],
        [
            run,
            pltpu.VMEM((2, tokens * heads // 2, dim), F32),
            pltpu.VMEM((2, tokens, dim), F32),
            pltpu.VMEM((far_rows * heads // 2, dim), BF16),
        ],
        0,
    )
    others = [swapped(part, device_count) for part in others]
    grad_queries = join(place, dq, others)
    grad_values = merge(place, dv, others[-1], "merge_dv")
    dk, dk_other = summed(place, dk_own, dk_back, (grad_queries, grad_values))
    grad_keys = merge(place, dk, swapped(dk_other, device_count), "merge_dk")
    return grad_queries, grad_keys, grad_values


def solution(mesh):
    spec = P(AXES, None, None)
    return jax.shard_map(
        local, mesh=mesh, in_specs=(spec,) * 4 + (P(),), out_specs=(spec,) * 3, check_vma=False
    )
```

```python
import functools

import jax
import jax.numpy as jnp
from jax import lax
from jax.experimental import pallas as pl
from jax.experimental.pallas import tpu as pltpu
from jax.sharding import PartitionSpec as P

AXES = ("ctx", "uly")
MASKED = -1e30
LOG2E = 1.4426950408889634
HEADS_AT_ONCE = 1
BF16, F32 = jnp.bfloat16, jnp.float32
NT = (((1,), (1,)), ((), ()))
VMEM_BYTES = 16 * 2**20


def moved(array, device_count, by):
    pairs = [(d, d + by) for d in range(device_count) if 0 <= d + by < device_count]
    return lax.ppermute(array, AXES, pairs)


def swapped(array, device_count):
    return lax.ppermute(array, AXES, [(d, d ^ 1) for d in range(device_count)])


def in_vmem(array):
    return pltpu.with_memory_space_constraint(array, pltpu.VMEM)


def in_hbm(array):
    return pltpu.with_memory_space_constraint(array, pltpu.HBM)


def call(kernel, name, grid, place, inputs, in_specs, outs, out_specs, scratch, flops, aliases={}):
    scalars = place if isinstance(place, tuple) else (place,)
    return pl.pallas_call(
        kernel,
        out_shape=outs,
        grid_spec=pltpu.PrefetchScalarGridSpec(
            num_scalar_prefetch=len(scalars),
            grid=grid,
            in_specs=in_specs,
            out_specs=out_specs,
            scratch_shapes=scratch,
        ),
        compiler_params=pltpu.CompilerParams(vmem_limit_bytes=VMEM_BYTES),
        cost_estimate=pl.CostEstimate(flops=flops, bytes_accessed=0, transcendentals=0),
        input_output_aliases=aliases,
        name=name,
    )(*scalars, *inputs)


def arrange_kernel(group, place_ref, q_ref, do_ref, q_other_ref, do_other_ref, out_ref, scr):
    core = place_ref[0]
    tokens, heads, dim = q_ref.shape
    half = heads // 2
    mine = pl.ds(pl.multiple_of(core * half, half), half)
    turn = 0
    for kind, (own, other) in enumerate([(q_ref, q_other_ref), (do_ref, do_other_ref)]):
        for which, ref in enumerate([own, other]):
            block = 1 - core if which else core
            wide = scr.at[turn % 2]
            wide[...] = ref[:, mine].astype(F32).reshape(tokens * half, dim)
            for h in range(half):
                out_ref[h // group, block, kind, h % group] = wide[pl.ds(h, tokens, stride=half), :].astype(BF16)
            turn += 1


def arrange(place, queries, grad_out, q_other, do_other, key_heads):
    tokens, heads, dim = queries.shape
    half, group = heads // 2, heads // key_heads
    whole = pl.BlockSpec(memory_space=pltpu.VMEM)
    return call(
        functools.partial(arrange_kernel, group),
        "arrange",
        (1,),
        place,
        [in_vmem(x) for x in (queries, grad_out, q_other, do_other)],
        [whole] * 4,
        pltpu.VMEM((key_heads // 2, 2, 2, group, tokens, dim), BF16),
        whole,
        [pltpu.VMEM((2, tokens * half, dim), F32)],
        10**9,
    )


def pack_block(raw, core, block, out_ref, scr):
    tokens, heads, dim = raw.shape
    half = heads // 2
    scr[...] = raw[...].astype(F32).reshape(tokens * heads, dim)
    for h in range(half):
        out_ref[h, block] = scr[pl.ds(core * half + h, tokens, stride=heads), :].astype(BF16)


def fetch_kernel(place_ref, key_ref, *refs):
    count = (len(refs) - 4) // 2
    sources, out_ref, targets = refs[:count], refs[count], refs[count + 1 : 2 * count + 1]
    raw, scr, sems = refs[-3:]
    first = pltpu.make_async_copy(key_ref, raw, sems.at[0])
    first.start()
    copies = [pltpu.make_async_copy(s, t, sems.at[i + 1]) for i, (s, t) in enumerate(zip(sources, targets))]
    for copy in copies:
        copy.start()
    first.wait()
    pack_block(raw, place_ref[0], place_ref[0], out_ref, scr)
    for copy in copies:
        copy.wait()


def fetch(place, keys, arrays):
    tokens, heads, dim = keys.shape
    out = (heads // 2, 2, tokens, dim)
    return call(
        fetch_kernel,
        "fetch",
        (1,),
        place,
        [in_hbm(x) for x in (keys, *arrays)],
        [pl.BlockSpec(memory_space=pltpu.HBM)] * (1 + len(arrays)),
        [pltpu.VMEM(out, BF16)] + [pltpu.VMEM(x.shape, x.dtype) for x in arrays],
        [pl.BlockSpec(memory_space=pltpu.VMEM)] * (1 + len(arrays)),
        [
            pltpu.VMEM(keys.shape, BF16),
            pltpu.VMEM((tokens * heads, dim), F32),
            pltpu.SemaphoreType.DMA((1 + len(arrays),)),
        ],
        10**9,
    )


def pack_other_kernel(place_ref, other_ref, _, out_ref, scr):
    pack_block(other_ref, place_ref[0], 1 - place_ref[0], out_ref, scr)


def pack_other(place, other, packed):
    tokens, heads, dim = other.shape
    whole = pl.BlockSpec(memory_space=pltpu.VMEM)
    return call(
        pack_other_kernel,
        "pack_other",
        (1,),
        place,
        (in_vmem(other), in_vmem(packed)),
        [whole] * 2,
        pltpu.VMEM(packed.shape, BF16),
        whole,
        [pltpu.VMEM((tokens * heads, dim), F32)],
        10**9,
        {2: 0},
    )


def pack_both_kernel(place_ref, own_ref, other_ref, out_ref, scr):
    core = place_ref[0]
    pack_block(own_ref, core, core, out_ref, scr)
    pack_block(other_ref, core, 1 - core, out_ref, scr)


def pack_both(place, own, other):
    tokens, heads, dim = own.shape
    out = (heads // 2, 2, tokens, dim)
    whole = pl.BlockSpec(memory_space=pltpu.VMEM)
    return call(
        pack_both_kernel,
        "pack_both",
        (1,),
        place,
        (in_vmem(own), in_vmem(other)),
        [whole] * 2,
        pltpu.VMEM(out, BF16),
        whole,
        [pltpu.VMEM((tokens * heads, dim), F32)],
        10**9,
    )


def folded(op, x):
    while x.shape[0] > 8:
        half = x.shape[0] // 2
        x = op(x[:half], x[half:])
    reduce = jnp.max if op is jnp.maximum else jnp.sum
    return reduce(x, axis=0, keepdims=True)


def first_allowed(lengths_ref, query_pos, window_start):
    def step(d, carry):
        start, first = carry
        first = jnp.where(query_pos + window_start >= start, start, first)
        return start + lengths_ref[d], first

    zero = jnp.zeros(query_pos.shape, jnp.int32)
    _, first = lax.fori_loop(0, lengths_ref.shape[0], step, (jnp.int32(0), zero))
    return first - window_start


def window_of(pair_refs, scr):
    halo = len(pair_refs) - 1
    for back, ref in enumerate(pair_refs):
        scr[pl.ds(2 * (halo - back), 2)] = ref[0]


def on_diagonal(tokens, copies):
    row = lax.broadcasted_iota(jnp.int32, (tokens, tokens), 0)
    lane = lax.broadcasted_iota(jnp.int32, (tokens, tokens), 1)
    return jnp.concatenate([row] * copies, axis=1), jnp.concatenate([lane] * copies, axis=1)


def store_tiles(ref, e, at, tiles, diagonal):
    tokens, pair = diagonal.shape
    lanes = slice(at, at + pair)
    ref[0, e, :tokens, lanes] = jnp.where(diagonal, 0.0, tiles[0]).astype(BF16)
    for j, tile in enumerate(tiles[1:], 1):
        ref[0, e, j * tokens : (j + 1) * tokens, lanes] = tile.astype(BF16)
    ref[0, e, -tokens:, lanes] = jnp.where(diagonal, tiles[0], 0.0).astype(BF16)


def prob_kernel(halo, place_ref, lengths_ref, qd_ref, *refs):
    k_refs = refs[: halo + 1]
    p_ref = refs[halo + 1]
    dv_refs = refs[halo + 2 : -3]
    k_scr, acc, firsts = refs[-3:]
    _, _, _, group, tokens, dim = qd_ref.shape
    count = 2 * halo + 1
    pair = HEADS_AT_ONCE * tokens
    row, lane = on_diagonal(tokens, HEADS_AT_ONCE)
    diagonal = row <= lane

    @pl.when(pl.program_id(0) == 0)
    def _():
        for e in range(2):
            query_pos = lane[:1] + (2 * halo + e) * tokens
            firsts[e] = first_allowed(lengths_ref, query_pos, place_ref[1])

    window_of(k_refs, k_scr)
    for e in range(2):
        first = firsts[e] - row
        k = k_scr[pl.ds(e, count)].reshape(count * tokens, dim)
        q = qd_ref[0, e, 0].reshape(group * tokens, dim)
        do = qd_ref[0, e, 1].reshape(group * tokens, dim)
        for at in range(0, group * tokens, pair):
            s = lax.dot_general(k, q[at : at + pair], NT, preferred_element_type=F32)
            tiles = [s[j * tokens : (j + 1) * tokens] for j in range(count)]
            last = (e + count - 1) * tokens
            bound = jnp.where(diagonal, last, e * tokens)
            tiles[0] = jnp.where(first <= bound, jnp.where(diagonal, tiles.pop(), tiles[0]), MASKED)
            for j in range(1, count - 1):
                tiles[j] = jnp.where(first <= (e + j) * tokens, tiles[j], MASKED)
            top = folded(jnp.maximum, functools.reduce(jnp.maximum, tiles))
            tiles = [jnp.exp2((tile - top) * (dim**-0.5 * LOG2E)) for tile in tiles]
            inv = 1.0 / folded(jnp.add, functools.reduce(jnp.add, tiles))
            store_tiles(p_ref, e, at, [tile * inv for tile in tiles], diagonal)
        keep = (2 * halo - e) * tokens
        dv = jnp.dot(p_ref[0, e, :keep], do, preferred_element_type=F32).reshape(2 * halo - e, tokens, dim)
        if e == 0:
            acc[...] = dv
        else:
            acc[1:] += dv
    for back, ref in zip(range(1, halo + 1), dv_refs):
        ref[0] = acc[pl.ds(2 * (halo - back), 2)].astype(BF16)


def dscore_kernel(halo, place_ref, qd_ref, p_ref, *refs):
    v_refs = refs[: halo + 1]
    ds_ref = refs[halo + 1]
    dk_refs = refs[halo + 2 : -2]
    v_scr, acc = refs[-2:]
    _, _, _, group, tokens, dim = qd_ref.shape
    count = 2 * halo + 1
    pair = HEADS_AT_ONCE * tokens
    window_of(v_refs, v_scr)
    row, lane = on_diagonal(tokens, HEADS_AT_ONCE)
    diagonal = row <= lane
    for e in range(2):
        v = v_scr[pl.ds(e, count)].reshape(count * tokens, dim)
        q = qd_ref[0, e, 0].reshape(group * tokens, dim)
        do = qd_ref[0, e, 1].reshape(group * tokens, dim)
        for at in range(0, group * tokens, pair):
            dp = lax.dot_general(v, do[at : at + pair], NT, preferred_element_type=F32)
            dps = [dp[j * tokens : (j + 1) * tokens] for j in range(count)]
            dps[0] = jnp.where(diagonal, dps.pop(), dps[0])
            ps = [p_ref[0, e, j * tokens : (j + 1) * tokens, at : at + pair] for j in range(count)]
            ps[0] += ps.pop()
            ps = [p.astype(F32) for p in ps]
            delta = folded(jnp.add, functools.reduce(jnp.add, [p * dp for p, dp in zip(ps, dps)]))
            store_tiles(ds_ref, e, at, [p * (dp - delta) for p, dp in zip(ps, dps)], diagonal)
        keep = (2 * halo - e) * tokens
        dk = jnp.dot(ds_ref[0, e, :keep], q, preferred_element_type=F32).reshape(2 * halo - e, tokens, dim)
        if e == 0:
            acc[...] = dk
        else:
            acc[1:] += dk
    for back, ref in zip(range(1, halo + 1), dk_refs):
        ref[0] = (acc[pl.ds(2 * (halo - back), 2)] * dim**-0.5).astype(BF16)


def own_kernel(halo, place_ref, qd_ref, p_ref, ds_ref, *refs):
    k_refs, back_refs = refs[: halo + 1], refs[halo + 1 : 2 * halo + 1]
    dq_ref, *other_refs, dk_ref, dv_ref, k_scr, dq_scr, dv_scr, far_dv = refs[2 * halo + 1 :]
    core, head = place_ref[0], pl.program_id(0)
    _, _, _, group, tokens, dim = qd_ref.shape
    rows = dq_ref.shape[1]
    count = 2 * halo + 1
    scale = dim**-0.5
    window_of(k_refs, k_scr)
    for e in range(2):
        q = qd_ref[0, e, 0].reshape(group * tokens, dim)
        do = qd_ref[0, e, 1].reshape(group * tokens, dim)
        k = k_scr[pl.ds(e, count)].reshape(count * tokens, dim)
        dqt = jnp.dot(k.T, ds_ref[0, e], preferred_element_type=F32) * scale
        for g in range(group):
            dq_scr[e, pl.ds(head * group + g, tokens, stride=rows), :] = dqt[:, g * tokens : (g + 1) * tokens].T
        keep = (2 * halo - e) * tokens
        dk = jnp.dot(ds_ref[0, e, keep:], q, preferred_element_type=F32) * scale
        dv = jnp.dot(p_ref[0, e, keep:], do, preferred_element_type=F32)
        if e == 0:
            dk_ref[0, 0], dv_scr[0] = dk, dv
        else:
            dk_ref[0, 0] += dk[:tokens]
            dv_scr[0] += dv[:tokens]
            dk_ref[0, 1], dv_scr[1] = dk[tokens:], dv[tokens:]
    for ref in back_refs:
        dv_scr[...] += ref[0].astype(F32)
    dv_ref[0] = dv_scr[core].astype(BF16)
    far_dv[pl.ds(pl.multiple_of(head * tokens, tokens), tokens)] = dv_scr[1 - core].astype(BF16)

    @pl.when(head == pl.num_programs(0) - 1)
    def _():
        dq_ref[...] = dq_scr[core].astype(BF16).reshape(dq_ref.shape)
        dq_rows, start = tokens * rows, 0
        for ref in other_refs:
            part = ref.shape[0] * rows
            here = min(part, dq_rows - start)
            ref[: here // rows] = dq_scr[1 - core, start : start + here].astype(BF16).reshape(-1, rows, dim)
            if here < part:
                ref[here // rows :] = far_dv[...].reshape(-1, rows, dim)
            start += part


def sum_kernel(count, place_ref, own_ref, *refs):
    back_refs, (mine_ref, other_ref) = refs[:count], refs[-2:]
    core = place_ref[0]
    for block, ref in [(1 - core, other_ref), (core, mine_ref)]:
        total = own_ref[:, block]
        for back in back_refs:
            total += back[:, block].astype(F32)
        ref[...] = total.astype(BF16)


def summed(place, own, backs, before):
    half, _, tokens, dim = own.shape
    pair_spec = pl.BlockSpec(own.shape, lambda i, place: (0, 0, 0, 0))
    one = (half, tokens, dim)
    return call(
        functools.partial(sum_kernel, len(backs)),
        "sum_dk",
        (1,),
        place,
        (own, *backs, *(in_hbm(x) for x in before)),
        [pair_spec] * (1 + len(backs)) + [pl.BlockSpec(memory_space=pltpu.HBM)] * len(before),
        [jax.ShapeDtypeStruct(one, BF16)] * 2,
        [pl.BlockSpec(one, lambda i, place: (0, 0, 0))] * 2,
        [],
        0,
    )


def merge_half(core, own_ref, other, out_ref, scr):
    rows, heads, dim = out_ref.shape
    half = heads // 2
    skip = other.shape[0] - half * rows
    for h in range(half):
        scr[pl.ds(core * half + h, rows, stride=heads), :] = own_ref[h].astype(F32)
        rest = other[skip + h * rows : skip + (h + 1) * rows]
        scr[pl.ds((1 - core) * half + h, rows, stride=heads), :] = rest.astype(F32)
    out_ref[...] = scr[...].astype(BF16).reshape(rows, heads, dim)


def join_kernel(parts, place_ref, dq_ref, dv_ref, *refs):
    others, (dq_out, dv_out, scr, sems) = refs[:parts], refs[parts:]
    core = place_ref[0]
    tokens, half, dim = dq_ref.shape
    at = pl.multiple_of(core * half, half)
    copies = [pltpu.make_async_copy(dq_ref, dq_out.at[:, pl.ds(at, half)], sems.at[0])]
    at = pl.multiple_of((1 - core) * half, half)
    first = 0
    for i, part in enumerate(others):
        count = min(part.shape[0], tokens - first)
        to = dq_out.at[pl.ds(first, count), pl.ds(at, half)]
        copies.append(pltpu.make_async_copy(part.at[pl.ds(0, count)], to, sems.at[1 + i]))
        first += count
    for copy in copies:
        copy.start()
    merge_half(core, dv_ref, others[-1][...].reshape(-1, dim), dv_out, scr)
    for copy in copies:
        copy.wait()


def join(place, dq, dv, others):
    tokens, half, dim = dq.shape
    out = (tokens, 2 * dv.shape[0], dim)
    vmem = pl.BlockSpec(memory_space=pltpu.VMEM)
    parts = len(others)
    return call(
        functools.partial(join_kernel, parts),
        "join",
        (1,),
        place,
        [in_vmem(x) for x in (dq, dv, *others)],
        [vmem] * (2 + parts),
        [jax.ShapeDtypeStruct((tokens, 2 * half, dim), BF16), jax.ShapeDtypeStruct(out, BF16)],
        [pl.BlockSpec(memory_space=pl.ANY), pl.BlockSpec(out, lambda i, place: (0, 0, 0))],
        [pltpu.VMEM((tokens * out[1], dim), F32), pltpu.SemaphoreType.DMA((1 + parts,))],
        0,
    )


def merge_kernel(place_ref, own_ref, other_ref, out_ref, scr):
    merge_half(place_ref[0], own_ref, other_ref[...].reshape(-1, own_ref.shape[2]), out_ref, scr)


def merge(place, own, other, name):
    half, tokens, dim = own.shape
    out = (tokens, 2 * half, dim)
    vmem = pl.BlockSpec(memory_space=pltpu.VMEM)
    return call(
        merge_kernel,
        name,
        (1,),
        place,
        (in_vmem(own), in_vmem(other)),
        [vmem] * 2,
        jax.ShapeDtypeStruct(out, BF16),
        pl.BlockSpec(out, lambda i, place: (0, 0, 0)),
        [pltpu.VMEM((tokens * 2 * half, dim), F32)],
        0,
    )


def local(queries, keys, values, grad_out, doc_lengths):
    uly_count = lax.axis_size("uly")
    device_count = lax.axis_size("ctx") * uly_count
    halo = uly_count // 2
    device = lax.axis_index("ctx") * uly_count + lax.axis_index("uly")
    core = device % 2
    tokens, heads, dim = queries.shape
    key_heads = keys.shape[1]
    group = heads // key_heads
    half = key_heads // 2
    window, count = 2 * halo + 2, 2 * halo + 1
    place = jnp.stack([core, (device // 2 - halo) * (2 * tokens)]).astype(jnp.int32)

    far_first = range(halo, 0, -1)
    k_other = swapped(keys, device_count)
    k_mine, v_mine = fetch(place, keys, (values,))
    k_own = pack_other(place, k_other, k_mine)
    k_own, queries, grad_out, v_mine = lax.optimization_barrier((k_own, queries, grad_out, v_mine))
    q_other, do_other, v_other = (swapped(x, device_count) for x in (queries, grad_out, v_mine))
    qd = arrange(place, queries, grad_out, q_other, do_other, key_heads)
    qd, v_mine, v_other = lax.optimization_barrier((qd, v_mine, v_other))
    v_own = pack_both(place, v_mine, v_other)

    def halo_of(own):
        received = {back: moved(own, device_count, 2 * back) for back in far_first}
        return [own] + [received[back] for back in range(1, halo + 1)]

    def sent_back(partials):
        return [moved(partials[back - 1], device_count, -2 * back) for back in far_first]

    def per_head(*shape):
        return pl.BlockSpec((1,) + shape, lambda h, *_: (h,) + (0,) * len(shape))

    qd_spec = per_head(2, 2, group, tokens, dim)
    p_spec = per_head(2, count * tokens, group * tokens)
    p_shape = pltpu.VMEM((half, 2, count * tokens, group * tokens), BF16)
    pair_spec = per_head(2, tokens, dim)
    pair = (half, 2, tokens, dim)
    one_spec = per_head(tokens, dim)
    one_shape = jax.ShapeDtypeStruct((half, tokens, dim), BF16)
    dq_shape = jax.ShapeDtypeStruct((tokens, heads // 2, dim), BF16)
    dq_spec = pl.BlockSpec(dq_shape.shape, lambda h, *_: (0, 0, 0))
    far_rows = tokens + half * tokens // (heads // 2)
    step = (far_rows // 3 + 7) // 8 * 8
    parts = [
        jax.ShapeDtypeStruct((rows, heads // 2, dim), BF16) for rows in (step, step, far_rows - 2 * step)
    ]
    part_specs = [pl.BlockSpec(part.shape, lambda h, *_: (0, 0, 0)) for part in parts]
    run = pltpu.VMEM((window, tokens, dim), BF16)
    acc = pltpu.VMEM((2 * halo, tokens, dim), F32)
    product = 2 * half * 2 * count * tokens * group * tokens * dim

    k_pairs = halo_of(k_own)
    v_pairs = halo_of(v_own)
    prob, *dv_halo = call(
        functools.partial(prob_kernel, halo),
        "prob",
        (half,),
        (place, doc_lengths),
        (in_vmem(qd), *k_pairs),
        [qd_spec] + [pair_spec] * (halo + 1),
        [p_shape] + [jax.ShapeDtypeStruct(pair, BF16)] * halo,
        [p_spec] + [pair_spec] * halo,
        [run, acc, pltpu.VMEM((2, 1, HEADS_AT_ONCE * tokens), jnp.int32)],
        4 * product,
    )
    dv_back = sent_back(dv_halo)
    dscore, *dk_halo = call(
        functools.partial(dscore_kernel, halo),
        "dscore",
        (half,),
        place,
        (in_vmem(qd), in_vmem(prob), *v_pairs),
        [qd_spec, p_spec] + [pair_spec] * (halo + 1),
        [p_shape] + [jax.ShapeDtypeStruct(pair, BF16)] * halo,
        [p_spec] + [pair_spec] * halo,
        [run, acc],
        4 * product,
    )
    dk_back = sent_back(dk_halo)
    dq, *others, dk_own, dv = call(
        functools.partial(own_kernel, halo),
        "own",
        (half,),
        place,
        (in_vmem(qd), in_vmem(prob), in_vmem(dscore), *k_pairs, *dv_back),
        [qd_spec, p_spec, p_spec] + [pair_spec] * (2 * halo + 1),
        [dq_shape, *parts, jax.ShapeDtypeStruct(pair, F32), one_shape],
        [dq_spec, *part_specs, pair_spec, one_spec],
        [
            run,
            pltpu.VMEM((2, tokens * heads // 2, dim), F32),
            pltpu.VMEM((2, tokens, dim), F32),
            pltpu.VMEM((half * tokens, dim), BF16),
        ],
        0,
    )
    others = [swapped(part, device_count) for part in others]
    grad_queries, grad_values = join(place, dq, dv, others)
    dk, dk_other = summed(place, dk_own, dk_back, (grad_queries, grad_values))
    grad_keys = merge(place, dk, swapped(dk_other, device_count), "merge_dk")
    return grad_queries, grad_keys, grad_values


def solution(mesh):
    spec = P(AXES, None, None)
    return jax.shard_map(
        local, mesh=mesh, in_specs=(spec,) * 4 + (P(),), out_specs=(spec,) * 3, check_vma=False
    )
```

```python
import functools

import jax
import jax.numpy as jnp
from jax import lax
from jax.experimental import pallas as pl
from jax.experimental.pallas import tpu as pltpu
from jax.sharding import PartitionSpec as P

AXES = ("ctx", "uly")
MASKED = -1e30
LOG2E = 1.4426950408889634
HEADS_AT_ONCE = 2
BF16, F32 = jnp.bfloat16, jnp.float32
NT = (((1,), (1,)), ((), ()))
VMEM_BYTES = 16 * 2**20


def moved(array, device_count, by):
    pairs = [(d, d + by) for d in range(device_count) if 0 <= d + by < device_count]
    return lax.ppermute(array, AXES, pairs)


def swapped(array, device_count):
    return lax.ppermute(array, AXES, [(d, d ^ 1) for d in range(device_count)])


def in_vmem(array):
    return pltpu.with_memory_space_constraint(array, pltpu.VMEM)


def in_hbm(array):
    return pltpu.with_memory_space_constraint(array, pltpu.HBM)


def call(kernel, name, grid, place, inputs, in_specs, outs, out_specs, scratch, flops, aliases={}):
    scalars = place if isinstance(place, tuple) else (place,)
    return pl.pallas_call(
        kernel,
        out_shape=outs,
        grid_spec=pltpu.PrefetchScalarGridSpec(
            num_scalar_prefetch=len(scalars),
            grid=grid,
            in_specs=in_specs,
            out_specs=out_specs,
            scratch_shapes=scratch,
        ),
        compiler_params=pltpu.CompilerParams(vmem_limit_bytes=VMEM_BYTES),
        cost_estimate=pl.CostEstimate(flops=flops, bytes_accessed=0, transcendentals=0),
        input_output_aliases=aliases,
        name=name,
    )(*scalars, *inputs)


def arrange_kernel(group, place_ref, q_ref, do_ref, q_other_ref, do_other_ref, out_ref, scr):
    core = place_ref[0]
    tokens, heads, dim = q_ref.shape
    half = heads // 2
    mine = pl.ds(pl.multiple_of(core * half, half), half)
    turn = 0
    for kind, (own, other) in enumerate([(q_ref, q_other_ref), (do_ref, do_other_ref)]):
        for which, ref in enumerate([own, other]):
            block = 1 - core if which else core
            wide = scr.at[turn % 2]
            wide[...] = ref[:, mine].astype(F32).reshape(tokens * half, dim)
            for h in range(half):
                out_ref[h // group, block, kind, h % group] = wide[pl.ds(h, tokens, stride=half), :].astype(BF16)
            turn += 1


def arrange(place, queries, grad_out, q_other, do_other, key_heads):
    tokens, heads, dim = queries.shape
    half, group = heads // 2, heads // key_heads
    whole = pl.BlockSpec(memory_space=pltpu.VMEM)
    return call(
        functools.partial(arrange_kernel, group),
        "arrange",
        (1,),
        place,
        [in_vmem(x) for x in (queries, grad_out, q_other, do_other)],
        [whole] * 4,
        pltpu.VMEM((key_heads // 2, 2, 2, group, tokens, dim), BF16),
        whole,
        [pltpu.VMEM((2, tokens * half, dim), F32)],
        10**9,
    )


def pack_block(raw, core, block, out_ref, scr):
    tokens, heads, dim = raw.shape
    half = heads // 2
    scr[...] = raw[...].astype(F32).reshape(tokens * heads, dim)
    for h in range(half):
        out_ref[h, block] = scr[pl.ds(core * half + h, tokens, stride=heads), :].astype(BF16)


def fetch_kernel(place_ref, key_ref, *refs):
    count = (len(refs) - 4) // 2
    sources, out_ref, targets = refs[:count], refs[count], refs[count + 1 : 2 * count + 1]
    raw, scr, sems = refs[-3:]
    first = pltpu.make_async_copy(key_ref, raw, sems.at[0])
    first.start()
    copies = [pltpu.make_async_copy(s, t, sems.at[i + 1]) for i, (s, t) in enumerate(zip(sources, targets))]
    for copy in copies:
        copy.start()
    first.wait()
    pack_block(raw, place_ref[0], place_ref[0], out_ref, scr)
    for copy in copies:
        copy.wait()


def fetch(place, keys, arrays):
    tokens, heads, dim = keys.shape
    out = (heads // 2, 2, tokens, dim)
    return call(
        fetch_kernel,
        "fetch",
        (1,),
        place,
        [in_hbm(x) for x in (keys, *arrays)],
        [pl.BlockSpec(memory_space=pltpu.HBM)] * (1 + len(arrays)),
        [pltpu.VMEM(out, BF16)] + [pltpu.VMEM(x.shape, x.dtype) for x in arrays],
        [pl.BlockSpec(memory_space=pltpu.VMEM)] * (1 + len(arrays)),
        [
            pltpu.VMEM(keys.shape, BF16),
            pltpu.VMEM((tokens * heads, dim), F32),
            pltpu.SemaphoreType.DMA((1 + len(arrays),)),
        ],
        10**9,
    )


def pack_other_kernel(place_ref, other_ref, _, out_ref, scr):
    pack_block(other_ref, place_ref[0], 1 - place_ref[0], out_ref, scr)


def pack_other(place, other, packed):
    tokens, heads, dim = other.shape
    whole = pl.BlockSpec(memory_space=pltpu.VMEM)
    return call(
        pack_other_kernel,
        "pack_other",
        (1,),
        place,
        (in_vmem(other), in_vmem(packed)),
        [whole] * 2,
        pltpu.VMEM(packed.shape, BF16),
        whole,
        [pltpu.VMEM((tokens * heads, dim), F32)],
        10**9,
        {2: 0},
    )


def pack_both_kernel(place_ref, own_ref, other_ref, out_ref, scr):
    core = place_ref[0]
    pack_block(own_ref, core, core, out_ref, scr)
    pack_block(other_ref, core, 1 - core, out_ref, scr)


def pack_both(place, own, other):
    tokens, heads, dim = own.shape
    out = (heads // 2, 2, tokens, dim)
    whole = pl.BlockSpec(memory_space=pltpu.VMEM)
    return call(
        pack_both_kernel,
        "pack_both",
        (1,),
        place,
        (in_vmem(own), in_vmem(other)),
        [whole] * 2,
        pltpu.VMEM(out, BF16),
        whole,
        [pltpu.VMEM((tokens * heads, dim), F32)],
        10**9,
    )


def folded(op, x):
    while x.shape[0] > 8:
        half = x.shape[0] // 2
        x = op(x[:half], x[half:])
    reduce = jnp.max if op is jnp.maximum else jnp.sum
    return reduce(x, axis=0, keepdims=True)


def first_allowed(lengths_ref, query_pos, window_start):
    def step(d, carry):
        start, first = carry
        first = jnp.where(query_pos + window_start >= start, start, first)
        return start + lengths_ref[d], first

    zero = jnp.zeros(query_pos.shape, jnp.int32)
    _, first = lax.fori_loop(0, lengths_ref.shape[0], step, (jnp.int32(0), zero))
    return first - window_start


def window_of(pair_refs, scr):
    halo = len(pair_refs) - 1
    for back, ref in enumerate(pair_refs):
        scr[pl.ds(2 * (halo - back), 2)] = ref[0]


def on_diagonal(tokens, copies):
    row = lax.broadcasted_iota(jnp.int32, (tokens, tokens), 0)
    lane = lax.broadcasted_iota(jnp.int32, (tokens, tokens), 1)
    return jnp.concatenate([row] * copies, axis=1), jnp.concatenate([lane] * copies, axis=1)


def store_tiles(ref, e, at, tiles, diagonal):
    tokens, pair = diagonal.shape
    lanes = slice(at, at + pair)
    ref[0, e, :tokens, lanes] = jnp.where(diagonal, 0.0, tiles[0]).astype(BF16)
    for j, tile in enumerate(tiles[1:], 1):
        ref[0, e, j * tokens : (j + 1) * tokens, lanes] = tile.astype(BF16)
    ref[0, e, -tokens:, lanes] = jnp.where(diagonal, tiles[0], 0.0).astype(BF16)


def chunks_of(lanes, pair):
    return [(e, at) for e in range(2) for at in range(0, lanes, pair)]


def prob_kernel(halo, place_ref, lengths_ref, qd_ref, *refs):
    k_refs = refs[: halo + 1]
    p_ref = refs[halo + 1]
    dv_refs = refs[halo + 2 : -4]
    k_scr, acc, bias, s_scr = refs[-4:]
    _, _, _, group, tokens, dim = qd_ref.shape
    count = 2 * halo + 1
    pair = HEADS_AT_ONCE * tokens
    row, lane = on_diagonal(tokens, HEADS_AT_ONCE)
    diagonal = row <= lane

    @pl.when(pl.program_id(0) == 0)
    def _():
        for e in range(2):
            query_pos = lane[:1, :tokens] + (2 * halo + e) * tokens
            first = first_allowed(lengths_ref, query_pos, place_ref[1]) - row[:, :tokens]
            last = (e + count - 1) * tokens
            bound = jnp.where(diagonal[:, :tokens], last, e * tokens)
            bias[e, 0] = jnp.where(first <= bound, 0.0, MASKED)
            for j in range(1, count - 1):
                bias[e, j] = jnp.where(first <= (e + j) * tokens, 0.0, MASKED)

    window_of(k_refs, k_scr)
    chunks = chunks_of(group * tokens, pair)

    def scores(i):
        e, at = chunks[i]
        k = k_scr[pl.ds(e, count)].reshape(count * tokens, dim)
        q = qd_ref[0, e, 0].reshape(group * tokens, dim)[at : at + pair]
        s_scr[i % 2] = lax.dot_general(k, q, NT, preferred_element_type=F32)

    scores(0)
    for i, (e, at) in enumerate(chunks):
        if i + 1 < len(chunks):
            scores(i + 1)
        tiles = [s_scr[i % 2, j * tokens : (j + 1) * tokens] for j in range(count)]
        tiles[0] = jnp.where(diagonal, tiles.pop(), tiles[0])
        tiles = [t + jnp.concatenate([bias[e, j]] * HEADS_AT_ONCE, axis=1) for j, t in enumerate(tiles)]
        top = folded(jnp.maximum, functools.reduce(jnp.maximum, tiles))
        tiles = [jnp.exp2((tile - top) * (dim**-0.5 * LOG2E)) for tile in tiles]
        inv = 1.0 / folded(jnp.add, functools.reduce(jnp.add, tiles))
        store_tiles(p_ref, e, at, [tile * inv for tile in tiles], diagonal)
        if at + pair == group * tokens:
            do = qd_ref[0, e, 1].reshape(group * tokens, dim)
            keep = (2 * halo - e) * tokens
            dv = jnp.dot(p_ref[0, e, :keep], do, preferred_element_type=F32).reshape(2 * halo - e, tokens, dim)
            if e == 0:
                acc[...] = dv
            else:
                acc[1:] += dv
    for back, ref in zip(range(1, halo + 1), dv_refs):
        ref[0] = acc[pl.ds(2 * (halo - back), 2)].astype(BF16)


def dscore_kernel(halo, place_ref, qd_ref, p_ref, *refs):
    v_refs = refs[: halo + 1]
    ds_ref = refs[halo + 1]
    dk_refs = refs[halo + 2 : -3]
    v_scr, acc, dp_scr = refs[-3:]
    _, _, _, group, tokens, dim = qd_ref.shape
    count = 2 * halo + 1
    pair = HEADS_AT_ONCE * tokens
    row, lane = on_diagonal(tokens, HEADS_AT_ONCE)
    diagonal = row <= lane
    window_of(v_refs, v_scr)
    chunks = chunks_of(group * tokens, pair)

    def dprobs(i):
        e, at = chunks[i]
        v = v_scr[pl.ds(e, count)].reshape(count * tokens, dim)
        do = qd_ref[0, e, 1].reshape(group * tokens, dim)[at : at + pair]
        dp_scr[i % 2] = lax.dot_general(v, do, NT, preferred_element_type=F32)

    dprobs(0)
    for i, (e, at) in enumerate(chunks):
        if i + 1 < len(chunks):
            dprobs(i + 1)
        dps = [dp_scr[i % 2, j * tokens : (j + 1) * tokens] for j in range(count)]
        dps[0] = jnp.where(diagonal, dps.pop(), dps[0])
        ps = [p_ref[0, e, j * tokens : (j + 1) * tokens, at : at + pair] for j in range(count)]
        ps[0] += ps.pop()
        ps = [p.astype(F32) for p in ps]
        delta = folded(jnp.add, functools.reduce(jnp.add, [p * dp for p, dp in zip(ps, dps)]))
        store_tiles(ds_ref, e, at, [p * (dp - delta) for p, dp in zip(ps, dps)], diagonal)
        if at + pair == group * tokens:
            q = qd_ref[0, e, 0].reshape(group * tokens, dim)
            keep = (2 * halo - e) * tokens
            dk = jnp.dot(ds_ref[0, e, :keep], q, preferred_element_type=F32).reshape(2 * halo - e, tokens, dim)
            if e == 0:
                acc[...] = dk
            else:
                acc[1:] += dk
    for back, ref in zip(range(1, halo + 1), dk_refs):
        ref[0] = (acc[pl.ds(2 * (halo - back), 2)] * dim**-0.5).astype(BF16)


def own_kernel(halo, place_ref, qd_ref, p_ref, ds_ref, *refs):
    k_refs, back_refs = refs[: halo + 1], refs[halo + 1 : 2 * halo + 1]
    dq_ref, *other_refs, dk_ref, dv_ref, k_scr, dq_scr, dv_scr, far_dv = refs[2 * halo + 1 :]
    core, head = place_ref[0], pl.program_id(0)
    _, _, _, group, tokens, dim = qd_ref.shape
    rows = dq_ref.shape[1]
    count = 2 * halo + 1
    scale = dim**-0.5
    window_of(k_refs, k_scr)
    for e in range(2):
        q = qd_ref[0, e, 0].reshape(group * tokens, dim)
        do = qd_ref[0, e, 1].reshape(group * tokens, dim)
        k = k_scr[pl.ds(e, count)].reshape(count * tokens, dim)
        dqt = jnp.dot(k.T, ds_ref[0, e], preferred_element_type=F32) * scale
        for g in range(group):
            dq_scr[e, pl.ds(head * group + g, tokens, stride=rows), :] = dqt[:, g * tokens : (g + 1) * tokens].T
        keep = (2 * halo - e) * tokens
        dk = jnp.dot(ds_ref[0, e, keep:], q, preferred_element_type=F32) * scale
        dv = jnp.dot(p_ref[0, e, keep:], do, preferred_element_type=F32)
        if e == 0:
            dk_ref[0, 0], dv_scr[0] = dk, dv
        else:
            dk_ref[0, 0] += dk[:tokens]
            dv_scr[0] += dv[:tokens]
            dk_ref[0, 1], dv_scr[1] = dk[tokens:], dv[tokens:]
    for ref in back_refs:
        dv_scr[...] += ref[0].astype(F32)
    dv_ref[0] = dv_scr[core].astype(BF16)
    far_dv[pl.ds(pl.multiple_of(head * tokens, tokens), tokens)] = dv_scr[1 - core].astype(BF16)

    @pl.when(head == pl.num_programs(0) - 1)
    def _():
        dq_ref[...] = dq_scr[core].astype(BF16).reshape(dq_ref.shape)
        dq_rows, start = tokens * rows, 0
        for ref in other_refs:
            part = ref.shape[0] * rows
            here = min(part, dq_rows - start)
            ref[: here // rows] = dq_scr[1 - core, start : start + here].astype(BF16).reshape(-1, rows, dim)
            if here < part:
                ref[here // rows :] = far_dv[...].reshape(-1, rows, dim)
            start += part


def sum_kernel(count, place_ref, own_ref, *refs):
    back_refs, (mine_ref, other_ref) = refs[:count], refs[-2:]
    core = place_ref[0]
    for block, ref in [(1 - core, other_ref), (core, mine_ref)]:
        total = own_ref[:, block]
        for back in back_refs:
            total += back[:, block].astype(F32)
        ref[...] = total.astype(BF16)


def summed(place, own, backs, before):
    half, _, tokens, dim = own.shape
    pair_spec = pl.BlockSpec(own.shape, lambda i, place: (0, 0, 0, 0))
    one = (half, tokens, dim)
    return call(
        functools.partial(sum_kernel, len(backs)),
        "sum_dk",
        (1,),
        place,
        (own, *backs, *(in_hbm(x) for x in before)),
        [pair_spec] * (1 + len(backs)) + [pl.BlockSpec(memory_space=pltpu.HBM)] * len(before),
        [jax.ShapeDtypeStruct(one, BF16)] * 2,
        [pl.BlockSpec(one, lambda i, place: (0, 0, 0))] * 2,
        [],
        0,
    )


def merge_half(core, own_ref, other, out_ref, scr):
    rows, heads, dim = out_ref.shape
    half = heads // 2
    skip = other.shape[0] - half * rows
    for h in range(half):
        scr[pl.ds(core * half + h, rows, stride=heads), :] = own_ref[h].astype(F32)
        rest = other[skip + h * rows : skip + (h + 1) * rows]
        scr[pl.ds((1 - core) * half + h, rows, stride=heads), :] = rest.astype(F32)
    out_ref[...] = scr[...].astype(BF16).reshape(rows, heads, dim)


def join_kernel(parts, place_ref, dq_ref, dv_ref, *refs):
    others, (dq_out, dv_out, scr, sems) = refs[:parts], refs[parts:]
    core = place_ref[0]
    tokens, half, dim = dq_ref.shape
    at = pl.multiple_of(core * half, half)
    copies = [pltpu.make_async_copy(dq_ref, dq_out.at[:, pl.ds(at, half)], sems.at[0])]
    at = pl.multiple_of((1 - core) * half, half)
    first = 0
    for i, part in enumerate(others):
        count = min(part.shape[0], tokens - first)
        to = dq_out.at[pl.ds(first, count), pl.ds(at, half)]
        copies.append(pltpu.make_async_copy(part.at[pl.ds(0, count)], to, sems.at[1 + i]))
        first += count
    for copy in copies:
        copy.start()
    merge_half(core, dv_ref, others[-1][...].reshape(-1, dim), dv_out, scr)
    for copy in copies:
        copy.wait()


def join(place, dq, dv, others):
    tokens, half, dim = dq.shape
    out = (tokens, 2 * dv.shape[0], dim)
    vmem = pl.BlockSpec(memory_space=pltpu.VMEM)
    parts = len(others)
    return call(
        functools.partial(join_kernel, parts),
        "join",
        (1,),
        place,
        [in_vmem(x) for x in (dq, dv, *others)],
        [vmem] * (2 + parts),
        [jax.ShapeDtypeStruct((tokens, 2 * half, dim), BF16), jax.ShapeDtypeStruct(out, BF16)],
        [pl.BlockSpec(memory_space=pl.ANY), pl.BlockSpec(out, lambda i, place: (0, 0, 0))],
        [pltpu.VMEM((tokens * out[1], dim), F32), pltpu.SemaphoreType.DMA((1 + parts,))],
        0,
    )


def merge_kernel(place_ref, own_ref, other_ref, out_ref, scr):
    merge_half(place_ref[0], own_ref, other_ref[...].reshape(-1, own_ref.shape[2]), out_ref, scr)


def merge(place, own, other, name):
    half, tokens, dim = own.shape
    out = (tokens, 2 * half, dim)
    vmem = pl.BlockSpec(memory_space=pltpu.VMEM)
    return call(
        merge_kernel,
        name,
        (1,),
        place,
        (in_vmem(own), in_vmem(other)),
        [vmem] * 2,
        jax.ShapeDtypeStruct(out, BF16),
        pl.BlockSpec(out, lambda i, place: (0, 0, 0)),
        [pltpu.VMEM((tokens * 2 * half, dim), F32)],
        0,
    )


def local(queries, keys, values, grad_out, doc_lengths):
    uly_count = lax.axis_size("uly")
    device_count = lax.axis_size("ctx") * uly_count
    halo = uly_count // 2
    device = lax.axis_index("ctx") * uly_count + lax.axis_index("uly")
    core = device % 2
    tokens, heads, dim = queries.shape
    key_heads = keys.shape[1]
    group = heads // key_heads
    half = key_heads // 2
    window, count = 2 * halo + 2, 2 * halo + 1
    place = jnp.stack([core, (device // 2 - halo) * (2 * tokens)]).astype(jnp.int32)

    far_first = range(halo, 0, -1)
    k_other = swapped(keys, device_count)
    k_mine, v_mine = fetch(place, keys, (values,))
    k_own = pack_other(place, k_other, k_mine)
    k_own, queries, grad_out, v_mine = lax.optimization_barrier((k_own, queries, grad_out, v_mine))
    q_other, do_other, v_other = (swapped(x, device_count) for x in (queries, grad_out, v_mine))
    qd = arrange(place, queries, grad_out, q_other, do_other, key_heads)
    qd, v_mine, v_other = lax.optimization_barrier((qd, v_mine, v_other))
    v_own = pack_both(place, v_mine, v_other)

    def halo_of(own):
        received = {back: moved(own, device_count, 2 * back) for back in far_first}
        return [own] + [received[back] for back in range(1, halo + 1)]

    def sent_back(partials):
        return [moved(partials[back - 1], device_count, -2 * back) for back in far_first]

    def per_head(*shape):
        return pl.BlockSpec((1,) + shape, lambda h, *_: (h,) + (0,) * len(shape))

    qd_spec = per_head(2, 2, group, tokens, dim)
    p_spec = per_head(2, count * tokens, group * tokens)
    p_shape = pltpu.VMEM((half, 2, count * tokens, group * tokens), BF16)
    pair_spec = per_head(2, tokens, dim)
    pair = (half, 2, tokens, dim)
    one_spec = per_head(tokens, dim)
    one_shape = jax.ShapeDtypeStruct((half, tokens, dim), BF16)
    dq_shape = jax.ShapeDtypeStruct((tokens, heads // 2, dim), BF16)
    dq_spec = pl.BlockSpec(dq_shape.shape, lambda h, *_: (0, 0, 0))
    far_rows = tokens + half * tokens // (heads // 2)
    step = (far_rows // 3 + 7) // 8 * 8
    parts = [
        jax.ShapeDtypeStruct((rows, heads // 2, dim), BF16) for rows in (step, step, far_rows - 2 * step)
    ]
    part_specs = [pl.BlockSpec(part.shape, lambda h, *_: (0, 0, 0)) for part in parts]
    run = pltpu.VMEM((window, tokens, dim), BF16)
    acc = pltpu.VMEM((2 * halo, tokens, dim), F32)
    products = pltpu.VMEM((2, count * tokens, HEADS_AT_ONCE * tokens), F32)
    product = 2 * half * 2 * count * tokens * group * tokens * dim

    k_pairs = halo_of(k_own)
    v_pairs = halo_of(v_own)
    prob, *dv_halo = call(
        functools.partial(prob_kernel, halo),
        "prob",
        (half,),
        (place, doc_lengths),
        (in_vmem(qd), *k_pairs),
        [qd_spec] + [pair_spec] * (halo + 1),
        [p_shape] + [jax.ShapeDtypeStruct(pair, BF16)] * halo,
        [p_spec] + [pair_spec] * halo,
        [run, acc, pltpu.VMEM((2, count - 1, tokens, tokens), F32), products],
        4 * product,
    )
    dv_back = sent_back(dv_halo)
    dscore, *dk_halo = call(
        functools.partial(dscore_kernel, halo),
        "dscore",
        (half,),
        place,
        (in_vmem(qd), in_vmem(prob), *v_pairs),
        [qd_spec, p_spec] + [pair_spec] * (halo + 1),
        [p_shape] + [jax.ShapeDtypeStruct(pair, BF16)] * halo,
        [p_spec] + [pair_spec] * halo,
        [run, acc, products],
        4 * product,
    )
    dk_back = sent_back(dk_halo)
    dq, *others, dk_own, dv = call(
        functools.partial(own_kernel, halo),
        "own",
        (half,),
        place,
        (in_vmem(qd), in_vmem(prob), in_vmem(dscore), *k_pairs, *dv_back),
        [qd_spec, p_spec, p_spec] + [pair_spec] * (2 * halo + 1),
        [dq_shape, *parts, jax.ShapeDtypeStruct(pair, F32), one_shape],
        [dq_spec, *part_specs, pair_spec, one_spec],
        [
            run,
            pltpu.VMEM((2, tokens * heads // 2, dim), F32),
            pltpu.VMEM((2, tokens, dim), F32),
            pltpu.VMEM((half * tokens, dim), BF16),
        ],
        0,
    )
    others = [swapped(part, device_count) for part in others]
    grad_queries, grad_values = join(place, dq, dv, others)
    dk, dk_other = summed(place, dk_own, dk_back, (grad_queries, grad_values))
    grad_keys = merge(place, dk, swapped(dk_other, device_count), "merge_dk")
    return grad_queries, grad_keys, grad_values


def solution(mesh):
    spec = P(AXES, None, None)
    return jax.shard_map(
        local, mesh=mesh, in_specs=(spec,) * 4 + (P(),), out_specs=(spec,) * 3, check_vma=False
    )
```

```python
import functools

import jax
import jax.numpy as jnp
from jax import lax
from jax.experimental import pallas as pl
from jax.experimental.pallas import tpu as pltpu
from jax.sharding import PartitionSpec as P

AXES = ("ctx", "uly")
MASKED = -1e30
LOG2E = 1.4426950408889634
HEADS_AT_ONCE = 2
BF16, F32 = jnp.bfloat16, jnp.float32
NT = (((1,), (1,)), ((), ()))
VMEM_BYTES = 16 * 2**20


def moved(array, device_count, by):
    pairs = [(d, d + by) for d in range(device_count) if 0 <= d + by < device_count]
    return lax.ppermute(array, AXES, pairs)


def swapped(array, device_count):
    return lax.ppermute(array, AXES, [(d, d ^ 1) for d in range(device_count)])


def in_vmem(array):
    return pltpu.with_memory_space_constraint(array, pltpu.VMEM)


def in_hbm(array):
    return pltpu.with_memory_space_constraint(array, pltpu.HBM)


def call(kernel, name, grid, place, inputs, in_specs, outs, out_specs, scratch, flops, aliases={}):
    scalars = place if isinstance(place, tuple) else (place,)
    return pl.pallas_call(
        kernel,
        out_shape=outs,
        grid_spec=pltpu.PrefetchScalarGridSpec(
            num_scalar_prefetch=len(scalars),
            grid=grid,
            in_specs=in_specs,
            out_specs=out_specs,
            scratch_shapes=scratch,
        ),
        compiler_params=pltpu.CompilerParams(vmem_limit_bytes=VMEM_BYTES),
        cost_estimate=pl.CostEstimate(flops=flops, bytes_accessed=0, transcendentals=0),
        input_output_aliases=aliases,
        name=name,
    )(*scalars, *inputs)


def arrange_kernel(group, place_ref, q_ref, do_ref, q_other_ref, do_other_ref, out_ref, scr):
    core = place_ref[0]
    tokens, heads, dim = q_ref.shape
    half = heads // 2
    mine = pl.ds(pl.multiple_of(core * half, half), half)
    turn = 0
    for kind, (own, other) in enumerate([(q_ref, q_other_ref), (do_ref, do_other_ref)]):
        for which, ref in enumerate([own, other]):
            block = 1 - core if which else core
            wide = scr.at[turn % 2]
            wide[...] = ref[:, mine].astype(F32).reshape(tokens * half, dim)
            for h in range(half):
                out_ref[h // group, block, kind, h % group] = wide[pl.ds(h, tokens, stride=half), :].astype(BF16)
            turn += 1


def arrange(place, queries, grad_out, q_other, do_other, key_heads):
    tokens, heads, dim = queries.shape
    half, group = heads // 2, heads // key_heads
    whole = pl.BlockSpec(memory_space=pltpu.VMEM)
    return call(
        functools.partial(arrange_kernel, group),
        "arrange",
        (1,),
        place,
        [in_vmem(x) for x in (queries, grad_out, q_other, do_other)],
        [whole] * 4,
        pltpu.VMEM((key_heads // 2, 2, 2, group, tokens, dim), BF16),
        whole,
        [pltpu.VMEM((2, tokens * half, dim), F32)],
        10**9,
    )


def pack_block(raw, core, block, out_ref, scr):
    tokens, heads, dim = raw.shape
    half = heads // 2
    scr[...] = raw[...].astype(F32).reshape(tokens * heads, dim)
    for h in range(half):
        out_ref[h, block] = scr[pl.ds(core * half + h, tokens, stride=heads), :].astype(BF16)


def fetch_kernel(place_ref, key_ref, *refs):
    count = (len(refs) - 4) // 2
    sources, out_ref, targets = refs[:count], refs[count], refs[count + 1 : 2 * count + 1]
    raw, scr, sems = refs[-3:]
    first = pltpu.make_async_copy(key_ref, raw, sems.at[0])
    first.start()
    copies = [pltpu.make_async_copy(s, t, sems.at[i + 1]) for i, (s, t) in enumerate(zip(sources, targets))]
    for copy in copies:
        copy.start()
    first.wait()
    pack_block(raw, place_ref[0], place_ref[0], out_ref, scr)
    for copy in copies:
        copy.wait()


def fetch(place, keys, arrays):
    tokens, heads, dim = keys.shape
    out = (heads // 2, 2, tokens, dim)
    return call(
        fetch_kernel,
        "fetch",
        (1,),
        place,
        [in_hbm(x) for x in (keys, *arrays)],
        [pl.BlockSpec(memory_space=pltpu.HBM)] * (1 + len(arrays)),
        [pltpu.VMEM(out, BF16)] + [pltpu.VMEM(x.shape, x.dtype) for x in arrays],
        [pl.BlockSpec(memory_space=pltpu.VMEM)] * (1 + len(arrays)),
        [
            pltpu.VMEM(keys.shape, BF16),
            pltpu.VMEM((tokens * heads, dim), F32),
            pltpu.SemaphoreType.DMA((1 + len(arrays),)),
        ],
        10**9,
    )


def pack_other_kernel(place_ref, other_ref, _, out_ref, scr):
    pack_block(other_ref, place_ref[0], 1 - place_ref[0], out_ref, scr)


def pack_other(place, other, packed):
    tokens, heads, dim = other.shape
    whole = pl.BlockSpec(memory_space=pltpu.VMEM)
    return call(
        pack_other_kernel,
        "pack_other",
        (1,),
        place,
        (in_vmem(other), in_vmem(packed)),
        [whole] * 2,
        pltpu.VMEM(packed.shape, BF16),
        whole,
        [pltpu.VMEM((tokens * heads, dim), F32)],
        10**9,
        {2: 0},
    )


def pack_both_kernel(place_ref, own_ref, other_ref, out_ref, scr):
    core = place_ref[0]
    pack_block(own_ref, core, core, out_ref, scr)
    pack_block(other_ref, core, 1 - core, out_ref, scr)


def pack_both(place, own, other):
    tokens, heads, dim = own.shape
    out = (heads // 2, 2, tokens, dim)
    whole = pl.BlockSpec(memory_space=pltpu.VMEM)
    return call(
        pack_both_kernel,
        "pack_both",
        (1,),
        place,
        (in_vmem(own), in_vmem(other)),
        [whole] * 2,
        pltpu.VMEM(out, BF16),
        whole,
        [pltpu.VMEM((tokens * heads, dim), F32)],
        10**9,
    )


def folded(op, x):
    while x.shape[0] > 8:
        half = x.shape[0] // 2
        x = op(x[:half], x[half:])
    reduce = jnp.max if op is jnp.maximum else jnp.sum
    return reduce(x, axis=0, keepdims=True)


def first_allowed(lengths_ref, query_pos, window_start):
    def step(d, carry):
        start, first = carry
        first = jnp.where(query_pos + window_start >= start, start, first)
        return start + lengths_ref[d], first

    zero = jnp.zeros(query_pos.shape, jnp.int32)
    _, first = lax.fori_loop(0, lengths_ref.shape[0], step, (jnp.int32(0), zero))
    return first - window_start


def window_of(pair_refs, scr):
    halo = len(pair_refs) - 1
    for back, ref in enumerate(pair_refs):
        scr[pl.ds(2 * (halo - back), 2)] = ref[0]


def on_diagonal(tokens, copies):
    row = lax.broadcasted_iota(jnp.int32, (tokens, tokens), 0)
    lane = lax.broadcasted_iota(jnp.int32, (tokens, tokens), 1)
    return jnp.concatenate([row] * copies, axis=1), jnp.concatenate([lane] * copies, axis=1)


def store_tiles(ref, e, at, tiles, diagonal):
    tokens, pair = diagonal.shape
    lanes = slice(at, at + pair)
    ref[0, e, :tokens, lanes] = jnp.where(diagonal, 0.0, tiles[0]).astype(BF16)
    for j, tile in enumerate(tiles[1:], 1):
        ref[0, e, j * tokens : (j + 1) * tokens, lanes] = tile.astype(BF16)
    ref[0, e, -tokens:, lanes] = jnp.where(diagonal, tiles[0], 0.0).astype(BF16)


def prob_kernel(halo, place_ref, lengths_ref, qd_ref, *refs):
    k_refs = refs[: halo + 1]
    p_ref = refs[halo + 1]
    dv_refs = refs[halo + 2 : -3]
    k_scr, acc, firsts = refs[-3:]
    _, _, _, group, tokens, dim = qd_ref.shape
    count = 2 * halo + 1
    pair = HEADS_AT_ONCE * tokens
    row, lane = on_diagonal(tokens, HEADS_AT_ONCE)
    diagonal = row <= lane

    @pl.when(pl.program_id(0) == 0)
    def _():
        for e in range(2):
            query_pos = lane[:1] + (2 * halo + e) * tokens
            firsts[e] = first_allowed(lengths_ref, query_pos, place_ref[1])

    window_of(k_refs, k_scr)
    for e in range(2):
        first = firsts[e] - row
        k = k_scr[pl.ds(e, count)].reshape(count * tokens, dim)
        q = qd_ref[0, e, 0].reshape(group * tokens, dim)
        do = qd_ref[0, e, 1].reshape(group * tokens, dim)
        for at in range(0, group * tokens, pair):
            s = lax.dot_general(k, q[at : at + pair], NT, preferred_element_type=F32)
            tiles = [s[j * tokens : (j + 1) * tokens] for j in range(count)]
            last = (e + count - 1) * tokens
            bound = jnp.where(diagonal, last, e * tokens)
            tiles[0] = jnp.where(first <= bound, jnp.where(diagonal, tiles.pop(), tiles[0]), MASKED)
            for j in range(1, count - 1):
                tiles[j] = jnp.where(first <= (e + j) * tokens, tiles[j], MASKED)
            top = folded(jnp.maximum, functools.reduce(jnp.maximum, tiles))
            tiles = [jnp.exp2((tile - top) * (dim**-0.5 * LOG2E)) for tile in tiles]
            inv = 1.0 / folded(jnp.add, functools.reduce(jnp.add, tiles))
            store_tiles(p_ref, e, at, [tile * inv for tile in tiles], diagonal)
        keep = (2 * halo - e) * tokens
        dv = jnp.dot(p_ref[0, e, :keep], do, preferred_element_type=F32).reshape(2 * halo - e, tokens, dim)
        if e == 0:
            acc[...] = dv
        else:
            acc[1:] += dv
    for back, ref in zip(range(1, halo + 1), dv_refs):
        ref[0] = acc[pl.ds(2 * (halo - back), 2)].astype(BF16)


def dscore_kernel(halo, place_ref, qd_ref, p_ref, *refs):
    v_refs = refs[: halo + 1]
    ds_ref = refs[halo + 1]
    dk_refs = refs[halo + 2 : -2]
    v_scr, acc = refs[-2:]
    _, _, _, group, tokens, dim = qd_ref.shape
    count = 2 * halo + 1
    pair = HEADS_AT_ONCE * tokens
    window_of(v_refs, v_scr)
    row, lane = on_diagonal(tokens, HEADS_AT_ONCE)
    diagonal = row <= lane
    for e in range(2):
        v = v_scr[pl.ds(e, count)].reshape(count * tokens, dim)
        q = qd_ref[0, e, 0].reshape(group * tokens, dim)
        do = qd_ref[0, e, 1].reshape(group * tokens, dim)
        for at in range(0, group * tokens, pair):
            dp = lax.dot_general(v, do[at : at + pair], NT, preferred_element_type=F32)
            dps = [dp[j * tokens : (j + 1) * tokens] for j in range(count)]
            dps[0] = jnp.where(diagonal, dps.pop(), dps[0])
            ps = [p_ref[0, e, j * tokens : (j + 1) * tokens, at : at + pair] for j in range(count)]
            ps[0] += ps.pop()
            ps = [p.astype(F32) for p in ps]
            delta = folded(jnp.add, functools.reduce(jnp.add, [p * dp for p, dp in zip(ps, dps)]))
            store_tiles(ds_ref, e, at, [p * (dp - delta) for p, dp in zip(ps, dps)], diagonal)
        keep = (2 * halo - e) * tokens
        dk = jnp.dot(ds_ref[0, e, :keep], q, preferred_element_type=F32).reshape(2 * halo - e, tokens, dim)
        if e == 0:
            acc[...] = dk
        else:
            acc[1:] += dk
    for back, ref in zip(range(1, halo + 1), dk_refs):
        ref[0] = (acc[pl.ds(2 * (halo - back), 2)] * dim**-0.5).astype(BF16)


def own_kernel(halo, place_ref, qd_ref, p_ref, ds_ref, *refs):
    k_refs, back_refs = refs[: halo + 1], refs[halo + 1 : 2 * halo + 1]
    dq_ref, *other_refs, dk_ref, dv_ref, k_scr, dq_scr, dv_scr, far_dv = refs[2 * halo + 1 :]
    core, head = place_ref[0], pl.program_id(0)
    _, _, _, group, tokens, dim = qd_ref.shape
    rows = dq_ref.shape[1]
    count = 2 * halo + 1
    scale = dim**-0.5
    window_of(k_refs, k_scr)
    for e in range(2):
        q = qd_ref[0, e, 0].reshape(group * tokens, dim)
        do = qd_ref[0, e, 1].reshape(group * tokens, dim)
        k = k_scr[pl.ds(e, count)].reshape(count * tokens, dim)
        dqt = jnp.dot(k.T, ds_ref[0, e], preferred_element_type=F32) * scale
        for g in range(group):
            dq_scr[e, pl.ds(head * group + g, tokens, stride=rows), :] = dqt[:, g * tokens : (g + 1) * tokens].T
        keep = (2 * halo - e) * tokens
        dk = jnp.dot(ds_ref[0, e, keep:], q, preferred_element_type=F32) * scale
        dv = jnp.dot(p_ref[0, e, keep:], do, preferred_element_type=F32)
        if e == 0:
            dk_ref[0, 0], dv_scr[0] = dk, dv
        else:
            dk_ref[0, 0] += dk[:tokens]
            dv_scr[0] += dv[:tokens]
            dk_ref[0, 1], dv_scr[1] = dk[tokens:], dv[tokens:]
    for ref in back_refs:
        dv_scr[...] += ref[0].astype(F32)
    dv_ref[0] = dv_scr[core].astype(BF16)
    far_dv[pl.ds(pl.multiple_of(head * tokens, tokens), tokens)] = dv_scr[1 - core].astype(BF16)

    @pl.when(head == pl.num_programs(0) - 1)
    def _():
        dq_ref[...] = dq_scr[core].astype(BF16).reshape(dq_ref.shape)
        dq_rows, start = tokens * rows, 0
        for ref in other_refs:
            part = ref.shape[0] * rows
            here = min(part, dq_rows - start)
            ref[: here // rows] = dq_scr[1 - core, start : start + here].astype(BF16).reshape(-1, rows, dim)
            if here < part:
                ref[here // rows :] = far_dv[...].reshape(-1, rows, dim)
            start += part


def sum_kernel(count, place_ref, own_ref, *refs):
    back_refs, (mine_ref, other_ref) = refs[:count], refs[-2:]
    core = place_ref[0]
    for block, ref in [(1 - core, other_ref), (core, mine_ref)]:
        total = own_ref[:, block]
        for back in back_refs:
            total += back[:, block].astype(F32)
        ref[...] = total.astype(BF16)


def summed(place, own, backs, before):
    half, _, tokens, dim = own.shape
    pair_spec = pl.BlockSpec(own.shape, lambda i, place: (0, 0, 0, 0))
    one = (half, tokens, dim)
    return call(
        functools.partial(sum_kernel, len(backs)),
        "sum_dk",
        (1,),
        place,
        (own, *backs, *(in_hbm(x) for x in before)),
        [pair_spec] * (1 + len(backs)) + [pl.BlockSpec(memory_space=pltpu.HBM)] * len(before),
        [jax.ShapeDtypeStruct(one, BF16)] * 2,
        [pl.BlockSpec(one, lambda i, place: (0, 0, 0))] * 2,
        [],
        0,
    )


def merge_half(core, own_ref, other, out_ref, scr):
    rows, heads, dim = out_ref.shape
    half = heads // 2
    skip = other.shape[0] - half * rows
    for h in range(half):
        scr[pl.ds(core * half + h, rows, stride=heads), :] = own_ref[h].astype(F32)
        rest = other[skip + h * rows : skip + (h + 1) * rows]
        scr[pl.ds((1 - core) * half + h, rows, stride=heads), :] = rest.astype(F32)
    out_ref[...] = scr[...].astype(BF16).reshape(rows, heads, dim)


def join_kernel(parts, place_ref, dq_ref, dv_ref, *refs):
    others, (dq_out, dv_out, scr, sems) = refs[:parts], refs[parts:]
    core = place_ref[0]
    tokens, half, dim = dq_ref.shape
    at = pl.multiple_of(core * half, half)
    copies = [pltpu.make_async_copy(dq_ref, dq_out.at[:, pl.ds(at, half)], sems.at[0])]
    at = pl.multiple_of((1 - core) * half, half)
    first = 0
    for i, part in enumerate(others):
        count = min(part.shape[0], tokens - first)
        to = dq_out.at[pl.ds(first, count), pl.ds(at, half)]
        copies.append(pltpu.make_async_copy(part.at[pl.ds(0, count)], to, sems.at[1 + i]))
        first += count
    for copy in copies:
        copy.start()
    merge_half(core, dv_ref, others[-1][...].reshape(-1, dim), dv_out, scr)
    for copy in copies:
        copy.wait()


def join(place, dq, dv, others):
    tokens, half, dim = dq.shape
    out = (tokens, 2 * dv.shape[0], dim)
    vmem = pl.BlockSpec(memory_space=pltpu.VMEM)
    parts = len(others)
    return call(
        functools.partial(join_kernel, parts),
        "join",
        (1,),
        place,
        [in_vmem(x) for x in (dq, dv, *others)],
        [vmem] * (2 + parts),
        [jax.ShapeDtypeStruct((tokens, 2 * half, dim), BF16), jax.ShapeDtypeStruct(out, BF16)],
        [pl.BlockSpec(memory_space=pl.ANY), pl.BlockSpec(out, lambda i, place: (0, 0, 0))],
        [pltpu.VMEM((tokens * out[1], dim), F32), pltpu.SemaphoreType.DMA((1 + parts,))],
        0,
    )


def merge_kernel(place_ref, own_ref, other_ref, out_ref, scr):
    merge_half(place_ref[0], own_ref, other_ref[...].reshape(-1, own_ref.shape[2]), out_ref, scr)


def merge(place, own, other, name):
    half, tokens, dim = own.shape
    out = (tokens, 2 * half, dim)
    vmem = pl.BlockSpec(memory_space=pltpu.VMEM)
    return call(
        merge_kernel,
        name,
        (1,),
        place,
        (in_vmem(own), in_vmem(other)),
        [vmem] * 2,
        jax.ShapeDtypeStruct(out, BF16),
        pl.BlockSpec(out, lambda i, place: (0, 0, 0)),
        [pltpu.VMEM((tokens * 2 * half, dim), F32)],
        0,
    )


def local(queries, keys, values, grad_out, doc_lengths):
    uly_count = lax.axis_size("uly")
    device_count = lax.axis_size("ctx") * uly_count
    halo = uly_count // 2
    device = lax.axis_index("ctx") * uly_count + lax.axis_index("uly")
    core = device % 2
    tokens, heads, dim = queries.shape
    key_heads = keys.shape[1]
    group = heads // key_heads
    half = key_heads // 2
    window, count = 2 * halo + 2, 2 * halo + 1
    place = jnp.stack([core, (device // 2 - halo) * (2 * tokens)]).astype(jnp.int32)

    far_first = range(halo, 0, -1)
    k_other = swapped(keys, device_count)
    k_mine, v_mine = fetch(place, keys, (values,))
    k_own = pack_other(place, k_other, k_mine)
    k_own, queries, grad_out, v_mine = lax.optimization_barrier((k_own, queries, grad_out, v_mine))
    q_other, do_other, v_other = (swapped(x, device_count) for x in (queries, grad_out, v_mine))
    qd = arrange(place, queries, grad_out, q_other, do_other, key_heads)
    qd, v_mine, v_other = lax.optimization_barrier((qd, v_mine, v_other))
    v_own = pack_both(place, v_mine, v_other)

    def halo_of(own):
        received = {back: moved(own, device_count, 2 * back) for back in far_first}
        return [own] + [received[back] for back in range(1, halo + 1)]

    def sent_back(partials):
        return [moved(partials[back - 1], device_count, -2 * back) for back in far_first]

    def per_head(*shape):
        return pl.BlockSpec((1,) + shape, lambda h, *_: (h,) + (0,) * len(shape))

    qd_spec = per_head(2, 2, group, tokens, dim)
    p_spec = per_head(2, count * tokens, group * tokens)
    p_shape = pltpu.VMEM((half, 2, count * tokens, group * tokens), BF16)
    pair_spec = per_head(2, tokens, dim)
    pair = (half, 2, tokens, dim)
    one_spec = per_head(tokens, dim)
    one_shape = jax.ShapeDtypeStruct((half, tokens, dim), BF16)
    dq_shape = jax.ShapeDtypeStruct((tokens, heads // 2, dim), BF16)
    dq_spec = pl.BlockSpec(dq_shape.shape, lambda h, *_: (0, 0, 0))
    far_rows = tokens + half * tokens // (heads // 2)
    step = (far_rows // 3 + 7) // 8 * 8
    parts = [
        jax.ShapeDtypeStruct((rows, heads // 2, dim), BF16) for rows in (step, step, far_rows - 2 * step)
    ]
    part_specs = [pl.BlockSpec(part.shape, lambda h, *_: (0, 0, 0)) for part in parts]
    run = pltpu.VMEM((window, tokens, dim), BF16)
    acc = pltpu.VMEM((2 * halo, tokens, dim), F32)
    product = 2 * half * 2 * count * tokens * group * tokens * dim

    k_pairs = halo_of(k_own)
    v_pairs = halo_of(v_own)
    prob, *dv_halo = call(
        functools.partial(prob_kernel, halo),
        "prob",
        (half,),
        (place, doc_lengths),
        (in_vmem(qd), *k_pairs),
        [qd_spec] + [pair_spec] * (halo + 1),
        [p_shape] + [jax.ShapeDtypeStruct(pair, BF16)] * halo,
        [p_spec] + [pair_spec] * halo,
        [run, acc, pltpu.VMEM((2, 1, HEADS_AT_ONCE * tokens), jnp.int32)],
        4 * product,
    )
    dv_back = sent_back(dv_halo)
    dscore, *dk_halo = call(
        functools.partial(dscore_kernel, halo),
        "dscore",
        (half,),
        place,
        (in_vmem(qd), in_vmem(prob), *v_pairs),
        [qd_spec, p_spec] + [pair_spec] * (halo + 1),
        [p_shape] + [jax.ShapeDtypeStruct(pair, BF16)] * halo,
        [p_spec] + [pair_spec] * halo,
        [run, acc],
        4 * product,
    )
    dk_back = sent_back(dk_halo)
    dq, *others, dk_own, dv = call(
        functools.partial(own_kernel, halo),
        "own",
        (half,),
        place,
        (in_vmem(qd), in_vmem(prob), in_vmem(dscore), *k_pairs, *dv_back),
        [qd_spec, p_spec, p_spec] + [pair_spec] * (2 * halo + 1),
        [dq_shape, *parts, jax.ShapeDtypeStruct(pair, F32), one_shape],
        [dq_spec, *part_specs, pair_spec, one_spec],
        [
            run,
            pltpu.VMEM((2, tokens * heads // 2, dim), F32),
            pltpu.VMEM((2, tokens, dim), F32),
            pltpu.VMEM((half * tokens, dim), BF16),
        ],
        0,
    )
    others = [swapped(part, device_count) for part in others]
    grad_queries, grad_values = join(place, dq, dv, others)
    dk, dk_other = summed(place, dk_own, dk_back, (grad_queries, grad_values))
    grad_keys = merge(place, dk, swapped(dk_other, device_count), "merge_dk")
    return grad_queries, grad_keys, grad_values


def solution(mesh):
    spec = P(AXES, None, None)
    return jax.shard_map(
        local, mesh=mesh, in_specs=(spec,) * 4 + (P(),), out_specs=(spec,) * 3, check_vma=False
    )
```

```python
import functools

import jax
import jax.numpy as jnp
from jax import lax
from jax.experimental import pallas as pl
from jax.experimental.pallas import tpu as pltpu
from jax.sharding import PartitionSpec as P

AXES = ("ctx", "uly")
MASKED = -1e30
LOG2E = 1.4426950408889634
HEADS_AT_ONCE = 2
BF16, F32 = jnp.bfloat16, jnp.float32
NT = (((1,), (1,)), ((), ()))
VMEM_BYTES = 16 * 2**20


def moved(array, device_count, by):
    pairs = [(d, d + by) for d in range(device_count) if 0 <= d + by < device_count]
    return lax.ppermute(array, AXES, pairs)


def swapped(array, device_count):
    return lax.ppermute(array, AXES, [(d, d ^ 1) for d in range(device_count)])


def in_vmem(array):
    return pltpu.with_memory_space_constraint(array, pltpu.VMEM)


def in_hbm(array):
    return pltpu.with_memory_space_constraint(array, pltpu.HBM)


def call(kernel, name, grid, place, inputs, in_specs, outs, out_specs, scratch, flops, aliases={}):
    scalars = place if isinstance(place, tuple) else (place,)
    return pl.pallas_call(
        kernel,
        out_shape=outs,
        grid_spec=pltpu.PrefetchScalarGridSpec(
            num_scalar_prefetch=len(scalars),
            grid=grid,
            in_specs=in_specs,
            out_specs=out_specs,
            scratch_shapes=scratch,
        ),
        compiler_params=pltpu.CompilerParams(vmem_limit_bytes=VMEM_BYTES),
        cost_estimate=pl.CostEstimate(flops=flops, bytes_accessed=0, transcendentals=0),
        input_output_aliases=aliases,
        name=name,
    )(*scalars, *inputs)


def arrange_kernel(group, place_ref, q_ref, do_ref, q_other_ref, do_other_ref, out_ref, scr):
    core = place_ref[0]
    tokens, heads, dim = q_ref.shape
    half = heads // 2
    mine = pl.ds(pl.multiple_of(core * half, half), half)
    turn = 0
    for kind, (own, other) in enumerate([(q_ref, q_other_ref), (do_ref, do_other_ref)]):
        for which, ref in enumerate([own, other]):
            block = 1 - core if which else core
            wide = scr.at[turn % 2]
            wide[...] = ref[:, mine].astype(F32).reshape(tokens * half, dim)
            for h in range(half):
                out_ref[h // group, block, kind, h % group] = wide[pl.ds(h, tokens, stride=half), :].astype(BF16)
            turn += 1


def arrange(place, queries, grad_out, q_other, do_other, key_heads):
    tokens, heads, dim = queries.shape
    half, group = heads // 2, heads // key_heads
    whole = pl.BlockSpec(memory_space=pltpu.VMEM)
    return call(
        functools.partial(arrange_kernel, group),
        "arrange",
        (1,),
        place,
        [in_vmem(x) for x in (queries, grad_out, q_other, do_other)],
        [whole] * 4,
        pltpu.VMEM((key_heads // 2, 2, 2, group, tokens, dim), BF16),
        whole,
        [pltpu.VMEM((2, tokens * half, dim), F32)],
        10**9,
    )


def pack_block(raw, core, block, out_ref, scr):
    tokens, heads, dim = raw.shape
    half = heads // 2
    scr[...] = raw[...].astype(F32).reshape(tokens * heads, dim)
    for h in range(half):
        out_ref[h, block] = scr[pl.ds(core * half + h, tokens, stride=heads), :].astype(BF16)


def fetch_kernel(place_ref, key_ref, *refs):
    count = (len(refs) - 4) // 2
    sources, out_ref, targets = refs[:count], refs[count], refs[count + 1 : 2 * count + 1]
    raw, scr, sems = refs[-3:]
    first = pltpu.make_async_copy(key_ref, raw, sems.at[0])
    first.start()
    copies = [pltpu.make_async_copy(s, t, sems.at[i + 1]) for i, (s, t) in enumerate(zip(sources, targets))]
    for copy in copies:
        copy.start()
    first.wait()
    pack_block(raw, place_ref[0], place_ref[0], out_ref, scr)
    for copy in copies:
        copy.wait()


def fetch(place, keys, arrays):
    tokens, heads, dim = keys.shape
    out = (heads // 2, 2, tokens, dim)
    return call(
        fetch_kernel,
        "fetch",
        (1,),
        place,
        [in_hbm(x) for x in (keys, *arrays)],
        [pl.BlockSpec(memory_space=pltpu.HBM)] * (1 + len(arrays)),
        [pltpu.VMEM(out, BF16)] + [pltpu.VMEM(x.shape, x.dtype) for x in arrays],
        [pl.BlockSpec(memory_space=pltpu.VMEM)] * (1 + len(arrays)),
        [
            pltpu.VMEM(keys.shape, BF16),
            pltpu.VMEM((tokens * heads, dim), F32),
            pltpu.SemaphoreType.DMA((1 + len(arrays),)),
        ],
        10**9,
    )


def pack_other_kernel(place_ref, other_ref, _, out_ref, scr):
    pack_block(other_ref, place_ref[0], 1 - place_ref[0], out_ref, scr)


def pack_other(place, other, packed):
    tokens, heads, dim = other.shape
    whole = pl.BlockSpec(memory_space=pltpu.VMEM)
    return call(
        pack_other_kernel,
        "pack_other",
        (1,),
        place,
        (in_vmem(other), in_vmem(packed)),
        [whole] * 2,
        pltpu.VMEM(packed.shape, BF16),
        whole,
        [pltpu.VMEM((tokens * heads, dim), F32)],
        10**9,
        {2: 0},
    )


def pack_both_kernel(place_ref, own_ref, other_ref, out_ref, scr):
    core = place_ref[0]
    pack_block(own_ref, core, core, out_ref, scr)
    pack_block(other_ref, core, 1 - core, out_ref, scr)


def pack_both(place, own, other):
    tokens, heads, dim = own.shape
    out = (heads // 2, 2, tokens, dim)
    whole = pl.BlockSpec(memory_space=pltpu.VMEM)
    return call(
        pack_both_kernel,
        "pack_both",
        (1,),
        place,
        (in_vmem(own), in_vmem(other)),
        [whole] * 2,
        pltpu.VMEM(out, BF16),
        whole,
        [pltpu.VMEM((tokens * heads, dim), F32)],
        10**9,
    )


def folded(op, x):
    while x.shape[0] > 8:
        half = x.shape[0] // 2
        x = op(x[:half], x[half:])
    reduce = jnp.max if op is jnp.maximum else jnp.sum
    return reduce(x, axis=0, keepdims=True)


def first_allowed(lengths_ref, query_pos, window_start):
    def step(d, carry):
        start, first = carry
        first = jnp.where(query_pos + window_start >= start, start, first)
        return start + lengths_ref[d], first

    zero = jnp.zeros(query_pos.shape, jnp.int32)
    _, first = lax.fori_loop(0, lengths_ref.shape[0], step, (jnp.int32(0), zero))
    return first - window_start


def window_of(pair_refs, scr):
    halo = len(pair_refs) - 1
    for back, ref in enumerate(pair_refs):
        scr[pl.ds(2 * (halo - back), 2)] = ref[0]


def on_diagonal(tokens, copies):
    row = lax.broadcasted_iota(jnp.int32, (tokens, tokens), 0)
    lane = lax.broadcasted_iota(jnp.int32, (tokens, tokens), 1)
    return jnp.concatenate([row] * copies, axis=1), jnp.concatenate([lane] * copies, axis=1)


def store_tile(ref, e, j, at, tile, diagonal):
    tokens, pair = diagonal.shape
    lanes = slice(at, at + pair)
    if j:
        ref[0, e, j * tokens : (j + 1) * tokens, lanes] = tile.astype(BF16)
    else:
        ref[0, e, :tokens, lanes] = jnp.where(diagonal, 0.0, tile).astype(BF16)
        ref[0, e, -tokens:, lanes] = jnp.where(diagonal, tile, 0.0).astype(BF16)


def load_tile(ref, e, j, at, pair, tokens):
    tile = ref[0, e, j * tokens : (j + 1) * tokens, at : at + pair]
    if j == 0:
        tile += ref[0, e, -tokens:, at : at + pair]
    return tile.astype(F32)


def prob_kernel(halo, place_ref, lengths_ref, qd_ref, *refs):
    k_refs = refs[: halo + 1]
    w_ref, inv_ref, do_ref = refs[halo + 1 : halo + 4]
    dv_refs = refs[halo + 4 : -4]
    k_scr, acc, bias, tiles = refs[-4:]
    _, _, _, group, tokens, dim = qd_ref.shape
    count = 2 * halo + 1
    pair = HEADS_AT_ONCE * tokens
    row, lane = on_diagonal(tokens, HEADS_AT_ONCE)
    diagonal = row <= lane

    @pl.when(pl.program_id(0) == 0)
    def _():
        for e in range(2):
            query_pos = lane[:1] + (2 * halo + e) * tokens
            first = first_allowed(lengths_ref, query_pos, place_ref[1]) - row
            last = (e + count - 1) * tokens
            bias[e, 0] = jnp.where(first <= jnp.where(diagonal, last, e * tokens), 0.0, MASKED)
            for j in range(1, count - 1):
                bias[e, j] = jnp.where(first <= (e + j) * tokens, 0.0, MASKED)

    window_of(k_refs, k_scr)
    scale = dim**-0.5 * LOG2E
    turn = 0
    for e in range(2):
        k = k_scr[pl.ds(e, count)].reshape(count * tokens, dim)
        q = qd_ref[0, e, 0].reshape(group * tokens, dim)
        for at in range(0, group * tokens, pair):
            scr = tiles.at[turn % 2]
            turn += 1
            s = lax.dot_general(k, q[at : at + pair], NT, preferred_element_type=F32)
            top = None
            for j in range(count - 1):
                tile = s[j * tokens : (j + 1) * tokens]
                if j == 0:
                    tile = jnp.where(diagonal, s[(count - 1) * tokens :], tile)
                tile += bias[e, j]
                scr[j] = tile
                top = tile if top is None else jnp.maximum(top, tile)
            top = folded(jnp.maximum, top) * scale
            total = None
            for j in range(count - 1):
                w = jnp.exp2(scr[j] * scale - top)
                store_tile(w_ref, e, j, at, w, diagonal)
                total = w if total is None else total + w
            inv = 1.0 / folded(jnp.add, total)
            inv_ref[0, e, :, at : at + pair] = inv
            for g in range(at // tokens, (at + pair) // tokens):
                of_row = jnp.broadcast_to(inv[:, g * tokens - at : (g + 1) * tokens - at], (8, tokens)).T
                do_ref[0, e, g] = (qd_ref[0, e, 1, g].astype(F32) * of_row[:, :1]).astype(BF16)
        do = do_ref[0, e].reshape(group * tokens, dim)
        keep = (2 * halo - e) * tokens
        dv = jnp.dot(w_ref[0, e, :keep], do, preferred_element_type=F32).reshape(2 * halo - e, tokens, dim)
        if e == 0:
            acc[...] = dv
        else:
            acc[1:] += dv
    for back, ref in zip(range(1, halo + 1), dv_refs):
        ref[0] = acc[pl.ds(2 * (halo - back), 2)].astype(BF16)


def dscore_kernel(halo, place_ref, qd_ref, w_ref, inv_ref, do_ref, *refs):
    v_refs = refs[: halo + 1]
    ds_ref = refs[halo + 1]
    dk_refs = refs[halo + 2 : -3]
    v_scr, acc, tiles = refs[-3:]
    _, _, _, group, tokens, dim = qd_ref.shape
    count = 2 * halo + 1
    pair = HEADS_AT_ONCE * tokens
    row, lane = on_diagonal(tokens, HEADS_AT_ONCE)
    diagonal = row <= lane
    window_of(v_refs, v_scr)
    turn = 0
    for e in range(2):
        v = v_scr[pl.ds(e, count)].reshape(count * tokens, dim)
        q = qd_ref[0, e, 0].reshape(group * tokens, dim)
        do = do_ref[0, e].reshape(group * tokens, dim)
        for at in range(0, group * tokens, pair):
            scr = tiles.at[turn % 2]
            turn += 1
            dp = lax.dot_general(v, do[at : at + pair], NT, preferred_element_type=F32)
            delta = None
            for j in range(count - 1):
                tile = dp[j * tokens : (j + 1) * tokens]
                if j == 0:
                    tile = jnp.where(diagonal, dp[(count - 1) * tokens :], tile)
                scr[j] = tile
                term = load_tile(w_ref, e, j, at, pair, tokens) * tile
                delta = term if delta is None else delta + term
            delta = folded(jnp.add, delta) * inv_ref[0, e, :, at : at + pair]
            for j in range(count - 1):
                w = load_tile(w_ref, e, j, at, pair, tokens)
                store_tile(ds_ref, e, j, at, w * (scr[j] - delta), diagonal)
        keep = (2 * halo - e) * tokens
        dk = jnp.dot(ds_ref[0, e, :keep], q, preferred_element_type=F32).reshape(2 * halo - e, tokens, dim)
        if e == 0:
            acc[...] = dk
        else:
            acc[1:] += dk
    for back, ref in zip(range(1, halo + 1), dk_refs):
        ref[0] = (acc[pl.ds(2 * (halo - back), 2)] * dim**-0.5).astype(BF16)


def own_kernel(halo, place_ref, qd_ref, w_ref, do_ref, ds_ref, *refs):
    k_refs, back_refs = refs[: halo + 1], refs[halo + 1 : 2 * halo + 1]
    dq_ref, *other_refs, dk_ref, dv_ref, k_scr, dq_scr, dv_scr, far_dv = refs[2 * halo + 1 :]
    core, head = place_ref[0], pl.program_id(0)
    _, _, _, group, tokens, dim = qd_ref.shape
    rows = dq_ref.shape[1]
    count = 2 * halo + 1
    scale = dim**-0.5
    window_of(k_refs, k_scr)
    for e in range(2):
        q = qd_ref[0, e, 0].reshape(group * tokens, dim)
        do = do_ref[0, e].reshape(group * tokens, dim)
        k = k_scr[pl.ds(e, count)].reshape(count * tokens, dim)
        dqt = jnp.dot(k.T, ds_ref[0, e], preferred_element_type=F32) * scale
        for g in range(group):
            dq_scr[e, pl.ds(head * group + g, tokens, stride=rows), :] = dqt[:, g * tokens : (g + 1) * tokens].T
        keep = (2 * halo - e) * tokens
        dk = jnp.dot(ds_ref[0, e, keep:], q, preferred_element_type=F32) * scale
        dv = jnp.dot(w_ref[0, e, keep:], do, preferred_element_type=F32)
        if e == 0:
            dk_ref[0, 0], dv_scr[0] = dk, dv
        else:
            dk_ref[0, 0] += dk[:tokens]
            dv_scr[0] += dv[:tokens]
            dk_ref[0, 1], dv_scr[1] = dk[tokens:], dv[tokens:]
    for ref in back_refs:
        dv_scr[...] += ref[0].astype(F32)
    dv_ref[0] = dv_scr[core].astype(BF16)
    far_dv[pl.ds(pl.multiple_of(head * tokens, tokens), tokens)] = dv_scr[1 - core].astype(BF16)

    @pl.when(head == pl.num_programs(0) - 1)
    def _():
        dq_ref[...] = dq_scr[core].astype(BF16).reshape(dq_ref.shape)
        dq_rows, start = tokens * rows, 0
        for ref in other_refs:
            part = ref.shape[0] * rows
            here = min(part, dq_rows - start)
            ref[: here // rows] = dq_scr[1 - core, start : start + here].astype(BF16).reshape(-1, rows, dim)
            if here < part:
                ref[here // rows :] = far_dv[...].reshape(-1, rows, dim)
            start += part


def sum_kernel(count, place_ref, own_ref, *refs):
    back_refs, (mine_ref, other_ref) = refs[:count], refs[-2:]
    core = place_ref[0]
    for block, ref in [(1 - core, other_ref), (core, mine_ref)]:
        total = own_ref[:, block]
        for back in back_refs:
            total += back[:, block].astype(F32)
        ref[...] = total.astype(BF16)


def summed(place, own, backs, before):
    half, _, tokens, dim = own.shape
    pair_spec = pl.BlockSpec(own.shape, lambda i, place: (0, 0, 0, 0))
    one = (half, tokens, dim)
    return call(
        functools.partial(sum_kernel, len(backs)),
        "sum_dk",
        (1,),
        place,
        (own, *backs, *(in_hbm(x) for x in before)),
        [pair_spec] * (1 + len(backs)) + [pl.BlockSpec(memory_space=pltpu.HBM)] * len(before),
        [jax.ShapeDtypeStruct(one, BF16)] * 2,
        [pl.BlockSpec(one, lambda i, place: (0, 0, 0))] * 2,
        [],
        0,
    )


def merge_half(core, own_ref, other, out_ref, scr):
    rows, heads, dim = out_ref.shape
    half = heads // 2
    skip = other.shape[0] - half * rows
    for h in range(half):
        scr[pl.ds(core * half + h, rows, stride=heads), :] = own_ref[h].astype(F32)
        rest = other[skip + h * rows : skip + (h + 1) * rows]
        scr[pl.ds((1 - core) * half + h, rows, stride=heads), :] = rest.astype(F32)
    out_ref[...] = scr[...].astype(BF16).reshape(rows, heads, dim)


def join_kernel(parts, place_ref, dq_ref, dv_ref, *refs):
    others, (dq_out, dv_out, scr, sems) = refs[:parts], refs[parts:]
    core = place_ref[0]
    tokens, half, dim = dq_ref.shape
    at = pl.multiple_of(core * half, half)
    copies = [pltpu.make_async_copy(dq_ref, dq_out.at[:, pl.ds(at, half)], sems.at[0])]
    at = pl.multiple_of((1 - core) * half, half)
    first = 0
    for i, part in enumerate(others):
        count = min(part.shape[0], tokens - first)
        to = dq_out.at[pl.ds(first, count), pl.ds(at, half)]
        copies.append(pltpu.make_async_copy(part.at[pl.ds(0, count)], to, sems.at[1 + i]))
        first += count
    for copy in copies:
        copy.start()
    merge_half(core, dv_ref, others[-1][...].reshape(-1, dim), dv_out, scr)
    for copy in copies:
        copy.wait()


def join(place, dq, dv, others):
    tokens, half, dim = dq.shape
    out = (tokens, 2 * dv.shape[0], dim)
    vmem = pl.BlockSpec(memory_space=pltpu.VMEM)
    parts = len(others)
    return call(
        functools.partial(join_kernel, parts),
        "join",
        (1,),
        place,
        [in_vmem(x) for x in (dq, dv, *others)],
        [vmem] * (2 + parts),
        [jax.ShapeDtypeStruct((tokens, 2 * half, dim), BF16), jax.ShapeDtypeStruct(out, BF16)],
        [pl.BlockSpec(memory_space=pl.ANY), pl.BlockSpec(out, lambda i, place: (0, 0, 0))],
        [pltpu.VMEM((tokens * out[1], dim), F32), pltpu.SemaphoreType.DMA((1 + parts,))],
        0,
    )


def merge_kernel(place_ref, own_ref, other_ref, out_ref, scr):
    merge_half(place_ref[0], own_ref, other_ref[...].reshape(-1, own_ref.shape[2]), out_ref, scr)


def merge(place, own, other, name):
    half, tokens, dim = own.shape
    out = (tokens, 2 * half, dim)
    vmem = pl.BlockSpec(memory_space=pltpu.VMEM)
    return call(
        merge_kernel,
        name,
        (1,),
        place,
        (in_vmem(own), in_vmem(other)),
        [vmem] * 2,
        jax.ShapeDtypeStruct(out, BF16),
        pl.BlockSpec(out, lambda i, place: (0, 0, 0)),
        [pltpu.VMEM((tokens * 2 * half, dim), F32)],
        0,
    )


def local(queries, keys, values, grad_out, doc_lengths):
    uly_count = lax.axis_size("uly")
    device_count = lax.axis_size("ctx") * uly_count
    halo = uly_count // 2
    device = lax.axis_index("ctx") * uly_count + lax.axis_index("uly")
    core = device % 2
    tokens, heads, dim = queries.shape
    key_heads = keys.shape[1]
    group = heads // key_heads
    half = key_heads // 2
    window, count = 2 * halo + 2, 2 * halo + 1
    place = jnp.stack([core, (device // 2 - halo) * (2 * tokens)]).astype(jnp.int32)

    far_first = range(halo, 0, -1)
    k_other = swapped(keys, device_count)
    k_mine, v_mine = fetch(place, keys, (values,))
    k_own = pack_other(place, k_other, k_mine)
    k_own, queries, grad_out, v_mine = lax.optimization_barrier((k_own, queries, grad_out, v_mine))
    q_other, do_other, v_other = (swapped(x, device_count) for x in (queries, grad_out, v_mine))
    qd = arrange(place, queries, grad_out, q_other, do_other, key_heads)
    qd, v_mine, v_other = lax.optimization_barrier((qd, v_mine, v_other))
    v_own = pack_both(place, v_mine, v_other)

    def halo_of(own):
        received = {back: moved(own, device_count, 2 * back) for back in far_first}
        return [own] + [received[back] for back in range(1, halo + 1)]

    def sent_back(partials):
        return [moved(partials[back - 1], device_count, -2 * back) for back in far_first]

    def per_head(*shape):
        return pl.BlockSpec((1,) + shape, lambda h, *_: (h,) + (0,) * len(shape))

    qd_spec = per_head(2, 2, group, tokens, dim)
    p_spec = per_head(2, count * tokens, group * tokens)
    p_shape = pltpu.VMEM((half, 2, count * tokens, group * tokens), BF16)
    inv_shape = pltpu.VMEM((half, 2, 1, group * tokens), F32)
    inv_spec = per_head(2, 1, group * tokens)
    do_shape = pltpu.VMEM((half, 2, group, tokens, dim), BF16)
    do_spec = per_head(2, group, tokens, dim)
    tiles = pltpu.VMEM((2, count - 1, tokens, HEADS_AT_ONCE * tokens), F32)
    pair_spec = per_head(2, tokens, dim)
    pair = (half, 2, tokens, dim)
    one_spec = per_head(tokens, dim)
    one_shape = jax.ShapeDtypeStruct((half, tokens, dim), BF16)
    dq_shape = jax.ShapeDtypeStruct((tokens, heads // 2, dim), BF16)
    dq_spec = pl.BlockSpec(dq_shape.shape, lambda h, *_: (0, 0, 0))
    far_rows = tokens + half * tokens // (heads // 2)
    step = (far_rows // 3 + 7) // 8 * 8
    parts = [
        jax.ShapeDtypeStruct((rows, heads // 2, dim), BF16) for rows in (step, step, far_rows - 2 * step)
    ]
    part_specs = [pl.BlockSpec(part.shape, lambda h, *_: (0, 0, 0)) for part in parts]
    run = pltpu.VMEM((window, tokens, dim), BF16)
    acc = pltpu.VMEM((2 * halo, tokens, dim), F32)
    product = 2 * half * 2 * count * tokens * group * tokens * dim

    k_pairs = halo_of(k_own)
    v_pairs = halo_of(v_own)
    prob, inverse, scaled, *dv_halo = call(
        functools.partial(prob_kernel, halo),
        "prob",
        (half,),
        (place, doc_lengths),
        (in_vmem(qd), *k_pairs),
        [qd_spec] + [pair_spec] * (halo + 1),
        [p_shape, inv_shape, do_shape] + [jax.ShapeDtypeStruct(pair, BF16)] * halo,
        [p_spec, inv_spec, do_spec] + [pair_spec] * halo,
        [run, acc, tiles, tiles],
        4 * product,
    )
    dv_back = sent_back(dv_halo)
    dscore, *dk_halo = call(
        functools.partial(dscore_kernel, halo),
        "dscore",
        (half,),
        place,
        (in_vmem(qd), in_vmem(prob), in_vmem(inverse), in_vmem(scaled), *v_pairs),
        [qd_spec, p_spec, inv_spec, do_spec] + [pair_spec] * (halo + 1),
        [p_shape] + [jax.ShapeDtypeStruct(pair, BF16)] * halo,
        [p_spec] + [pair_spec] * halo,
        [run, acc, tiles],
        4 * product,
    )
    dk_back = sent_back(dk_halo)
    dq, *others, dk_own, dv = call(
        functools.partial(own_kernel, halo),
        "own",
        (half,),
        place,
        (in_vmem(qd), in_vmem(prob), in_vmem(scaled), in_vmem(dscore), *k_pairs, *dv_back),
        [qd_spec, p_spec, do_spec, p_spec] + [pair_spec] * (2 * halo + 1),
        [dq_shape, *parts, jax.ShapeDtypeStruct(pair, F32), one_shape],
        [dq_spec, *part_specs, pair_spec, one_spec],
        [
            run,
            pltpu.VMEM((2, tokens * heads // 2, dim), F32),
            pltpu.VMEM((2, tokens, dim), F32),
            pltpu.VMEM((half * tokens, dim), BF16),
        ],
        0,
    )
    others = [swapped(part, device_count) for part in others]
    grad_queries, grad_values = join(place, dq, dv, others)
    dk, dk_other = summed(place, dk_own, dk_back, (grad_queries, grad_values))
    grad_keys = merge(place, dk, swapped(dk_other, device_count), "merge_dk")
    return grad_queries, grad_keys, grad_values


def solution(mesh):
    spec = P(AXES, None, None)
    return jax.shard_map(
        local, mesh=mesh, in_specs=(spec,) * 4 + (P(),), out_specs=(spec,) * 3, check_vma=False
    )
```

```python
import functools

import jax
import jax.numpy as jnp
from jax import lax
from jax.experimental import pallas as pl
from jax.experimental.pallas import tpu as pltpu
from jax.sharding import PartitionSpec as P

AXES = ("ctx", "uly")
MASKED = -1e30
LOG2E = 1.4426950408889634
HEADS_AT_ONCE = 2
BF16, F32 = jnp.bfloat16, jnp.float32
NT = (((1,), (1,)), ((), ()))
VMEM_BYTES = 16 * 2**20


def moved(array, device_count, by):
    pairs = [(d, d + by) for d in range(device_count) if 0 <= d + by < device_count]
    return lax.ppermute(array, AXES, pairs)


def swapped(array, device_count):
    return lax.ppermute(array, AXES, [(d, d ^ 1) for d in range(device_count)])


def in_vmem(array):
    return pltpu.with_memory_space_constraint(array, pltpu.VMEM)


def in_hbm(array):
    return pltpu.with_memory_space_constraint(array, pltpu.HBM)


def call(kernel, name, grid, place, inputs, in_specs, outs, out_specs, scratch, flops, aliases={}):
    scalars = place if isinstance(place, tuple) else (place,)
    return pl.pallas_call(
        kernel,
        out_shape=outs,
        grid_spec=pltpu.PrefetchScalarGridSpec(
            num_scalar_prefetch=len(scalars),
            grid=grid,
            in_specs=in_specs,
            out_specs=out_specs,
            scratch_shapes=scratch,
        ),
        compiler_params=pltpu.CompilerParams(vmem_limit_bytes=VMEM_BYTES),
        cost_estimate=pl.CostEstimate(flops=flops, bytes_accessed=0, transcendentals=0),
        input_output_aliases=aliases,
        name=name,
    )(*scalars, *inputs)


def arrange_kernel(group, place_ref, q_ref, do_ref, q_other_ref, do_other_ref, out_ref, scr):
    core = place_ref[0]
    tokens, heads, dim = q_ref.shape
    half = heads // 2
    mine = pl.ds(pl.multiple_of(core * half, half), half)
    turn = 0
    for kind, (own, other) in enumerate([(q_ref, q_other_ref), (do_ref, do_other_ref)]):
        for which, ref in enumerate([own, other]):
            block = 1 - core if which else core
            wide = scr.at[turn % 2]
            wide[...] = ref[:, mine].astype(F32).reshape(tokens * half, dim)
            for h in range(half):
                out_ref[h // group, block, kind, h % group] = wide[pl.ds(h, tokens, stride=half), :].astype(BF16)
            turn += 1


def arrange(place, queries, grad_out, q_other, do_other, key_heads):
    tokens, heads, dim = queries.shape
    half, group = heads // 2, heads // key_heads
    whole = pl.BlockSpec(memory_space=pltpu.VMEM)
    return call(
        functools.partial(arrange_kernel, group),
        "arrange",
        (1,),
        place,
        [in_vmem(x) for x in (queries, grad_out, q_other, do_other)],
        [whole] * 4,
        pltpu.VMEM((key_heads // 2, 2, 2, group, tokens, dim), BF16),
        whole,
        [pltpu.VMEM((2, tokens * half, dim), F32)],
        10**9,
    )


def pack_block(raw, core, block, out_ref, scr):
    tokens, heads, dim = raw.shape
    half = heads // 2
    scr[...] = raw[...].astype(F32).reshape(tokens * heads, dim)
    for h in range(half):
        out_ref[h, block] = scr[pl.ds(core * half + h, tokens, stride=heads), :].astype(BF16)


def fetch_kernel(place_ref, key_ref, *refs):
    count = (len(refs) - 4) // 2
    sources, out_ref, targets = refs[:count], refs[count], refs[count + 1 : 2 * count + 1]
    raw, scr, sems = refs[-3:]
    first = pltpu.make_async_copy(key_ref, raw, sems.at[0])
    first.start()
    copies = [pltpu.make_async_copy(s, t, sems.at[i + 1]) for i, (s, t) in enumerate(zip(sources, targets))]
    for copy in copies:
        copy.start()
    first.wait()
    pack_block(raw, place_ref[0], place_ref[0], out_ref, scr)
    for copy in copies:
        copy.wait()


def fetch(place, keys, arrays):
    tokens, heads, dim = keys.shape
    out = (heads // 2, 2, tokens, dim)
    return call(
        fetch_kernel,
        "fetch",
        (1,),
        place,
        [in_hbm(x) for x in (keys, *arrays)],
        [pl.BlockSpec(memory_space=pltpu.HBM)] * (1 + len(arrays)),
        [pltpu.VMEM(out, BF16)] + [pltpu.VMEM(x.shape, x.dtype) for x in arrays],
        [pl.BlockSpec(memory_space=pltpu.VMEM)] * (1 + len(arrays)),
        [
            pltpu.VMEM(keys.shape, BF16),
            pltpu.VMEM((tokens * heads, dim), F32),
            pltpu.SemaphoreType.DMA((1 + len(arrays),)),
        ],
        10**9,
    )


def pack_other_kernel(place_ref, other_ref, _, out_ref, scr):
    pack_block(other_ref, place_ref[0], 1 - place_ref[0], out_ref, scr)


def pack_other(place, other, packed):
    tokens, heads, dim = other.shape
    whole = pl.BlockSpec(memory_space=pltpu.VMEM)
    return call(
        pack_other_kernel,
        "pack_other",
        (1,),
        place,
        (in_vmem(other), in_vmem(packed)),
        [whole] * 2,
        pltpu.VMEM(packed.shape, BF16),
        whole,
        [pltpu.VMEM((tokens * heads, dim), F32)],
        10**9,
        {2: 0},
    )


def pack_both_kernel(place_ref, own_ref, other_ref, out_ref, scr):
    core = place_ref[0]
    pack_block(own_ref, core, core, out_ref, scr)
    pack_block(other_ref, core, 1 - core, out_ref, scr)


def pack_both(place, own, other):
    tokens, heads, dim = own.shape
    out = (heads // 2, 2, tokens, dim)
    whole = pl.BlockSpec(memory_space=pltpu.VMEM)
    return call(
        pack_both_kernel,
        "pack_both",
        (1,),
        place,
        (in_vmem(own), in_vmem(other)),
        [whole] * 2,
        pltpu.VMEM(out, BF16),
        whole,
        [pltpu.VMEM((tokens * heads, dim), F32)],
        10**9,
    )


def folded(op, x):
    while x.shape[0] > 8:
        half = x.shape[0] // 2
        x = op(x[:half], x[half:])
    reduce = jnp.max if op is jnp.maximum else jnp.sum
    return reduce(x, axis=0, keepdims=True)


def first_allowed(lengths_ref, query_pos, window_start):
    def step(d, carry):
        start, first = carry
        first = jnp.where(query_pos + window_start >= start, start, first)
        return start + lengths_ref[d], first

    zero = jnp.zeros(query_pos.shape, jnp.int32)
    _, first = lax.fori_loop(0, lengths_ref.shape[0], step, (jnp.int32(0), zero))
    return first - window_start


def window_of(pair_refs, scr):
    halo = len(pair_refs) - 1
    for back, ref in enumerate(pair_refs):
        scr[pl.ds(2 * (halo - back), 2)] = ref[0]


def on_diagonal(tokens, copies):
    row = lax.broadcasted_iota(jnp.int32, (tokens, tokens), 0)
    lane = lax.broadcasted_iota(jnp.int32, (tokens, tokens), 1)
    return jnp.concatenate([row] * copies, axis=1), jnp.concatenate([lane] * copies, axis=1)


def store_tiles(ref, e, at, tiles, diagonal):
    tokens, pair = diagonal.shape
    lanes = slice(at, at + pair)
    shared = tiles[0].astype(F32)
    ref[0, e, :tokens, lanes] = jnp.where(diagonal, 0.0, shared).astype(BF16)
    for j, tile in enumerate(tiles[1:], 1):
        ref[0, e, j * tokens : (j + 1) * tokens, lanes] = tile.astype(BF16)
    ref[0, e, -tokens:, lanes] = jnp.where(diagonal, shared, 0.0).astype(BF16)


def prob_kernel(halo, place_ref, lengths_ref, qd_ref, *refs):
    k_refs = refs[: halo + 1]
    p_ref = refs[halo + 1]
    dv_refs = refs[halo + 2 : -3]
    k_scr, acc, bias = refs[-3:]
    _, _, _, group, tokens, dim = qd_ref.shape
    count = 2 * halo + 1
    pair = HEADS_AT_ONCE * tokens
    row, lane = on_diagonal(tokens, HEADS_AT_ONCE)
    diagonal = row <= lane

    @pl.when(pl.program_id(0) == 0)
    def _():
        for e in range(2):
            query_pos = lane[:1] + (2 * halo + e) * tokens
            first = first_allowed(lengths_ref, query_pos, place_ref[1]) - row
            last = (e + count - 1) * tokens
            bias[e, 0] = jnp.where(first <= jnp.where(diagonal, last, e * tokens), 0.0, MASKED)
            for j in range(1, count - 1):
                bias[e, j] = jnp.where(first <= (e + j) * tokens, 0.0, MASKED)

    window_of(k_refs, k_scr)
    for e in range(2):
        k = k_scr[pl.ds(e, count)].reshape(count * tokens, dim)
        q = qd_ref[0, e, 0].reshape(group * tokens, dim)
        do = qd_ref[0, e, 1].reshape(group * tokens, dim)
        for at in range(0, group * tokens, pair):
            s = lax.dot_general(k, q[at : at + pair], NT, preferred_element_type=F32)
            tiles = [s[j * tokens : (j + 1) * tokens] for j in range(count)]
            tiles[0] = jnp.where(diagonal, tiles.pop(), tiles[0])
            tiles = [tile + bias[e, j] for j, tile in enumerate(tiles)]
            top = folded(jnp.maximum, functools.reduce(jnp.maximum, tiles))
            tiles = [jnp.exp2((tile - top) * (dim**-0.5 * LOG2E)) for tile in tiles]
            inv = 1.0 / folded(jnp.add, functools.reduce(jnp.add, tiles))
            store_tiles(p_ref, e, at, [tile * inv for tile in tiles], diagonal)
        keep = (2 * halo - e) * tokens
        dv = jnp.dot(p_ref[0, e, :keep], do, preferred_element_type=F32).reshape(2 * halo - e, tokens, dim)
        if e == 0:
            acc[...] = dv
        else:
            acc[1:] += dv
    for back, ref in zip(range(1, halo + 1), dv_refs):
        ref[0] = acc[pl.ds(2 * (halo - back), 2)].astype(BF16)


def dscore_kernel(halo, place_ref, qd_ref, p_ref, *refs):
    v_refs = refs[: halo + 1]
    ds_ref = refs[halo + 1]
    dk_refs = refs[halo + 2 : -2]
    v_scr, acc = refs[-2:]
    _, _, _, group, tokens, dim = qd_ref.shape
    count = 2 * halo + 1
    pair = HEADS_AT_ONCE * tokens
    window_of(v_refs, v_scr)
    row, lane = on_diagonal(tokens, HEADS_AT_ONCE)
    diagonal = row <= lane
    for e in range(2):
        v = v_scr[pl.ds(e, count)].reshape(count * tokens, dim)
        q = qd_ref[0, e, 0].reshape(group * tokens, dim)
        do = qd_ref[0, e, 1].reshape(group * tokens, dim)
        for at in range(0, group * tokens, pair):
            dp = lax.dot_general(v, do[at : at + pair], NT, preferred_element_type=F32)
            dps = [dp[j * tokens : (j + 1) * tokens] for j in range(count)]
            dps[0] = jnp.where(diagonal, dps.pop(), dps[0])
            ps = [p_ref[0, e, j * tokens : (j + 1) * tokens, at : at + pair] for j in range(count)]
            ps[0] += ps.pop()
            delta = folded(jnp.add, functools.reduce(jnp.add, [p.astype(F32) * dp for p, dp in zip(ps, dps)]))
            store_tiles(ds_ref, e, at, [p * (dp - delta).astype(BF16) for p, dp in zip(ps, dps)], diagonal)
        keep = (2 * halo - e) * tokens
        dk = jnp.dot(ds_ref[0, e, :keep], q, preferred_element_type=F32).reshape(2 * halo - e, tokens, dim)
        if e == 0:
            acc[...] = dk
        else:
            acc[1:] += dk
    for back, ref in zip(range(1, halo + 1), dk_refs):
        ref[0] = (acc[pl.ds(2 * (halo - back), 2)] * dim**-0.5).astype(BF16)


def own_kernel(halo, place_ref, qd_ref, p_ref, ds_ref, *refs):
    k_refs, back_refs = refs[: halo + 1], refs[halo + 1 : 2 * halo + 1]
    dq_ref, *other_refs, dk_ref, dv_ref, k_scr, dq_scr, dv_scr, far_dv = refs[2 * halo + 1 :]
    core, head = place_ref[0], pl.program_id(0)
    _, _, _, group, tokens, dim = qd_ref.shape
    rows = dq_ref.shape[1]
    count = 2 * halo + 1
    scale = dim**-0.5
    window_of(k_refs, k_scr)
    for e in range(2):
        q = qd_ref[0, e, 0].reshape(group * tokens, dim)
        do = qd_ref[0, e, 1].reshape(group * tokens, dim)
        k = k_scr[pl.ds(e, count)].reshape(count * tokens, dim)
        dqt = jnp.dot(k.T, ds_ref[0, e], preferred_element_type=F32) * scale
        for g in range(group):
            dq_scr[e, pl.ds(head * group + g, tokens, stride=rows), :] = dqt[:, g * tokens : (g + 1) * tokens].T
        keep = (2 * halo - e) * tokens
        dk = jnp.dot(ds_ref[0, e, keep:], q, preferred_element_type=F32) * scale
        dv = jnp.dot(p_ref[0, e, keep:], do, preferred_element_type=F32)
        if e == 0:
            dk_ref[0, 0], dv_scr[0] = dk, dv
        else:
            dk_ref[0, 0] += dk[:tokens]
            dv_scr[0] += dv[:tokens]
            dk_ref[0, 1], dv_scr[1] = dk[tokens:], dv[tokens:]
    for ref in back_refs:
        dv_scr[...] += ref[0].astype(F32)
    dv_ref[0] = dv_scr[core].astype(BF16)
    far_dv[pl.ds(pl.multiple_of(head * tokens, tokens), tokens)] = dv_scr[1 - core].astype(BF16)

    @pl.when(head == pl.num_programs(0) - 1)
    def _():
        dq_ref[...] = dq_scr[core].astype(BF16).reshape(dq_ref.shape)
        dq_rows, start = tokens * rows, 0
        for ref in other_refs:
            part = ref.shape[0] * rows
            here = min(part, dq_rows - start)
            ref[: here // rows] = dq_scr[1 - core, start : start + here].astype(BF16).reshape(-1, rows, dim)
            if here < part:
                ref[here // rows :] = far_dv[...].reshape(-1, rows, dim)
            start += part


def sum_kernel(count, place_ref, own_ref, *refs):
    back_refs, (mine_ref, other_ref) = refs[:count], refs[-2:]
    core = place_ref[0]
    for block, ref in [(1 - core, other_ref), (core, mine_ref)]:
        total = own_ref[:, block]
        for back in back_refs:
            total += back[:, block].astype(F32)
        ref[...] = total.astype(BF16)


def summed(place, own, backs, before):
    half, _, tokens, dim = own.shape
    pair_spec = pl.BlockSpec(own.shape, lambda i, place: (0, 0, 0, 0))
    one = (half, tokens, dim)
    return call(
        functools.partial(sum_kernel, len(backs)),
        "sum_dk",
        (1,),
        place,
        (own, *backs, *(in_hbm(x) for x in before)),
        [pair_spec] * (1 + len(backs)) + [pl.BlockSpec(memory_space=pltpu.HBM)] * len(before),
        [jax.ShapeDtypeStruct(one, BF16)] * 2,
        [pl.BlockSpec(one, lambda i, place: (0, 0, 0))] * 2,
        [],
        0,
    )


def merge_half(core, own_ref, other, out_ref, scr):
    rows, heads, dim = out_ref.shape
    half = heads // 2
    skip = other.shape[0] - half * rows
    for h in range(half):
        scr[pl.ds(core * half + h, rows, stride=heads), :] = own_ref[h].astype(F32)
        rest = other[skip + h * rows : skip + (h + 1) * rows]
        scr[pl.ds((1 - core) * half + h, rows, stride=heads), :] = rest.astype(F32)
    out_ref[...] = scr[...].astype(BF16).reshape(rows, heads, dim)


def join_kernel(parts, place_ref, dq_ref, dv_ref, *refs):
    others, (dq_out, dv_out, scr, sems) = refs[:parts], refs[parts:]
    core = place_ref[0]
    tokens, half, dim = dq_ref.shape
    at = pl.multiple_of(core * half, half)
    copies = [pltpu.make_async_copy(dq_ref, dq_out.at[:, pl.ds(at, half)], sems.at[0])]
    at = pl.multiple_of((1 - core) * half, half)
    first = 0
    for i, part in enumerate(others):
        count = min(part.shape[0], tokens - first)
        to = dq_out.at[pl.ds(first, count), pl.ds(at, half)]
        copies.append(pltpu.make_async_copy(part.at[pl.ds(0, count)], to, sems.at[1 + i]))
        first += count
    for copy in copies:
        copy.start()
    merge_half(core, dv_ref, others[-1][...].reshape(-1, dim), dv_out, scr)
    for copy in copies:
        copy.wait()


def join(place, dq, dv, others):
    tokens, half, dim = dq.shape
    out = (tokens, 2 * dv.shape[0], dim)
    vmem = pl.BlockSpec(memory_space=pltpu.VMEM)
    parts = len(others)
    return call(
        functools.partial(join_kernel, parts),
        "join",
        (1,),
        place,
        [in_vmem(x) for x in (dq, dv, *others)],
        [vmem] * (2 + parts),
        [jax.ShapeDtypeStruct((tokens, 2 * half, dim), BF16), jax.ShapeDtypeStruct(out, BF16)],
        [pl.BlockSpec(memory_space=pl.ANY), pl.BlockSpec(out, lambda i, place: (0, 0, 0))],
        [pltpu.VMEM((tokens * out[1], dim), F32), pltpu.SemaphoreType.DMA((1 + parts,))],
        0,
    )


def merge_kernel(place_ref, own_ref, other_ref, out_ref, scr):
    merge_half(place_ref[0], own_ref, other_ref[...].reshape(-1, own_ref.shape[2]), out_ref, scr)


def merge(place, own, other, name):
    half, tokens, dim = own.shape
    out = (tokens, 2 * half, dim)
    vmem = pl.BlockSpec(memory_space=pltpu.VMEM)
    return call(
        merge_kernel,
        name,
        (1,),
        place,
        (in_vmem(own), in_vmem(other)),
        [vmem] * 2,
        jax.ShapeDtypeStruct(out, BF16),
        pl.BlockSpec(out, lambda i, place: (0, 0, 0)),
        [pltpu.VMEM((tokens * 2 * half, dim), F32)],
        0,
    )


def local(queries, keys, values, grad_out, doc_lengths):
    uly_count = lax.axis_size("uly")
    device_count = lax.axis_size("ctx") * uly_count
    halo = uly_count // 2
    device = lax.axis_index("ctx") * uly_count + lax.axis_index("uly")
    core = device % 2
    tokens, heads, dim = queries.shape
    key_heads = keys.shape[1]
    group = heads // key_heads
    half = key_heads // 2
    window, count = 2 * halo + 2, 2 * halo + 1
    place = jnp.stack([core, (device // 2 - halo) * (2 * tokens)]).astype(jnp.int32)

    far_first = range(halo, 0, -1)
    k_other = swapped(keys, device_count)
    k_mine, v_mine = fetch(place, keys, (values,))
    k_own = pack_other(place, k_other, k_mine)
    k_own, queries, grad_out, v_mine = lax.optimization_barrier((k_own, queries, grad_out, v_mine))
    q_other, do_other, v_other = (swapped(x, device_count) for x in (queries, grad_out, v_mine))
    qd = arrange(place, queries, grad_out, q_other, do_other, key_heads)
    qd, v_mine, v_other = lax.optimization_barrier((qd, v_mine, v_other))
    v_own = pack_both(place, v_mine, v_other)

    def halo_of(own):
        received = {back: moved(own, device_count, 2 * back) for back in far_first}
        return [own] + [received[back] for back in range(1, halo + 1)]

    def sent_back(partials):
        return [moved(partials[back - 1], device_count, -2 * back) for back in far_first]

    def per_head(*shape):
        return pl.BlockSpec((1,) + shape, lambda h, *_: (h,) + (0,) * len(shape))

    qd_spec = per_head(2, 2, group, tokens, dim)
    p_spec = per_head(2, count * tokens, group * tokens)
    p_shape = pltpu.VMEM((half, 2, count * tokens, group * tokens), BF16)
    pair_spec = per_head(2, tokens, dim)
    pair = (half, 2, tokens, dim)
    one_spec = per_head(tokens, dim)
    one_shape = jax.ShapeDtypeStruct((half, tokens, dim), BF16)
    dq_shape = jax.ShapeDtypeStruct((tokens, heads // 2, dim), BF16)
    dq_spec = pl.BlockSpec(dq_shape.shape, lambda h, *_: (0, 0, 0))
    far_rows = tokens + half * tokens // (heads // 2)
    step = (far_rows // 3 + 7) // 8 * 8
    parts = [
        jax.ShapeDtypeStruct((rows, heads // 2, dim), BF16) for rows in (step, step, far_rows - 2 * step)
    ]
    part_specs = [pl.BlockSpec(part.shape, lambda h, *_: (0, 0, 0)) for part in parts]
    run = pltpu.VMEM((window, tokens, dim), BF16)
    acc = pltpu.VMEM((2 * halo, tokens, dim), F32)
    product = 2 * half * 2 * count * tokens * group * tokens * dim

    k_pairs = halo_of(k_own)
    v_pairs = halo_of(v_own)
    prob, *dv_halo = call(
        functools.partial(prob_kernel, halo),
        "prob",
        (half,),
        (place, doc_lengths),
        (in_vmem(qd), *k_pairs),
        [qd_spec] + [pair_spec] * (halo + 1),
        [p_shape] + [jax.ShapeDtypeStruct(pair, BF16)] * halo,
        [p_spec] + [pair_spec] * halo,
        [run, acc, pltpu.VMEM((2, count - 1, tokens, HEADS_AT_ONCE * tokens), F32)],
        4 * product,
    )
    dv_back = sent_back(dv_halo)
    dscore, *dk_halo = call(
        functools.partial(dscore_kernel, halo),
        "dscore",
        (half,),
        place,
        (in_vmem(qd), in_vmem(prob), *v_pairs),
        [qd_spec, p_spec] + [pair_spec] * (halo + 1),
        [p_shape] + [jax.ShapeDtypeStruct(pair, BF16)] * halo,
        [p_spec] + [pair_spec] * halo,
        [run, acc],
        4 * product,
    )
    dk_back = sent_back(dk_halo)
    dq, *others, dk_own, dv = call(
        functools.partial(own_kernel, halo),
        "own",
        (half,),
        place,
        (in_vmem(qd), in_vmem(prob), in_vmem(dscore), *k_pairs, *dv_back),
        [qd_spec, p_spec, p_spec] + [pair_spec] * (2 * halo + 1),
        [dq_shape, *parts, jax.ShapeDtypeStruct(pair, F32), one_shape],
        [dq_spec, *part_specs, pair_spec, one_spec],
        [
            run,
            pltpu.VMEM((2, tokens * heads // 2, dim), F32),
            pltpu.VMEM((2, tokens, dim), F32),
            pltpu.VMEM((half * tokens, dim), BF16),
        ],
        0,
    )
    others = [swapped(part, device_count) for part in others]
    grad_queries, grad_values = join(place, dq, dv, others)
    dk, dk_other = summed(place, dk_own, dk_back, (grad_queries, grad_values))
    grad_keys = merge(place, dk, swapped(dk_other, device_count), "merge_dk")
    return grad_queries, grad_keys, grad_values


def solution(mesh):
    spec = P(AXES, None, None)
    return jax.shard_map(
        local, mesh=mesh, in_specs=(spec,) * 4 + (P(),), out_specs=(spec,) * 3, check_vma=False
    )
```

```python
import functools

import jax
import jax.numpy as jnp
from jax import lax
from jax.experimental import pallas as pl
from jax.experimental.pallas import tpu as pltpu
from jax.sharding import PartitionSpec as P

AXES = ("ctx", "uly")
MASKED = -1e30
LOG2E = 1.4426950408889634
HEADS_AT_ONCE = 2
BF16, F32 = jnp.bfloat16, jnp.float32
NT = (((1,), (1,)), ((), ()))
VMEM_BYTES = 16 * 2**20


def moved(array, device_count, by):
    pairs = [(d, d + by) for d in range(device_count) if 0 <= d + by < device_count]
    return lax.ppermute(array, AXES, pairs)


def swapped(array, device_count):
    return lax.ppermute(array, AXES, [(d, d ^ 1) for d in range(device_count)])


def in_vmem(array):
    return pltpu.with_memory_space_constraint(array, pltpu.VMEM)


def in_hbm(array):
    return pltpu.with_memory_space_constraint(array, pltpu.HBM)


def call(kernel, name, grid, place, inputs, in_specs, outs, out_specs, scratch, flops, aliases={}):
    scalars = place if isinstance(place, tuple) else (place,)
    return pl.pallas_call(
        kernel,
        out_shape=outs,
        grid_spec=pltpu.PrefetchScalarGridSpec(
            num_scalar_prefetch=len(scalars),
            grid=grid,
            in_specs=in_specs,
            out_specs=out_specs,
            scratch_shapes=scratch,
        ),
        compiler_params=pltpu.CompilerParams(vmem_limit_bytes=VMEM_BYTES),
        cost_estimate=pl.CostEstimate(flops=flops, bytes_accessed=0, transcendentals=0),
        input_output_aliases=aliases,
        name=name,
    )(*scalars, *inputs)


def arrange_kernel(group, place_ref, q_ref, do_ref, q_other_ref, do_other_ref, out_ref, scr):
    core = place_ref[0]
    tokens, heads, dim = q_ref.shape
    half = heads // 2
    mine = pl.ds(pl.multiple_of(core * half, half), half)
    turn = 0
    for kind, (own, other) in enumerate([(q_ref, q_other_ref), (do_ref, do_other_ref)]):
        for which, ref in enumerate([own, other]):
            block = 1 - core if which else core
            wide = scr.at[turn % 2]
            wide[...] = ref[:, mine].astype(F32).reshape(tokens * half, dim)
            for h in range(half):
                out_ref[h // group, block, kind, h % group] = wide[pl.ds(h, tokens, stride=half), :].astype(BF16)
            turn += 1


def arrange(place, queries, grad_out, q_other, do_other, key_heads):
    tokens, heads, dim = queries.shape
    half, group = heads // 2, heads // key_heads
    whole = pl.BlockSpec(memory_space=pltpu.VMEM)
    return call(
        functools.partial(arrange_kernel, group),
        "arrange",
        (1,),
        place,
        [in_vmem(x) for x in (queries, grad_out, q_other, do_other)],
        [whole] * 4,
        pltpu.VMEM((key_heads // 2, 2, 2, group, tokens, dim), BF16),
        whole,
        [pltpu.VMEM((2, tokens * half, dim), F32)],
        10**9,
    )


def pack_block(raw, core, block, out_ref, scr):
    tokens, heads, dim = raw.shape
    half = heads // 2
    scr[...] = raw[...].astype(F32).reshape(tokens * heads, dim)
    for h in range(half):
        out_ref[h, block] = scr[pl.ds(core * half + h, tokens, stride=heads), :].astype(BF16)


def fetch_kernel(place_ref, key_ref, *refs):
    count = (len(refs) - 4) // 2
    sources, out_ref, targets = refs[:count], refs[count], refs[count + 1 : 2 * count + 1]
    raw, scr, sems = refs[-3:]
    first = pltpu.make_async_copy(key_ref, raw, sems.at[0])
    first.start()
    copies = [pltpu.make_async_copy(s, t, sems.at[i + 1]) for i, (s, t) in enumerate(zip(sources, targets))]
    for copy in copies:
        copy.start()
    first.wait()
    pack_block(raw, place_ref[0], place_ref[0], out_ref, scr)
    for copy in copies:
        copy.wait()


def fetch(place, keys, arrays):
    tokens, heads, dim = keys.shape
    out = (heads // 2, 2, tokens, dim)
    return call(
        fetch_kernel,
        "fetch",
        (1,),
        place,
        [in_hbm(x) for x in (keys, *arrays)],
        [pl.BlockSpec(memory_space=pltpu.HBM)] * (1 + len(arrays)),
        [pltpu.VMEM(out, BF16)] + [pltpu.VMEM(x.shape, x.dtype) for x in arrays],
        [pl.BlockSpec(memory_space=pltpu.VMEM)] * (1 + len(arrays)),
        [
            pltpu.VMEM(keys.shape, BF16),
            pltpu.VMEM((tokens * heads, dim), F32),
            pltpu.SemaphoreType.DMA((1 + len(arrays),)),
        ],
        10**9,
    )


def pack_other_kernel(place_ref, other_ref, _, out_ref, scr):
    pack_block(other_ref, place_ref[0], 1 - place_ref[0], out_ref, scr)


def pack_other(place, other, packed):
    tokens, heads, dim = other.shape
    whole = pl.BlockSpec(memory_space=pltpu.VMEM)
    return call(
        pack_other_kernel,
        "pack_other",
        (1,),
        place,
        (in_vmem(other), in_vmem(packed)),
        [whole] * 2,
        pltpu.VMEM(packed.shape, BF16),
        whole,
        [pltpu.VMEM((tokens * heads, dim), F32)],
        10**9,
        {2: 0},
    )


def pack_both_kernel(place_ref, own_ref, other_ref, out_ref, scr):
    core = place_ref[0]
    pack_block(own_ref, core, core, out_ref, scr)
    pack_block(other_ref, core, 1 - core, out_ref, scr)


def pack_both(place, own, other):
    tokens, heads, dim = own.shape
    out = (heads // 2, 2, tokens, dim)
    whole = pl.BlockSpec(memory_space=pltpu.VMEM)
    return call(
        pack_both_kernel,
        "pack_both",
        (1,),
        place,
        (in_vmem(own), in_vmem(other)),
        [whole] * 2,
        pltpu.VMEM(out, BF16),
        whole,
        [pltpu.VMEM((tokens * heads, dim), F32)],
        10**9,
    )


def folded(op, x):
    while x.shape[0] > 8:
        half = x.shape[0] // 2
        x = op(x[:half], x[half:])
    reduce = jnp.max if op is jnp.maximum else jnp.sum
    return reduce(x, axis=0, keepdims=True)


def first_allowed(lengths_ref, query_pos, window_start):
    def step(d, carry):
        start, first = carry
        first = jnp.where(query_pos + window_start >= start, start, first)
        return start + lengths_ref[d], first

    zero = jnp.zeros(query_pos.shape, jnp.int32)
    _, first = lax.fori_loop(0, lengths_ref.shape[0], step, (jnp.int32(0), zero))
    return first - window_start


def window_of(pair_refs, scr):
    for i, ref in enumerate(pair_refs):
        scr[pl.ds(2 * i, 2)] = ref[0]


def on_diagonal(tokens, copies):
    row = lax.broadcasted_iota(jnp.int32, (tokens, tokens), 0)
    lane = lax.broadcasted_iota(jnp.int32, (tokens, tokens), 1)
    return jnp.concatenate([row] * copies, axis=1), jnp.concatenate([lane] * copies, axis=1)


def store_tiles(ref, e, at, tiles, diagonal):
    tokens, pair = diagonal.shape
    lanes = slice(at, at + pair)
    shared = tiles[0].astype(F32)
    ref[0, e, :tokens, lanes] = jnp.where(diagonal, 0.0, shared).astype(BF16)
    for j, tile in enumerate(tiles[1:], 1):
        ref[0, e, j * tokens : (j + 1) * tokens, lanes] = tile.astype(BF16)
    ref[0, e, -tokens:, lanes] = jnp.where(diagonal, shared, 0.0).astype(BF16)


def prob_kernel(halo, place_ref, lengths_ref, qd_ref, *refs):
    k_refs = refs[: halo + 1]
    p_ref = refs[halo + 1]
    dv_refs = refs[halo + 2 : -3]
    k_scr, acc, bias = refs[-3:]
    _, _, _, group, tokens, dim = qd_ref.shape
    count = 2 * halo + 1
    pair = HEADS_AT_ONCE * tokens
    row, lane = on_diagonal(tokens, HEADS_AT_ONCE)
    diagonal = row <= lane

    @pl.when(pl.program_id(0) == 0)
    def _():
        for e in range(2):
            query_pos = lane[:1] + (2 * halo + e) * tokens
            first = first_allowed(lengths_ref, query_pos, place_ref[1]) - row
            last = (e + count - 1) * tokens
            bias[e, 0] = jnp.where(first <= jnp.where(diagonal, last, e * tokens), 0.0, MASKED)
            for j in range(1, count - 1):
                bias[e, j] = jnp.where(first <= (e + j) * tokens, 0.0, MASKED)

    window_of(k_refs, k_scr)
    for e in range(2):
        k = k_scr[pl.ds(e, count)].reshape(count * tokens, dim)
        q = qd_ref[0, e, 0].reshape(group * tokens, dim)
        do = qd_ref[0, e, 1].reshape(group * tokens, dim)
        for at in range(0, group * tokens, pair):
            s = lax.dot_general(k, q[at : at + pair], NT, preferred_element_type=F32)
            tiles = [s[j * tokens : (j + 1) * tokens] for j in range(count)]
            tiles[0] = jnp.where(diagonal, tiles.pop(), tiles[0])
            tiles = [tile + bias[e, j] for j, tile in enumerate(tiles)]
            top = folded(jnp.maximum, functools.reduce(jnp.maximum, tiles))
            tiles = [jnp.exp2((tile - top) * (dim**-0.5 * LOG2E)) for tile in tiles]
            inv = 1.0 / folded(jnp.add, functools.reduce(jnp.add, tiles))
            store_tiles(p_ref, e, at, [tile * inv for tile in tiles], diagonal)
        keep = (2 * halo - e) * tokens
        dv = jnp.dot(p_ref[0, e, :keep], do, preferred_element_type=F32).reshape(2 * halo - e, tokens, dim)
        if e == 0:
            acc[...] = dv
        else:
            acc[1:] += dv
    for back, ref in zip(range(1, halo + 1), dv_refs):
        ref[0] = acc[pl.ds(2 * (halo - back), 2)].astype(BF16)


def dscore_kernel(halo, place_ref, qd_ref, p_ref, *refs):
    v_refs = refs[: halo + 1]
    ds_ref = refs[halo + 1]
    dk_refs = refs[halo + 2 : -2]
    v_scr, acc = refs[-2:]
    _, _, _, group, tokens, dim = qd_ref.shape
    count = 2 * halo + 1
    pair = HEADS_AT_ONCE * tokens
    window_of(v_refs, v_scr)
    row, lane = on_diagonal(tokens, HEADS_AT_ONCE)
    diagonal = row <= lane
    for e in range(2):
        v = v_scr[pl.ds(e, count)].reshape(count * tokens, dim)
        q = qd_ref[0, e, 0].reshape(group * tokens, dim)
        do = qd_ref[0, e, 1].reshape(group * tokens, dim)
        for at in range(0, group * tokens, pair):
            dp = lax.dot_general(v, do[at : at + pair], NT, preferred_element_type=F32)
            dps = [dp[j * tokens : (j + 1) * tokens] for j in range(count)]
            dps[0] = jnp.where(diagonal, dps.pop(), dps[0])
            ps = [p_ref[0, e, j * tokens : (j + 1) * tokens, at : at + pair] for j in range(count)]
            ps[0] += ps.pop()
            delta = folded(jnp.add, functools.reduce(jnp.add, [p.astype(F32) * dp for p, dp in zip(ps, dps)]))
            store_tiles(ds_ref, e, at, [p * (dp - delta).astype(BF16) for p, dp in zip(ps, dps)], diagonal)
        keep = (2 * halo - e) * tokens
        dk = jnp.dot(ds_ref[0, e, :keep], q, preferred_element_type=F32).reshape(2 * halo - e, tokens, dim)
        if e == 0:
            acc[...] = dk
        else:
            acc[1:] += dk
    for back, ref in zip(range(1, halo + 1), dk_refs):
        ref[0] = (acc[pl.ds(2 * (halo - back), 2)] * dim**-0.5).astype(BF16)


def own_kernel(halo, place_ref, qd_ref, p_ref, ds_ref, *refs):
    k_refs, back_refs = refs[: halo + 1], refs[halo + 1 : 2 * halo + 1]
    dq_ref, *other_refs, dk_ref, dv_ref, k_scr, dq_scr, dv_scr, far_dv = refs[2 * halo + 1 :]
    core, head = place_ref[0], pl.program_id(0)
    _, _, _, group, tokens, dim = qd_ref.shape
    rows = dq_ref.shape[1]
    count = 2 * halo + 1
    scale = dim**-0.5
    window_of(k_refs, k_scr)
    for e in range(2):
        q = qd_ref[0, e, 0].reshape(group * tokens, dim)
        do = qd_ref[0, e, 1].reshape(group * tokens, dim)
        k = k_scr[pl.ds(e, count)].reshape(count * tokens, dim)
        dqt = jnp.dot(k.T, ds_ref[0, e], preferred_element_type=F32) * scale
        for g in range(group):
            dq_scr[e, pl.ds(head * group + g, tokens, stride=rows), :] = dqt[:, g * tokens : (g + 1) * tokens].T
        keep = (2 * halo - e) * tokens
        dk = jnp.dot(ds_ref[0, e, keep:], q, preferred_element_type=F32) * scale
        dv = jnp.dot(p_ref[0, e, keep:], do, preferred_element_type=F32)
        if e == 0:
            dk_ref[0, 0], dv_scr[0] = dk, dv
        else:
            dk_ref[0, 0] += dk[:tokens]
            dv_scr[0] += dv[:tokens]
            dk_ref[0, 1], dv_scr[1] = dk[tokens:], dv[tokens:]
    for ref in back_refs:
        dv_scr[...] += ref[0].astype(F32)
    dv_ref[0] = dv_scr[core].astype(BF16)
    far_dv[pl.ds(pl.multiple_of(head * tokens, tokens), tokens)] = dv_scr[1 - core].astype(BF16)

    @pl.when(head == pl.num_programs(0) - 1)
    def _():
        dq_ref[...] = dq_scr[core].astype(BF16).reshape(dq_ref.shape)
        dq_rows, start = tokens * rows, 0
        for ref in other_refs:
            part = ref.shape[0] * rows
            here = min(part, dq_rows - start)
            ref[: here // rows] = dq_scr[1 - core, start : start + here].astype(BF16).reshape(-1, rows, dim)
            if here < part:
                ref[here // rows :] = far_dv[...].reshape(-1, rows, dim)
            start += part


def sum_kernel(count, place_ref, own_ref, *refs):
    back_refs, (mine_ref, other_ref) = refs[:count], refs[-2:]
    core = place_ref[0]
    for block, ref in [(1 - core, other_ref), (core, mine_ref)]:
        total = own_ref[:, block]
        for back in back_refs:
            total += back[:, block].astype(F32)
        ref[...] = total.astype(BF16)


def summed(place, own, backs, before):
    half, _, tokens, dim = own.shape
    pair_spec = pl.BlockSpec(own.shape, lambda i, place: (0, 0, 0, 0))
    one = (half, tokens, dim)
    return call(
        functools.partial(sum_kernel, len(backs)),
        "sum_dk",
        (1,),
        place,
        (own, *backs, *(in_hbm(x) for x in before)),
        [pair_spec] * (1 + len(backs)) + [pl.BlockSpec(memory_space=pltpu.HBM)] * len(before),
        [jax.ShapeDtypeStruct(one, BF16)] * 2,
        [pl.BlockSpec(one, lambda i, place: (0, 0, 0))] * 2,
        [],
        0,
    )


def merge_half(core, own_ref, other, out_ref, scr):
    rows, heads, dim = out_ref.shape
    half = heads // 2
    skip = other.shape[0] - half * rows
    for h in range(half):
        scr[pl.ds(core * half + h, rows, stride=heads), :] = own_ref[h].astype(F32)
        rest = other[skip + h * rows : skip + (h + 1) * rows]
        scr[pl.ds((1 - core) * half + h, rows, stride=heads), :] = rest.astype(F32)
    out_ref[...] = scr[...].astype(BF16).reshape(rows, heads, dim)


def join_kernel(parts, place_ref, dq_ref, dv_ref, *refs):
    others, (dq_out, dv_out, scr, sems) = refs[:parts], refs[parts:]
    core = place_ref[0]
    tokens, half, dim = dq_ref.shape
    at = pl.multiple_of(core * half, half)
    copies = [pltpu.make_async_copy(dq_ref, dq_out.at[:, pl.ds(at, half)], sems.at[0])]
    at = pl.multiple_of((1 - core) * half, half)
    first = 0
    for i, part in enumerate(others):
        count = min(part.shape[0], tokens - first)
        to = dq_out.at[pl.ds(first, count), pl.ds(at, half)]
        copies.append(pltpu.make_async_copy(part.at[pl.ds(0, count)], to, sems.at[1 + i]))
        first += count
    for copy in copies:
        copy.start()
    merge_half(core, dv_ref, others[-1][...].reshape(-1, dim), dv_out, scr)
    for copy in copies:
        copy.wait()


def join(place, dq, dv, others):
    tokens, half, dim = dq.shape
    out = (tokens, 2 * dv.shape[0], dim)
    vmem = pl.BlockSpec(memory_space=pltpu.VMEM)
    parts = len(others)
    return call(
        functools.partial(join_kernel, parts),
        "join",
        (1,),
        place,
        [in_vmem(x) for x in (dq, dv, *others)],
        [vmem] * (2 + parts),
        [jax.ShapeDtypeStruct((tokens, 2 * half, dim), BF16), jax.ShapeDtypeStruct(out, BF16)],
        [pl.BlockSpec(memory_space=pl.ANY), pl.BlockSpec(out, lambda i, place: (0, 0, 0))],
        [pltpu.VMEM((tokens * out[1], dim), F32), pltpu.SemaphoreType.DMA((1 + parts,))],
        0,
    )


def merge_kernel(place_ref, own_ref, other_ref, out_ref, scr):
    merge_half(place_ref[0], own_ref, other_ref[...].reshape(-1, own_ref.shape[2]), out_ref, scr)


def merge(place, own, other, name):
    half, tokens, dim = own.shape
    out = (tokens, 2 * half, dim)
    vmem = pl.BlockSpec(memory_space=pltpu.VMEM)
    return call(
        merge_kernel,
        name,
        (1,),
        place,
        (in_vmem(own), in_vmem(other)),
        [vmem] * 2,
        jax.ShapeDtypeStruct(out, BF16),
        pl.BlockSpec(out, lambda i, place: (0, 0, 0)),
        [pltpu.VMEM((tokens * 2 * half, dim), F32)],
        0,
    )


def local(queries, keys, values, grad_out, doc_lengths):
    uly_count = lax.axis_size("uly")
    device_count = lax.axis_size("ctx") * uly_count
    halo = uly_count // 2
    device = lax.axis_index("ctx") * uly_count + lax.axis_index("uly")
    core = device % 2
    tokens, heads, dim = queries.shape
    key_heads = keys.shape[1]
    group = heads // key_heads
    half = key_heads // 2
    window, count = 2 * halo + 2, 2 * halo + 1
    place = jnp.stack([core, (device // 2 - halo) * (2 * tokens)]).astype(jnp.int32)

    near_first = range(1, halo + 1)
    k_other = swapped(keys, device_count)
    k_mine, v_mine = fetch(place, keys, (values,))
    k_own = pack_other(place, k_other, k_mine)
    k_own, queries, grad_out, v_mine = lax.optimization_barrier((k_own, queries, grad_out, v_mine))
    q_other, do_other, v_other = (swapped(x, device_count) for x in (queries, grad_out, v_mine))
    qd = arrange(place, queries, grad_out, q_other, do_other, key_heads)
    qd, v_mine, v_other = lax.optimization_barrier((qd, v_mine, v_other))
    v_own = pack_both(place, v_mine, v_other)

    def halo_of(own):
        received = {back: moved(own, device_count, 2 * back) for back in near_first}
        return [received[back] for back in range(halo, 0, -1)] + [own]

    def sent_back(partials):
        return [moved(partials[back - 1], device_count, -2 * back) for back in near_first]

    def per_head(*shape):
        return pl.BlockSpec((1,) + shape, lambda h, *_: (h,) + (0,) * len(shape))

    qd_spec = per_head(2, 2, group, tokens, dim)
    p_spec = per_head(2, count * tokens, group * tokens)
    p_shape = pltpu.VMEM((half, 2, count * tokens, group * tokens), BF16)
    pair_spec = per_head(2, tokens, dim)
    pair = (half, 2, tokens, dim)
    one_spec = per_head(tokens, dim)
    one_shape = jax.ShapeDtypeStruct((half, tokens, dim), BF16)
    dq_shape = jax.ShapeDtypeStruct((tokens, heads // 2, dim), BF16)
    dq_spec = pl.BlockSpec(dq_shape.shape, lambda h, *_: (0, 0, 0))
    far_rows = tokens + half * tokens // (heads // 2)
    step = (far_rows // 3 + 7) // 8 * 8
    parts = [
        jax.ShapeDtypeStruct((rows, heads // 2, dim), BF16) for rows in (step, step, far_rows - 2 * step)
    ]
    part_specs = [pl.BlockSpec(part.shape, lambda h, *_: (0, 0, 0)) for part in parts]
    run = pltpu.VMEM((window, tokens, dim), BF16)
    acc = pltpu.VMEM((2 * halo, tokens, dim), F32)
    product = 2 * half * 2 * count * tokens * group * tokens * dim

    k_pairs = halo_of(k_own)
    v_pairs = halo_of(v_own)
    prob, *dv_halo = call(
        functools.partial(prob_kernel, halo),
        "prob",
        (half,),
        (place, doc_lengths),
        (in_vmem(qd), *k_pairs),
        [qd_spec] + [pair_spec] * (halo + 1),
        [p_shape] + [jax.ShapeDtypeStruct(pair, BF16)] * halo,
        [p_spec] + [pair_spec] * halo,
        [run, acc, pltpu.VMEM((2, count - 1, tokens, HEADS_AT_ONCE * tokens), F32)],
        4 * product,
    )
    dv_back = sent_back(dv_halo)
    dscore, *dk_halo = call(
        functools.partial(dscore_kernel, halo),
        "dscore",
        (half,),
        place,
        (in_vmem(qd), in_vmem(prob), *v_pairs),
        [qd_spec, p_spec] + [pair_spec] * (halo + 1),
        [p_shape] + [jax.ShapeDtypeStruct(pair, BF16)] * halo,
        [p_spec] + [pair_spec] * halo,
        [run, acc],
        4 * product,
    )
    dk_back = sent_back(dk_halo)
    dq, *others, dk_own, dv = call(
        functools.partial(own_kernel, halo),
        "own",
        (half,),
        place,
        (in_vmem(qd), in_vmem(prob), in_vmem(dscore), *k_pairs, *dv_back),
        [qd_spec, p_spec, p_spec] + [pair_spec] * (2 * halo + 1),
        [dq_shape, *parts, jax.ShapeDtypeStruct(pair, F32), one_shape],
        [dq_spec, *part_specs, pair_spec, one_spec],
        [
            run,
            pltpu.VMEM((2, tokens * heads // 2, dim), F32),
            pltpu.VMEM((2, tokens, dim), F32),
            pltpu.VMEM((half * tokens, dim), BF16),
        ],
        0,
    )
    others = [swapped(part, device_count) for part in others]
    grad_queries, grad_values = join(place, dq, dv, others)
    dk, dk_other = summed(place, dk_own, dk_back, (grad_queries, grad_values))
    grad_keys = merge(place, dk, swapped(dk_other, device_count), "merge_dk")
    return grad_queries, grad_keys, grad_values


def solution(mesh):
    spec = P(AXES, None, None)
    return jax.shard_map(
        local, mesh=mesh, in_specs=(spec,) * 4 + (P(),), out_specs=(spec,) * 3, check_vma=False
    )
```

```python
import functools

import jax
import jax.numpy as jnp
from jax import lax
from jax.experimental import pallas as pl
from jax.experimental.pallas import tpu as pltpu
from jax.sharding import PartitionSpec as P

AXES = ("ctx", "uly")
MASKED = -1e30
LOG2E = 1.4426950408889634
HEADS_AT_ONCE = 2
BF16, F32 = jnp.bfloat16, jnp.float32
NT = (((1,), (1,)), ((), ()))
VMEM_BYTES = 16 * 2**20


def moved(array, device_count, by, ring=False):
    pairs = [(d, d + by) for d in range(device_count)]
    if ring:
        return lax.ppermute(array, AXES, [(d, to % device_count) for d, to in pairs])
    return lax.ppermute(array, AXES, [(d, to) for d, to in pairs if 0 <= to < device_count])


def swapped(array, device_count):
    return lax.ppermute(array, AXES, [(d, d ^ 1) for d in range(device_count)])


def in_vmem(array):
    return pltpu.with_memory_space_constraint(array, pltpu.VMEM)


def in_hbm(array):
    return pltpu.with_memory_space_constraint(array, pltpu.HBM)


def call(kernel, name, grid, place, inputs, in_specs, outs, out_specs, scratch, flops, aliases={}):
    scalars = place if isinstance(place, tuple) else (place,)
    return pl.pallas_call(
        kernel,
        out_shape=outs,
        grid_spec=pltpu.PrefetchScalarGridSpec(
            num_scalar_prefetch=len(scalars),
            grid=grid,
            in_specs=in_specs,
            out_specs=out_specs,
            scratch_shapes=scratch,
        ),
        compiler_params=pltpu.CompilerParams(vmem_limit_bytes=VMEM_BYTES),
        cost_estimate=pl.CostEstimate(flops=flops, bytes_accessed=0, transcendentals=0),
        input_output_aliases=aliases,
        name=name,
    )(*scalars, *inputs)


def arrange_kernel(group, place_ref, q_ref, do_ref, q_other_ref, do_other_ref, out_ref, scr):
    core = place_ref[0]
    tokens, heads, dim = q_ref.shape
    half = heads // 2
    mine = pl.ds(pl.multiple_of(core * half, half), half)
    turn = 0
    for kind, (own, other) in enumerate([(q_ref, q_other_ref), (do_ref, do_other_ref)]):
        for which, ref in enumerate([own, other]):
            block = 1 - core if which else core
            wide = scr.at[turn % 2]
            wide[...] = ref[:, mine].astype(F32).reshape(tokens * half, dim)
            for h in range(half):
                out_ref[h // group, block, kind, h % group] = wide[pl.ds(h, tokens, stride=half), :].astype(BF16)
            turn += 1


def arrange(place, queries, grad_out, q_other, do_other, key_heads):
    tokens, heads, dim = queries.shape
    half, group = heads // 2, heads // key_heads
    whole = pl.BlockSpec(memory_space=pltpu.VMEM)
    return call(
        functools.partial(arrange_kernel, group),
        "arrange",
        (1,),
        place,
        [in_vmem(x) for x in (queries, grad_out, q_other, do_other)],
        [whole] * 4,
        pltpu.VMEM((key_heads // 2, 2, 2, group, tokens, dim), BF16),
        whole,
        [pltpu.VMEM((2, tokens * half, dim), F32)],
        10**9,
    )


def pack_block(raw, core, block, out_ref, scr):
    tokens, heads, dim = raw.shape
    half = heads // 2
    scr[...] = raw[...].astype(F32).reshape(tokens * heads, dim)
    for h in range(half):
        out_ref[h, block] = scr[pl.ds(core * half + h, tokens, stride=heads), :].astype(BF16)


def fetch_kernel(place_ref, key_ref, *refs):
    count = (len(refs) - 4) // 2
    sources, out_ref, targets = refs[:count], refs[count], refs[count + 1 : 2 * count + 1]
    raw, scr, sems = refs[-3:]
    first = pltpu.make_async_copy(key_ref, raw, sems.at[0])
    first.start()
    copies = [pltpu.make_async_copy(s, t, sems.at[i + 1]) for i, (s, t) in enumerate(zip(sources, targets))]
    for copy in copies:
        copy.start()
    first.wait()
    pack_block(raw, place_ref[0], place_ref[0], out_ref, scr)
    for copy in copies:
        copy.wait()


def fetch(place, keys, arrays):
    tokens, heads, dim = keys.shape
    out = (heads // 2, 2, tokens, dim)
    return call(
        fetch_kernel,
        "fetch",
        (1,),
        place,
        [in_hbm(x) for x in (keys, *arrays)],
        [pl.BlockSpec(memory_space=pltpu.HBM)] * (1 + len(arrays)),
        [pltpu.VMEM(out, BF16)] + [pltpu.VMEM(x.shape, x.dtype) for x in arrays],
        [pl.BlockSpec(memory_space=pltpu.VMEM)] * (1 + len(arrays)),
        [
            pltpu.VMEM(keys.shape, BF16),
            pltpu.VMEM((tokens * heads, dim), F32),
            pltpu.SemaphoreType.DMA((1 + len(arrays),)),
        ],
        10**9,
    )


def pack_other_kernel(place_ref, other_ref, _, out_ref, scr):
    pack_block(other_ref, place_ref[0], 1 - place_ref[0], out_ref, scr)


def pack_other(place, other, packed):
    tokens, heads, dim = other.shape
    whole = pl.BlockSpec(memory_space=pltpu.VMEM)
    return call(
        pack_other_kernel,
        "pack_other",
        (1,),
        place,
        (in_vmem(other), in_vmem(packed)),
        [whole] * 2,
        pltpu.VMEM(packed.shape, BF16),
        whole,
        [pltpu.VMEM((tokens * heads, dim), F32)],
        10**9,
        {2: 0},
    )


def pack_both_kernel(place_ref, own_ref, other_ref, out_ref, scr):
    core = place_ref[0]
    pack_block(own_ref, core, core, out_ref, scr)
    pack_block(other_ref, core, 1 - core, out_ref, scr)


def pack_both(place, own, other):
    tokens, heads, dim = own.shape
    out = (heads // 2, 2, tokens, dim)
    whole = pl.BlockSpec(memory_space=pltpu.VMEM)
    return call(
        pack_both_kernel,
        "pack_both",
        (1,),
        place,
        (in_vmem(own), in_vmem(other)),
        [whole] * 2,
        pltpu.VMEM(out, BF16),
        whole,
        [pltpu.VMEM((tokens * heads, dim), F32)],
        10**9,
    )


def folded(op, x):
    while x.shape[0] > 8:
        half = x.shape[0] // 2
        x = op(x[:half], x[half:])
    reduce = jnp.max if op is jnp.maximum else jnp.sum
    return reduce(x, axis=0, keepdims=True)


def first_allowed(lengths_ref, query_pos, window_start):
    def step(d, carry):
        start, first = carry
        first = jnp.where(query_pos + window_start >= start, start, first)
        return start + lengths_ref[d], first

    zero = jnp.zeros(query_pos.shape, jnp.int32)
    _, first = lax.fori_loop(0, lengths_ref.shape[0], step, (jnp.int32(0), zero))
    return first - window_start


def window_of(pair_refs, scr):
    halo = len(pair_refs) - 1
    for back, ref in enumerate(pair_refs):
        scr[pl.ds(2 * (halo - back), 2)] = ref[0]


def on_diagonal(tokens, copies):
    row = lax.broadcasted_iota(jnp.int32, (tokens, tokens), 0)
    lane = lax.broadcasted_iota(jnp.int32, (tokens, tokens), 1)
    return jnp.concatenate([row] * copies, axis=1), jnp.concatenate([lane] * copies, axis=1)


def store_tiles(ref, e, at, tiles, diagonal):
    tokens, pair = diagonal.shape
    lanes = slice(at, at + pair)
    shared = tiles[0].astype(F32)
    ref[0, e, :tokens, lanes] = jnp.where(diagonal, 0.0, shared).astype(BF16)
    for j, tile in enumerate(tiles[1:], 1):
        ref[0, e, j * tokens : (j + 1) * tokens, lanes] = tile.astype(BF16)
    ref[0, e, -tokens:, lanes] = jnp.where(diagonal, shared, 0.0).astype(BF16)


def prob_kernel(halo, place_ref, lengths_ref, qd_ref, *refs):
    k_refs = refs[: halo + 1]
    p_ref = refs[halo + 1]
    dv_refs = refs[halo + 2 : -3]
    k_scr, acc, bias = refs[-3:]
    _, _, _, group, tokens, dim = qd_ref.shape
    count = 2 * halo + 1
    pair = HEADS_AT_ONCE * tokens
    row, lane = on_diagonal(tokens, HEADS_AT_ONCE)
    diagonal = row <= lane

    @pl.when(pl.program_id(0) == 0)
    def _():
        for e in range(2):
            query_pos = lane[:1] + (2 * halo + e) * tokens
            first = first_allowed(lengths_ref, query_pos, place_ref[1]) - row
            last = (e + count - 1) * tokens
            bias[e, 0] = jnp.where(first <= jnp.where(diagonal, last, e * tokens), 0.0, MASKED)
            for j in range(1, count - 1):
                bias[e, j] = jnp.where(first <= (e + j) * tokens, 0.0, MASKED)

    window_of(k_refs, k_scr)
    for e in range(2):
        k = k_scr[pl.ds(e, count)].reshape(count * tokens, dim)
        q = qd_ref[0, e, 0].reshape(group * tokens, dim)
        do = qd_ref[0, e, 1].reshape(group * tokens, dim)
        for at in range(0, group * tokens, pair):
            s = lax.dot_general(k, q[at : at + pair], NT, preferred_element_type=F32)
            tiles = [s[j * tokens : (j + 1) * tokens] for j in range(count)]
            tiles[0] = jnp.where(diagonal, tiles.pop(), tiles[0])
            tiles = [tile + bias[e, j] for j, tile in enumerate(tiles)]
            top = folded(jnp.maximum, functools.reduce(jnp.maximum, tiles))
            tiles = [jnp.exp2((tile - top) * (dim**-0.5 * LOG2E)) for tile in tiles]
            inv = 1.0 / folded(jnp.add, functools.reduce(jnp.add, tiles))
            store_tiles(p_ref, e, at, [tile * inv for tile in tiles], diagonal)
        keep = (2 * halo - e) * tokens
        dv = jnp.dot(p_ref[0, e, :keep], do, preferred_element_type=F32).reshape(2 * halo - e, tokens, dim)
        if e == 0:
            acc[...] = dv
        else:
            acc[1:] += dv
    for back, ref in zip(range(1, halo + 1), dv_refs):
        ref[0] = acc[pl.ds(2 * (halo - back), 2)].astype(BF16)


def dscore_kernel(halo, place_ref, qd_ref, p_ref, *refs):
    v_refs = refs[: halo + 1]
    ds_ref = refs[halo + 1]
    dk_refs = refs[halo + 2 : -2]
    v_scr, acc = refs[-2:]
    _, _, _, group, tokens, dim = qd_ref.shape
    count = 2 * halo + 1
    pair = HEADS_AT_ONCE * tokens
    window_of(v_refs, v_scr)
    row, lane = on_diagonal(tokens, HEADS_AT_ONCE)
    diagonal = row <= lane
    for e in range(2):
        v = v_scr[pl.ds(e, count)].reshape(count * tokens, dim)
        q = qd_ref[0, e, 0].reshape(group * tokens, dim)
        do = qd_ref[0, e, 1].reshape(group * tokens, dim)
        for at in range(0, group * tokens, pair):
            dp = lax.dot_general(v, do[at : at + pair], NT, preferred_element_type=F32)
            dps = [dp[j * tokens : (j + 1) * tokens] for j in range(count)]
            dps[0] = jnp.where(diagonal, dps.pop(), dps[0])
            ps = [p_ref[0, e, j * tokens : (j + 1) * tokens, at : at + pair] for j in range(count)]
            ps[0] += ps.pop()
            delta = folded(jnp.add, functools.reduce(jnp.add, [p.astype(F32) * dp for p, dp in zip(ps, dps)]))
            store_tiles(ds_ref, e, at, [p * (dp - delta).astype(BF16) for p, dp in zip(ps, dps)], diagonal)
        keep = (2 * halo - e) * tokens
        dk = jnp.dot(ds_ref[0, e, :keep], q, preferred_element_type=F32).reshape(2 * halo - e, tokens, dim)
        if e == 0:
            acc[...] = dk
        else:
            acc[1:] += dk
    for back, ref in zip(range(1, halo + 1), dk_refs):
        ref[0] = (acc[pl.ds(2 * (halo - back), 2)] * dim**-0.5).astype(BF16)


def own_kernel(halo, place_ref, qd_ref, p_ref, ds_ref, *refs):
    k_refs, back_refs = refs[: halo + 1], refs[halo + 1 : 2 * halo + 1]
    dq_ref, *other_refs, dk_ref, dv_ref, k_scr, dq_scr, dv_scr, far_dv = refs[2 * halo + 1 :]
    core, head = place_ref[0], pl.program_id(0)
    _, _, _, group, tokens, dim = qd_ref.shape
    rows = dq_ref.shape[1]
    count = 2 * halo + 1
    scale = dim**-0.5
    window_of(k_refs, k_scr)
    for e in range(2):
        q = qd_ref[0, e, 0].reshape(group * tokens, dim)
        do = qd_ref[0, e, 1].reshape(group * tokens, dim)
        k = k_scr[pl.ds(e, count)].reshape(count * tokens, dim)
        dqt = jnp.dot(k.T, ds_ref[0, e], preferred_element_type=F32) * scale
        for g in range(group):
            dq_scr[e, pl.ds(head * group + g, tokens, stride=rows), :] = dqt[:, g * tokens : (g + 1) * tokens].T
        keep = (2 * halo - e) * tokens
        dk = jnp.dot(ds_ref[0, e, keep:], q, preferred_element_type=F32) * scale
        dv = jnp.dot(p_ref[0, e, keep:], do, preferred_element_type=F32)
        if e == 0:
            dk_ref[0, 0], dv_scr[0] = dk, dv
        else:
            dk_ref[0, 0] += dk[:tokens]
            dv_scr[0] += dv[:tokens]
            dk_ref[0, 1], dv_scr[1] = dk[tokens:], dv[tokens:]
    for ref in back_refs:
        dv_scr[...] += ref[0].astype(F32)
    dv_ref[0] = dv_scr[core].astype(BF16)
    far_dv[pl.ds(pl.multiple_of(head * tokens, tokens), tokens)] = dv_scr[1 - core].astype(BF16)

    @pl.when(head == pl.num_programs(0) - 1)
    def _():
        dq_ref[...] = dq_scr[core].astype(BF16).reshape(dq_ref.shape)
        dq_rows, start = tokens * rows, 0
        for ref in other_refs:
            part = ref.shape[0] * rows
            here = min(part, dq_rows - start)
            ref[: here // rows] = dq_scr[1 - core, start : start + here].astype(BF16).reshape(-1, rows, dim)
            if here < part:
                ref[here // rows :] = far_dv[...].reshape(-1, rows, dim)
            start += part


def sum_kernel(count, place_ref, own_ref, *refs):
    back_refs, (mine_ref, other_ref) = refs[:count], refs[-2:]
    core = place_ref[0]
    for block, ref in [(1 - core, other_ref), (core, mine_ref)]:
        total = own_ref[:, block]
        for back in back_refs:
            total += back[:, block].astype(F32)
        ref[...] = total.astype(BF16)


def summed(place, own, backs, before):
    half, _, tokens, dim = own.shape
    pair_spec = pl.BlockSpec(own.shape, lambda i, place: (0, 0, 0, 0))
    one = (half, tokens, dim)
    return call(
        functools.partial(sum_kernel, len(backs)),
        "sum_dk",
        (1,),
        place,
        (own, *backs, *(in_hbm(x) for x in before)),
        [pair_spec] * (1 + len(backs)) + [pl.BlockSpec(memory_space=pltpu.HBM)] * len(before),
        [jax.ShapeDtypeStruct(one, BF16)] * 2,
        [pl.BlockSpec(one, lambda i, place: (0, 0, 0))] * 2,
        [],
        0,
    )


def merge_half(core, own_ref, other, out_ref, scr):
    rows, heads, dim = out_ref.shape
    half = heads // 2
    skip = other.shape[0] - half * rows
    for h in range(half):
        scr[pl.ds(core * half + h, rows, stride=heads), :] = own_ref[h].astype(F32)
        rest = other[skip + h * rows : skip + (h + 1) * rows]
        scr[pl.ds((1 - core) * half + h, rows, stride=heads), :] = rest.astype(F32)
    out_ref[...] = scr[...].astype(BF16).reshape(rows, heads, dim)


def join_kernel(parts, place_ref, dq_ref, dv_ref, *refs):
    others, (dq_out, dv_out, scr, sems) = refs[:parts], refs[parts:]
    core = place_ref[0]
    tokens, half, dim = dq_ref.shape
    at = pl.multiple_of(core * half, half)
    copies = [pltpu.make_async_copy(dq_ref, dq_out.at[:, pl.ds(at, half)], sems.at[0])]
    at = pl.multiple_of((1 - core) * half, half)
    first = 0
    for i, part in enumerate(others):
        count = min(part.shape[0], tokens - first)
        to = dq_out.at[pl.ds(first, count), pl.ds(at, half)]
        copies.append(pltpu.make_async_copy(part.at[pl.ds(0, count)], to, sems.at[1 + i]))
        first += count
    for copy in copies:
        copy.start()
    merge_half(core, dv_ref, others[-1][...].reshape(-1, dim), dv_out, scr)
    for copy in copies:
        copy.wait()


def join(place, dq, dv, others):
    tokens, half, dim = dq.shape
    out = (tokens, 2 * dv.shape[0], dim)
    vmem = pl.BlockSpec(memory_space=pltpu.VMEM)
    parts = len(others)
    return call(
        functools.partial(join_kernel, parts),
        "join",
        (1,),
        place,
        [in_vmem(x) for x in (dq, dv, *others)],
        [vmem] * (2 + parts),
        [jax.ShapeDtypeStruct((tokens, 2 * half, dim), BF16), jax.ShapeDtypeStruct(out, BF16)],
        [pl.BlockSpec(memory_space=pl.ANY), pl.BlockSpec(out, lambda i, place: (0, 0, 0))],
        [pltpu.VMEM((tokens * out[1], dim), F32), pltpu.SemaphoreType.DMA((1 + parts,))],
        0,
    )


def merge_kernel(place_ref, own_ref, other_ref, out_ref, scr):
    merge_half(place_ref[0], own_ref, other_ref[...].reshape(-1, own_ref.shape[2]), out_ref, scr)


def merge(place, own, other, name):
    half, tokens, dim = own.shape
    out = (tokens, 2 * half, dim)
    vmem = pl.BlockSpec(memory_space=pltpu.VMEM)
    return call(
        merge_kernel,
        name,
        (1,),
        place,
        (in_vmem(own), in_vmem(other)),
        [vmem] * 2,
        jax.ShapeDtypeStruct(out, BF16),
        pl.BlockSpec(out, lambda i, place: (0, 0, 0)),
        [pltpu.VMEM((tokens * 2 * half, dim), F32)],
        0,
    )


def local(queries, keys, values, grad_out, doc_lengths):
    uly_count = lax.axis_size("uly")
    device_count = lax.axis_size("ctx") * uly_count
    halo = uly_count // 2
    device = lax.axis_index("ctx") * uly_count + lax.axis_index("uly")
    core = device % 2
    tokens, heads, dim = queries.shape
    key_heads = keys.shape[1]
    group = heads // key_heads
    half = key_heads // 2
    window, count = 2 * halo + 2, 2 * halo + 1
    place = jnp.stack([core, (device // 2 - halo) * (2 * tokens)]).astype(jnp.int32)

    far_first = range(halo, 0, -1)
    k_other = swapped(keys, device_count)
    k_mine, v_mine = fetch(place, keys, (values,))
    k_own = pack_other(place, k_other, k_mine)
    k_own, queries, grad_out, v_mine = lax.optimization_barrier((k_own, queries, grad_out, v_mine))
    q_other, do_other, v_other = (swapped(x, device_count) for x in (queries, grad_out, v_mine))
    qd = arrange(place, queries, grad_out, q_other, do_other, key_heads)
    qd, v_mine, v_other = lax.optimization_barrier((qd, v_mine, v_other))
    v_own = pack_both(place, v_mine, v_other)

    def halo_of(own, ring=False):
        received = {back: moved(own, device_count, 2 * back, ring) for back in far_first}
        return [own] + [received[back] for back in range(1, halo + 1)]

    def sent_back(partials):
        return [moved(partials[back - 1], device_count, -2 * back) for back in far_first]

    def per_head(*shape):
        return pl.BlockSpec((1,) + shape, lambda h, *_: (h,) + (0,) * len(shape))

    qd_spec = per_head(2, 2, group, tokens, dim)
    p_spec = per_head(2, count * tokens, group * tokens)
    p_shape = pltpu.VMEM((half, 2, count * tokens, group * tokens), BF16)
    pair_spec = per_head(2, tokens, dim)
    pair = (half, 2, tokens, dim)
    one_spec = per_head(tokens, dim)
    one_shape = jax.ShapeDtypeStruct((half, tokens, dim), BF16)
    dq_shape = jax.ShapeDtypeStruct((tokens, heads // 2, dim), BF16)
    dq_spec = pl.BlockSpec(dq_shape.shape, lambda h, *_: (0, 0, 0))
    far_rows = tokens + half * tokens // (heads // 2)
    step = (far_rows // 3 + 7) // 8 * 8
    parts = [
        jax.ShapeDtypeStruct((rows, heads // 2, dim), BF16) for rows in (step, step, far_rows - 2 * step)
    ]
    part_specs = [pl.BlockSpec(part.shape, lambda h, *_: (0, 0, 0)) for part in parts]
    run = pltpu.VMEM((window, tokens, dim), BF16)
    acc = pltpu.VMEM((2 * halo, tokens, dim), F32)
    product = 2 * half * 2 * count * tokens * group * tokens * dim

    k_pairs = halo_of(k_own, ring=True)
    v_pairs = halo_of(v_own)
    prob, *dv_halo = call(
        functools.partial(prob_kernel, halo),
        "prob",
        (half,),
        (place, doc_lengths),
        (in_vmem(qd), *k_pairs),
        [qd_spec] + [pair_spec] * (halo + 1),
        [p_shape] + [jax.ShapeDtypeStruct(pair, BF16)] * halo,
        [p_spec] + [pair_spec] * halo,
        [run, acc, pltpu.VMEM((2, count - 1, tokens, HEADS_AT_ONCE * tokens), F32)],
        4 * product,
    )
    dv_back = sent_back(dv_halo)
    dscore, *dk_halo = call(
        functools.partial(dscore_kernel, halo),
        "dscore",
        (half,),
        place,
        (in_vmem(qd), in_vmem(prob), *v_pairs),
        [qd_spec, p_spec] + [pair_spec] * (halo + 1),
        [p_shape] + [jax.ShapeDtypeStruct(pair, BF16)] * halo,
        [p_spec] + [pair_spec] * halo,
        [run, acc],
        4 * product,
    )
    dk_back = sent_back(dk_halo)
    dq, *others, dk_own, dv = call(
        functools.partial(own_kernel, halo),
        "own",
        (half,),
        place,
        (in_vmem(qd), in_vmem(prob), in_vmem(dscore), *k_pairs, *dv_back),
        [qd_spec, p_spec, p_spec] + [pair_spec] * (2 * halo + 1),
        [dq_shape, *parts, jax.ShapeDtypeStruct(pair, F32), one_shape],
        [dq_spec, *part_specs, pair_spec, one_spec],
        [
            run,
            pltpu.VMEM((2, tokens * heads // 2, dim), F32),
            pltpu.VMEM((2, tokens, dim), F32),
            pltpu.VMEM((half * tokens, dim), BF16),
        ],
        0,
    )
    others = [swapped(part, device_count) for part in others]
    grad_queries, grad_values = join(place, dq, dv, others)
    dk, dk_other = summed(place, dk_own, dk_back, (grad_queries, grad_values))
    grad_keys = merge(place, dk, swapped(dk_other, device_count), "merge_dk")
    return grad_queries, grad_keys, grad_values


def solution(mesh):
    spec = P(AXES, None, None)
    return jax.shard_map(
        local, mesh=mesh, in_specs=(spec,) * 4 + (P(),), out_specs=(spec,) * 3, check_vma=False
    )
```

```python
import functools

import jax
import jax.numpy as jnp
from jax import lax
from jax.experimental import pallas as pl
from jax.experimental.pallas import tpu as pltpu
from jax.sharding import PartitionSpec as P

AXES = ("ctx", "uly")
MASKED = -1e30
LOG2E = 1.4426950408889634
HEADS_AT_ONCE = 2
BF16, F32 = jnp.bfloat16, jnp.float32
NT = (((1,), (1,)), ((), ()))
VMEM_BYTES = 16 * 2**20


def moved(array, device_count, by, ring):
    pairs = [(d, d + by) for d in range(device_count)]
    if ring:
        return lax.ppermute(array, AXES, [(d, to % device_count) for d, to in pairs])
    return lax.ppermute(array, AXES, [(d, to) for d, to in pairs if 0 <= to < device_count])


def swapped(array, device_count):
    return lax.ppermute(array, AXES, [(d, d ^ 1) for d in range(device_count)])


def in_vmem(array):
    return pltpu.with_memory_space_constraint(array, pltpu.VMEM)


def in_hbm(array):
    return pltpu.with_memory_space_constraint(array, pltpu.HBM)


def call(kernel, name, grid, place, inputs, in_specs, outs, out_specs, scratch, flops, aliases={}):
    scalars = place if isinstance(place, tuple) else (place,)
    return pl.pallas_call(
        kernel,
        out_shape=outs,
        grid_spec=pltpu.PrefetchScalarGridSpec(
            num_scalar_prefetch=len(scalars),
            grid=grid,
            in_specs=in_specs,
            out_specs=out_specs,
            scratch_shapes=scratch,
        ),
        compiler_params=pltpu.CompilerParams(vmem_limit_bytes=VMEM_BYTES),
        cost_estimate=pl.CostEstimate(flops=flops, bytes_accessed=0, transcendentals=0),
        input_output_aliases=aliases,
        name=name,
    )(*scalars, *inputs)


def arrange_kernel(group, place_ref, q_ref, do_ref, q_other_ref, do_other_ref, out_ref, scr):
    core = place_ref[0]
    tokens, heads, dim = q_ref.shape
    half = heads // 2
    mine = pl.ds(pl.multiple_of(core * half, half), half)
    turn = 0
    for kind, (own, other) in enumerate([(q_ref, q_other_ref), (do_ref, do_other_ref)]):
        for which, ref in enumerate([own, other]):
            block = 1 - core if which else core
            wide = scr.at[turn % 2]
            wide[...] = ref[:, mine].astype(F32).reshape(tokens * half, dim)
            for h in range(half):
                out_ref[h // group, block, kind, h % group] = wide[pl.ds(h, tokens, stride=half), :].astype(BF16)
            turn += 1


def arrange(place, queries, grad_out, q_other, do_other, key_heads):
    tokens, heads, dim = queries.shape
    half, group = heads // 2, heads // key_heads
    whole = pl.BlockSpec(memory_space=pltpu.VMEM)
    return call(
        functools.partial(arrange_kernel, group),
        "arrange",
        (1,),
        place,
        [in_vmem(x) for x in (queries, grad_out, q_other, do_other)],
        [whole] * 4,
        pltpu.VMEM((key_heads // 2, 2, 2, group, tokens, dim), BF16),
        whole,
        [pltpu.VMEM((2, tokens * half, dim), F32)],
        10**9,
    )


def pack_block(raw, core, block, out_ref, scr):
    tokens, heads, dim = raw.shape
    half = heads // 2
    scr[...] = raw[...].astype(F32).reshape(tokens * heads, dim)
    for h in range(half):
        out_ref[h, block] = scr[pl.ds(core * half + h, tokens, stride=heads), :].astype(BF16)


def fetch_kernel(place_ref, key_ref, *refs):
    count = (len(refs) - 4) // 2
    sources, out_ref, targets = refs[:count], refs[count], refs[count + 1 : 2 * count + 1]
    raw, scr, sems = refs[-3:]
    first = pltpu.make_async_copy(key_ref, raw, sems.at[0])
    first.start()
    copies = [pltpu.make_async_copy(s, t, sems.at[i + 1]) for i, (s, t) in enumerate(zip(sources, targets))]
    for copy in copies:
        copy.start()
    first.wait()
    pack_block(raw, place_ref[0], place_ref[0], out_ref, scr)
    for copy in copies:
        copy.wait()


def fetch(place, keys, arrays):
    tokens, heads, dim = keys.shape
    out = (heads // 2, 2, tokens, dim)
    return call(
        fetch_kernel,
        "fetch",
        (1,),
        place,
        [in_hbm(x) for x in (keys, *arrays)],
        [pl.BlockSpec(memory_space=pltpu.HBM)] * (1 + len(arrays)),
        [pltpu.VMEM(out, BF16)] + [pltpu.VMEM(x.shape, x.dtype) for x in arrays],
        [pl.BlockSpec(memory_space=pltpu.VMEM)] * (1 + len(arrays)),
        [
            pltpu.VMEM(keys.shape, BF16),
            pltpu.VMEM((tokens * heads, dim), F32),
            pltpu.SemaphoreType.DMA((1 + len(arrays),)),
        ],
        10**9,
    )


def pack_other_kernel(place_ref, other_ref, _, out_ref, scr):
    pack_block(other_ref, place_ref[0], 1 - place_ref[0], out_ref, scr)


def pack_other(place, other, packed):
    tokens, heads, dim = other.shape
    whole = pl.BlockSpec(memory_space=pltpu.VMEM)
    return call(
        pack_other_kernel,
        "pack_other",
        (1,),
        place,
        (in_vmem(other), in_vmem(packed)),
        [whole] * 2,
        pltpu.VMEM(packed.shape, BF16),
        whole,
        [pltpu.VMEM((tokens * heads, dim), F32)],
        10**9,
        {2: 0},
    )


def pack_both_kernel(place_ref, own_ref, other_ref, out_ref, scr):
    core = place_ref[0]
    pack_block(own_ref, core, core, out_ref, scr)
    pack_block(other_ref, core, 1 - core, out_ref, scr)


def pack_both(place, own, other):
    tokens, heads, dim = own.shape
    out = (heads // 2, 2, tokens, dim)
    whole = pl.BlockSpec(memory_space=pltpu.VMEM)
    return call(
        pack_both_kernel,
        "pack_both",
        (1,),
        place,
        (in_vmem(own), in_vmem(other)),
        [whole] * 2,
        pltpu.VMEM(out, BF16),
        whole,
        [pltpu.VMEM((tokens * heads, dim), F32)],
        10**9,
    )


def folded(op, x):
    while x.shape[0] > 8:
        half = x.shape[0] // 2
        x = op(x[:half], x[half:])
    reduce = jnp.max if op is jnp.maximum else jnp.sum
    return reduce(x, axis=0, keepdims=True)


def first_allowed(lengths_ref, query_pos, window_start):
    def step(d, carry):
        start, first = carry
        first = jnp.where(query_pos + window_start >= start, start, first)
        return start + lengths_ref[d], first

    zero = jnp.zeros(query_pos.shape, jnp.int32)
    _, first = lax.fori_loop(0, lengths_ref.shape[0], step, (jnp.int32(0), zero))
    return first - window_start


def window_of(pair_refs, scr):
    halo = len(pair_refs) - 1
    for back, ref in enumerate(pair_refs):
        scr[pl.ds(2 * (halo - back), 2)] = ref[0]


def on_diagonal(tokens, copies):
    row = lax.broadcasted_iota(jnp.int32, (tokens, tokens), 0)
    lane = lax.broadcasted_iota(jnp.int32, (tokens, tokens), 1)
    return jnp.concatenate([row] * copies, axis=1), jnp.concatenate([lane] * copies, axis=1)


def store_tiles(ref, e, at, tiles, diagonal):
    tokens, pair = diagonal.shape
    lanes = slice(at, at + pair)
    shared = tiles[0].astype(F32)
    ref[0, e, :tokens, lanes] = jnp.where(diagonal, 0.0, shared).astype(BF16)
    for j, tile in enumerate(tiles[1:], 1):
        ref[0, e, j * tokens : (j + 1) * tokens, lanes] = tile.astype(BF16)
    ref[0, e, -tokens:, lanes] = jnp.where(diagonal, shared, 0.0).astype(BF16)


def prob_kernel(halo, place_ref, lengths_ref, qd_ref, *refs):
    k_refs = refs[: halo + 1]
    p_ref = refs[halo + 1]
    dv_refs = refs[halo + 2 : -3]
    k_scr, acc, bias = refs[-3:]
    _, _, _, group, tokens, dim = qd_ref.shape
    count = 2 * halo + 1
    pair = HEADS_AT_ONCE * tokens
    row, lane = on_diagonal(tokens, HEADS_AT_ONCE)
    diagonal = row <= lane

    @pl.when(pl.program_id(0) == 0)
    def _():
        for e in range(2):
            query_pos = lane[:1] + (2 * halo + e) * tokens
            first = first_allowed(lengths_ref, query_pos, place_ref[1]) - row
            last = (e + count - 1) * tokens
            bias[e, 0] = jnp.where(first <= jnp.where(diagonal, last, e * tokens), 0.0, MASKED)
            for j in range(1, count - 1):
                bias[e, j] = jnp.where(first <= (e + j) * tokens, 0.0, MASKED)

    window_of(k_refs, k_scr)
    for e in range(2):
        k = k_scr[pl.ds(e, count)].reshape(count * tokens, dim)
        q = qd_ref[0, e, 0].reshape(group * tokens, dim)
        do = qd_ref[0, e, 1].reshape(group * tokens, dim)
        for at in range(0, group * tokens, pair):
            s = lax.dot_general(k, q[at : at + pair], NT, preferred_element_type=F32)
            tiles = [s[j * tokens : (j + 1) * tokens] for j in range(count)]
            tiles[0] = jnp.where(diagonal, tiles.pop(), tiles[0])
            tiles = [tile + bias[e, j] for j, tile in enumerate(tiles)]
            top = folded(jnp.maximum, functools.reduce(jnp.maximum, tiles))
            tiles = [jnp.exp2((tile - top) * (dim**-0.5 * LOG2E)) for tile in tiles]
            inv = 1.0 / folded(jnp.add, functools.reduce(jnp.add, tiles))
            store_tiles(p_ref, e, at, [tile * inv for tile in tiles], diagonal)
        keep = (2 * halo - e) * tokens
        dv = jnp.dot(p_ref[0, e, :keep], do, preferred_element_type=F32).reshape(2 * halo - e, tokens, dim)
        if e == 0:
            acc[...] = dv
        else:
            acc[1:] += dv
    for back, ref in zip(range(1, halo + 1), dv_refs):
        ref[0] = acc[pl.ds(2 * (halo - back), 2)].astype(BF16)


def dscore_kernel(halo, place_ref, qd_ref, p_ref, *refs):
    v_refs = refs[: halo + 1]
    ds_ref = refs[halo + 1]
    dk_refs = refs[halo + 2 : -2]
    v_scr, acc = refs[-2:]
    _, _, _, group, tokens, dim = qd_ref.shape
    count = 2 * halo + 1
    pair = HEADS_AT_ONCE * tokens
    window_of(v_refs, v_scr)
    row, lane = on_diagonal(tokens, HEADS_AT_ONCE)
    diagonal = row <= lane
    for e in range(2):
        v = v_scr[pl.ds(e, count)].reshape(count * tokens, dim)
        q = qd_ref[0, e, 0].reshape(group * tokens, dim)
        do = qd_ref[0, e, 1].reshape(group * tokens, dim)
        for at in range(0, group * tokens, pair):
            dp = lax.dot_general(v, do[at : at + pair], NT, preferred_element_type=F32)
            dps = [dp[j * tokens : (j + 1) * tokens] for j in range(count)]
            dps[0] = jnp.where(diagonal, dps.pop(), dps[0])
            ps = [p_ref[0, e, j * tokens : (j + 1) * tokens, at : at + pair] for j in range(count)]
            ps[0] += ps.pop()
            delta = folded(jnp.add, functools.reduce(jnp.add, [p.astype(F32) * dp for p, dp in zip(ps, dps)]))
            store_tiles(ds_ref, e, at, [p * (dp - delta).astype(BF16) for p, dp in zip(ps, dps)], diagonal)
        keep = (2 * halo - e) * tokens
        dk = jnp.dot(ds_ref[0, e, :keep], q, preferred_element_type=F32).reshape(2 * halo - e, tokens, dim)
        if e == 0:
            acc[...] = dk
        else:
            acc[1:] += dk
    for back, ref in zip(range(1, halo + 1), dk_refs):
        ref[0] = (acc[pl.ds(2 * (halo - back), 2)] * dim**-0.5).astype(BF16)


def own_kernel(halo, place_ref, qd_ref, p_ref, ds_ref, *refs):
    k_refs, back_refs = refs[: halo + 1], refs[halo + 1 : 2 * halo + 1]
    dq_ref, *other_refs, dk_ref, dv_ref, k_scr, dq_scr, dv_scr, far_dv = refs[2 * halo + 1 :]
    core, head = place_ref[0], pl.program_id(0)
    _, _, _, group, tokens, dim = qd_ref.shape
    rows = dq_ref.shape[1]
    count = 2 * halo + 1
    scale = dim**-0.5
    window_of(k_refs, k_scr)
    for e in range(2):
        q = qd_ref[0, e, 0].reshape(group * tokens, dim)
        do = qd_ref[0, e, 1].reshape(group * tokens, dim)
        k = k_scr[pl.ds(e, count)].reshape(count * tokens, dim)
        dqt = jnp.dot(k.T, ds_ref[0, e], preferred_element_type=F32) * scale
        for g in range(group):
            dq_scr[e, pl.ds(head * group + g, tokens, stride=rows), :] = dqt[:, g * tokens : (g + 1) * tokens].T
        keep = (2 * halo - e) * tokens
        dk = jnp.dot(ds_ref[0, e, keep:], q, preferred_element_type=F32) * scale
        dv = jnp.dot(p_ref[0, e, keep:], do, preferred_element_type=F32)
        if e == 0:
            dk_ref[0, 0], dv_scr[0] = dk, dv
        else:
            dk_ref[0, 0] += dk[:tokens]
            dv_scr[0] += dv[:tokens]
            dk_ref[0, 1], dv_scr[1] = dk[tokens:], dv[tokens:]
    for ref in back_refs:
        dv_scr[...] += ref[0].astype(F32)
    dv_ref[0] = dv_scr[core].astype(BF16)
    far_dv[pl.ds(pl.multiple_of(head * tokens, tokens), tokens)] = dv_scr[1 - core].astype(BF16)

    @pl.when(head == pl.num_programs(0) - 1)
    def _():
        dq_ref[...] = dq_scr[core].astype(BF16).reshape(dq_ref.shape)
        dq_rows, start = tokens * rows, 0
        for ref in other_refs:
            part = ref.shape[0] * rows
            here = min(part, dq_rows - start)
            ref[: here // rows] = dq_scr[1 - core, start : start + here].astype(BF16).reshape(-1, rows, dim)
            if here < part:
                ref[here // rows :] = far_dv[...].reshape(-1, rows, dim)
            start += part


def sum_kernel(count, place_ref, own_ref, *refs):
    back_refs, (mine_ref, other_ref) = refs[:count], refs[-2:]
    core = place_ref[0]
    for block, ref in [(1 - core, other_ref), (core, mine_ref)]:
        total = own_ref[:, block]
        for back in back_refs:
            total += back[:, block].astype(F32)
        ref[...] = total.astype(BF16)


def summed(place, own, backs, before):
    half, _, tokens, dim = own.shape
    pair_spec = pl.BlockSpec(own.shape, lambda i, place: (0, 0, 0, 0))
    one = (half, tokens, dim)
    return call(
        functools.partial(sum_kernel, len(backs)),
        "sum_dk",
        (1,),
        place,
        (own, *backs, *(in_hbm(x) for x in before)),
        [pair_spec] * (1 + len(backs)) + [pl.BlockSpec(memory_space=pltpu.HBM)] * len(before),
        [jax.ShapeDtypeStruct(one, BF16)] * 2,
        [pl.BlockSpec(one, lambda i, place: (0, 0, 0))] * 2,
        [],
        0,
    )


def merge_half(core, own_ref, other, out_ref, scr):
    rows, heads, dim = out_ref.shape
    half = heads // 2
    skip = other.shape[0] - half * rows
    for h in range(half):
        scr[pl.ds(core * half + h, rows, stride=heads), :] = own_ref[h].astype(F32)
        rest = other[skip + h * rows : skip + (h + 1) * rows]
        scr[pl.ds((1 - core) * half + h, rows, stride=heads), :] = rest.astype(F32)
    out_ref[...] = scr[...].astype(BF16).reshape(rows, heads, dim)


def join_kernel(parts, place_ref, dq_ref, dv_ref, *refs):
    others, (dq_out, dv_out, scr, sems) = refs[:parts], refs[parts:]
    core = place_ref[0]
    tokens, half, dim = dq_ref.shape
    at = pl.multiple_of(core * half, half)
    copies = [pltpu.make_async_copy(dq_ref, dq_out.at[:, pl.ds(at, half)], sems.at[0])]
    at = pl.multiple_of((1 - core) * half, half)
    first = 0
    for i, part in enumerate(others):
        count = min(part.shape[0], tokens - first)
        to = dq_out.at[pl.ds(first, count), pl.ds(at, half)]
        copies.append(pltpu.make_async_copy(part.at[pl.ds(0, count)], to, sems.at[1 + i]))
        first += count
    for copy in copies:
        copy.start()
    merge_half(core, dv_ref, others[-1][...].reshape(-1, dim), dv_out, scr)
    for copy in copies:
        copy.wait()


def join(place, dq, dv, others):
    tokens, half, dim = dq.shape
    out = (tokens, 2 * dv.shape[0], dim)
    vmem = pl.BlockSpec(memory_space=pltpu.VMEM)
    parts = len(others)
    return call(
        functools.partial(join_kernel, parts),
        "join",
        (1,),
        place,
        [in_vmem(x) for x in (dq, dv, *others)],
        [vmem] * (2 + parts),
        [jax.ShapeDtypeStruct((tokens, 2 * half, dim), BF16), jax.ShapeDtypeStruct(out, BF16)],
        [pl.BlockSpec(memory_space=pl.ANY), pl.BlockSpec(out, lambda i, place: (0, 0, 0))],
        [pltpu.VMEM((tokens * out[1], dim), F32), pltpu.SemaphoreType.DMA((1 + parts,))],
        0,
    )


def merge_kernel(place_ref, own_ref, other_ref, out_ref, scr):
    merge_half(place_ref[0], own_ref, other_ref[...].reshape(-1, own_ref.shape[2]), out_ref, scr)


def merge(place, own, other, name):
    half, tokens, dim = own.shape
    out = (tokens, 2 * half, dim)
    vmem = pl.BlockSpec(memory_space=pltpu.VMEM)
    return call(
        merge_kernel,
        name,
        (1,),
        place,
        (in_vmem(own), in_vmem(other)),
        [vmem] * 2,
        jax.ShapeDtypeStruct(out, BF16),
        pl.BlockSpec(out, lambda i, place: (0, 0, 0)),
        [pltpu.VMEM((tokens * 2 * half, dim), F32)],
        0,
    )


def local(queries, keys, values, grad_out, doc_lengths):
    uly_count = lax.axis_size("uly")
    device_count = lax.axis_size("ctx") * uly_count
    halo = uly_count // 2
    device = lax.axis_index("ctx") * uly_count + lax.axis_index("uly")
    core = device % 2
    tokens, heads, dim = queries.shape
    key_heads = keys.shape[1]
    group = heads // key_heads
    half = key_heads // 2
    window, count = 2 * halo + 2, 2 * halo + 1
    place = jnp.stack([core, (device // 2 - halo) * (2 * tokens)]).astype(jnp.int32)

    far_first = range(halo, 0, -1)
    k_other = swapped(keys, device_count)
    k_mine, v_mine = fetch(place, keys, (values,))
    k_own = pack_other(place, k_other, k_mine)
    k_own, queries, grad_out, v_mine = lax.optimization_barrier((k_own, queries, grad_out, v_mine))
    q_other, do_other, v_other = (swapped(x, device_count) for x in (queries, grad_out, v_mine))
    qd = arrange(place, queries, grad_out, q_other, do_other, key_heads)
    qd, v_mine, v_other = lax.optimization_barrier((qd, v_mine, v_other))
    v_own = pack_both(place, v_mine, v_other)

    def halo_of(own, ring):
        received = {back: moved(own, device_count, 2 * back, ring) for back in far_first}
        return [own] + [received[back] for back in range(1, halo + 1)]

    def sent_back(partials, ring):
        return [moved(partials[back - 1], device_count, -2 * back, ring) for back in far_first]

    def per_head(*shape):
        return pl.BlockSpec((1,) + shape, lambda h, *_: (h,) + (0,) * len(shape))

    qd_spec = per_head(2, 2, group, tokens, dim)
    p_spec = per_head(2, count * tokens, group * tokens)
    p_shape = pltpu.VMEM((half, 2, count * tokens, group * tokens), BF16)
    pair_spec = per_head(2, tokens, dim)
    pair = (half, 2, tokens, dim)
    one_spec = per_head(tokens, dim)
    one_shape = jax.ShapeDtypeStruct((half, tokens, dim), BF16)
    dq_shape = jax.ShapeDtypeStruct((tokens, heads // 2, dim), BF16)
    dq_spec = pl.BlockSpec(dq_shape.shape, lambda h, *_: (0, 0, 0))
    far_rows = tokens + half * tokens // (heads // 2)
    step = (far_rows // 3 + 7) // 8 * 8
    parts = [
        jax.ShapeDtypeStruct((rows, heads // 2, dim), BF16) for rows in (step, step, far_rows - 2 * step)
    ]
    part_specs = [pl.BlockSpec(part.shape, lambda h, *_: (0, 0, 0)) for part in parts]
    run = pltpu.VMEM((window, tokens, dim), BF16)
    acc = pltpu.VMEM((2 * halo, tokens, dim), F32)
    product = 2 * half * 2 * count * tokens * group * tokens * dim

    k_pairs = halo_of(k_own, ring=True)
    v_pairs = halo_of(v_own, ring=False)
    prob, *dv_halo = call(
        functools.partial(prob_kernel, halo),
        "prob",
        (half,),
        (place, doc_lengths),
        (in_vmem(qd), *k_pairs),
        [qd_spec] + [pair_spec] * (halo + 1),
        [p_shape] + [jax.ShapeDtypeStruct(pair, BF16)] * halo,
        [p_spec] + [pair_spec] * halo,
        [run, acc, pltpu.VMEM((2, count - 1, tokens, HEADS_AT_ONCE * tokens), F32)],
        4 * product,
    )
    dv_back = sent_back(dv_halo, ring=False)
    dscore, *dk_halo = call(
        functools.partial(dscore_kernel, halo),
        "dscore",
        (half,),
        place,
        (in_vmem(qd), in_vmem(prob), *v_pairs),
        [qd_spec, p_spec] + [pair_spec] * (halo + 1),
        [p_shape] + [jax.ShapeDtypeStruct(pair, BF16)] * halo,
        [p_spec] + [pair_spec] * halo,
        [run, acc],
        4 * product,
    )
    dk_back = sent_back(dk_halo, ring=True)
    dq, *others, dk_own, dv = call(
        functools.partial(own_kernel, halo),
        "own",
        (half,),
        place,
        (in_vmem(qd), in_vmem(prob), in_vmem(dscore), *k_pairs, *dv_back),
        [qd_spec, p_spec, p_spec] + [pair_spec] * (2 * halo + 1),
        [dq_shape, *parts, jax.ShapeDtypeStruct(pair, F32), one_shape],
        [dq_spec, *part_specs, pair_spec, one_spec],
        [
            run,
            pltpu.VMEM((2, tokens * heads // 2, dim), F32),
            pltpu.VMEM((2, tokens, dim), F32),
            pltpu.VMEM((half * tokens, dim), BF16),
        ],
        0,
    )
    others = [swapped(part, device_count) for part in others]
    grad_queries, grad_values = join(place, dq, dv, others)
    dk, dk_other = summed(place, dk_own, dk_back, (grad_queries, grad_values))
    grad_keys = merge(place, dk, swapped(dk_other, device_count), "merge_dk")
    return grad_queries, grad_keys, grad_values


def solution(mesh):
    spec = P(AXES, None, None)
    return jax.shard_map(
        local, mesh=mesh, in_specs=(spec,) * 4 + (P(),), out_specs=(spec,) * 3, check_vma=False
    )
```

```python
import functools

import jax
import jax.numpy as jnp
from jax import lax
from jax.experimental import pallas as pl
from jax.experimental.pallas import tpu as pltpu
from jax.sharding import PartitionSpec as P

AXES = ("ctx", "uly")
MASKED = -1e30
LOG2E = 1.4426950408889634
HEADS_AT_ONCE = 2
BF16, F32 = jnp.bfloat16, jnp.float32
NT = (((1,), (1,)), ((), ()))
VMEM_BYTES = 16 * 2**20


def moved(array, device_count, by, ring):
    pairs = [(d, d + by) for d in range(device_count)]
    if ring:
        return lax.ppermute(array, AXES, [(d, to % device_count) for d, to in pairs])
    return lax.ppermute(array, AXES, [(d, to) for d, to in pairs if 0 <= to < device_count])


def swapped(array, device_count):
    return lax.ppermute(array, AXES, [(d, d ^ 1) for d in range(device_count)])


def in_vmem(array):
    return pltpu.with_memory_space_constraint(array, pltpu.VMEM)


def in_hbm(array):
    return pltpu.with_memory_space_constraint(array, pltpu.HBM)


def call(kernel, name, grid, place, inputs, in_specs, outs, out_specs, scratch, flops, aliases={}):
    scalars = place if isinstance(place, tuple) else (place,)
    return pl.pallas_call(
        kernel,
        out_shape=outs,
        grid_spec=pltpu.PrefetchScalarGridSpec(
            num_scalar_prefetch=len(scalars),
            grid=grid,
            in_specs=in_specs,
            out_specs=out_specs,
            scratch_shapes=scratch,
        ),
        compiler_params=pltpu.CompilerParams(vmem_limit_bytes=VMEM_BYTES),
        cost_estimate=pl.CostEstimate(flops=flops, bytes_accessed=0, transcendentals=0),
        input_output_aliases=aliases,
        name=name,
    )(*scalars, *inputs)


def arrange_kernel(group, place_ref, q_ref, do_ref, q_other_ref, do_other_ref, out_ref, scr):
    core = place_ref[0]
    tokens, heads, dim = q_ref.shape
    half = heads // 2
    mine = pl.ds(pl.multiple_of(core * half, half), half)
    turn = 0
    for kind, (own, other) in enumerate([(q_ref, q_other_ref), (do_ref, do_other_ref)]):
        for which, ref in enumerate([own, other]):
            block = 1 - core if which else core
            wide = scr.at[turn % 2]
            wide[...] = ref[:, mine].astype(F32).reshape(tokens * half, dim)
            for h in range(half):
                out_ref[h // group, block, kind, h % group] = wide[pl.ds(h, tokens, stride=half), :].astype(BF16)
            turn += 1


def arrange(place, queries, grad_out, q_other, do_other, key_heads):
    tokens, heads, dim = queries.shape
    half, group = heads // 2, heads // key_heads
    whole = pl.BlockSpec(memory_space=pltpu.VMEM)
    return call(
        functools.partial(arrange_kernel, group),
        "arrange",
        (1,),
        place,
        [in_vmem(x) for x in (queries, grad_out, q_other, do_other)],
        [whole] * 4,
        pltpu.VMEM((key_heads // 2, 2, 2, group, tokens, dim), BF16),
        whole,
        [pltpu.VMEM((2, tokens * half, dim), F32)],
        10**9,
    )


def pack_block(raw, core, block, out_ref, scr):
    tokens, heads, dim = raw.shape
    half = heads // 2
    scr[...] = raw[...].astype(F32).reshape(tokens * heads, dim)
    for h in range(half):
        out_ref[h, block] = scr[pl.ds(core * half + h, tokens, stride=heads), :].astype(BF16)


def fetch_kernel(place_ref, key_ref, *refs):
    count = (len(refs) - 4) // 2
    sources, out_ref, targets = refs[:count], refs[count], refs[count + 1 : 2 * count + 1]
    raw, scr, sems = refs[-3:]
    first = pltpu.make_async_copy(key_ref, raw, sems.at[0])
    first.start()
    copies = [pltpu.make_async_copy(s, t, sems.at[i + 1]) for i, (s, t) in enumerate(zip(sources, targets))]
    for copy in copies:
        copy.start()
    first.wait()
    pack_block(raw, place_ref[0], place_ref[0], out_ref, scr)
    for copy in copies:
        copy.wait()


def fetch(place, keys, arrays):
    tokens, heads, dim = keys.shape
    out = (heads // 2, 2, tokens, dim)
    return call(
        fetch_kernel,
        "fetch",
        (1,),
        place,
        [in_hbm(x) for x in (keys, *arrays)],
        [pl.BlockSpec(memory_space=pltpu.HBM)] * (1 + len(arrays)),
        [pltpu.VMEM(out, BF16)] + [pltpu.VMEM(x.shape, x.dtype) for x in arrays],
        [pl.BlockSpec(memory_space=pltpu.VMEM)] * (1 + len(arrays)),
        [
            pltpu.VMEM(keys.shape, BF16),
            pltpu.VMEM((tokens * heads, dim), F32),
            pltpu.SemaphoreType.DMA((1 + len(arrays),)),
        ],
        10**9,
    )


def pack_other_kernel(place_ref, other_ref, _, out_ref, scr):
    pack_block(other_ref, place_ref[0], 1 - place_ref[0], out_ref, scr)


def pack_other(place, other, packed):
    tokens, heads, dim = other.shape
    whole = pl.BlockSpec(memory_space=pltpu.VMEM)
    return call(
        pack_other_kernel,
        "pack_other",
        (1,),
        place,
        (in_vmem(other), in_vmem(packed)),
        [whole] * 2,
        pltpu.VMEM(packed.shape, BF16),
        whole,
        [pltpu.VMEM((tokens * heads, dim), F32)],
        10**9,
        {2: 0},
    )


def pack_both_kernel(place_ref, own_ref, other_ref, out_ref, scr):
    core = place_ref[0]
    pack_block(own_ref, core, core, out_ref, scr)
    pack_block(other_ref, core, 1 - core, out_ref, scr)


def pack_both(place, own, other):
    tokens, heads, dim = own.shape
    out = (heads // 2, 2, tokens, dim)
    whole = pl.BlockSpec(memory_space=pltpu.VMEM)
    return call(
        pack_both_kernel,
        "pack_both",
        (1,),
        place,
        (in_vmem(own), in_vmem(other)),
        [whole] * 2,
        pltpu.VMEM(out, BF16),
        whole,
        [pltpu.VMEM((tokens * heads, dim), F32)],
        10**9,
    )


def folded(op, x):
    while x.shape[0] > 8:
        half = x.shape[0] // 2
        x = op(x[:half], x[half:])
    reduce = jnp.max if op is jnp.maximum else jnp.sum
    return reduce(x, axis=0, keepdims=True)


def first_allowed(lengths_ref, query_pos, window_start):
    def step(d, carry):
        start, first = carry
        first = jnp.where(query_pos + window_start >= start, start, first)
        return start + lengths_ref[d], first

    zero = jnp.zeros(query_pos.shape, jnp.int32)
    _, first = lax.fori_loop(0, lengths_ref.shape[0], step, (jnp.int32(0), zero))
    return first - window_start


def window_of(pair_refs, scr):
    halo = len(pair_refs) - 1
    for back, ref in enumerate(pair_refs):
        scr[pl.ds(2 * (halo - back), 2)] = ref[0]


def on_diagonal(tokens, copies):
    row = lax.broadcasted_iota(jnp.int32, (tokens, tokens), 0)
    lane = lax.broadcasted_iota(jnp.int32, (tokens, tokens), 1)
    return jnp.concatenate([row] * copies, axis=1), jnp.concatenate([lane] * copies, axis=1)


def store_tiles(ref, e, at, tiles, diagonal):
    tokens, pair = diagonal.shape
    lanes = slice(at, at + pair)
    shared = tiles[0].astype(F32)
    ref[0, e, :tokens, lanes] = jnp.where(diagonal, 0.0, shared).astype(BF16)
    for j, tile in enumerate(tiles[1:], 1):
        ref[0, e, j * tokens : (j + 1) * tokens, lanes] = tile.astype(BF16)
    ref[0, e, -tokens:, lanes] = jnp.where(diagonal, shared, 0.0).astype(BF16)


def prob_kernel(halo, place_ref, lengths_ref, qd_ref, *refs):
    k_refs = refs[: halo + 1]
    p_ref = refs[halo + 1]
    dv_refs = refs[halo + 2 : -3]
    k_scr, acc, bias = refs[-3:]
    _, _, _, group, tokens, dim = qd_ref.shape
    count = 2 * halo + 1
    pair = HEADS_AT_ONCE * tokens
    row, lane = on_diagonal(tokens, HEADS_AT_ONCE)
    diagonal = row <= lane

    @pl.when(pl.program_id(0) == 0)
    def _():
        for e in range(2):
            query_pos = lane[:1] + (2 * halo + e) * tokens
            first = first_allowed(lengths_ref, query_pos, place_ref[1]) - row
            last = (e + count - 1) * tokens
            bias[e, 0] = jnp.where(first <= jnp.where(diagonal, last, e * tokens), 0.0, MASKED)
            for j in range(1, count - 1):
                bias[e, j] = jnp.where(first <= (e + j) * tokens, 0.0, MASKED)

    window_of(k_refs, k_scr)
    for e in range(2):
        k = k_scr[pl.ds(e, count)].reshape(count * tokens, dim)
        q = qd_ref[0, e, 0].reshape(group * tokens, dim)
        do = qd_ref[0, e, 1].reshape(group * tokens, dim)
        for at in range(0, group * tokens, pair):
            s = lax.dot_general(k, q[at : at + pair], NT, preferred_element_type=F32)
            tiles = [s[j * tokens : (j + 1) * tokens] for j in range(count)]
            tiles[0] = jnp.where(diagonal, tiles.pop(), tiles[0])
            tiles = [tile + bias[e, j] for j, tile in enumerate(tiles)]
            top = folded(jnp.maximum, functools.reduce(jnp.maximum, tiles))
            tiles = [jnp.exp2((tile - top) * (dim**-0.5 * LOG2E)) for tile in tiles]
            inv = 1.0 / folded(jnp.add, functools.reduce(jnp.add, tiles))
            store_tiles(p_ref, e, at, [tile * inv for tile in tiles], diagonal)
        keep = (2 * halo - e) * tokens
        dv = jnp.dot(p_ref[0, e, :keep], do, preferred_element_type=F32).reshape(2 * halo - e, tokens, dim)
        if e == 0:
            acc[...] = dv
        else:
            acc[1:] += dv
    for back, ref in zip(range(1, halo + 1), dv_refs):
        ref[0] = acc[pl.ds(2 * (halo - back), 2)].astype(BF16)


def dscore_kernel(halo, place_ref, qd_ref, p_ref, *refs):
    v_refs = refs[: halo + 1]
    ds_ref = refs[halo + 1]
    dk_refs = refs[halo + 2 : -2]
    v_scr, acc = refs[-2:]
    _, _, _, group, tokens, dim = qd_ref.shape
    count = 2 * halo + 1
    pair = HEADS_AT_ONCE * tokens
    window_of(v_refs, v_scr)
    row, lane = on_diagonal(tokens, HEADS_AT_ONCE)
    diagonal = row <= lane
    for e in range(2):
        v = v_scr[pl.ds(e, count)].reshape(count * tokens, dim)
        q = qd_ref[0, e, 0].reshape(group * tokens, dim)
        do = qd_ref[0, e, 1].reshape(group * tokens, dim)
        for at in range(0, group * tokens, pair):
            dp = lax.dot_general(v, do[at : at + pair], NT, preferred_element_type=F32)
            dps = [dp[j * tokens : (j + 1) * tokens] for j in range(count)]
            dps[0] = jnp.where(diagonal, dps.pop(), dps[0])
            ps = [p_ref[0, e, j * tokens : (j + 1) * tokens, at : at + pair] for j in range(count)]
            ps[0] += ps.pop()
            delta = folded(jnp.add, functools.reduce(jnp.add, [p.astype(F32) * dp for p, dp in zip(ps, dps)]))
            store_tiles(ds_ref, e, at, [p * (dp - delta).astype(BF16) for p, dp in zip(ps, dps)], diagonal)
        keep = (2 * halo - e) * tokens
        dk = jnp.dot(ds_ref[0, e, :keep], q, preferred_element_type=F32).reshape(2 * halo - e, tokens, dim)
        if e == 0:
            acc[...] = dk
        else:
            acc[1:] += dk
    for back, ref in zip(range(1, halo + 1), dk_refs):
        ref[0] = (acc[pl.ds(2 * (halo - back), 2)] * dim**-0.5).astype(BF16)


def own_kernel(halo, place_ref, qd_ref, p_ref, ds_ref, *refs):
    k_refs, back_refs = refs[: halo + 1], refs[halo + 1 : 2 * halo + 1]
    dq_ref, *other_refs, dk_ref, dv_ref, k_scr, dq_scr, dv_scr, far_dv = refs[2 * halo + 1 :]
    core, head = place_ref[0], pl.program_id(0)
    _, _, _, group, tokens, dim = qd_ref.shape
    rows = dq_ref.shape[1]
    count = 2 * halo + 1
    scale = dim**-0.5
    window_of(k_refs, k_scr)
    for e in range(2):
        q = qd_ref[0, e, 0].reshape(group * tokens, dim)
        do = qd_ref[0, e, 1].reshape(group * tokens, dim)
        k = k_scr[pl.ds(e, count)].reshape(count * tokens, dim)
        dqt = jnp.dot(k.T, ds_ref[0, e], preferred_element_type=F32) * scale
        for g in range(group):
            dq_scr[e, pl.ds(head * group + g, tokens, stride=rows), :] = dqt[:, g * tokens : (g + 1) * tokens].T
        keep = (2 * halo - e) * tokens
        dk = jnp.dot(ds_ref[0, e, keep:], q, preferred_element_type=F32) * scale
        dv = jnp.dot(p_ref[0, e, keep:], do, preferred_element_type=F32)
        if e == 0:
            dk_ref[0, 0], dv_scr[0] = dk, dv
        else:
            dk_ref[0, 0] += dk[:tokens]
            dv_scr[0] += dv[:tokens]
            dk_ref[0, 1], dv_scr[1] = dk[tokens:], dv[tokens:]
    for ref in back_refs:
        dv_scr[...] += ref[0].astype(F32)
    dv_ref[0] = dv_scr[core].astype(BF16)
    far_dv[pl.ds(pl.multiple_of(head * tokens, tokens), tokens)] = dv_scr[1 - core].astype(BF16)

    @pl.when(head == pl.num_programs(0) - 1)
    def _():
        dq_ref[...] = dq_scr[core].astype(BF16).reshape(dq_ref.shape)
        dq_rows, start = tokens * rows, 0
        for ref in other_refs:
            part = ref.shape[0] * rows
            here = min(part, dq_rows - start)
            ref[: here // rows] = dq_scr[1 - core, start : start + here].astype(BF16).reshape(-1, rows, dim)
            if here < part:
                ref[here // rows :] = far_dv[...].reshape(-1, rows, dim)
            start += part


def sum_kernel(count, place_ref, own_ref, *refs):
    back_refs, (mine_ref, other_ref) = refs[:count], refs[-2:]
    core = place_ref[0]
    for block, ref in [(1 - core, other_ref), (core, mine_ref)]:
        total = own_ref[:, block]
        for back in back_refs:
            total += back[:, block].astype(F32)
        ref[...] = total.astype(BF16)


def summed(place, own, backs, before):
    half, _, tokens, dim = own.shape
    pair_spec = pl.BlockSpec(own.shape, lambda i, place: (0, 0, 0, 0))
    one = (half, tokens, dim)
    return call(
        functools.partial(sum_kernel, len(backs)),
        "sum_dk",
        (1,),
        place,
        (own, *backs, *(in_hbm(x) for x in before)),
        [pair_spec] * (1 + len(backs)) + [pl.BlockSpec(memory_space=pltpu.HBM)] * len(before),
        [jax.ShapeDtypeStruct(one, BF16)] * 2,
        [pl.BlockSpec(one, lambda i, place: (0, 0, 0))] * 2,
        [],
        0,
    )


def merge_half(core, own_ref, other, out_ref, scr):
    rows, heads, dim = out_ref.shape
    half = heads // 2
    skip = other.shape[0] - half * rows
    for h in range(half):
        scr[pl.ds(core * half + h, rows, stride=heads), :] = own_ref[h].astype(F32)
        rest = other[skip + h * rows : skip + (h + 1) * rows]
        scr[pl.ds((1 - core) * half + h, rows, stride=heads), :] = rest.astype(F32)
    out_ref[...] = scr[...].astype(BF16).reshape(rows, heads, dim)


def join_kernel(parts, place_ref, dq_ref, dv_ref, *refs):
    others, (dq_out, dv_out, scr, sems) = refs[:parts], refs[parts:]
    core = place_ref[0]
    tokens, half, dim = dq_ref.shape
    at = pl.multiple_of(core * half, half)
    copies = [pltpu.make_async_copy(dq_ref, dq_out.at[:, pl.ds(at, half)], sems.at[0])]
    at = pl.multiple_of((1 - core) * half, half)
    first = 0
    for i, part in enumerate(others):
        count = min(part.shape[0], tokens - first)
        to = dq_out.at[pl.ds(first, count), pl.ds(at, half)]
        copies.append(pltpu.make_async_copy(part.at[pl.ds(0, count)], to, sems.at[1 + i]))
        first += count
    for copy in copies:
        copy.start()
    merge_half(core, dv_ref, others[-1][...].reshape(-1, dim), dv_out, scr)
    for copy in copies:
        copy.wait()


def join(place, dq, dv, others):
    tokens, half, dim = dq.shape
    out = (tokens, 2 * dv.shape[0], dim)
    vmem = pl.BlockSpec(memory_space=pltpu.VMEM)
    parts = len(others)
    return call(
        functools.partial(join_kernel, parts),
        "join",
        (1,),
        place,
        [in_vmem(x) for x in (dq, dv, *others)],
        [vmem] * (2 + parts),
        [jax.ShapeDtypeStruct((tokens, 2 * half, dim), BF16), jax.ShapeDtypeStruct(out, BF16)],
        [pl.BlockSpec(memory_space=pl.ANY), pl.BlockSpec(out, lambda i, place: (0, 0, 0))],
        [pltpu.VMEM((tokens * out[1], dim), F32), pltpu.SemaphoreType.DMA((1 + parts,))],
        0,
    )


def merge_kernel(place_ref, own_ref, other_ref, out_ref, scr):
    merge_half(place_ref[0], own_ref, other_ref[...].reshape(-1, own_ref.shape[2]), out_ref, scr)


def merge(place, own, other, name):
    half, tokens, dim = own.shape
    out = (tokens, 2 * half, dim)
    vmem = pl.BlockSpec(memory_space=pltpu.VMEM)
    return call(
        merge_kernel,
        name,
        (1,),
        place,
        (in_vmem(own), in_vmem(other)),
        [vmem] * 2,
        jax.ShapeDtypeStruct(out, BF16),
        pl.BlockSpec(out, lambda i, place: (0, 0, 0)),
        [pltpu.VMEM((tokens * 2 * half, dim), F32)],
        0,
    )


def local(queries, keys, values, grad_out, doc_lengths):
    uly_count = lax.axis_size("uly")
    device_count = lax.axis_size("ctx") * uly_count
    halo = uly_count // 2
    device = lax.axis_index("ctx") * uly_count + lax.axis_index("uly")
    core = device % 2
    tokens, heads, dim = queries.shape
    key_heads = keys.shape[1]
    group = heads // key_heads
    half = key_heads // 2
    window, count = 2 * halo + 2, 2 * halo + 1
    place = jnp.stack([core, (device // 2 - halo) * (2 * tokens)]).astype(jnp.int32)

    far_first = range(halo, 0, -1)
    k_other = swapped(keys, device_count)
    k_mine, v_mine = fetch(place, keys, (values,))
    k_own = pack_other(place, k_other, k_mine)
    k_own, queries, grad_out, v_mine = lax.optimization_barrier((k_own, queries, grad_out, v_mine))
    q_other, do_other, v_other = (swapped(x, device_count) for x in (queries, grad_out, v_mine))
    qd = arrange(place, queries, grad_out, q_other, do_other, key_heads)
    qd, v_mine, v_other = lax.optimization_barrier((qd, v_mine, v_other))
    v_own = pack_both(place, v_mine, v_other)

    def halo_of(own, ring):
        received = {back: moved(own, device_count, 2 * back, ring) for back in far_first}
        return [own] + [received[back] for back in range(1, halo + 1)]

    def sent_back(partials, ring):
        return [moved(partials[back - 1], device_count, -2 * back, ring) for back in far_first]

    def per_head(*shape):
        return pl.BlockSpec((1,) + shape, lambda h, *_: (h,) + (0,) * len(shape))

    qd_spec = per_head(2, 2, group, tokens, dim)
    p_spec = per_head(2, count * tokens, group * tokens)
    p_shape = pltpu.VMEM((half, 2, count * tokens, group * tokens), BF16)
    pair_spec = per_head(2, tokens, dim)
    pair = (half, 2, tokens, dim)
    one_spec = per_head(tokens, dim)
    one_shape = jax.ShapeDtypeStruct((half, tokens, dim), BF16)
    dq_shape = jax.ShapeDtypeStruct((tokens, heads // 2, dim), BF16)
    dq_spec = pl.BlockSpec(dq_shape.shape, lambda h, *_: (0, 0, 0))
    far_rows = tokens + half * tokens // (heads // 2)
    step = (far_rows // 3 + 7) // 8 * 8
    parts = [
        jax.ShapeDtypeStruct((rows, heads // 2, dim), BF16) for rows in (step, step, far_rows - 2 * step)
    ]
    part_specs = [pl.BlockSpec(part.shape, lambda h, *_: (0, 0, 0)) for part in parts]
    run = pltpu.VMEM((window, tokens, dim), BF16)
    acc = pltpu.VMEM((2 * halo, tokens, dim), F32)
    product = 2 * half * 2 * count * tokens * group * tokens * dim

    k_pairs = halo_of(k_own, ring=True)
    k_pairs[-1], v_own = lax.optimization_barrier((k_pairs[-1], v_own))
    v_pairs = halo_of(v_own, ring=True)
    prob, *dv_halo = call(
        functools.partial(prob_kernel, halo),
        "prob",
        (half,),
        (place, doc_lengths),
        (in_vmem(qd), *k_pairs),
        [qd_spec] + [pair_spec] * (halo + 1),
        [p_shape] + [jax.ShapeDtypeStruct(pair, BF16)] * halo,
        [p_spec] + [pair_spec] * halo,
        [run, acc, pltpu.VMEM((2, count - 1, tokens, HEADS_AT_ONCE * tokens), F32)],
        4 * product,
    )
    dv_back = sent_back(dv_halo, ring=False)
    dscore, *dk_halo = call(
        functools.partial(dscore_kernel, halo),
        "dscore",
        (half,),
        place,
        (in_vmem(qd), in_vmem(prob), *v_pairs),
        [qd_spec, p_spec] + [pair_spec] * (halo + 1),
        [p_shape] + [jax.ShapeDtypeStruct(pair, BF16)] * halo,
        [p_spec] + [pair_spec] * halo,
        [run, acc],
        4 * product,
    )
    dk_back = sent_back(dk_halo, ring=True)
    dq, *others, dk_own, dv = call(
        functools.partial(own_kernel, halo),
        "own",
        (half,),
        place,
        (in_vmem(qd), in_vmem(prob), in_vmem(dscore), *k_pairs, *dv_back),
        [qd_spec, p_spec, p_spec] + [pair_spec] * (2 * halo + 1),
        [dq_shape, *parts, jax.ShapeDtypeStruct(pair, F32), one_shape],
        [dq_spec, *part_specs, pair_spec, one_spec],
        [
            run,
            pltpu.VMEM((2, tokens * heads // 2, dim), F32),
            pltpu.VMEM((2, tokens, dim), F32),
            pltpu.VMEM((half * tokens, dim), BF16),
        ],
        0,
    )
    others = [swapped(part, device_count) for part in others]
    grad_queries, grad_values = join(place, dq, dv, others)
    dk, dk_other = summed(place, dk_own, dk_back, (grad_queries, grad_values))
    grad_keys = merge(place, dk, swapped(dk_other, device_count), "merge_dk")
    return grad_queries, grad_keys, grad_values


def solution(mesh):
    spec = P(AXES, None, None)
    return jax.shard_map(
        local, mesh=mesh, in_specs=(spec,) * 4 + (P(),), out_specs=(spec,) * 3, check_vma=False
    )
```

```python
import functools

import jax
import jax.numpy as jnp
from jax import lax
from jax.experimental import pallas as pl
from jax.experimental.pallas import tpu as pltpu
from jax.sharding import PartitionSpec as P

AXES = ("ctx", "uly")
MASKED = -1e30
LOG2E = 1.4426950408889634
HEADS_AT_ONCE = 2
BF16, F32 = jnp.bfloat16, jnp.float32
NT = (((1,), (1,)), ((), ()))
VMEM_BYTES = 16 * 2**20


def moved(array, device_count, by, ring):
    pairs = [(d, d + by) for d in range(device_count)]
    if ring:
        return lax.ppermute(array, AXES, [(d, to % device_count) for d, to in pairs])
    return lax.ppermute(array, AXES, [(d, to) for d, to in pairs if 0 <= to < device_count])


def swapped(array, device_count):
    return lax.ppermute(array, AXES, [(d, d ^ 1) for d in range(device_count)])


def in_vmem(array):
    return pltpu.with_memory_space_constraint(array, pltpu.VMEM)


def in_hbm(array):
    return pltpu.with_memory_space_constraint(array, pltpu.HBM)


def call(kernel, name, grid, place, inputs, in_specs, outs, out_specs, scratch, flops, aliases={}):
    scalars = place if isinstance(place, tuple) else (place,)
    return pl.pallas_call(
        kernel,
        out_shape=outs,
        grid_spec=pltpu.PrefetchScalarGridSpec(
            num_scalar_prefetch=len(scalars),
            grid=grid,
            in_specs=in_specs,
            out_specs=out_specs,
            scratch_shapes=scratch,
        ),
        compiler_params=pltpu.CompilerParams(vmem_limit_bytes=VMEM_BYTES),
        cost_estimate=pl.CostEstimate(flops=flops, bytes_accessed=0, transcendentals=0),
        input_output_aliases=aliases,
        name=name,
    )(*scalars, *inputs)


def arrange_kernel(group, place_ref, q_ref, do_ref, q_other_ref, do_other_ref, out_ref, scr):
    core = place_ref[0]
    tokens, heads, dim = q_ref.shape
    half = heads // 2
    mine = pl.ds(pl.multiple_of(core * half, half), half)
    turn = 0
    for kind, (own, other) in enumerate([(q_ref, q_other_ref), (do_ref, do_other_ref)]):
        for which, ref in enumerate([own, other]):
            block = 1 - core if which else core
            wide = scr.at[turn % 2]
            wide[...] = ref[:, mine].astype(F32).reshape(tokens * half, dim)
            for h in range(half):
                out_ref[h // group, block, kind, h % group] = wide[pl.ds(h, tokens, stride=half), :].astype(BF16)
            turn += 1


def arrange(place, queries, grad_out, q_other, do_other, key_heads):
    tokens, heads, dim = queries.shape
    half, group = heads // 2, heads // key_heads
    whole = pl.BlockSpec(memory_space=pltpu.VMEM)
    return call(
        functools.partial(arrange_kernel, group),
        "arrange",
        (1,),
        place,
        [in_vmem(x) for x in (queries, grad_out, q_other, do_other)],
        [whole] * 4,
        pltpu.VMEM((key_heads // 2, 2, 2, group, tokens, dim), BF16),
        whole,
        [pltpu.VMEM((2, tokens * half, dim), F32)],
        10**9,
    )


def pack_block(raw, core, block, out_ref, scr):
    tokens, heads, dim = raw.shape
    half = heads // 2
    scr[...] = raw[...].astype(F32).reshape(tokens * heads, dim)
    for h in range(half):
        out_ref[h, block] = scr[pl.ds(core * half + h, tokens, stride=heads), :].astype(BF16)


def fetch_kernel(place_ref, key_ref, *refs):
    count = (len(refs) - 4) // 2
    sources, out_ref, targets = refs[:count], refs[count], refs[count + 1 : 2 * count + 1]
    raw, scr, sems = refs[-3:]
    first = pltpu.make_async_copy(key_ref, raw, sems.at[0])
    first.start()
    copies = [pltpu.make_async_copy(s, t, sems.at[i + 1]) for i, (s, t) in enumerate(zip(sources, targets))]
    for copy in copies:
        copy.start()
    first.wait()
    pack_block(raw, place_ref[0], place_ref[0], out_ref, scr)
    for copy in copies:
        copy.wait()


def fetch(place, keys, arrays):
    tokens, heads, dim = keys.shape
    out = (heads // 2, 2, tokens, dim)
    return call(
        fetch_kernel,
        "fetch",
        (1,),
        place,
        [in_hbm(x) for x in (keys, *arrays)],
        [pl.BlockSpec(memory_space=pltpu.HBM)] * (1 + len(arrays)),
        [pltpu.VMEM(out, BF16)] + [pltpu.VMEM(x.shape, x.dtype) for x in arrays],
        [pl.BlockSpec(memory_space=pltpu.VMEM)] * (1 + len(arrays)),
        [
            pltpu.VMEM(keys.shape, BF16),
            pltpu.VMEM((tokens * heads, dim), F32),
            pltpu.SemaphoreType.DMA((1 + len(arrays),)),
        ],
        10**9,
    )


def pack_other_kernel(place_ref, other_ref, _, out_ref, scr):
    pack_block(other_ref, place_ref[0], 1 - place_ref[0], out_ref, scr)


def pack_other(place, other, packed):
    tokens, heads, dim = other.shape
    whole = pl.BlockSpec(memory_space=pltpu.VMEM)
    return call(
        pack_other_kernel,
        "pack_other",
        (1,),
        place,
        (in_vmem(other), in_vmem(packed)),
        [whole] * 2,
        pltpu.VMEM(packed.shape, BF16),
        whole,
        [pltpu.VMEM((tokens * heads, dim), F32)],
        10**9,
        {2: 0},
    )


def pack_both_kernel(place_ref, own_ref, other_ref, out_ref, scr):
    core = place_ref[0]
    pack_block(own_ref, core, core, out_ref, scr)
    pack_block(other_ref, core, 1 - core, out_ref, scr)


def pack_both(place, own, other):
    tokens, heads, dim = own.shape
    out = (heads // 2, 2, tokens, dim)
    whole = pl.BlockSpec(memory_space=pltpu.VMEM)
    return call(
        pack_both_kernel,
        "pack_both",
        (1,),
        place,
        (in_vmem(own), in_vmem(other)),
        [whole] * 2,
        pltpu.VMEM(out, BF16),
        whole,
        [pltpu.VMEM((tokens * heads, dim), F32)],
        10**9,
    )


def folded(op, x):
    while x.shape[0] > 8:
        half = x.shape[0] // 2
        x = op(x[:half], x[half:])
    reduce = jnp.max if op is jnp.maximum else jnp.sum
    return reduce(x, axis=0, keepdims=True)


def first_allowed(lengths_ref, query_pos, window_start):
    def step(d, carry):
        start, first = carry
        first = jnp.where(query_pos + window_start >= start, start, first)
        return start + lengths_ref[d], first

    zero = jnp.zeros(query_pos.shape, jnp.int32)
    _, first = lax.fori_loop(0, lengths_ref.shape[0], step, (jnp.int32(0), zero))
    return first - window_start


def window_of(pair_refs, scr):
    halo = len(pair_refs) - 1
    for back, ref in enumerate(pair_refs):
        scr[pl.ds(2 * (halo - back), 2)] = ref[0]


def on_diagonal(tokens, copies):
    row = lax.broadcasted_iota(jnp.int32, (tokens, tokens), 0)
    lane = lax.broadcasted_iota(jnp.int32, (tokens, tokens), 1)
    return jnp.concatenate([row] * copies, axis=1), jnp.concatenate([lane] * copies, axis=1)


def store_tiles(ref, e, at, tiles, diagonal):
    tokens, pair = diagonal.shape
    lanes = slice(at, at + pair)
    shared = tiles[0].astype(F32)
    ref[0, e, :tokens, lanes] = jnp.where(diagonal, 0.0, shared).astype(BF16)
    for j, tile in enumerate(tiles[1:], 1):
        ref[0, e, j * tokens : (j + 1) * tokens, lanes] = tile.astype(BF16)
    ref[0, e, -tokens:, lanes] = jnp.where(diagonal, shared, 0.0).astype(BF16)


def prob_kernel(halo, place_ref, lengths_ref, qd_ref, *refs):
    k_refs = refs[: halo + 1]
    p_ref = refs[halo + 1]
    dv_refs = refs[halo + 2 : -3]
    k_scr, acc, bias = refs[-3:]
    _, _, _, group, tokens, dim = qd_ref.shape
    count = 2 * halo + 1
    pair = HEADS_AT_ONCE * tokens
    row, lane = on_diagonal(tokens, HEADS_AT_ONCE)
    diagonal = row <= lane

    @pl.when(pl.program_id(0) == 0)
    def _():
        for e in range(2):
            query_pos = lane[:1] + (2 * halo + e) * tokens
            first = first_allowed(lengths_ref, query_pos, place_ref[1]) - row
            last = (e + count - 1) * tokens
            bias[e, 0] = jnp.where(first <= jnp.where(diagonal, last, e * tokens), 0.0, MASKED)
            for j in range(1, count - 1):
                bias[e, j] = jnp.where(first <= (e + j) * tokens, 0.0, MASKED)

    window_of(k_refs, k_scr)
    for e in range(2):
        k = k_scr[pl.ds(e, count)].reshape(count * tokens, dim)
        q = qd_ref[0, e, 0].reshape(group * tokens, dim)
        do = qd_ref[0, e, 1].reshape(group * tokens, dim)
        for at in range(0, group * tokens, pair):
            s = lax.dot_general(k, q[at : at + pair], NT, preferred_element_type=F32)
            tiles = [s[j * tokens : (j + 1) * tokens] for j in range(count)]
            tiles[0] = jnp.where(diagonal, tiles.pop(), tiles[0])
            tiles = [tile + bias[e, j] for j, tile in enumerate(tiles)]
            top = folded(jnp.maximum, functools.reduce(jnp.maximum, tiles))
            tiles = [jnp.exp2((tile - top) * (dim**-0.5 * LOG2E)) for tile in tiles]
            inv = 1.0 / folded(jnp.add, functools.reduce(jnp.add, tiles))
            store_tiles(p_ref, e, at, [tile * inv for tile in tiles], diagonal)
        keep = (2 * halo - e) * tokens
        dv = jnp.dot(p_ref[0, e, :keep], do, preferred_element_type=F32).reshape(2 * halo - e, tokens, dim)
        if e == 0:
            acc[...] = dv
        else:
            acc[1:] += dv
    for back, ref in zip(range(1, halo + 1), dv_refs):
        ref[0] = acc[pl.ds(2 * (halo - back), 2)].astype(BF16)


def dscore_kernel(halo, place_ref, qd_ref, p_ref, *refs):
    v_refs = refs[: halo + 1]
    ds_ref = refs[halo + 1]
    dk_refs = refs[halo + 2 : -2]
    v_scr, acc = refs[-2:]
    _, _, _, group, tokens, dim = qd_ref.shape
    count = 2 * halo + 1
    pair = HEADS_AT_ONCE * tokens
    window_of(v_refs, v_scr)
    row, lane = on_diagonal(tokens, HEADS_AT_ONCE)
    diagonal = row <= lane
    for e in range(2):
        v = v_scr[pl.ds(e, count)].reshape(count * tokens, dim)
        q = qd_ref[0, e, 0].reshape(group * tokens, dim)
        do = qd_ref[0, e, 1].reshape(group * tokens, dim)
        for at in range(0, group * tokens, pair):
            dp = lax.dot_general(v, do[at : at + pair], NT, preferred_element_type=F32)
            dps = [dp[j * tokens : (j + 1) * tokens] for j in range(count)]
            dps[0] = jnp.where(diagonal, dps.pop(), dps[0])
            ps = [p_ref[0, e, j * tokens : (j + 1) * tokens, at : at + pair] for j in range(count)]
            ps[0] += ps.pop()
            delta = folded(jnp.add, functools.reduce(jnp.add, [p.astype(F32) * dp for p, dp in zip(ps, dps)]))
            store_tiles(ds_ref, e, at, [p * (dp - delta).astype(BF16) for p, dp in zip(ps, dps)], diagonal)
        keep = (2 * halo - e) * tokens
        dk = jnp.dot(ds_ref[0, e, :keep], q, preferred_element_type=F32).reshape(2 * halo - e, tokens, dim)
        if e == 0:
            acc[...] = dk
        else:
            acc[1:] += dk
    for back, ref in zip(range(1, halo + 1), dk_refs):
        ref[0] = (acc[pl.ds(2 * (halo - back), 2)] * dim**-0.5).astype(BF16)


def own_kernel(halo, place_ref, qd_ref, p_ref, ds_ref, *refs):
    k_refs, back_refs = refs[: halo + 1], refs[halo + 1 : 2 * halo + 1]
    dq_ref, *other_refs, dk_ref, dv_ref, k_scr, dq_scr, dv_scr, far_dv = refs[2 * halo + 1 :]
    core, head = place_ref[0], pl.program_id(0)
    _, _, _, group, tokens, dim = qd_ref.shape
    rows = dq_ref.shape[1]
    count = 2 * halo + 1
    scale = dim**-0.5
    window_of(k_refs, k_scr)
    for e in range(2):
        q = qd_ref[0, e, 0].reshape(group * tokens, dim)
        do = qd_ref[0, e, 1].reshape(group * tokens, dim)
        k = k_scr[pl.ds(e, count)].reshape(count * tokens, dim)
        dqt = jnp.dot(k.T, ds_ref[0, e], preferred_element_type=F32) * scale
        for g in range(group):
            dq_scr[e, pl.ds(head * group + g, tokens, stride=rows), :] = dqt[:, g * tokens : (g + 1) * tokens].T
        keep = (2 * halo - e) * tokens
        dk = jnp.dot(ds_ref[0, e, keep:], q, preferred_element_type=F32) * scale
        dv = jnp.dot(p_ref[0, e, keep:], do, preferred_element_type=F32)
        if e == 0:
            dk_ref[0, 0], dv_scr[0] = dk, dv
        else:
            dk_ref[0, 0] += dk[:tokens]
            dv_scr[0] += dv[:tokens]
            dk_ref[0, 1], dv_scr[1] = dk[tokens:], dv[tokens:]
    for ref in back_refs:
        dv_scr[...] += ref[0].astype(F32)
    dv_ref[0] = dv_scr[core].astype(BF16)
    far_dv[pl.ds(pl.multiple_of(head * tokens, tokens), tokens)] = dv_scr[1 - core].astype(BF16)

    @pl.when(head == pl.num_programs(0) - 1)
    def _():
        dq_ref[...] = dq_scr[core].astype(BF16).reshape(dq_ref.shape)
        dq_rows, start = tokens * rows, 0
        for ref in other_refs:
            part = ref.shape[0] * rows
            here = min(part, dq_rows - start)
            ref[: here // rows] = dq_scr[1 - core, start : start + here].astype(BF16).reshape(-1, rows, dim)
            if here < part:
                ref[here // rows :] = far_dv[...].reshape(-1, rows, dim)
            start += part


def sum_kernel(count, place_ref, own_ref, *refs):
    back_refs, (mine_ref, other_ref) = refs[:count], refs[-2:]
    core = place_ref[0]
    for block, ref in [(1 - core, other_ref), (core, mine_ref)]:
        total = own_ref[:, block]
        for back in back_refs:
            total += back[:, block].astype(F32)
        ref[...] = total.astype(BF16)


def summed(place, own, backs, before):
    half, _, tokens, dim = own.shape
    pair_spec = pl.BlockSpec(own.shape, lambda i, place: (0, 0, 0, 0))
    one = (half, tokens, dim)
    return call(
        functools.partial(sum_kernel, len(backs)),
        "sum_dk",
        (1,),
        place,
        (own, *backs, *(in_hbm(x) for x in before)),
        [pair_spec] * (1 + len(backs)) + [pl.BlockSpec(memory_space=pltpu.HBM)] * len(before),
        [jax.ShapeDtypeStruct(one, BF16)] * 2,
        [pl.BlockSpec(one, lambda i, place: (0, 0, 0))] * 2,
        [],
        0,
    )


def merge_half(core, own_ref, other, out_ref, scr):
    rows, heads, dim = out_ref.shape
    half = heads // 2
    skip = other.shape[0] - half * rows
    for h in range(half):
        scr[pl.ds(core * half + h, rows, stride=heads), :] = own_ref[h].astype(F32)
        rest = other[skip + h * rows : skip + (h + 1) * rows]
        scr[pl.ds((1 - core) * half + h, rows, stride=heads), :] = rest.astype(F32)
    out_ref[...] = scr[...].astype(BF16).reshape(rows, heads, dim)


def join_kernel(parts, place_ref, dq_ref, dv_ref, *refs):
    others, (dq_out, dv_out, scr, sems) = refs[:parts], refs[parts:]
    core = place_ref[0]
    tokens, half, dim = dq_ref.shape
    at = pl.multiple_of(core * half, half)
    copies = [pltpu.make_async_copy(dq_ref, dq_out.at[:, pl.ds(at, half)], sems.at[0])]
    at = pl.multiple_of((1 - core) * half, half)
    first = 0
    for i, part in enumerate(others):
        count = min(part.shape[0], tokens - first)
        to = dq_out.at[pl.ds(first, count), pl.ds(at, half)]
        copies.append(pltpu.make_async_copy(part.at[pl.ds(0, count)], to, sems.at[1 + i]))
        first += count
    for copy in copies:
        copy.start()
    merge_half(core, dv_ref, others[-1][...].reshape(-1, dim), dv_out, scr)
    for copy in copies:
        copy.wait()


def join(place, dq, dv, others):
    tokens, half, dim = dq.shape
    out = (tokens, 2 * dv.shape[0], dim)
    vmem = pl.BlockSpec(memory_space=pltpu.VMEM)
    parts = len(others)
    return call(
        functools.partial(join_kernel, parts),
        "join",
        (1,),
        place,
        [in_vmem(x) for x in (dq, dv, *others)],
        [vmem] * (2 + parts),
        [jax.ShapeDtypeStruct((tokens, 2 * half, dim), BF16), jax.ShapeDtypeStruct(out, BF16)],
        [pl.BlockSpec(memory_space=pl.ANY), pl.BlockSpec(out, lambda i, place: (0, 0, 0))],
        [pltpu.VMEM((tokens * out[1], dim), F32), pltpu.SemaphoreType.DMA((1 + parts,))],
        0,
    )


def merge_kernel(place_ref, own_ref, other_ref, out_ref, scr):
    merge_half(place_ref[0], own_ref, other_ref[...].reshape(-1, own_ref.shape[2]), out_ref, scr)


def merge(place, own, other, name):
    half, tokens, dim = own.shape
    out = (tokens, 2 * half, dim)
    vmem = pl.BlockSpec(memory_space=pltpu.VMEM)
    return call(
        merge_kernel,
        name,
        (1,),
        place,
        (in_vmem(own), in_vmem(other)),
        [vmem] * 2,
        jax.ShapeDtypeStruct(out, BF16),
        pl.BlockSpec(out, lambda i, place: (0, 0, 0)),
        [pltpu.VMEM((tokens * 2 * half, dim), F32)],
        0,
    )


def local(queries, keys, values, grad_out, doc_lengths):
    uly_count = lax.axis_size("uly")
    device_count = lax.axis_size("ctx") * uly_count
    halo = uly_count // 2
    device = lax.axis_index("ctx") * uly_count + lax.axis_index("uly")
    core = device % 2
    tokens, heads, dim = queries.shape
    key_heads = keys.shape[1]
    group = heads // key_heads
    half = key_heads // 2
    window, count = 2 * halo + 2, 2 * halo + 1
    place = jnp.stack([core, (device // 2 - halo) * (2 * tokens)]).astype(jnp.int32)

    far_first = range(halo, 0, -1)
    k_other = swapped(keys, device_count)
    k_mine, v_mine = fetch(place, keys, (values,))
    k_own = pack_other(place, k_other, k_mine)
    k_own, queries, grad_out, v_mine = lax.optimization_barrier((k_own, queries, grad_out, v_mine))
    q_other, do_other, v_other = (swapped(x, device_count) for x in (queries, grad_out, v_mine))
    qd = arrange(place, queries, grad_out, q_other, do_other, key_heads)
    qd, v_mine, v_other = lax.optimization_barrier((qd, v_mine, v_other))
    v_own = pack_both(place, v_mine, v_other)

    def halo_of(own, ring):
        received = {back: moved(own, device_count, 2 * back, ring[back == halo]) for back in far_first}
        return [own] + [received[back] for back in range(1, halo + 1)]

    def sent_back(partials, ring):
        return [moved(partials[back - 1], device_count, -2 * back, ring[back == halo]) for back in far_first]

    def per_head(*shape):
        return pl.BlockSpec((1,) + shape, lambda h, *_: (h,) + (0,) * len(shape))

    qd_spec = per_head(2, 2, group, tokens, dim)
    p_spec = per_head(2, count * tokens, group * tokens)
    p_shape = pltpu.VMEM((half, 2, count * tokens, group * tokens), BF16)
    pair_spec = per_head(2, tokens, dim)
    pair = (half, 2, tokens, dim)
    one_spec = per_head(tokens, dim)
    one_shape = jax.ShapeDtypeStruct((half, tokens, dim), BF16)
    dq_shape = jax.ShapeDtypeStruct((tokens, heads // 2, dim), BF16)
    dq_spec = pl.BlockSpec(dq_shape.shape, lambda h, *_: (0, 0, 0))
    far_rows = tokens + half * tokens // (heads // 2)
    step = (far_rows // 3 + 7) // 8 * 8
    parts = [
        jax.ShapeDtypeStruct((rows, heads // 2, dim), BF16) for rows in (step, step, far_rows - 2 * step)
    ]
    part_specs = [pl.BlockSpec(part.shape, lambda h, *_: (0, 0, 0)) for part in parts]
    run = pltpu.VMEM((window, tokens, dim), BF16)
    acc = pltpu.VMEM((2 * halo, tokens, dim), F32)
    product = 2 * half * 2 * count * tokens * group * tokens * dim

    k_pairs = halo_of(k_own, ring=(True, True))
    v_pairs = halo_of(v_own, ring=(False, False))
    prob, *dv_halo = call(
        functools.partial(prob_kernel, halo),
        "prob",
        (half,),
        (place, doc_lengths),
        (in_vmem(qd), *k_pairs),
        [qd_spec] + [pair_spec] * (halo + 1),
        [p_shape] + [jax.ShapeDtypeStruct(pair, BF16)] * halo,
        [p_spec] + [pair_spec] * halo,
        [run, acc, pltpu.VMEM((2, count - 1, tokens, HEADS_AT_ONCE * tokens), F32)],
        4 * product,
    )
    dv_back = sent_back(dv_halo, ring=(True, False))
    dscore, *dk_halo = call(
        functools.partial(dscore_kernel, halo),
        "dscore",
        (half,),
        place,
        (in_vmem(qd), in_vmem(prob), *v_pairs),
        [qd_spec, p_spec] + [pair_spec] * (halo + 1),
        [p_shape] + [jax.ShapeDtypeStruct(pair, BF16)] * halo,
        [p_spec] + [pair_spec] * halo,
        [run, acc],
        4 * product,
    )
    dk_back = sent_back(dk_halo, ring=(True, False))
    dq, *others, dk_own, dv = call(
        functools.partial(own_kernel, halo),
        "own",
        (half,),
        place,
        (in_vmem(qd), in_vmem(prob), in_vmem(dscore), *k_pairs, *dv_back),
        [qd_spec, p_spec, p_spec] + [pair_spec] * (2 * halo + 1),
        [dq_shape, *parts, jax.ShapeDtypeStruct(pair, F32), one_shape],
        [dq_spec, *part_specs, pair_spec, one_spec],
        [
            run,
            pltpu.VMEM((2, tokens * heads // 2, dim), F32),
            pltpu.VMEM((2, tokens, dim), F32),
            pltpu.VMEM((half * tokens, dim), BF16),
        ],
        0,
    )
    others = [swapped(part, device_count) for part in others]
    grad_queries, grad_values = join(place, dq, dv, others)
    dk, dk_other = summed(place, dk_own, dk_back, (grad_queries, grad_values))
    grad_keys = merge(place, dk, swapped(dk_other, device_count), "merge_dk")
    return grad_queries, grad_keys, grad_values


def solution(mesh):
    spec = P(AXES, None, None)
    return jax.shard_map(
        local, mesh=mesh, in_specs=(spec,) * 4 + (P(),), out_specs=(spec,) * 3, check_vma=False
    )
```

```python
import functools

import jax
import jax.numpy as jnp
from jax import lax
from jax.experimental import pallas as pl
from jax.experimental.pallas import tpu as pltpu
from jax.sharding import PartitionSpec as P

AXES = ("ctx", "uly")
MASKED = -1e30
LOG2E = 1.4426950408889634
HEADS_AT_ONCE = 2
BF16, F32 = jnp.bfloat16, jnp.float32
NT = (((1,), (1,)), ((), ()))
VMEM_BYTES = 16 * 2**20


def moved(array, device_count, by, ring):
    pairs = [(d, d + by) for d in range(device_count)]
    if ring:
        return lax.ppermute(array, AXES, [(d, to % device_count) for d, to in pairs])
    return lax.ppermute(array, AXES, [(d, to) for d, to in pairs if 0 <= to < device_count])


def swapped(array, device_count):
    return lax.ppermute(array, AXES, [(d, d ^ 1) for d in range(device_count)])


def in_vmem(array):
    return pltpu.with_memory_space_constraint(array, pltpu.VMEM)


def in_hbm(array):
    return pltpu.with_memory_space_constraint(array, pltpu.HBM)


def call(kernel, name, grid, place, inputs, in_specs, outs, out_specs, scratch, flops, aliases={}):
    scalars = place if isinstance(place, tuple) else (place,)
    return pl.pallas_call(
        kernel,
        out_shape=outs,
        grid_spec=pltpu.PrefetchScalarGridSpec(
            num_scalar_prefetch=len(scalars),
            grid=grid,
            in_specs=in_specs,
            out_specs=out_specs,
            scratch_shapes=scratch,
        ),
        compiler_params=pltpu.CompilerParams(vmem_limit_bytes=VMEM_BYTES),
        cost_estimate=pl.CostEstimate(flops=flops, bytes_accessed=0, transcendentals=0),
        input_output_aliases=aliases,
        name=name,
    )(*scalars, *inputs)


def arrange_kernel(group, place_ref, q_ref, do_ref, q_other_ref, do_other_ref, out_ref, scr):
    core = place_ref[0]
    tokens, heads, dim = q_ref.shape
    half = heads // 2
    mine = pl.ds(pl.multiple_of(core * half, half), half)
    turn = 0
    for kind, (own, other) in enumerate([(q_ref, q_other_ref), (do_ref, do_other_ref)]):
        for which, ref in enumerate([own, other]):
            block = 1 - core if which else core
            wide = scr.at[turn % 2]
            wide[...] = ref[:, mine].astype(F32).reshape(tokens * half, dim)
            for h in range(half):
                out_ref[h // group, block, kind, h % group] = wide[pl.ds(h, tokens, stride=half), :].astype(BF16)
            turn += 1


def arrange(place, queries, grad_out, q_other, do_other, key_heads):
    tokens, heads, dim = queries.shape
    half, group = heads // 2, heads // key_heads
    whole = pl.BlockSpec(memory_space=pltpu.VMEM)
    return call(
        functools.partial(arrange_kernel, group),
        "arrange",
        (1,),
        place,
        [in_vmem(x) for x in (queries, grad_out, q_other, do_other)],
        [whole] * 4,
        pltpu.VMEM((key_heads // 2, 2, 2, group, tokens, dim), BF16),
        whole,
        [pltpu.VMEM((2, tokens * half, dim), F32)],
        10**9,
    )


def pack_block(raw, core, block, out_ref, scr):
    tokens, heads, dim = raw.shape
    half = heads // 2
    scr[...] = raw[...].astype(F32).reshape(tokens * heads, dim)
    for h in range(half):
        out_ref[h, block] = scr[pl.ds(core * half + h, tokens, stride=heads), :].astype(BF16)


def fetch_kernel(place_ref, key_ref, *refs):
    count = (len(refs) - 4) // 2
    sources, out_ref, targets = refs[:count], refs[count], refs[count + 1 : 2 * count + 1]
    raw, scr, sems = refs[-3:]
    first = pltpu.make_async_copy(key_ref, raw, sems.at[0])
    first.start()
    copies = [pltpu.make_async_copy(s, t, sems.at[i + 1]) for i, (s, t) in enumerate(zip(sources, targets))]
    for copy in copies:
        copy.start()
    first.wait()
    pack_block(raw, place_ref[0], place_ref[0], out_ref, scr)
    for copy in copies:
        copy.wait()


def fetch(place, keys, arrays):
    tokens, heads, dim = keys.shape
    out = (heads // 2, 2, tokens, dim)
    return call(
        fetch_kernel,
        "fetch",
        (1,),
        place,
        [in_hbm(x) for x in (keys, *arrays)],
        [pl.BlockSpec(memory_space=pltpu.HBM)] * (1 + len(arrays)),
        [pltpu.VMEM(out, BF16)] + [pltpu.VMEM(x.shape, x.dtype) for x in arrays],
        [pl.BlockSpec(memory_space=pltpu.VMEM)] * (1 + len(arrays)),
        [
            pltpu.VMEM(keys.shape, BF16),
            pltpu.VMEM((tokens * heads, dim), F32),
            pltpu.SemaphoreType.DMA((1 + len(arrays),)),
        ],
        10**9,
    )


def pack_other_kernel(place_ref, other_ref, _, out_ref, scr):
    pack_block(other_ref, place_ref[0], 1 - place_ref[0], out_ref, scr)


def pack_other(place, other, packed):
    tokens, heads, dim = other.shape
    whole = pl.BlockSpec(memory_space=pltpu.VMEM)
    return call(
        pack_other_kernel,
        "pack_other",
        (1,),
        place,
        (in_vmem(other), in_vmem(packed)),
        [whole] * 2,
        pltpu.VMEM(packed.shape, BF16),
        whole,
        [pltpu.VMEM((tokens * heads, dim), F32)],
        10**9,
        {2: 0},
    )


def pack_both_kernel(place_ref, own_ref, other_ref, out_ref, scr):
    core = place_ref[0]
    pack_block(own_ref, core, core, out_ref, scr)
    pack_block(other_ref, core, 1 - core, out_ref, scr)


def pack_both(place, own, other):
    tokens, heads, dim = own.shape
    out = (heads // 2, 2, tokens, dim)
    whole = pl.BlockSpec(memory_space=pltpu.VMEM)
    return call(
        pack_both_kernel,
        "pack_both",
        (1,),
        place,
        (in_vmem(own), in_vmem(other)),
        [whole] * 2,
        pltpu.VMEM(out, BF16),
        whole,
        [pltpu.VMEM((tokens * heads, dim), F32)],
        10**9,
    )


def folded(op, x):
    while x.shape[0] > 8:
        half = x.shape[0] // 2
        x = op(x[:half], x[half:])
    reduce = jnp.max if op is jnp.maximum else jnp.sum
    return reduce(x, axis=0, keepdims=True)


def first_allowed(lengths_ref, query_pos, window_start):
    def step(d, carry):
        start, first = carry
        first = jnp.where(query_pos + window_start >= start, start, first)
        return start + lengths_ref[d], first

    zero = jnp.zeros(query_pos.shape, jnp.int32)
    _, first = lax.fori_loop(0, lengths_ref.shape[0], step, (jnp.int32(0), zero))
    return first - window_start


def window_of(pair_refs, scr):
    halo = len(pair_refs) - 1
    for back, ref in enumerate(pair_refs):
        scr[pl.ds(2 * (halo - back), 2)] = ref[0]


def on_diagonal(tokens, copies):
    row = lax.broadcasted_iota(jnp.int32, (tokens, tokens), 0)
    lane = lax.broadcasted_iota(jnp.int32, (tokens, tokens), 1)
    return jnp.concatenate([row] * copies, axis=1), jnp.concatenate([lane] * copies, axis=1)


def store_tiles(ref, e, at, tiles, diagonal):
    tokens, pair = diagonal.shape
    lanes = slice(at, at + pair)
    shared = tiles[0].astype(F32)
    ref[0, e, :tokens, lanes] = jnp.where(diagonal, 0.0, shared).astype(BF16)
    for j, tile in enumerate(tiles[1:], 1):
        ref[0, e, j * tokens : (j + 1) * tokens, lanes] = tile.astype(BF16)
    ref[0, e, -tokens:, lanes] = jnp.where(diagonal, shared, 0.0).astype(BF16)


def prob_kernel(halo, place_ref, lengths_ref, qd_ref, *refs):
    k_refs = refs[: halo + 1]
    p_ref = refs[halo + 1]
    dv_refs = refs[halo + 2 : -3]
    k_scr, acc, bias = refs[-3:]
    _, _, _, group, tokens, dim = qd_ref.shape
    count = 2 * halo + 1
    pair = HEADS_AT_ONCE * tokens
    row, lane = on_diagonal(tokens, HEADS_AT_ONCE)
    diagonal = row <= lane

    @pl.when(pl.program_id(0) == 0)
    def _():
        for e in range(2):
            query_pos = lane[:1] + (2 * halo + e) * tokens
            first = first_allowed(lengths_ref, query_pos, place_ref[1]) - row
            last = (e + count - 1) * tokens
            bias[e, 0] = jnp.where(first <= jnp.where(diagonal, last, e * tokens), 0.0, MASKED)
            for j in range(1, count - 1):
                bias[e, j] = jnp.where(first <= (e + j) * tokens, 0.0, MASKED)

    window_of(k_refs, k_scr)
    for e in range(2):
        k = k_scr[pl.ds(e, count)].reshape(count * tokens, dim)
        q = qd_ref[0, e, 0].reshape(group * tokens, dim)
        do = qd_ref[0, e, 1].reshape(group * tokens, dim)
        for at in range(0, group * tokens, pair):
            s = lax.dot_general(k, q[at : at + pair], NT, preferred_element_type=F32)
            tiles = [s[j * tokens : (j + 1) * tokens] for j in range(count)]
            tiles[0] = jnp.where(diagonal, tiles.pop(), tiles[0])
            tiles = [tile + bias[e, j] for j, tile in enumerate(tiles)]
            top = folded(jnp.maximum, functools.reduce(jnp.maximum, tiles))
            tiles = [jnp.exp2((tile - top) * (dim**-0.5 * LOG2E)) for tile in tiles]
            inv = 1.0 / folded(jnp.add, functools.reduce(jnp.add, tiles))
            store_tiles(p_ref, e, at, [tile * inv for tile in tiles], diagonal)
        keep = (2 * halo - e) * tokens
        dv = jnp.dot(p_ref[0, e, :keep], do, preferred_element_type=F32).reshape(2 * halo - e, tokens, dim)
        if e == 0:
            acc[...] = dv
        else:
            acc[1:] += dv
    for back, ref in zip(range(1, halo + 1), dv_refs):
        ref[0] = acc[pl.ds(2 * (halo - back), 2)].astype(BF16)


def dscore_kernel(halo, place_ref, qd_ref, p_ref, *refs):
    v_refs = refs[: halo + 1]
    ds_ref = refs[halo + 1]
    dk_refs = refs[halo + 2 : -2]
    v_scr, acc = refs[-2:]
    _, _, _, group, tokens, dim = qd_ref.shape
    count = 2 * halo + 1
    pair = HEADS_AT_ONCE * tokens
    window_of(v_refs, v_scr)
    row, lane = on_diagonal(tokens, HEADS_AT_ONCE)
    diagonal = row <= lane
    for e in range(2):
        v = v_scr[pl.ds(e, count)].reshape(count * tokens, dim)
        q = qd_ref[0, e, 0].reshape(group * tokens, dim)
        do = qd_ref[0, e, 1].reshape(group * tokens, dim)
        for at in range(0, group * tokens, pair):
            dp = lax.dot_general(v, do[at : at + pair], NT, preferred_element_type=F32)
            dps = [dp[j * tokens : (j + 1) * tokens] for j in range(count)]
            dps[0] = jnp.where(diagonal, dps.pop(), dps[0])
            ps = [p_ref[0, e, j * tokens : (j + 1) * tokens, at : at + pair] for j in range(count)]
            ps[0] += ps.pop()
            delta = folded(jnp.add, functools.reduce(jnp.add, [p.astype(F32) * dp for p, dp in zip(ps, dps)]))
            store_tiles(ds_ref, e, at, [p * (dp - delta).astype(BF16) for p, dp in zip(ps, dps)], diagonal)
        keep = (2 * halo - e) * tokens
        dk = jnp.dot(ds_ref[0, e, :keep], q, preferred_element_type=F32).reshape(2 * halo - e, tokens, dim)
        if e == 0:
            acc[...] = dk
        else:
            acc[1:] += dk
    for back, ref in zip(range(1, halo + 1), dk_refs):
        ref[0] = (acc[pl.ds(2 * (halo - back), 2)] * dim**-0.5).astype(BF16)


def own_kernel(halo, place_ref, qd_ref, p_ref, ds_ref, *refs):
    k_refs, back_refs = refs[: halo + 1], refs[halo + 1 : 2 * halo + 1]
    dq_ref, *other_refs, dk_ref, dv_ref, k_scr, dq_scr, dv_scr, far_dv = refs[2 * halo + 1 :]
    core, head = place_ref[0], pl.program_id(0)
    _, _, _, group, tokens, dim = qd_ref.shape
    rows = dq_ref.shape[1]
    count = 2 * halo + 1
    scale = dim**-0.5
    window_of(k_refs, k_scr)
    for e in range(2):
        q = qd_ref[0, e, 0].reshape(group * tokens, dim)
        do = qd_ref[0, e, 1].reshape(group * tokens, dim)
        k = k_scr[pl.ds(e, count)].reshape(count * tokens, dim)
        dqt = jnp.dot(k.T, ds_ref[0, e], preferred_element_type=F32) * scale
        for g in range(group):
            dq_scr[e, pl.ds(head * group + g, tokens, stride=rows), :] = dqt[:, g * tokens : (g + 1) * tokens].T
        keep = (2 * halo - e) * tokens
        dk = jnp.dot(ds_ref[0, e, keep:], q, preferred_element_type=F32) * scale
        dv = jnp.dot(p_ref[0, e, keep:], do, preferred_element_type=F32)
        if e == 0:
            dk_ref[0, 0], dv_scr[0] = dk, dv
        else:
            dk_ref[0, 0] += dk[:tokens]
            dv_scr[0] += dv[:tokens]
            dk_ref[0, 1], dv_scr[1] = dk[tokens:], dv[tokens:]
    for ref in back_refs:
        dv_scr[...] += ref[0].astype(F32)
    dv_ref[0] = dv_scr[core].astype(BF16)
    far_dv[pl.ds(pl.multiple_of(head * tokens, tokens), tokens)] = dv_scr[1 - core].astype(BF16)

    @pl.when(head == pl.num_programs(0) - 1)
    def _():
        dq_ref[...] = dq_scr[core].astype(BF16).reshape(dq_ref.shape)
        dq_rows, start = tokens * rows, 0
        for ref in other_refs:
            part = ref.shape[0] * rows
            here = min(part, dq_rows - start)
            ref[: here // rows] = dq_scr[1 - core, start : start + here].astype(BF16).reshape(-1, rows, dim)
            if here < part:
                ref[here // rows :] = far_dv[...].reshape(-1, rows, dim)
            start += part


def sum_kernel(count, place_ref, own_ref, *refs):
    back_refs, (mine_ref, other_ref) = refs[:count], refs[-2:]
    core = place_ref[0]
    for block, ref in [(1 - core, other_ref), (core, mine_ref)]:
        total = own_ref[:, block]
        for back in back_refs:
            total += back[:, block].astype(F32)
        ref[...] = total.astype(BF16)


def summed(place, own, backs, before):
    half, _, tokens, dim = own.shape
    pair_spec = pl.BlockSpec(own.shape, lambda i, place: (0, 0, 0, 0))
    one = (half, tokens, dim)
    return call(
        functools.partial(sum_kernel, len(backs)),
        "sum_dk",
        (1,),
        place,
        (own, *backs, *(in_hbm(x) for x in before)),
        [pair_spec] * (1 + len(backs)) + [pl.BlockSpec(memory_space=pltpu.HBM)] * len(before),
        [jax.ShapeDtypeStruct(one, BF16)] * 2,
        [pl.BlockSpec(one, lambda i, place: (0, 0, 0))] * 2,
        [],
        0,
    )


def merge_half(core, own_ref, other, out_ref, scr):
    rows, heads, dim = out_ref.shape
    half = heads // 2
    skip = other.shape[0] - half * rows
    for h in range(half):
        scr[pl.ds(core * half + h, rows, stride=heads), :] = own_ref[h].astype(F32)
        rest = other[skip + h * rows : skip + (h + 1) * rows]
        scr[pl.ds((1 - core) * half + h, rows, stride=heads), :] = rest.astype(F32)
    out_ref[...] = scr[...].astype(BF16).reshape(rows, heads, dim)


def join_kernel(parts, place_ref, dq_ref, dv_ref, *refs):
    others, (dq_out, dv_out, scr, sems) = refs[:parts], refs[parts:]
    core = place_ref[0]
    tokens, half, dim = dq_ref.shape
    at = pl.multiple_of(core * half, half)
    copies = [pltpu.make_async_copy(dq_ref, dq_out.at[:, pl.ds(at, half)], sems.at[0])]
    at = pl.multiple_of((1 - core) * half, half)
    first = 0
    for i, part in enumerate(others):
        count = min(part.shape[0], tokens - first)
        to = dq_out.at[pl.ds(first, count), pl.ds(at, half)]
        copies.append(pltpu.make_async_copy(part.at[pl.ds(0, count)], to, sems.at[1 + i]))
        first += count
    for copy in copies:
        copy.start()
    merge_half(core, dv_ref, others[-1][...].reshape(-1, dim), dv_out, scr)
    for copy in copies:
        copy.wait()


def join(place, dq, dv, others):
    tokens, half, dim = dq.shape
    out = (tokens, 2 * dv.shape[0], dim)
    vmem = pl.BlockSpec(memory_space=pltpu.VMEM)
    parts = len(others)
    return call(
        functools.partial(join_kernel, parts),
        "join",
        (1,),
        place,
        [in_vmem(x) for x in (dq, dv, *others)],
        [vmem] * (2 + parts),
        [jax.ShapeDtypeStruct((tokens, 2 * half, dim), BF16), jax.ShapeDtypeStruct(out, BF16)],
        [pl.BlockSpec(memory_space=pl.ANY), pl.BlockSpec(out, lambda i, place: (0, 0, 0))],
        [pltpu.VMEM((tokens * out[1], dim), F32), pltpu.SemaphoreType.DMA((1 + parts,))],
        0,
    )


def merge_kernel(place_ref, own_ref, other_ref, out_ref, scr):
    merge_half(place_ref[0], own_ref, other_ref[...].reshape(-1, own_ref.shape[2]), out_ref, scr)


def merge(place, own, other, name):
    half, tokens, dim = own.shape
    out = (tokens, 2 * half, dim)
    vmem = pl.BlockSpec(memory_space=pltpu.VMEM)
    return call(
        merge_kernel,
        name,
        (1,),
        place,
        (in_vmem(own), in_vmem(other)),
        [vmem] * 2,
        jax.ShapeDtypeStruct(out, BF16),
        pl.BlockSpec(out, lambda i, place: (0, 0, 0)),
        [pltpu.VMEM((tokens * 2 * half, dim), F32)],
        0,
    )


def local(queries, keys, values, grad_out, doc_lengths):
    uly_count = lax.axis_size("uly")
    device_count = lax.axis_size("ctx") * uly_count
    halo = uly_count // 2
    device = lax.axis_index("ctx") * uly_count + lax.axis_index("uly")
    core = device % 2
    tokens, heads, dim = queries.shape
    key_heads = keys.shape[1]
    group = heads // key_heads
    half = key_heads // 2
    window, count = 2 * halo + 2, 2 * halo + 1
    place = jnp.stack([core, (device // 2 - halo) * (2 * tokens)]).astype(jnp.int32)

    far_first = range(halo, 0, -1)
    k_other = swapped(keys, device_count)
    k_mine, v_mine = fetch(place, keys, (values,))
    k_own = pack_other(place, k_other, k_mine)
    k_own, queries, grad_out, v_mine = lax.optimization_barrier((k_own, queries, grad_out, v_mine))
    q_other, do_other, v_other = (swapped(x, device_count) for x in (queries, grad_out, v_mine))
    qd = arrange(place, queries, grad_out, q_other, do_other, key_heads)
    qd, v_mine, v_other = lax.optimization_barrier((qd, v_mine, v_other))
    v_own = pack_both(place, v_mine, v_other)

    def halo_of(own, ring):
        received = {back: moved(own, device_count, 2 * back, ring[back == halo]) for back in far_first}
        return [own] + [received[back] for back in range(1, halo + 1)]

    def sent_back(partials, ring, order):
        return [moved(partials[back - 1], device_count, -2 * back, ring[back == halo]) for back in order]

    def per_head(*shape):
        return pl.BlockSpec((1,) + shape, lambda h, *_: (h,) + (0,) * len(shape))

    qd_spec = per_head(2, 2, group, tokens, dim)
    p_spec = per_head(2, count * tokens, group * tokens)
    p_shape = pltpu.VMEM((half, 2, count * tokens, group * tokens), BF16)
    pair_spec = per_head(2, tokens, dim)
    pair = (half, 2, tokens, dim)
    one_spec = per_head(tokens, dim)
    one_shape = jax.ShapeDtypeStruct((half, tokens, dim), BF16)
    dq_shape = jax.ShapeDtypeStruct((tokens, heads // 2, dim), BF16)
    dq_spec = pl.BlockSpec(dq_shape.shape, lambda h, *_: (0, 0, 0))
    far_rows = tokens + half * tokens // (heads // 2)
    step = (far_rows // 3 + 7) // 8 * 8
    parts = [
        jax.ShapeDtypeStruct((rows, heads // 2, dim), BF16) for rows in (step, step, far_rows - 2 * step)
    ]
    part_specs = [pl.BlockSpec(part.shape, lambda h, *_: (0, 0, 0)) for part in parts]
    run = pltpu.VMEM((window, tokens, dim), BF16)
    acc = pltpu.VMEM((2 * halo, tokens, dim), F32)
    product = 2 * half * 2 * count * tokens * group * tokens * dim

    k_pairs = halo_of(k_own, ring=(True, True))
    v_pairs = halo_of(v_own, ring=(False, False))
    prob, *dv_halo = call(
        functools.partial(prob_kernel, halo),
        "prob",
        (half,),
        (place, doc_lengths),
        (in_vmem(qd), *k_pairs),
        [qd_spec] + [pair_spec] * (halo + 1),
        [p_shape] + [jax.ShapeDtypeStruct(pair, BF16)] * halo,
        [p_spec] + [pair_spec] * halo,
        [run, acc, pltpu.VMEM((2, count - 1, tokens, HEADS_AT_ONCE * tokens), F32)],
        4 * product,
    )
    dv_back = sent_back(dv_halo, (True, False), range(1, halo + 1))
    dscore, *dk_halo = call(
        functools.partial(dscore_kernel, halo),
        "dscore",
        (half,),
        place,
        (in_vmem(qd), in_vmem(prob), *v_pairs),
        [qd_spec, p_spec] + [pair_spec] * (halo + 1),
        [p_shape] + [jax.ShapeDtypeStruct(pair, BF16)] * halo,
        [p_spec] + [pair_spec] * halo,
        [run, acc],
        4 * product,
    )
    dk_back = sent_back(dk_halo, (True, False), range(1, halo + 1))
    dq, *others, dk_own, dv = call(
        functools.partial(own_kernel, halo),
        "own",
        (half,),
        place,
        (in_vmem(qd), in_vmem(prob), in_vmem(dscore), *k_pairs, *dv_back),
        [qd_spec, p_spec, p_spec] + [pair_spec] * (2 * halo + 1),
        [dq_shape, *parts, jax.ShapeDtypeStruct(pair, F32), one_shape],
        [dq_spec, *part_specs, pair_spec, one_spec],
        [
            run,
            pltpu.VMEM((2, tokens * heads // 2, dim), F32),
            pltpu.VMEM((2, tokens, dim), F32),
            pltpu.VMEM((half * tokens, dim), BF16),
        ],
        0,
    )
    others = [swapped(part, device_count) for part in others]
    grad_queries, grad_values = join(place, dq, dv, others)
    dk, dk_other = summed(place, dk_own, dk_back, (grad_queries, grad_values))
    grad_keys = merge(place, dk, swapped(dk_other, device_count), "merge_dk")
    return grad_queries, grad_keys, grad_values


def solution(mesh):
    spec = P(AXES, None, None)
    return jax.shard_map(
        local, mesh=mesh, in_specs=(spec,) * 4 + (P(),), out_specs=(spec,) * 3, check_vma=False
    )
```
